32 devices in a mesh: fsdp: 4 (over y, x), ctx: 4 (over z), tp: 2 (over core).
Axes of the slice: x: 2, y: 2, z: 4, core: 2. Of those that a mesh axis runs over, the one named last changes fastest.
Arguments:
- layer_input: float32 [8, 1024, 2048], P(None, ('fsdp', 'ctx')), may hold values from -6 to 6
- cotangent: float32 [8, 1024, 2048], P(None, ('fsdp', 'ctx')), may hold values from -6 to 6
- seq_lengths: int32 [8], replicated, may hold values from 512 to 1024, as said below
- dealing: int32 [8], replicated, may hold values from 0 to 7, each once
- attn_gain: bfloat16 [2048], P('fsdp'), may hold values from 0.5 to 1.5
- attn_shift: bfloat16 [2048], P('fsdp'), may hold values from -1 to 1
- query_weight: bfloat16 [2048, 2048], P('fsdp', 'tp')
- query_bias: bfloat16 [16, 128], P('tp', 'fsdp'), may hold values from -1.5 to 1.5
- key_weight: bfloat16 [2048, 2048], P('fsdp', 'tp'), may hold values from -0.125 to 0.125
- value_weight: bfloat16 [2048, 2048], P('fsdp', 'tp'), may hold values from -0.125 to 0.125
- value_bias: bfloat16 [16, 128], P('tp', 'fsdp'), may hold values from -0.29882812 to 0.29882812
- out_weight: bfloat16 [2048, 2048], P('tp', 'fsdp'), may hold values from -2 to 2
- out_bias: bfloat16 [2048], P('fsdp'), may hold values from -1 to 1
- mlp_gain: bfloat16 [2048], P('fsdp'), may hold values from 0.5 to 1.5
- mlp_shift: bfloat16 [2048], P('fsdp'), may hold values from -1 to 1
- up_weight: bfloat16 [2048, 8192], P('fsdp', 'tp'), may hold values from -0.125 to 0.125
- up_bias: bfloat16 [4, 2048], P('tp', 'fsdp'), may hold values from -1 to 1
- down_weight: bfloat16 [8192, 2048], P('tp', 'fsdp'), may hold values from -0.0625 to 0.0625
- down_bias: bfloat16 [2048], P('fsdp'), may hold values from -1 to 1
- clip_level: float32 [1], replicated, may hold values from 5 to 9
Outputs:
- layer_output: float32 [8, 1024, 2048], P(None, ('fsdp', 'ctx'))
- input_grad: float32 [8, 1024, 2048], P(None, ('fsdp', 'ctx'))
- attn_gain_grad: float32 [2048], P('fsdp')
- attn_shift_grad: float32 [2048], P('fsdp')
- query_weight_grad: float32 [2048, 2048], P('fsdp', 'tp')
- query_bias_grad: float32 [16, 128], P('tp', 'fsdp')
- key_weight_grad: float32 [2048, 2048], P('fsdp', 'tp')
- value_weight_grad: float32 [2048, 2048], P('fsdp', 'tp')
- value_bias_grad: float32 [16, 128], P('tp', 'fsdp')
- out_weight_grad: float32 [2048, 2048], P('tp', 'fsdp')
- out_bias_grad: float32 [2048], P('fsdp')
- mlp_gain_grad: float32 [2048], P('fsdp')
- mlp_shift_grad: float32 [2048], P('fsdp')
- up_weight_grad: float32 [2048, 8192], P('fsdp', 'tp')
- up_bias_grad: float32 [4, 2048], P('tp', 'fsdp')
- down_weight_grad: float32 [8192, 2048], P('tp', 'fsdp')
- down_bias_grad: float32 [2048], P('fsdp')
- head_peak: float32 [16], P('tp')
- query_clipped: bfloat16 [2048, 2048], P('fsdp', 'tp')
- key_clipped: bfloat16 [2048, 2048], P('fsdp', 'tp')
The draws below stay inside these ranges and needn't reach their ends.
Inputs may be any that keep to these rules, and one draw needn't show every extreme that they name: `seq_lengths`: valid tokens of each slot; its places from the length on are padding. `dealing`: a permutation of the 8 slots; dealt places j with j // 2 = g go to index g of fsdp.
All inputs are finite; a program needn't handle non-finite values.
Results may differ from the reference program's by a relative error of at most 0.019.
Values may be sent and summed in bfloat16 or wider, within the bound.
A program may use at most 320 MiB of HBM per device.

```python
import math
import jax
import jax.numpy as jnp
from jax import lax

D = 2048
H = 16
HD = 128
FF = 8192
SLOT = 1024
NSEQ = 8


def draw_seq_lengths(key, part):
    key = jax.random.fold_in(key, 3)
    first, second = jax.random.split(key)
    drawn = jax.random.randint(first, (NSEQ,), SLOT // 2, SLOT + 1)
    picks = jax.random.permutation(second, NSEQ)
    drawn = drawn.at[picks[0]].set(SLOT).at[picks[1]].set(SLOT // 2)
    return drawn.astype(jnp.int32)


def draw_query_weight(key, part):
    key = jax.random.fold_in(key, 7)
    first, second = jax.random.split(key)
    head_scale = jnp.exp(jax.random.uniform(second, (H,), jnp.float32, 0.0, 1.0986))
    base = jax.random.truncated_normal(first, -4.0, 4.0, (D, D), jnp.float32)
    column_scale = jnp.repeat(head_scale, HD)
    return (base * column_scale[None, :] * D ** (-0.5)).astype(jnp.bfloat16)


def block_scale(own_key, shape, pieces, least, top_value):
    level, own = 1.0, jax.random.fold_in(own_key, 6)
    for dim, shards_of in pieces:
        heights = jnp.exp(jax.random.uniform(jax.random.fold_in(own, dim), (shards_of,), jnp.float32, least / len(pieces), top_value / len(pieces)))
        level = level * jnp.repeat(heights, shape[dim] // shards_of).reshape([-1 if axis == dim else 1 for axis in range(len(shape))])
    return level


def centred(stream_key, extent, scale, most, shards=(), kind=jnp.bfloat16):
    values = scale * jax.random.normal(stream_key, extent, jnp.float32)
    if shards:
        values = values * block_scale(stream_key, extent, shards, -0.22, 0.18)
    return jnp.clip(values, -most, most).astype(kind)


def setup_inputs(seed: int = 0) -> dict:
    key_of = jax.random.split(jax.random.key(seed), 21)
    return {
        "layer_input": centred(key_of[0], (NSEQ, SLOT, D), 1.0, 6.0, ((1, 16),), jnp.float32),
        "cotangent": centred(key_of[1], (NSEQ, SLOT, D), 1.0, 6.0, ((1, 16),), jnp.float32),
        "seq_lengths": draw_seq_lengths(jax.random.fold_in(key_of[20], 71), 0),
        "dealing": jax.random.permutation(key_of[3], NSEQ).astype(jnp.int32),
        "attn_gain": jnp.clip(1.0 + 0.1 * jax.random.normal(key_of[4], (D,), jnp.float32), 0.5, 1.5).astype(jnp.bfloat16),
        "attn_shift": centred(key_of[5], (D,), 0.2, 1.0, ((0, 4),)),
        "query_weight": draw_query_weight(jax.random.fold_in(key_of[20], 71), 0),
        "query_bias": centred(key_of[7], (H, HD), 0.3, 1.5, ((0, 2), (1, 4))),
        "key_weight": centred(key_of[8], (D, D), D ** -0.5, 0.125, ((0, 4), (1, 2))),
        "value_weight": centred(key_of[9], (D, D), D ** -0.5, 0.125, ((0, 4), (1, 2))),
        "value_bias": centred(key_of[10], (H, HD), 0.05, 0.29882812, ((0, 2), (1, 4))),
        "out_weight": centred(key_of[11], (D, D), (max(D // 256, 2)) ** -0.5, 2.0, ((0, 2), (1, 4))),
        "out_bias": centred(key_of[12], (D,), 0.2, 1.0, ((0, 4),)),
        "mlp_gain": jnp.clip(1.0 + 0.1 * jax.random.normal(key_of[13], (D,), jnp.float32), 0.5, 1.5).astype(jnp.bfloat16),
        "mlp_shift": centred(key_of[14], (D,), 0.2, 1.0, ((0, 4),)),
        "up_weight": centred(key_of[15], (D, FF), D ** -0.5, 0.125, ((0, 4), (1, 2))),
        "up_bias": centred(key_of[16], (FF // D, D), 0.2, 1.0, ((0, 2), (1, 4))),
        "down_weight": centred(key_of[17], (FF, D), FF ** -0.5, 0.0625, ((0, 2), (1, 4))),
        "down_bias": centred(key_of[18], (D,), 0.2, 1.0, ((0, 4),)),
        "clip_level": jnp.clip(jax.random.uniform(key_of[19], (1,), jnp.float32, 5.0, 9.0), 5.0, 9.0),
    }


EPS = 1e-05
NEG = -1e+30

@jax.custom_vjp
def lowered_forward(v):
    return lax.optimization_barrier(v.astype(jnp.bfloat16)).astype(jnp.float32)

@jax.custom_vjp
def lowered_backward(v):
    return v

def low_keep(v):
    return (lowered_forward(v), None)

def low_pass(kept, grad):
    return (grad,)

def back_keep(v):
    return (v, None)

def back_low(kept, grad):
    return (lowered_forward(grad),)
lowered_forward.defvjp(low_keep, low_pass)
lowered_backward.defvjp(back_keep, back_low)

def layer_norm(values, scale_vec, offset_vec):
    center = values - lax.optimization_barrier(jnp.mean(values, -1, keepdims=True))
    inverse = lax.rsqrt(lax.optimization_barrier(jnp.mean(center * center, -1, keepdims=True)) + EPS)
    return center * inverse * scale_vec + offset_vec

def project(left, right):
    return jnp.einsum('bsd,de->bse', left, right, precision=lax.Precision.HIGHEST)

def reference(layer_input, cotangent, seq_lengths, dealing, attn_gain, attn_shift, query_weight, query_bias, key_weight, value_weight, value_bias, out_weight, out_bias, mlp_gain, mlp_shift, up_weight, up_bias, down_weight, down_bias, clip_level):
    params = tuple((item.astype(jnp.float32) for item in (attn_gain, attn_shift, query_weight, query_bias, key_weight, value_weight, value_bias, out_weight, out_bias, mlp_gain, mlp_shift, up_weight, up_bias, down_weight, down_bias)))
    batch = math.gcd(NSEQ, max(1, 4096 // SLOT))
    places = jnp.arange(SLOT, dtype=jnp.int32)
    dealt_len = jnp.take(seq_lengths, dealing).reshape(NSEQ // batch, batch)
    scale_of_scores = 1.0 / math.sqrt(HD)
    highest_score = lax.Precision.HIGHEST

    def block(weights, slab, lens):
        gain_one, shift_one, query_mat, query_vec, key_mat, value_mat, value_vec, out_mat, out_vec, gain_two, shift_two, up_mat, up_vec, down_mat, down_vec = weights
        normed_one = lowered_forward(layer_norm(slab, gain_one, shift_one))
        queries = lowered_forward(lowered_backward(project(normed_one, query_mat)) + query_vec.reshape(D))
        keys = lowered_forward(lowered_backward(project(normed_one, key_mat)))
        values = lowered_forward(lowered_backward(project(normed_one, value_mat)) + value_vec.reshape(D))
        allowed = (places[None, None, :] <= places[None, :, None]) & (places[None, None, :] < lens[:, None, None])
        query_live = places[None, :] < lens[:, None]

        def per_head(inputs):
            head_queries, head_keys, head_values = inputs
            logit_scores = lowered_backward(jnp.einsum('zyu,zmu->zym', head_queries, head_keys, precision=highest_score) * scale_of_scores)
            masked = jnp.where(allowed, logit_scores, NEG)
            row_top = lax.optimization_barrier(jnp.max(masked, -1, keepdims=True))
            exp_terms = jnp.where(allowed, jnp.exp(masked - row_top), 0.0)
            attention_probabilities = exp_terms / lax.optimization_barrier(jnp.sum(exp_terms, -1, keepdims=True))
            attended_rows = jnp.einsum('prf,pfe->pre', lowered_forward(attention_probabilities), head_values, precision=highest_score)
            peak = jnp.max(jnp.where(query_live, row_top[..., 0], NEG))
            return (attended_rows, peak)

        def split_heads(array):
            return array.reshape(array.shape[0], SLOT, H, HD).transpose(2, 0, 1, 3)
        attended_rows, peaks = lax.map(jax.checkpoint(per_head), (split_heads(queries), split_heads(keys), split_heads(values)))
        attended_rows = lowered_forward(lowered_backward(attended_rows.transpose(1, 2, 0, 3).reshape(slab.shape)))
        hidden = slab + lowered_backward(project(attended_rows, out_mat)) + out_vec
        normed_two = lowered_forward(layer_norm(hidden, gain_two, shift_two))
        pre = lowered_backward(project(normed_two, up_mat)) + up_vec.reshape(FF)
        activated = lowered_forward(jax.nn.gelu(pre, approximate=False))
        return (hidden + lowered_backward(project(activated, down_mat)) + down_vec, peaks)

    def forward(weights, inputs):
        slabs = jnp.take(inputs, dealing, axis=0).reshape(NSEQ // batch, batch, SLOT, D)
        step = jax.checkpoint(block)

        def scan_step(carry, pair):
            result, peaks = step(weights, pair[0], pair[1])
            return (jnp.maximum(carry, peaks), result)
        top_all, results = lax.scan(scan_step, jnp.full((H,), NEG, jnp.float32), (slabs, dealt_len))
        return (results.reshape(NSEQ, SLOT, D), top_all)
    layer_output, pull, head_peak = jax.vjp(forward, params, layer_input, has_aux=True)
    grads, input_grad = pull(cotangent)
    input_grad = jnp.take(input_grad, dealing, axis=0)
    level = clip_level[0]
    factor = jnp.repeat(jnp.sqrt(level / jnp.maximum(head_peak, level)), HD)
    query_clipped = (params[2] * factor[None, :]).astype(jnp.bfloat16)
    key_clipped = (params[4] * factor[None, :]).astype(jnp.bfloat16)
    return (layer_output, input_grad, grads[0], grads[1], grads[2], grads[3], grads[4], grads[5], grads[6], grads[7], grads[8], grads[9], grads[10], grads[11], grads[12], grads[13], grads[14], head_peak, query_clipped, key_clipped)
```

```python
import functools
import math

import jax
import jax.numpy as jnp
from jax import lax
from jax.experimental import pallas as pl
from jax.experimental.pallas import tpu as pltpu
from jax.sharding import PartitionSpec as P

EPS = 1e-05
NEG = -1e30
INV_ROOT_TWO = 0.7071067811865476
INV_ROOT_TWO_PI = 0.3989422804014327


def normalize(values, scale_vec, offset_vec):
    center = values - jnp.mean(values, -1, keepdims=True)
    inverse = lax.rsqrt(jnp.mean(center * center, -1, keepdims=True) + EPS)
    normed = center * inverse
    return (normed * scale_vec + offset_vec, normed, inverse)


def norm_back(upstream, normed, inverse, scale_vec):
    scaled = upstream * scale_vec
    inner = (
        scaled
        - jnp.mean(scaled, -1, keepdims=True)
        - normed * jnp.mean(scaled * normed, -1, keepdims=True)
    )
    return (inverse * inner, jnp.sum(upstream * normed, 0), jnp.sum(upstream, 0))


def pick_slots(rows, dealing, first, count):
    return jnp.concatenate(
        [lax.dynamic_slice_in_dim(rows, dealing[first + j], 1, 0) for j in range(count)], 0
    )


def matmul(left, right):
    return jnp.dot(left, right, preferred_element_type=jnp.float32)


def weight_product(left, right):
    return jnp.einsum("td,te->de", left, right, preferred_element_type=jnp.float32)


def back_product(left, right):
    return jnp.einsum("te,de->td", left, right, preferred_element_type=jnp.float32)


def gathered_body(
    layer_input,
    cotangent,
    seq_lengths,
    dealing,
    attn_gain,
    attn_shift,
    query_weight,
    query_bias,
    key_weight,
    value_weight,
    value_bias,
    out_weight,
    out_bias,
    mlp_gain,
    mlp_shift,
    up_weight,
    up_bias,
    down_weight,
    down_bias,
    clip_level,
):
    shard_count = lax.axis_size("fsdp")
    ctx_count = lax.axis_size("ctx")
    my_group = lax.axis_index("fsdp")
    ctx_place = lax.axis_index("ctx")
    slot_count, block_rows, width = layer_input.shape
    per_group = slot_count // shard_count
    local_rows = shard_count * block_rows
    tokens = per_group * local_rows
    dealt_input = pick_slots(layer_input, dealing, 0, slot_count).reshape(
        shard_count, per_group, block_rows, width
    )
    dealt_grad = cotangent.reshape(shard_count, per_group, block_rows, width)
    arrived_input, arrived_grad = (
        lax.all_to_all(dealt_input, "fsdp", split_axis=0, concat_axis=2, tiled=True),
        lax.all_to_all(dealt_grad, "fsdp", split_axis=0, concat_axis=2, tiled=True),
    )
    resid = arrived_input.reshape(tokens, width)
    upstream = arrived_grad.reshape(tokens, width)
    seq_lens = lax.dynamic_slice_in_dim(
        jnp.take(seq_lengths, dealing), my_group * per_group, per_group
    )
    gathered = (
        lax.all_gather(attn_gain, "fsdp", axis=0, tiled=True),
        lax.all_gather(attn_shift, "fsdp", axis=0, tiled=True),
        lax.all_gather(query_weight, "fsdp", axis=0, tiled=True),
        lax.all_gather(query_bias, "fsdp", axis=1, tiled=True),
        lax.all_gather(key_weight, "fsdp", axis=0, tiled=True),
        lax.all_gather(value_weight, "fsdp", axis=0, tiled=True),
        lax.all_gather(value_bias, "fsdp", axis=1, tiled=True),
        lax.all_gather(out_weight, "fsdp", axis=1, tiled=True),
        lax.all_gather(out_bias, "fsdp", axis=0, tiled=True),
        lax.all_gather(mlp_gain, "fsdp", axis=0, tiled=True),
        lax.all_gather(mlp_shift, "fsdp", axis=0, tiled=True),
        lax.all_gather(up_weight, "fsdp", axis=0, tiled=True),
        lax.all_gather(up_bias, "fsdp", axis=1, tiled=True),
        lax.all_gather(down_weight, "fsdp", axis=1, tiled=True),
        lax.all_gather(down_bias, "fsdp", axis=0, tiled=True),
    )
    (
        gain_one,
        shift_one,
        query_mat,
        query_vec,
        key_mat,
        value_mat,
        value_vec,
        out_mat,
        out_vec,
        gain_two,
        shift_two,
        up_mat,
        up_vec,
        down_mat,
        down_vec,
    ) = gathered
    head_count, head_size = query_vec.shape
    features = head_count * head_size
    scale_of_scores = 1.0 / math.sqrt(head_size)
    row_ids = jnp.arange(local_rows, dtype=jnp.int32)
    query_pos = (row_ids // block_rows * ctx_count + ctx_place) * block_rows + row_ids % block_rows
    key_ids = jnp.arange(ctx_count * local_rows, dtype=jnp.int32)
    key_rows = key_ids % local_rows
    key_pos = (
        key_rows // block_rows * ctx_count + key_ids // local_rows
    ) * block_rows + key_rows % block_rows
    allowed = (key_pos[None, None, :] <= query_pos[None, :, None]) & (
        key_pos[None, None, :] < seq_lens[:, None, None]
    )
    query_live = query_pos[None, :] < seq_lens[:, None]
    normed_a, unit_one, inverse_one = normalize(
        resid, gain_one.astype(jnp.float32), shift_one.astype(jnp.float32)
    )
    act_one = normed_a.astype(jnp.bfloat16)
    queries = (
        (matmul(act_one, query_mat) + query_vec.reshape(features).astype(jnp.float32))
        .astype(jnp.bfloat16)
        .reshape(per_group, local_rows, features)
    )
    keys_mine = (
        matmul(act_one, key_mat).astype(jnp.bfloat16).reshape(per_group, local_rows, features)
    )
    values_mine = (
        (matmul(act_one, value_mat) + value_vec.reshape(features).astype(jnp.float32))
        .astype(jnp.bfloat16)
        .reshape(per_group, local_rows, features)
    )
    keys_all, values_all = (
        lax.all_gather(keys_mine, "ctx", axis=1, tiled=True),
        lax.all_gather(values_mine, "ctx", axis=1, tiled=True),
    )

    def head_cut(array, head_index):
        return lax.dynamic_slice_in_dim(array, head_index * head_size, head_size, 2)

    def head_scores(head_queries, head_keys):
        return (
            jnp.einsum("sqd,skd->sqk", head_queries, head_keys, preferred_element_type=jnp.float32)
            * scale_of_scores
        )

    def forward_head(head_index):
        logit_scores = head_scores(head_cut(queries, head_index), head_cut(keys_all, head_index))
        masked = jnp.where(allowed, logit_scores, NEG)
        row_top = jnp.max(masked, -1, keepdims=True)
        exp_terms = jnp.where(allowed, jnp.exp(masked - row_top), 0.0)
        total = jnp.sum(exp_terms, -1, keepdims=True)
        attention_probabilities = exp_terms / total
        attended_rows = jnp.einsum(
            "sqk,skd->sqd",
            attention_probabilities.astype(jnp.bfloat16),
            head_cut(values_all, head_index),
            preferred_element_type=jnp.float32,
        )
        log_total = row_top[..., 0] + jnp.log(total[..., 0])
        peak = jnp.max(jnp.where(query_live, row_top[..., 0], NEG))
        return (attended_rows, log_total, peak)

    attended_rows, log_totals, peaks = lax.map(forward_head, jnp.arange(head_count))
    attn_low = attended_rows.transpose(1, 2, 0, 3).reshape(tokens, features).astype(jnp.bfloat16)
    attn_sum = lax.psum(matmul(attn_low, out_mat), "tp")
    hidden = resid + attn_sum + out_vec.astype(jnp.float32)
    normed_b, unit_two, inverse_two = normalize(
        hidden, gain_two.astype(jnp.float32), shift_two.astype(jnp.float32)
    )
    act_two = normed_b.astype(jnp.bfloat16)
    pre = matmul(act_two, up_mat) + up_vec.reshape(-1).astype(jnp.float32)
    gelu_low = jax.nn.gelu(pre, approximate=False).astype(jnp.bfloat16)
    mlp_sum = lax.psum(matmul(gelu_low, down_mat).astype(jnp.bfloat16), "tp").astype(jnp.float32)
    layer_output = hidden + mlp_sum + down_vec.astype(jnp.float32)
    peak_all = lax.pmax(peaks, ("fsdp", "ctx"))
    level = clip_level[0]
    factor = jnp.repeat(jnp.sqrt(level / jnp.maximum(peak_all, level)), head_size)
    query_clipped = (query_weight.astype(jnp.float32) * factor[None, :]).astype(jnp.bfloat16)
    key_clipped = (key_weight.astype(jnp.float32) * factor[None, :]).astype(jnp.bfloat16)
    grad_low = upstream.astype(jnp.bfloat16)
    down_weight_grad = weight_product(gelu_low, grad_low)
    down_bias_grad = jnp.sum(upstream, 0)
    cdf = 0.5 * (1.0 + lax.erf(pre * INV_ROOT_TWO))
    density = jnp.exp(-0.5 * pre * pre) * INV_ROOT_TWO_PI
    pre_grad = back_product(grad_low, down_mat) * (cdf + pre * density)
    pre_low = pre_grad.astype(jnp.bfloat16)
    up_weight_grad = weight_product(act_two, pre_low)
    up_bias_grad = jnp.sum(pre_grad, 0).reshape(up_vec.shape)
    normed_two_grad = lax.psum(back_product(pre_low, up_mat), "tp")
    hidden_in, mlp_gain_grad, mlp_shift_grad = norm_back(
        normed_two_grad, unit_two, inverse_two, gain_two.astype(jnp.float32)
    )
    hidden_grad = upstream + hidden_in
    hidden_low = hidden_grad.astype(jnp.bfloat16)
    out_weight_grad = weight_product(attn_low, hidden_low)
    out_bias_grad = jnp.sum(hidden_grad, 0)
    attended_grad = (
        back_product(hidden_low, out_mat)
        .astype(jnp.bfloat16)
        .reshape(per_group, local_rows, features)
    )

    def backward_head(head_index):
        head_queries = head_cut(queries, head_index)
        head_keys = head_cut(keys_all, head_index)
        head_values = head_cut(values_all, head_index)
        grad_head = head_cut(attended_grad, head_index)
        logit_scores = head_scores(head_queries, head_keys)
        masked = jnp.where(allowed, logit_scores, NEG)
        attention_probabilities = jnp.where(
            allowed, jnp.exp(masked - log_totals[head_index][..., None]), 0.0
        )
        prob_grad = jnp.einsum(
            "sqd,skd->sqk", grad_head, head_values, preferred_element_type=jnp.float32
        )
        inner = jnp.sum(attention_probabilities * prob_grad, -1, keepdims=True)
        score_grad = (attention_probabilities * (prob_grad - inner)).astype(jnp.bfloat16)
        query_grad = (
            jnp.einsum("sqk,skd->sqd", score_grad, head_keys, preferred_element_type=jnp.float32)
            * scale_of_scores
        )
        key_grad = (
            jnp.einsum("sqk,sqd->skd", score_grad, head_queries, preferred_element_type=jnp.float32)
            * scale_of_scores
        )
        value_grad = jnp.einsum(
            "sqk,sqd->skd",
            attention_probabilities.astype(jnp.bfloat16),
            grad_head,
            preferred_element_type=jnp.float32,
        )
        return (query_grad, key_grad, value_grad)

    query_parts, key_parts, value_parts = lax.map(backward_head, jnp.arange(head_count))
    query_grads = query_parts.transpose(1, 2, 0, 3).reshape(tokens, features)
    key_whole = key_parts.transpose(1, 2, 0, 3).reshape(per_group, ctx_count * local_rows, features)
    value_whole = value_parts.transpose(1, 2, 0, 3).reshape(
        per_group, ctx_count * local_rows, features
    )
    key_summed, value_summed = (
        lax.psum_scatter(key_whole, "ctx", scatter_dimension=1, tiled=True),
        lax.psum_scatter(value_whole, "ctx", scatter_dimension=1, tiled=True),
    )
    key_grads = key_summed.reshape(tokens, features)
    value_grads = value_summed.reshape(tokens, features)
    query_bias_grad = jnp.sum(query_grads, 0).reshape(head_count, head_size)
    value_bias_grad = jnp.sum(value_grads, 0).reshape(head_count, head_size)
    query_low = query_grads.astype(jnp.bfloat16)
    key_low = key_grads.astype(jnp.bfloat16)
    value_low = value_grads.astype(jnp.bfloat16)
    query_weight_grad = weight_product(act_one, query_low)
    key_weight_grad = weight_product(act_one, key_low)
    value_weight_grad = weight_product(act_one, value_low)
    normed_one_grad = lax.psum(
        (
            back_product(query_low, query_mat)
            + back_product(key_low, key_mat)
            + back_product(value_low, value_mat)
        ).astype(jnp.bfloat16),
        "tp",
    ).astype(jnp.float32)
    input_in, attn_gain_grad, attn_shift_grad = norm_back(
        normed_one_grad, unit_one, inverse_one, gain_one.astype(jnp.float32)
    )
    input_grad = hidden_grad + input_in
    partial_sums = (
        lax.psum_scatter(
            attn_gain_grad.astype(jnp.bfloat16), "fsdp", scatter_dimension=0, tiled=True
        ).astype(jnp.float32),
        lax.psum_scatter(
            attn_shift_grad.astype(jnp.bfloat16), "fsdp", scatter_dimension=0, tiled=True
        ).astype(jnp.float32),
        lax.psum_scatter(
            query_weight_grad.astype(jnp.bfloat16), "fsdp", scatter_dimension=0, tiled=True
        ).astype(jnp.float32),
        lax.psum_scatter(
            query_bias_grad.astype(jnp.bfloat16), "fsdp", scatter_dimension=1, tiled=True
        ).astype(jnp.float32),
        lax.psum_scatter(
            key_weight_grad.astype(jnp.bfloat16), "fsdp", scatter_dimension=0, tiled=True
        ).astype(jnp.float32),
        lax.psum_scatter(
            value_weight_grad.astype(jnp.bfloat16), "fsdp", scatter_dimension=0, tiled=True
        ).astype(jnp.float32),
        lax.psum_scatter(
            value_bias_grad.astype(jnp.bfloat16), "fsdp", scatter_dimension=1, tiled=True
        ).astype(jnp.float32),
        lax.psum_scatter(
            out_weight_grad.astype(jnp.bfloat16), "fsdp", scatter_dimension=1, tiled=True
        ).astype(jnp.float32),
        lax.psum_scatter(
            out_bias_grad.astype(jnp.bfloat16), "fsdp", scatter_dimension=0, tiled=True
        ).astype(jnp.float32),
        lax.psum_scatter(
            mlp_gain_grad.astype(jnp.bfloat16), "fsdp", scatter_dimension=0, tiled=True
        ).astype(jnp.float32),
        lax.psum_scatter(
            mlp_shift_grad.astype(jnp.bfloat16), "fsdp", scatter_dimension=0, tiled=True
        ).astype(jnp.float32),
        lax.psum_scatter(
            up_weight_grad.astype(jnp.bfloat16), "fsdp", scatter_dimension=0, tiled=True
        ).astype(jnp.float32),
        lax.psum_scatter(
            up_bias_grad.astype(jnp.bfloat16), "fsdp", scatter_dimension=1, tiled=True
        ).astype(jnp.float32),
        lax.psum_scatter(
            down_weight_grad.astype(jnp.bfloat16), "fsdp", scatter_dimension=1, tiled=True
        ).astype(jnp.float32),
        lax.psum_scatter(
            down_bias_grad.astype(jnp.bfloat16), "fsdp", scatter_dimension=0, tiled=True
        ).astype(jnp.float32),
    )
    shards = (
        lax.psum(partial_sums[0].astype(jnp.bfloat16), "ctx").astype(jnp.float32),
        lax.psum(partial_sums[1].astype(jnp.bfloat16), "ctx").astype(jnp.float32),
        lax.psum(partial_sums[2].astype(jnp.bfloat16), "ctx").astype(jnp.float32),
        lax.psum(partial_sums[3].astype(jnp.bfloat16), "ctx").astype(jnp.float32),
        lax.psum(partial_sums[4].astype(jnp.bfloat16), "ctx").astype(jnp.float32),
        lax.psum(partial_sums[5].astype(jnp.bfloat16), "ctx").astype(jnp.float32),
        lax.psum(partial_sums[6].astype(jnp.bfloat16), "ctx").astype(jnp.float32),
        lax.psum(partial_sums[7].astype(jnp.bfloat16), "ctx").astype(jnp.float32),
        lax.psum(partial_sums[8].astype(jnp.bfloat16), "ctx").astype(jnp.float32),
        lax.psum(partial_sums[9].astype(jnp.bfloat16), "ctx").astype(jnp.float32),
        lax.psum(partial_sums[10].astype(jnp.bfloat16), "ctx").astype(jnp.float32),
        lax.psum(partial_sums[11].astype(jnp.bfloat16), "ctx").astype(jnp.float32),
        lax.psum(partial_sums[12].astype(jnp.bfloat16), "ctx").astype(jnp.float32),
        lax.psum(partial_sums[13].astype(jnp.bfloat16), "ctx").astype(jnp.float32),
        lax.psum(partial_sums[14].astype(jnp.bfloat16), "ctx").astype(jnp.float32),
    )
    sent_output = layer_output.reshape(1, per_group, local_rows, width)
    sent_grad = input_grad.reshape(1, per_group, local_rows, width)
    back_output, back_grad = (
        lax.all_to_all(
            sent_output.astype(jnp.bfloat16), "fsdp", split_axis=2, concat_axis=0, tiled=True
        ).astype(sent_output.dtype),
        lax.all_to_all(
            sent_grad.astype(jnp.bfloat16), "fsdp", split_axis=2, concat_axis=0, tiled=True
        ).astype(sent_grad.dtype),
    )
    final_output = back_output.reshape(slot_count, block_rows, width)
    final_grad = back_grad.reshape(slot_count, block_rows, width)
    return (
        final_output,
        final_grad,
        shards[0],
        shards[1],
        shards[2],
        shards[3],
        shards[4],
        shards[5],
        shards[6],
        shards[7],
        shards[8],
        shards[9],
        shards[10],
        shards[11],
        shards[12],
        shards[13],
        shards[14],
        peak_all,
        query_clipped,
        key_clipped,
    )


def attention_probs(query_block, key_rows, block, length):
    rows, cols = query_block.shape[0], key_rows.shape[0]
    scores = lax.dot_general(
        query_block, key_rows, (((1,), (1,)), ((), ())), preferred_element_type=jnp.float32
    ) * (1.0 / math.sqrt(query_block.shape[1]))
    row_pos = block * rows + lax.broadcasted_iota(jnp.int32, (rows, cols), 0)
    col_pos = lax.broadcasted_iota(jnp.int32, (rows, cols), 1)
    scores = jnp.where((col_pos <= row_pos) & (col_pos < length), scores, NEG)
    top = jnp.max(scores, -1, keepdims=True)
    terms = jnp.exp(scores - top)
    return terms / jnp.sum(terms, -1, keepdims=True), top


def attention_forward_kernel(ranks, info, q_ref, k_ref, v_ref, out_ref, peak_ref, keys, values):
    rows = keys.shape[0] // ranks
    length = info[ranks]
    for block in range(ranks):
        at = pl.ds(pl.multiple_of(info[block], rows), rows)
        keys[pl.ds(block * rows, rows), :] = k_ref[at, :]
        values[pl.ds(block * rows, rows), :] = v_ref[at, :]
    peak = jnp.full((1, 1), NEG, jnp.float32)
    for block in range(ranks):
        at = pl.ds(pl.multiple_of(info[block], rows), rows)
        extent = (block + 1) * rows
        probs, top = attention_probs(q_ref[at, :], keys[pl.ds(0, extent), :], block, length)
        out_ref[at, :] = jnp.dot(
            probs.astype(jnp.bfloat16),
            values[pl.ds(0, extent), :],
            preferred_element_type=jnp.float32,
        ).astype(out_ref.dtype)
        live = block * rows + lax.broadcasted_iota(jnp.int32, top.shape, 0) < length
        peak = jnp.maximum(peak, jnp.max(jnp.where(live, top, NEG), 0, keepdims=True))
    peak_ref[...] = jnp.broadcast_to(peak[None], peak_ref.shape)


def attention_forward(info, qkv, head_size):
    tokens, features = qkv.shape[0], qkv.shape[1] // 3
    heads, ranks = features // head_size, info.shape[0] - 1

    def part(k):
        return pl.BlockSpec((tokens, head_size), lambda h, info: (0, k * heads + h))

    attended, peaks = pl.pallas_call(
        functools.partial(attention_forward_kernel, ranks),
        out_shape=(
            jax.ShapeDtypeStruct((tokens, features), jnp.bfloat16),
            jax.ShapeDtypeStruct((heads, 8, 128), jnp.float32),
        ),
        grid_spec=pltpu.PrefetchScalarGridSpec(
            num_scalar_prefetch=1,
            grid=(heads,),
            in_specs=[part(0), part(1), part(2)],
            out_specs=(
                pl.BlockSpec((tokens, head_size), lambda h, info: (0, h)),
                pl.BlockSpec((1, 8, 128), lambda h, info: (h, 0, 0)),
            ),
            scratch_shapes=[pltpu.VMEM((tokens, head_size), jnp.bfloat16)] * 2,
        ),
        compiler_params=pltpu.CompilerParams(vmem_limit_bytes=40 << 20),
        cost_estimate=pl.CostEstimate(
            flops=4 * tokens * tokens * features, bytes_accessed=8 * tokens * features, transcendentals=0
        ),
    )(info, qkv, qkv, qkv)
    return attended, peaks[:, 0, 0]


def attention_backward_kernel(
    ranks, heads, info, q_ref, k_ref, v_ref, g_ref, out_ref, bias_ref, keys, values, key_sum, value_sum
):
    tokens, size = keys.shape
    rows = tokens // ranks
    scale = 1.0 / math.sqrt(size)
    head = pl.program_id(0)
    length = info[ranks]

    def lanes(k):
        return pl.ds(pl.multiple_of((k * heads + head) * size, size), size)

    for block in range(ranks):
        at = pl.ds(pl.multiple_of(info[block], rows), rows)
        keys[pl.ds(block * rows, rows), :] = k_ref[at, :]
        values[pl.ds(block * rows, rows), :] = v_ref[at, :]
    key_sum[...] = jnp.zeros_like(key_sum)
    value_sum[...] = jnp.zeros_like(value_sum)
    query_bias = jnp.zeros((1, size), jnp.float32)
    for block in range(ranks):
        at = pl.ds(pl.multiple_of(info[block], rows), rows)
        extent = (block + 1) * rows
        part = pl.ds(0, extent)
        queries, grads = q_ref[at, :], g_ref[at, :]
        probs, _ = attention_probs(queries, keys[part, :], block, length)
        prob_grad = lax.dot_general(
            grads, values[part, :], (((1,), (1,)), ((), ())), preferred_element_type=jnp.float32
        )
        inner = jnp.sum(probs * prob_grad, -1, keepdims=True)
        score_grad = (probs * (prob_grad - inner)).astype(jnp.bfloat16)
        query_grad = (
            jnp.dot(score_grad, keys[part, :], preferred_element_type=jnp.float32) * scale
        )
        query_bias += jnp.sum(query_grad, 0, keepdims=True)
        out_ref[at, lanes(0)] = query_grad.astype(out_ref.dtype)
        key_sum[part, :] += lax.dot_general(
            score_grad, queries, (((0,), (0,)), ((), ())), preferred_element_type=jnp.float32
        )
        value_sum[part, :] += lax.dot_general(
            probs.astype(jnp.bfloat16), grads, (((0,), (0,)), ((), ())), preferred_element_type=jnp.float32
        )
    for block in range(ranks):
        at = pl.ds(pl.multiple_of(info[block], rows), rows)
        out_ref[at, lanes(1)] = (key_sum[pl.ds(block * rows, rows), :] * scale).astype(out_ref.dtype)
        out_ref[at, lanes(2)] = value_sum[pl.ds(block * rows, rows), :].astype(out_ref.dtype)
    bias_ref[0, pl.ds(0, 1), :] = query_bias
    bias_ref[0, pl.ds(1, 1), :] = jnp.sum(value_sum[...], 0, keepdims=True)


def attention_backward(info, qkv, grads, head_size):
    tokens, features = grads.shape
    heads, ranks = features // head_size, info.shape[0] - 1

    def part(k):
        return pl.BlockSpec((tokens, head_size), lambda h, info: (0, k * heads + h))

    return pl.pallas_call(
        functools.partial(attention_backward_kernel, ranks, heads),
        out_shape=(
            jax.ShapeDtypeStruct((tokens, 3 * features), jnp.bfloat16),
            jax.ShapeDtypeStruct((heads, 8, head_size), jnp.float32),
        ),
        grid_spec=pltpu.PrefetchScalarGridSpec(
            num_scalar_prefetch=1,
            grid=(heads,),
            in_specs=[part(0), part(1), part(2), part(0)],
            out_specs=(
                pl.BlockSpec((tokens, 3 * features), lambda h, info: (0, 0)),
                pl.BlockSpec((1, 8, head_size), lambda h, info: (h, 0, 0)),
            ),
            scratch_shapes=[pltpu.VMEM((tokens, head_size), jnp.bfloat16)] * 2
            + [pltpu.VMEM((tokens, head_size), jnp.float32)] * 2,
        ),
        compiler_params=pltpu.CompilerParams(vmem_limit_bytes=48 << 20),
        cost_estimate=pl.CostEstimate(
            flops=10 * tokens * tokens * features, bytes_accessed=14 * tokens * features, transcendentals=0
        ),
    )(info, qkv, qkv, qkv, grads)


def split_body(
    layer_input,
    cotangent,
    seq_lengths,
    dealing,
    attn_gain,
    attn_shift,
    query_weight,
    query_bias,
    key_weight,
    value_weight,
    value_bias,
    out_weight,
    out_bias,
    mlp_gain,
    mlp_shift,
    up_weight,
    up_bias,
    down_weight,
    down_bias,
    clip_level,
):
    f32, bf16 = jnp.float32, jnp.bfloat16
    f = lax.axis_index("fsdp")
    z = lax.axis_index("ctx")
    t = lax.axis_index("tp")
    y, x = f // 2, f % 2
    depth = lax.axis_size("ctx")
    slots, block_rows, width = layer_input.shape
    local_heads = query_bias.shape[0] // 2
    head_size = 4 * query_bias.shape[1]
    features = local_heads * head_size
    hidden_units = up_weight.shape[1] // 2
    strip = query_weight.shape[0]
    own_rows = depth * block_rows

    over_x = [(0, 1), (1, 0), (2, 3), (3, 2)]
    over_y = [(0, 2), (2, 0), (1, 3), (3, 1)]
    x_core = [(0, 0), (1, 2), (2, 1), (3, 3), (4, 4), (5, 6), (6, 5), (7, 7)]

    def across_x(v):
        return lax.ppermute(v, "fsdp", over_x)

    def across_y(v):
        return lax.ppermute(v, "fsdp", over_y)

    def across_core(v):
        return lax.ppermute(v, "tp", [(0, 1), (1, 0)])

    def half(v, which, axis):
        size = v.shape[axis] // 2
        return lax.dynamic_slice_in_dim(v, which * size, size, axis)

    def deal_rows(part):
        part = lax.ppermute(part, ("fsdp", "tp"), x_core)
        part = lax.all_to_all(part, "ctx", split_axis=0, concat_axis=0, tiled=True)
        return part.reshape(own_rows, part.shape[-1])

    def return_rows(rows):
        part = rows.reshape(depth, block_rows, rows.shape[-1])
        part = lax.all_to_all(part, "ctx", split_axis=0, concat_axis=0, tiled=True)
        part = lax.ppermute(part, ("fsdp", "tp"), x_core)
        other = across_core(part)
        both = jnp.where(t == 0, jnp.stack([part, other]), jnp.stack([other, part]))
        return both.reshape(slots, block_rows, rows.shape[-1]).astype(f32)

    def gather_rows(own):
        peer = across_core(own)
        far = across_y(own)
        far_peer = across_core(far)
        return jnp.concatenate([own, peer], 0), jnp.concatenate([far, far_peer], 0)

    def scatter_rows(near, far):
        far_mine = far[:own_rows] + across_core(far[own_rows:].astype(bf16)).astype(f32)
        arrived = across_y(far_mine.astype(bf16)).astype(f32)
        return near[:own_rows] + across_core(near[own_rows:].astype(bf16)).astype(f32) + arrived

    def gather_weight(shard, column_split):
        cut = 1 if column_split else 0
        own, sent = half(shard, y, cut), half(shard, 1 - y, cut)
        far = across_y(sent)
        own_x, far_x = across_x(own), across_x(far)
        axis = 1 - cut
        shape = list(own.shape)
        shape[axis] *= 4
        whole = jnp.zeros(shape, shard.dtype)
        for piece, home in ((own, f), (own_x, 2 * y + 1 - x), (far, 2 * (1 - y) + x), (far_x, 2 * (1 - y) + 1 - x)):
            whole = lax.dynamic_update_slice_in_dim(whole, piece, home * strip, axis)
        return whole

    def z_sum(v):
        first = lax.ppermute(v, "ctx", [(0, 1), (3, 2)])
        pair = lax.optimization_barrier((v.astype(f32) + first.astype(f32)).astype(bf16))
        second = lax.ppermute(pair, "ctx", [(1, 2), (2, 1)])
        total = lax.optimization_barrier((pair.astype(f32) + second.astype(f32)).astype(bf16))
        back = lax.ppermute(total, "ctx", [(1, 0), (2, 3)])
        return jnp.where((z == 1) | (z == 2), total, back)

    def strip_of(v, home):
        return lax.dynamic_slice_in_dim(v, home * strip, strip, 1)

    def reduce_weight(product, cut, join):
        near_send = product(2 * y + 1 - x).astype(bf16)
        far_send = product(2 * (1 - y) + 1 - x).astype(bf16)
        near_got, far_got = across_x(near_send), across_x(far_send)
        near = (product(f) + near_got.astype(f32)).astype(bf16)
        far = (product(2 * (1 - y) + x) + far_got.astype(f32)).astype(bf16)
        other = across_y(far)
        mine, other = z_sum(near), z_sum(other)
        return join(mine, other)

    def join_on(axis):
        def join(mine, other):
            return jnp.where(
                y == 0,
                jnp.concatenate([mine, other], axis),
                jnp.concatenate([other, mine], axis),
            ).astype(f32)

        return join

    slot = x * depth + z
    length = seq_lengths[dealing[slot]]
    own_rank = 2 * y + t
    near_rank = 2 * y + 1 - t
    far_rank = 2 * (1 - y) + t
    places = jnp.zeros((4,), jnp.int32)
    for k, rank in enumerate((own_rank, near_rank, far_rank, 2 * (1 - y) + 1 - t)):
        places = places.at[rank].set(k * own_rows)
    info = jnp.concatenate([places, length[None]])

    small = jnp.stack([attn_gain, attn_shift, out_bias, mlp_gain, mlp_shift, down_bias])
    small = lax.all_gather(small, "fsdp", axis=1, tiled=True).astype(f32)
    gain_one, shift_one, out_vec, gain_two, shift_two, down_vec = [small[k] for k in range(6)]
    vectors = jnp.concatenate([query_bias, value_bias, up_bias.reshape(-1, query_bias.shape[1])], 0)
    vectors = lax.all_gather(vectors, "fsdp", axis=0, tiled=False)
    nb = query_bias.shape[0]
    query_vec = half(vectors[:, :nb].transpose(1, 0, 2).reshape(-1), y, 0).astype(f32)
    value_vec = half(vectors[:, nb : 2 * nb].transpose(1, 0, 2).reshape(-1), y, 0).astype(f32)
    up_vec = half(
        vectors[:, 2 * nb :].reshape(4, up_bias.shape[0], -1).transpose(1, 0, 2).reshape(-1), y, 0
    ).astype(f32)

    arrived = pick_slots(layer_input, dealing, t * depth, depth)
    cot_part = lax.dynamic_slice_in_dim(cotangent, t * depth, depth, 0)
    down_bias_part = jnp.sum(cot_part, (0, 1))
    act_part = normalize(arrived, gain_one, shift_one)[0].astype(bf16)
    act_own = deal_rows(act_part)
    act_near, act_far = gather_rows(act_own)
    act_one = jnp.concatenate([act_near, act_far], 0)
    qkv_shard = jnp.concatenate([query_weight, key_weight, value_weight], 1)
    qkv_shard = qkv_shard.reshape(strip, 3, 2, features).transpose(0, 2, 1, 3).reshape(strip, 6 * features)
    qkv_mat = gather_weight(qkv_shard, True)
    out_mat = gather_weight(out_weight, False)
    up_mat = gather_weight(up_weight, True)
    down_mat = gather_weight(down_weight, False)
    resid = deal_rows(arrived)
    cot_own = deal_rows(cot_part.astype(bf16))
    cot_low = jnp.concatenate(gather_rows(cot_own), 0)

    qkv_vec = jnp.concatenate([query_vec, jnp.zeros_like(query_vec), value_vec])
    qkv = jnp.concatenate(
        [(matmul(rows, qkv_mat) + qkv_vec).astype(bf16) for rows in (act_near, act_far)], 0
    )
    attended, peaks = attention_forward(info, qkv, head_size)
    chip_rows = 2 * own_rows
    attn_far = matmul(attended[chip_rows:], out_mat)
    attn_near = matmul(attended[:chip_rows], out_mat)
    hidden = resid + scatter_rows(attn_near, attn_far) + out_vec
    normed_b, unit_two, inverse_two = normalize(hidden, gain_two, shift_two)
    act_two = jnp.concatenate(gather_rows(normed_b.astype(bf16)), 0)

    pre = matmul(act_two, up_mat) + up_vec
    cdf = 0.5 * (1.0 + lax.erf(pre * INV_ROOT_TWO))
    gelu_low = (pre * cdf).astype(bf16)
    slope = cdf + pre * (jnp.exp(-0.5 * pre * pre) * INV_ROOT_TWO_PI)
    pre_grad = back_product(cot_low, down_mat) * slope
    pre_low = pre_grad.astype(bf16)
    up_bias_part = jnp.sum(pre_grad, 0)
    two_far = back_product(pre_low[chip_rows:], up_mat)
    two_near = back_product(pre_low[:chip_rows], up_mat)
    normed_two_grad = scatter_rows(two_near, two_far)
    hidden_in, mlp_gain_part, mlp_shift_part = norm_back(
        normed_two_grad, unit_two, inverse_two, gain_two
    )
    hidden_grad = cot_own.astype(f32) + hidden_in
    out_bias_part = jnp.sum(hidden_grad, 0)
    hidden_low = jnp.concatenate(gather_rows(hidden_grad.astype(bf16)), 0)
    attended_grad = back_product(hidden_low, out_mat).astype(bf16)
    qkv_low, bias_parts = attention_backward(info, qkv, attended_grad, head_size)

    down_weight_grad = reduce_weight(
        lambda home: weight_product(gelu_low, strip_of(cot_low, home)), 0, join_on(0)
    )
    up_weight_grad = reduce_weight(
        lambda home: weight_product(strip_of(act_two, home), pre_low), 1, join_on(1)
    )
    out_weight_grad = reduce_weight(
        lambda home: weight_product(attended, strip_of(hidden_low, home)), 0, join_on(0)
    )
    mlp_far = matmul(gelu_low[chip_rows:], down_mat)
    mlp_near = matmul(gelu_low[:chip_rows], down_mat)
    layer_output = hidden + scatter_rows(mlp_near, mlp_far) + down_vec
    final_output = return_rows(layer_output.astype(bf16))

    one_far = back_product(qkv_low[chip_rows:], qkv_mat)
    one_near = back_product(qkv_low[:chip_rows], qkv_mat)
    normed_one_grad = scatter_rows(one_near, one_far)
    _, unit_one, inverse_one = normalize(resid, gain_one, shift_one)
    input_in, attn_gain_part, attn_shift_part = norm_back(
        normed_one_grad, unit_one, inverse_one, gain_one
    )
    final_grad = return_rows((hidden_grad + input_in).astype(bf16))

    def join_qkv(mine, other):
        mine, other = mine.reshape(strip, 3, features), other.reshape(strip, 3, features)
        both = jnp.where(
            y == 0, jnp.concatenate([mine, other], 2), jnp.concatenate([other, mine], 2)
        ).astype(f32)
        return both[:, 0], both[:, 1], both[:, 2]

    query_weight_grad, key_weight_grad, value_weight_grad = reduce_weight(
        lambda home: weight_product(strip_of(act_one, home), qkv_low), 1, join_qkv
    )

    def placed(v, which):
        whole = jnp.zeros((4,) + v.shape, f32)
        return lax.dynamic_update_slice_in_dim(whole, v[None], which, 0)

    column = 2 * t + y
    rows_sum = jnp.stack(
        [attn_gain_part, attn_shift_part, out_bias_part, mlp_gain_part, mlp_shift_part, down_bias_part]
    )
    head_sum = placed(jnp.stack([bias_parts[:, 0].reshape(-1), bias_parts[:, 1].reshape(-1)]), column)
    unit_sum = placed(up_bias_part, column)
    flat = jnp.concatenate([rows_sum.reshape(-1), head_sum.reshape(-1), unit_sum.reshape(-1)])
    flat = lax.psum(flat, ("fsdp", "ctx", "tp"))
    cut_one, cut_two = rows_sum.size, rows_sum.size + head_sum.size
    rows_sum = lax.dynamic_slice_in_dim(flat[:cut_one].reshape(6, width), f * strip, strip, 1)
    head_sum = lax.dynamic_slice_in_dim(flat[cut_one:cut_two].reshape(4, 2, features), 2 * t, 2, 0)
    head_sum = head_sum.transpose(1, 0, 2).reshape(2, 2 * local_heads, head_size)
    head_sum = lax.dynamic_slice_in_dim(head_sum, f * query_bias.shape[1], query_bias.shape[1], 2)
    unit_sum = lax.dynamic_slice_in_dim(
        flat[cut_two:].reshape(2, up_bias.shape[0], width), t, 1, 0
    )[0]
    unit_sum = lax.dynamic_slice_in_dim(unit_sum, f * strip, strip, 1)

    my_peaks = lax.dynamic_update_slice_in_dim(
        jnp.full((2, local_heads), NEG, f32), peaks[None], y, 0
    ).reshape(-1)
    peak_all = lax.pmax(my_peaks, ("fsdp", "ctx"))
    level = clip_level[0]
    factor = jnp.repeat(jnp.sqrt(level / jnp.maximum(peak_all, level)), head_size)
    query_clipped = (query_weight.astype(f32) * factor[None, :]).astype(bf16)
    key_clipped = (key_weight.astype(f32) * factor[None, :]).astype(bf16)
    return (
        final_output,
        final_grad,
        rows_sum[0],
        rows_sum[1],
        query_weight_grad,
        head_sum[0],
        key_weight_grad,
        value_weight_grad,
        head_sum[1],
        out_weight_grad,
        rows_sum[2],
        rows_sum[3],
        rows_sum[4],
        up_weight_grad,
        unit_sum,
        down_weight_grad,
        rows_sum[5],
        peak_all,
        query_clipped,
        key_clipped,
    )


def solution(mesh):
    sizes = dict(mesh.shape)
    small_slice = sizes == {"fsdp": 4, "ctx": 4, "tp": 2}
    return jax.shard_map(
        split_body if small_slice else gathered_body,
        mesh=mesh,
        in_specs=(
            P(None, ("fsdp", "ctx"), None),
            P(None, ("fsdp", "ctx"), None),
            P(),
            P(),
            P("fsdp"),
            P("fsdp"),
            P("fsdp", "tp"),
            P("tp", "fsdp"),
            P("fsdp", "tp"),
            P("fsdp", "tp"),
            P("tp", "fsdp"),
            P("tp", "fsdp"),
            P("fsdp"),
            P("fsdp"),
            P("fsdp"),
            P("fsdp", "tp"),
            P("tp", "fsdp"),
            P("tp", "fsdp"),
            P("fsdp"),
            P(),
        ),
        out_specs=(
            P(None, ("fsdp", "ctx"), None),
            P(None, ("fsdp", "ctx"), None),
            P("fsdp"),
            P("fsdp"),
            P("fsdp", "tp"),
            P("tp", "fsdp"),
            P("fsdp", "tp"),
            P("fsdp", "tp"),
            P("tp", "fsdp"),
            P("tp", "fsdp"),
            P("fsdp"),
            P("fsdp"),
            P("fsdp"),
            P("fsdp", "tp"),
            P("tp", "fsdp"),
            P("tp", "fsdp"),
            P("fsdp"),
            P("tp"),
            P("fsdp", "tp"),
            P("fsdp", "tp"),
        ),
        check_vma=False,
    )
```

```python
import functools
import math

import jax
import jax.numpy as jnp
from jax import lax
from jax.experimental import pallas as pl
from jax.experimental.pallas import tpu as pltpu
from jax.sharding import PartitionSpec as P

EPS = 1e-05
NEG = -1e30
INV_ROOT_TWO = 0.7071067811865476
INV_ROOT_TWO_PI = 0.3989422804014327


def normalize(values, scale_vec, offset_vec):
    center = values - jnp.mean(values, -1, keepdims=True)
    inverse = lax.rsqrt(jnp.mean(center * center, -1, keepdims=True) + EPS)
    normed = center * inverse
    return (normed * scale_vec + offset_vec, normed, inverse)


def norm_back(upstream, normed, inverse, scale_vec):
    scaled = upstream * scale_vec
    inner = (
        scaled
        - jnp.mean(scaled, -1, keepdims=True)
        - normed * jnp.mean(scaled * normed, -1, keepdims=True)
    )
    return (inverse * inner, jnp.sum(upstream * normed, 0), jnp.sum(upstream, 0))


def pick_slots(rows, dealing, first, count):
    return jnp.concatenate(
        [lax.dynamic_slice_in_dim(rows, dealing[first + j], 1, 0) for j in range(count)], 0
    )


def matmul(left, right):
    return jnp.dot(left, right, preferred_element_type=jnp.float32)


def weight_product(left, right):
    return jnp.einsum("td,te->de", left, right, preferred_element_type=jnp.float32)


def back_product(left, right):
    return jnp.einsum("te,de->td", left, right, preferred_element_type=jnp.float32)


def gathered_body(
    layer_input,
    cotangent,
    seq_lengths,
    dealing,
    attn_gain,
    attn_shift,
    query_weight,
    query_bias,
    key_weight,
    value_weight,
    value_bias,
    out_weight,
    out_bias,
    mlp_gain,
    mlp_shift,
    up_weight,
    up_bias,
    down_weight,
    down_bias,
    clip_level,
):
    shard_count = lax.axis_size("fsdp")
    ctx_count = lax.axis_size("ctx")
    my_group = lax.axis_index("fsdp")
    ctx_place = lax.axis_index("ctx")
    slot_count, block_rows, width = layer_input.shape
    per_group = slot_count // shard_count
    local_rows = shard_count * block_rows
    tokens = per_group * local_rows
    dealt_input = pick_slots(layer_input, dealing, 0, slot_count).reshape(
        shard_count, per_group, block_rows, width
    )
    dealt_grad = cotangent.reshape(shard_count, per_group, block_rows, width)
    arrived_input, arrived_grad = (
        lax.all_to_all(dealt_input, "fsdp", split_axis=0, concat_axis=2, tiled=True),
        lax.all_to_all(dealt_grad, "fsdp", split_axis=0, concat_axis=2, tiled=True),
    )
    resid = arrived_input.reshape(tokens, width)
    upstream = arrived_grad.reshape(tokens, width)
    seq_lens = lax.dynamic_slice_in_dim(
        jnp.take(seq_lengths, dealing), my_group * per_group, per_group
    )
    gathered = (
        lax.all_gather(attn_gain, "fsdp", axis=0, tiled=True),
        lax.all_gather(attn_shift, "fsdp", axis=0, tiled=True),
        lax.all_gather(query_weight, "fsdp", axis=0, tiled=True),
        lax.all_gather(query_bias, "fsdp", axis=1, tiled=True),
        lax.all_gather(key_weight, "fsdp", axis=0, tiled=True),
        lax.all_gather(value_weight, "fsdp", axis=0, tiled=True),
        lax.all_gather(value_bias, "fsdp", axis=1, tiled=True),
        lax.all_gather(out_weight, "fsdp", axis=1, tiled=True),
        lax.all_gather(out_bias, "fsdp", axis=0, tiled=True),
        lax.all_gather(mlp_gain, "fsdp", axis=0, tiled=True),
        lax.all_gather(mlp_shift, "fsdp", axis=0, tiled=True),
        lax.all_gather(up_weight, "fsdp", axis=0, tiled=True),
        lax.all_gather(up_bias, "fsdp", axis=1, tiled=True),
        lax.all_gather(down_weight, "fsdp", axis=1, tiled=True),
        lax.all_gather(down_bias, "fsdp", axis=0, tiled=True),
    )
    (
        gain_one,
        shift_one,
        query_mat,
        query_vec,
        key_mat,
        value_mat,
        value_vec,
        out_mat,
        out_vec,
        gain_two,
        shift_two,
        up_mat,
        up_vec,
        down_mat,
        down_vec,
    ) = gathered
    head_count, head_size = query_vec.shape
    features = head_count * head_size
    scale_of_scores = 1.0 / math.sqrt(head_size)
    row_ids = jnp.arange(local_rows, dtype=jnp.int32)
    query_pos = (row_ids // block_rows * ctx_count + ctx_place) * block_rows + row_ids % block_rows
    key_ids = jnp.arange(ctx_count * local_rows, dtype=jnp.int32)
    key_rows = key_ids % local_rows
    key_pos = (
        key_rows // block_rows * ctx_count + key_ids // local_rows
    ) * block_rows + key_rows % block_rows
    allowed = (key_pos[None, None, :] <= query_pos[None, :, None]) & (
        key_pos[None, None, :] < seq_lens[:, None, None]
    )
    query_live = query_pos[None, :] < seq_lens[:, None]
    normed_a, unit_one, inverse_one = normalize(
        resid, gain_one.astype(jnp.float32), shift_one.astype(jnp.float32)
    )
    act_one = normed_a.astype(jnp.bfloat16)
    queries = (
        (matmul(act_one, query_mat) + query_vec.reshape(features).astype(jnp.float32))
        .astype(jnp.bfloat16)
        .reshape(per_group, local_rows, features)
    )
    keys_mine = (
        matmul(act_one, key_mat).astype(jnp.bfloat16).reshape(per_group, local_rows, features)
    )
    values_mine = (
        (matmul(act_one, value_mat) + value_vec.reshape(features).astype(jnp.float32))
        .astype(jnp.bfloat16)
        .reshape(per_group, local_rows, features)
    )
    keys_all, values_all = (
        lax.all_gather(keys_mine, "ctx", axis=1, tiled=True),
        lax.all_gather(values_mine, "ctx", axis=1, tiled=True),
    )

    def head_cut(array, head_index):
        return lax.dynamic_slice_in_dim(array, head_index * head_size, head_size, 2)

    def head_scores(head_queries, head_keys):
        return (
            jnp.einsum("sqd,skd->sqk", head_queries, head_keys, preferred_element_type=jnp.float32)
            * scale_of_scores
        )

    def forward_head(head_index):
        logit_scores = head_scores(head_cut(queries, head_index), head_cut(keys_all, head_index))
        masked = jnp.where(allowed, logit_scores, NEG)
        row_top = jnp.max(masked, -1, keepdims=True)
        exp_terms = jnp.where(allowed, jnp.exp(masked - row_top), 0.0)
        total = jnp.sum(exp_terms, -1, keepdims=True)
        attention_probabilities = exp_terms / total
        attended_rows = jnp.einsum(
            "sqk,skd->sqd",
            attention_probabilities.astype(jnp.bfloat16),
            head_cut(values_all, head_index),
            preferred_element_type=jnp.float32,
        )
        log_total = row_top[..., 0] + jnp.log(total[..., 0])
        peak = jnp.max(jnp.where(query_live, row_top[..., 0], NEG))
        return (attended_rows, log_total, peak)

    attended_rows, log_totals, peaks = lax.map(forward_head, jnp.arange(head_count))
    attn_low = attended_rows.transpose(1, 2, 0, 3).reshape(tokens, features).astype(jnp.bfloat16)
    attn_sum = lax.psum(matmul(attn_low, out_mat), "tp")
    hidden = resid + attn_sum + out_vec.astype(jnp.float32)
    normed_b, unit_two, inverse_two = normalize(
        hidden, gain_two.astype(jnp.float32), shift_two.astype(jnp.float32)
    )
    act_two = normed_b.astype(jnp.bfloat16)
    pre = matmul(act_two, up_mat) + up_vec.reshape(-1).astype(jnp.float32)
    gelu_low = jax.nn.gelu(pre, approximate=False).astype(jnp.bfloat16)
    mlp_sum = lax.psum(matmul(gelu_low, down_mat).astype(jnp.bfloat16), "tp").astype(jnp.float32)
    layer_output = hidden + mlp_sum + down_vec.astype(jnp.float32)
    peak_all = lax.pmax(peaks, ("fsdp", "ctx"))
    level = clip_level[0]
    factor = jnp.repeat(jnp.sqrt(level / jnp.maximum(peak_all, level)), head_size)
    query_clipped = (query_weight.astype(jnp.float32) * factor[None, :]).astype(jnp.bfloat16)
    key_clipped = (key_weight.astype(jnp.float32) * factor[None, :]).astype(jnp.bfloat16)
    grad_low = upstream.astype(jnp.bfloat16)
    down_weight_grad = weight_product(gelu_low, grad_low)
    down_bias_grad = jnp.sum(upstream, 0)
    cdf = 0.5 * (1.0 + lax.erf(pre * INV_ROOT_TWO))
    density = jnp.exp(-0.5 * pre * pre) * INV_ROOT_TWO_PI
    pre_grad = back_product(grad_low, down_mat) * (cdf + pre * density)
    pre_low = pre_grad.astype(jnp.bfloat16)
    up_weight_grad = weight_product(act_two, pre_low)
    up_bias_grad = jnp.sum(pre_grad, 0).reshape(up_vec.shape)
    normed_two_grad = lax.psum(back_product(pre_low, up_mat), "tp")
    hidden_in, mlp_gain_grad, mlp_shift_grad = norm_back(
        normed_two_grad, unit_two, inverse_two, gain_two.astype(jnp.float32)
    )
    hidden_grad = upstream + hidden_in
    hidden_low = hidden_grad.astype(jnp.bfloat16)
    out_weight_grad = weight_product(attn_low, hidden_low)
    out_bias_grad = jnp.sum(hidden_grad, 0)
    attended_grad = (
        back_product(hidden_low, out_mat)
        .astype(jnp.bfloat16)
        .reshape(per_group, local_rows, features)
    )

    def backward_head(head_index):
        head_queries = head_cut(queries, head_index)
        head_keys = head_cut(keys_all, head_index)
        head_values = head_cut(values_all, head_index)
        grad_head = head_cut(attended_grad, head_index)
        logit_scores = head_scores(head_queries, head_keys)
        masked = jnp.where(allowed, logit_scores, NEG)
        attention_probabilities = jnp.where(
            allowed, jnp.exp(masked - log_totals[head_index][..., None]), 0.0
        )
        prob_grad = jnp.einsum(
            "sqd,skd->sqk", grad_head, head_values, preferred_element_type=jnp.float32
        )
        inner = jnp.sum(attention_probabilities * prob_grad, -1, keepdims=True)
        score_grad = (attention_probabilities * (prob_grad - inner)).astype(jnp.bfloat16)
        query_grad = (
            jnp.einsum("sqk,skd->sqd", score_grad, head_keys, preferred_element_type=jnp.float32)
            * scale_of_scores
        )
        key_grad = (
            jnp.einsum("sqk,sqd->skd", score_grad, head_queries, preferred_element_type=jnp.float32)
            * scale_of_scores
        )
        value_grad = jnp.einsum(
            "sqk,sqd->skd",
            attention_probabilities.astype(jnp.bfloat16),
            grad_head,
            preferred_element_type=jnp.float32,
        )
        return (query_grad, key_grad, value_grad)

    query_parts, key_parts, value_parts = lax.map(backward_head, jnp.arange(head_count))
    query_grads = query_parts.transpose(1, 2, 0, 3).reshape(tokens, features)
    key_whole = key_parts.transpose(1, 2, 0, 3).reshape(per_group, ctx_count * local_rows, features)
    value_whole = value_parts.transpose(1, 2, 0, 3).reshape(
        per_group, ctx_count * local_rows, features
    )
    key_summed, value_summed = (
        lax.psum_scatter(key_whole, "ctx", scatter_dimension=1, tiled=True),
        lax.psum_scatter(value_whole, "ctx", scatter_dimension=1, tiled=True),
    )
    key_grads = key_summed.reshape(tokens, features)
    value_grads = value_summed.reshape(tokens, features)
    query_bias_grad = jnp.sum(query_grads, 0).reshape(head_count, head_size)
    value_bias_grad = jnp.sum(value_grads, 0).reshape(head_count, head_size)
    query_low = query_grads.astype(jnp.bfloat16)
    key_low = key_grads.astype(jnp.bfloat16)
    value_low = value_grads.astype(jnp.bfloat16)
    query_weight_grad = weight_product(act_one, query_low)
    key_weight_grad = weight_product(act_one, key_low)
    value_weight_grad = weight_product(act_one, value_low)
    normed_one_grad = lax.psum(
        (
            back_product(query_low, query_mat)
            + back_product(key_low, key_mat)
            + back_product(value_low, value_mat)
        ).astype(jnp.bfloat16),
        "tp",
    ).astype(jnp.float32)
    input_in, attn_gain_grad, attn_shift_grad = norm_back(
        normed_one_grad, unit_one, inverse_one, gain_one.astype(jnp.float32)
    )
    input_grad = hidden_grad + input_in
    partial_sums = (
        lax.psum_scatter(
            attn_gain_grad.astype(jnp.bfloat16), "fsdp", scatter_dimension=0, tiled=True
        ).astype(jnp.float32),
        lax.psum_scatter(
            attn_shift_grad.astype(jnp.bfloat16), "fsdp", scatter_dimension=0, tiled=True
        ).astype(jnp.float32),
        lax.psum_scatter(
            query_weight_grad.astype(jnp.bfloat16), "fsdp", scatter_dimension=0, tiled=True
        ).astype(jnp.float32),
        lax.psum_scatter(
            query_bias_grad.astype(jnp.bfloat16), "fsdp", scatter_dimension=1, tiled=True
        ).astype(jnp.float32),
        lax.psum_scatter(
            key_weight_grad.astype(jnp.bfloat16), "fsdp", scatter_dimension=0, tiled=True
        ).astype(jnp.float32),
        lax.psum_scatter(
            value_weight_grad.astype(jnp.bfloat16), "fsdp", scatter_dimension=0, tiled=True
        ).astype(jnp.float32),
        lax.psum_scatter(
            value_bias_grad.astype(jnp.bfloat16), "fsdp", scatter_dimension=1, tiled=True
        ).astype(jnp.float32),
        lax.psum_scatter(
            out_weight_grad.astype(jnp.bfloat16), "fsdp", scatter_dimension=1, tiled=True
        ).astype(jnp.float32),
        lax.psum_scatter(
            out_bias_grad.astype(jnp.bfloat16), "fsdp", scatter_dimension=0, tiled=True
        ).astype(jnp.float32),
        lax.psum_scatter(
            mlp_gain_grad.astype(jnp.bfloat16), "fsdp", scatter_dimension=0, tiled=True
        ).astype(jnp.float32),
        lax.psum_scatter(
            mlp_shift_grad.astype(jnp.bfloat16), "fsdp", scatter_dimension=0, tiled=True
        ).astype(jnp.float32),
        lax.psum_scatter(
            up_weight_grad.astype(jnp.bfloat16), "fsdp", scatter_dimension=0, tiled=True
        ).astype(jnp.float32),
        lax.psum_scatter(
            up_bias_grad.astype(jnp.bfloat16), "fsdp", scatter_dimension=1, tiled=True
        ).astype(jnp.float32),
        lax.psum_scatter(
            down_weight_grad.astype(jnp.bfloat16), "fsdp", scatter_dimension=1, tiled=True
        ).astype(jnp.float32),
        lax.psum_scatter(
            down_bias_grad.astype(jnp.bfloat16), "fsdp", scatter_dimension=0, tiled=True
        ).astype(jnp.float32),
    )
    shards = (
        lax.psum(partial_sums[0].astype(jnp.bfloat16), "ctx").astype(jnp.float32),
        lax.psum(partial_sums[1].astype(jnp.bfloat16), "ctx").astype(jnp.float32),
        lax.psum(partial_sums[2].astype(jnp.bfloat16), "ctx").astype(jnp.float32),
        lax.psum(partial_sums[3].astype(jnp.bfloat16), "ctx").astype(jnp.float32),
        lax.psum(partial_sums[4].astype(jnp.bfloat16), "ctx").astype(jnp.float32),
        lax.psum(partial_sums[5].astype(jnp.bfloat16), "ctx").astype(jnp.float32),
        lax.psum(partial_sums[6].astype(jnp.bfloat16), "ctx").astype(jnp.float32),
        lax.psum(partial_sums[7].astype(jnp.bfloat16), "ctx").astype(jnp.float32),
        lax.psum(partial_sums[8].astype(jnp.bfloat16), "ctx").astype(jnp.float32),
        lax.psum(partial_sums[9].astype(jnp.bfloat16), "ctx").astype(jnp.float32),
        lax.psum(partial_sums[10].astype(jnp.bfloat16), "ctx").astype(jnp.float32),
        lax.psum(partial_sums[11].astype(jnp.bfloat16), "ctx").astype(jnp.float32),
        lax.psum(partial_sums[12].astype(jnp.bfloat16), "ctx").astype(jnp.float32),
        lax.psum(partial_sums[13].astype(jnp.bfloat16), "ctx").astype(jnp.float32),
        lax.psum(partial_sums[14].astype(jnp.bfloat16), "ctx").astype(jnp.float32),
    )
    sent_output = layer_output.reshape(1, per_group, local_rows, width)
    sent_grad = input_grad.reshape(1, per_group, local_rows, width)
    back_output, back_grad = (
        lax.all_to_all(
            sent_output.astype(jnp.bfloat16), "fsdp", split_axis=2, concat_axis=0, tiled=True
        ).astype(sent_output.dtype),
        lax.all_to_all(
            sent_grad.astype(jnp.bfloat16), "fsdp", split_axis=2, concat_axis=0, tiled=True
        ).astype(sent_grad.dtype),
    )
    final_output = back_output.reshape(slot_count, block_rows, width)
    final_grad = back_grad.reshape(slot_count, block_rows, width)
    return (
        final_output,
        final_grad,
        shards[0],
        shards[1],
        shards[2],
        shards[3],
        shards[4],
        shards[5],
        shards[6],
        shards[7],
        shards[8],
        shards[9],
        shards[10],
        shards[11],
        shards[12],
        shards[13],
        shards[14],
        peak_all,
        query_clipped,
        key_clipped,
    )


def attention_probs(query_block, key_rows, block, length):
    rows, cols = query_block.shape[0], key_rows.shape[0]
    scores = lax.dot_general(
        query_block, key_rows, (((1,), (1,)), ((), ())), preferred_element_type=jnp.float32
    ) * (1.0 / math.sqrt(query_block.shape[1]))
    row_pos = block * rows + lax.broadcasted_iota(jnp.int32, (rows, cols), 0)
    col_pos = lax.broadcasted_iota(jnp.int32, (rows, cols), 1)
    scores = jnp.where((col_pos <= row_pos) & (col_pos < length), scores, NEG)
    top = jnp.max(scores, -1, keepdims=True)
    terms = jnp.exp(scores - top)
    return terms / jnp.sum(terms, -1, keepdims=True), top


def attention_forward_kernel(ranks, info, q_ref, k_ref, v_ref, out_ref, peak_ref, keys, values):
    rows = keys.shape[0] // ranks
    length = info[ranks]
    for block in range(ranks):
        at = pl.ds(pl.multiple_of(info[block], rows), rows)
        keys[pl.ds(block * rows, rows), :] = k_ref[at, :]
        values[pl.ds(block * rows, rows), :] = v_ref[at, :]
    peak = jnp.full((1, 1), NEG, jnp.float32)
    for block in range(ranks):
        at = pl.ds(pl.multiple_of(info[block], rows), rows)
        extent = (block + 1) * rows
        probs, top = attention_probs(q_ref[at, :], keys[pl.ds(0, extent), :], block, length)
        out_ref[at, :] = jnp.dot(
            probs.astype(jnp.bfloat16),
            values[pl.ds(0, extent), :],
            preferred_element_type=jnp.float32,
        ).astype(out_ref.dtype)
        live = block * rows + lax.broadcasted_iota(jnp.int32, top.shape, 0) < length
        peak = jnp.maximum(peak, jnp.max(jnp.where(live, top, NEG), 0, keepdims=True))
    peak_ref[...] = jnp.broadcast_to(peak[None], peak_ref.shape)


def attention_forward(info, qkv, head_size):
    tokens, features = qkv.shape[0], qkv.shape[1] // 3
    heads, ranks = features // head_size, info.shape[0] - 1

    def part(k):
        return pl.BlockSpec((tokens, head_size), lambda h, info: (0, k * heads + h))

    attended, peaks = pl.pallas_call(
        functools.partial(attention_forward_kernel, ranks),
        out_shape=(
            jax.ShapeDtypeStruct((tokens, features), jnp.bfloat16),
            jax.ShapeDtypeStruct((heads, 8, 128), jnp.float32),
        ),
        grid_spec=pltpu.PrefetchScalarGridSpec(
            num_scalar_prefetch=1,
            grid=(heads,),
            in_specs=[part(0), part(1), part(2)],
            out_specs=(
                pl.BlockSpec((tokens, head_size), lambda h, info: (0, h)),
                pl.BlockSpec((1, 8, 128), lambda h, info: (h, 0, 0)),
            ),
            scratch_shapes=[pltpu.VMEM((tokens, head_size), jnp.bfloat16)] * 2,
        ),
        compiler_params=pltpu.CompilerParams(vmem_limit_bytes=40 << 20),
        cost_estimate=pl.CostEstimate(
            flops=4 * tokens * tokens * features, bytes_accessed=8 * tokens * features, transcendentals=0
        ),
    )(info, qkv, qkv, qkv)
    return attended, peaks[:, 0, 0]


def attention_backward_kernel(
    ranks, heads, info, q_ref, k_ref, v_ref, g_ref, out_ref, bias_ref, keys, values, key_sum, value_sum
):
    tokens, size = keys.shape
    rows = tokens // ranks
    scale = 1.0 / math.sqrt(size)
    head = pl.program_id(0)
    length = info[ranks]

    def lanes(k):
        return pl.ds(pl.multiple_of((k * heads + head) * size, size), size)

    for block in range(ranks):
        at = pl.ds(pl.multiple_of(info[block], rows), rows)
        keys[pl.ds(block * rows, rows), :] = k_ref[at, :]
        values[pl.ds(block * rows, rows), :] = v_ref[at, :]
    key_sum[...] = jnp.zeros_like(key_sum)
    value_sum[...] = jnp.zeros_like(value_sum)
    query_bias = jnp.zeros((1, size), jnp.float32)
    for block in range(ranks):
        at = pl.ds(pl.multiple_of(info[block], rows), rows)
        extent = (block + 1) * rows
        part = pl.ds(0, extent)
        queries, grads = q_ref[at, :], g_ref[at, :]
        probs, _ = attention_probs(queries, keys[part, :], block, length)
        prob_grad = lax.dot_general(
            grads, values[part, :], (((1,), (1,)), ((), ())), preferred_element_type=jnp.float32
        )
        inner = jnp.sum(probs * prob_grad, -1, keepdims=True)
        score_grad = (probs * (prob_grad - inner)).astype(jnp.bfloat16)
        query_grad = (
            jnp.dot(score_grad, keys[part, :], preferred_element_type=jnp.float32) * scale
        )
        query_bias += jnp.sum(query_grad, 0, keepdims=True)
        out_ref[at, lanes(0)] = query_grad.astype(out_ref.dtype)
        key_sum[part, :] += lax.dot_general(
            score_grad, queries, (((0,), (0,)), ((), ())), preferred_element_type=jnp.float32
        )
        value_sum[part, :] += lax.dot_general(
            probs.astype(jnp.bfloat16), grads, (((0,), (0,)), ((), ())), preferred_element_type=jnp.float32
        )
    for block in range(ranks):
        at = pl.ds(pl.multiple_of(info[block], rows), rows)
        out_ref[at, lanes(1)] = (key_sum[pl.ds(block * rows, rows), :] * scale).astype(out_ref.dtype)
        out_ref[at, lanes(2)] = value_sum[pl.ds(block * rows, rows), :].astype(out_ref.dtype)
    bias_ref[0, pl.ds(0, 1), :] = query_bias
    bias_ref[0, pl.ds(1, 1), :] = jnp.sum(value_sum[...], 0, keepdims=True)


def attention_backward(info, qkv, grads, head_size):
    tokens, features = grads.shape
    heads, ranks = features // head_size, info.shape[0] - 1

    def part(k):
        return pl.BlockSpec((tokens, head_size), lambda h, info: (0, k * heads + h))

    return pl.pallas_call(
        functools.partial(attention_backward_kernel, ranks, heads),
        out_shape=(
            jax.ShapeDtypeStruct((tokens, 3 * features), jnp.bfloat16),
            jax.ShapeDtypeStruct((heads, 8, head_size), jnp.float32),
        ),
        grid_spec=pltpu.PrefetchScalarGridSpec(
            num_scalar_prefetch=1,
            grid=(heads,),
            in_specs=[part(0), part(1), part(2), part(0)],
            out_specs=(
                pl.BlockSpec((tokens, 3 * features), lambda h, info: (0, 0)),
                pl.BlockSpec((1, 8, head_size), lambda h, info: (h, 0, 0)),
            ),
            scratch_shapes=[pltpu.VMEM((tokens, head_size), jnp.bfloat16)] * 2
            + [pltpu.VMEM((tokens, head_size), jnp.float32)] * 2,
        ),
        compiler_params=pltpu.CompilerParams(vmem_limit_bytes=48 << 20),
        cost_estimate=pl.CostEstimate(
            flops=10 * tokens * tokens * features, bytes_accessed=14 * tokens * features, transcendentals=0
        ),
    )(info, qkv, qkv, qkv, grads)


def entry_barrier(targets):
    barrier = pltpu.get_barrier_semaphore()
    for target in targets:
        pl.semaphore_signal(barrier, inc=1, device_id=target, device_id_type=pl.DeviceIdType.MESH)
    pl.semaphore_wait(barrier, len(targets))


def gather_kernel(
    q_ref,
    k_ref,
    v_ref,
    o_ref,
    u_ref,
    d_ref,
    act_ref,
    cot_ref,
    res_ref,
    qkv_all,
    out_all,
    up_all,
    down_all,
    act_all,
    cot_all,
    res_own,
    local_sem,
    send_sem,
    recv_sem,
    row_send,
    row_recv,
    join_send,
    join_recv,
):
    f = lax.axis_index("fsdp")
    z = lax.axis_index("ctx")
    t = lax.axis_index("tp")
    y, x = f // 2, f % 2
    depth = act_ref.shape[0]
    block_rows = act_ref.shape[1]
    own_rows = depth * block_rows
    strip = q_ref.shape[0]
    features = q_ref.shape[1] // 2
    hidden = u_ref.shape[1] // 2
    even = z % 2 == 0
    mate_z = z + 1 - 2 * (z % 2)
    over_x = {"fsdp": 2 * y + 1 - x, "ctx": z, "tp": t}
    over_y = {"fsdp": 2 * (1 - y) + x, "ctx": z, "tp": t}
    over_z = {"fsdp": f, "ctx": mate_z, "tp": t}
    over_core = {"fsdp": f, "ctx": z, "tp": 1 - t}
    turned = x != t

    def row_target(k):
        return {"fsdp": 2 * y + t, "ctx": k, "tp": x}

    targets = [over_x, over_y, over_z, over_core]
    targets += [row_target(lax.rem(z + k, depth)) for k in range(1, depth)]
    targets.append({"fsdp": 2 * y + 1 - x, "ctx": z, "tp": 1 - t})
    entry_barrier(targets)

    def at(start, size):
        return pl.ds(pl.multiple_of(start, 128), size)

    chunks = []
    for k, ref in enumerate((q_ref, k_ref, v_ref)):
        chunks.append(
            (
                lambda w, ref=ref: ref.at[:, at(w * features, features)],
                lambda home, k=k: qkv_all.at[at(home * strip, strip), pl.ds(k * features, features)],
            )
        )
    chunks.append(
        (
            lambda w: o_ref.at[at(w * features, features), :],
            lambda home: out_all.at[:, at(home * strip, strip)],
        )
    )
    pieces = 4
    for k in range(pieces):
        size = strip // pieces
        chunks.append(
            (
                lambda w, k=k, size=size: u_ref.at[pl.ds(k * size, size), at(w * hidden, hidden)],
                lambda home, k=k, size=size: up_all.at[at(home * strip + k * size, size), :],
            )
        )
    for k in range(pieces):
        size = hidden // pieces
        chunks.append(
            (
                lambda w, k=k, size=size: d_ref.at[at(w * hidden + k * size, size), :],
                lambda home, k=k, size=size: down_all.at[pl.ds(k * size, size), at(home * strip, strip)],
            )
        )
    count = len(chunks)

    def remote(src, dst, send, recv, target):
        return pltpu.make_async_remote_copy(
            src_ref=src,
            dst_ref=dst,
            send_sem=send,
            recv_sem=recv,
            device_id=target,
            device_id_type=pl.DeviceIdType.MESH,
        )

    far_home = 2 * (1 - y) + x

    def own_copy(i):
        source, place = chunks[i]
        return pltpu.make_async_copy(source(y), place(f), local_sem.at[i])

    def y_copy(i):
        source, place = chunks[i]
        return remote(source(1 - y), place(f), send_sem.at[0, i], recv_sem.at[0, i], over_y)

    def x_copy(i, is_even):
        source, place = chunks[i]
        if is_even:
            return remote(source(y), place(f), send_sem.at[1, i], recv_sem.at[1, i], over_x)
        return remote(
            place(far_home), place(far_home), send_sem.at[1, i], recv_sem.at[1, i], over_x
        )

    def z_copy(i, is_even):
        source, place = chunks[i]
        home = 2 * y + 1 - x if is_even else 2 * (1 - y) + 1 - x
        return remote(place(home), place(home), send_sem.at[2, i], recv_sem.at[2, i], over_z)

    rows_of = ((act_ref, act_all), (cot_ref, cot_all), (res_ref, res_own))

    def row_copy(a, k):
        source, place = rows_of[a]
        return remote(
            source.at[k],
            place.at[pl.ds(pl.multiple_of(z * block_rows, block_rows), block_rows), :],
            row_send.at[a, k],
            row_recv.at[a, z],
            row_target(k),
        )

    def row_arrival(a, k):
        source, place = rows_of[a]
        return remote(
            source.at[k],
            place.at[pl.ds(k * block_rows, block_rows), :],
            row_send.at[a, k],
            row_recv.at[a, k],
            row_target(k),
        )

    def row_stay(a, k):
        source, place = rows_of[a]
        return pltpu.make_async_copy(
            source.at[k], place.at[pl.ds(k * block_rows, block_rows), :], row_send.at[a, k]
        )

    def rows_start(a):
        for k in range(depth):
            stays = (z == k) & (x == t)
            pl.when(stays)(lambda k=k: row_stay(a, k).start())
            pl.when(jnp.logical_not(stays))(lambda k=k: row_copy(a, k).start())

    def rows_wait(a):
        for k in range(depth):
            stays = (z == k) & (x == t)
            pl.when(stays)(lambda k=k: row_stay(a, k).wait())

            @pl.when(jnp.logical_not(stays))
            def _(k=k):
                row_copy(a, k).wait_send()
                row_arrival(a, k).wait_recv()

    def block(a, k):
        return rows_of[a][1].at[pl.ds(k * own_rows, own_rows), :]

    def join_copy(a, step):
        source, place, target = (
            (0, 1, over_core),
            (0, 2, over_y),
            (2, 3, over_core),
        )[step]
        return remote(
            block(a, source), block(a, place), join_send.at[a, step], join_recv.at[a, step], target
        )

    def join_start(a):
        rows_wait(a)
        join_copy(a, 0).start()
        join_copy(a, 1).start()

    def join_pass(a):
        join_copy(a, 1).wait_recv()
        join_copy(a, 2).start()

    events = {
        0: [lambda: rows_start(0)],
        2: [lambda: rows_start(1), lambda: join_start(0)],
        4: [lambda: rows_start(2), lambda: join_pass(0)],
        6: [lambda: join_start(1)],
        9: [lambda: join_pass(1)],
    }
    lag = 2
    for i in range(count + 2 * lag):
        for event in events.get(i, ()):
            event()
        if i < count:
            y_copy(i).start()
            pl.when(even)(lambda i=i: x_copy(i, True).start())
            own_copy(i).start()
        j = i - lag
        if 0 <= j < count:
            y_copy(j).wait_recv()

            @pl.when(even)
            def _(j=j):
                x_copy(j, True).wait_recv()
                z_copy(j, True).start()

            pl.when(jnp.logical_not(even))(lambda j=j: x_copy(j, False).start())
        j = i - 2 * lag
        if 0 <= j < count:

            @pl.when(jnp.logical_not(even))
            def _(j=j):
                x_copy(j, False).wait_recv()
                z_copy(j, False).start()

    for i in range(count):
        own_copy(i).wait()
        y_copy(i).wait_send()
        x_copy(i, True).wait_send()
        z_copy(i, True).wait()
    for a in range(2):
        join_copy(a, 0).wait()
        join_copy(a, 1).wait_send()
        join_copy(a, 2).wait()
    rows_wait(2)


def gather_all(query_weight, key_weight, value_weight, out_weight, up_weight, down_weight, act, cot, res):
    strip, features, hidden = query_weight.shape[0], query_weight.shape[1] // 2, up_weight.shape[1] // 2
    width = 4 * strip
    own_rows = act.shape[0] * act.shape[1]
    bf16 = jnp.bfloat16
    hbm = pl.BlockSpec(memory_space=pl.ANY)
    count = 12
    dma = pltpu.SemaphoreType.DMA
    return pl.pallas_call(
        gather_kernel,
        out_shape=(
            jax.ShapeDtypeStruct((width, 3 * features), bf16),
            jax.ShapeDtypeStruct((features, width), bf16),
            jax.ShapeDtypeStruct((width, hidden), bf16),
            jax.ShapeDtypeStruct((hidden, width), bf16),
            jax.ShapeDtypeStruct((4 * own_rows, width), bf16),
            jax.ShapeDtypeStruct((4 * own_rows, width), bf16),
            jax.ShapeDtypeStruct((own_rows, width), jnp.float32),
        ),
        in_specs=[hbm] * 9,
        out_specs=(hbm,) * 7,
        scratch_shapes=[
            dma((count,)),
            dma((3, count)),
            dma((3, count)),
            dma((3, act.shape[0])),
            dma((3, act.shape[0])),
            dma((2, 3)),
            dma((2, 3)),
        ],
        compiler_params=pltpu.CompilerParams(collective_id=0, has_side_effects=True),
        cost_estimate=pl.CostEstimate(flops=0, bytes_accessed=64 << 20, transcendentals=0),
    )(query_weight, key_weight, value_weight, out_weight, up_weight, down_weight, act, cot, res)


def reduce_kernel(
    down_parts, up_parts, out_parts, qkv_parts, down_sum, up_sum, out_sum, qkv_sums, scratch
):
    (
        x_slot,
        own_slot,
        pair_slot,
        y_slot,
        z_slot,
        z_pair,
        inner_slot,
        total_slot,
        x_send,
        x_recv,
        own_sem,
        y_send,
        y_recv,
        outer_send,
        outer_recv,
        inner_send,
        inner_recv,
        out_sem,
        x_free,
        y_free,
        outer_free,
        inner_free,
    ) = scratch
    f = lax.axis_index("fsdp")
    z = lax.axis_index("ctx")
    t = lax.axis_index("tp")
    y, x = f // 2, f % 2
    outer = (z == 0) | (z == 3)
    inner = (z == 1) | (z == 2)
    over_x = {"fsdp": 2 * y + 1 - x, "ctx": z, "tp": t}
    over_y = {"fsdp": 2 * (1 - y) + x, "ctx": z, "tp": t}
    mate = {"fsdp": f, "ctx": z + 1 - 2 * (z % 2), "tp": t}
    middle = {"fsdp": f, "ctx": 3 - z, "tp": t}
    entry_barrier([over_x, over_y, mate, middle])
    slots, rows, cols = x_slot.shape

    def remote(src, dst, send, recv, target):
        return pltpu.make_async_remote_copy(
            src_ref=src,
            dst_ref=dst,
            send_sem=send,
            recv_sem=recv,
            device_id=target,
            device_id_type=pl.DeviceIdType.MESH,
        )

    def grant(semaphore, target):
        pl.semaphore_signal(semaphore, inc=1, device_id=target, device_id_type=pl.DeviceIdType.MESH)

    def at(start, size):
        return pl.ds(pl.multiple_of(start, 128), size)

    near_items, far_items = [], []

    def add_items(parts, row_count, col_count, place):
        near_send, far_send, near_own, far_own = parts
        for r in range(row_count):
            for c in range(col_count):
                cut = (pl.ds(r * rows, rows), pl.ds(c * cols, cols))
                near_items.append((near_send.at[cut], near_own.at[cut], place(y, r, c)))
                far_items.append((far_send.at[cut], far_own.at[cut], place(1 - y, r, c)))

    down_rows = down_sum.shape[0] // 2
    add_items(
        down_parts,
        down_rows // rows,
        1,
        lambda h, r, c: down_sum.at[at(h * down_rows + r * rows, rows), :],
    )
    up_cols = up_sum.shape[1] // 2
    add_items(
        up_parts,
        up_sum.shape[0] // rows,
        up_cols // cols,
        lambda h, r, c: up_sum.at[pl.ds(r * rows, rows), at(h * up_cols + c * cols, cols)],
    )
    out_rows = out_sum.shape[0] // 2
    add_items(
        out_parts,
        out_rows // rows,
        1,
        lambda h, r, c: out_sum.at[at(h * out_rows + r * rows, rows), :],
    )
    add_items(
        qkv_parts,
        out_sum.shape[1] // rows,
        3,
        lambda h, r, c: qkv_sums[c].at[pl.ds(r * rows, rows), at(h * cols, cols)],
    )
    items = []
    for near, far in zip(near_items, far_items):
        items += [(True, *far), (False, *near)]
    count = len(items)
    far_count = count // 2
    far_slots = y_slot.shape[0]

    def x_copy(i):
        k = i % slots
        return remote(items[i][1], x_slot.at[k], x_send.at[k], x_recv.at[k], over_x)

    def own_copy(i):
        k = i % slots
        return pltpu.make_async_copy(items[i][2], own_slot.at[k], own_sem.at[k])

    def y_copy(i):
        k = i % slots
        g = (i // 2) % far_slots
        return remote(pair_slot.at[k], y_slot.at[g], y_send.at[g], y_recv.at[g], over_y)

    def summed(i):
        return y_slot.at[(i // 2) % far_slots] if items[i][0] else pair_slot.at[i % slots]

    def outward(i):
        k = i % slots
        return remote(summed(i), z_slot.at[k], outer_send.at[k], outer_recv.at[k], mate)

    def across(i):
        k = i % slots
        return remote(z_pair.at[k], inner_slot.at[k], inner_send.at[k], inner_recv.at[k], middle)

    def backward(i):
        k = i % slots
        return remote(total_slot.at[k], z_slot.at[k], outer_send.at[k], outer_recv.at[k], mate)

    def result_inner(i):
        k = i % slots
        return pltpu.make_async_copy(total_slot.at[k], items[i][3], out_sem.at[k])

    def result_outer(i):
        k = i % slots
        return pltpu.make_async_copy(z_slot.at[k], items[i][3], out_sem.at[k])

    def add(left, right, target):
        target[...] = (left[...].astype(jnp.float32) + right[...].astype(jnp.float32)).astype(
            target.dtype
        )

    def stage_send(i):
        if i >= slots:
            pl.semaphore_wait(x_free, 1)
        x_copy(i).start()
        own_copy(i).start()

    def stage_pair(i):
        x_copy(i).wait()
        own_copy(i).wait()
        k = i % slots
        add(x_slot.at[k], own_slot.at[k], pair_slot.at[k])
        if i + slots < count:
            grant(x_free, over_x)
        if items[i][0]:
            if i // 2 >= far_slots:
                pl.semaphore_wait(y_free, 1)
            y_copy(i).start()

    def stage_outward(i):
        if items[i][0]:
            y_copy(i).wait()

        @pl.when(outer)
        def _():
            if i >= slots:
                pl.semaphore_wait(outer_free, 1)
            outward(i).start()

    def stage_across(i):
        k = i % slots

        @pl.when(outer)
        def _():
            outward(i).wait_send()

        @pl.when(inner)
        def _():
            outward(i).wait_recv()
            add(summed(i), z_slot.at[k], z_pair.at[k])
            if i + slots < count:
                grant(outer_free, mate)
            if i >= slots:
                pl.semaphore_wait(inner_free, 1)
            across(i).start()

        if items[i][0] and i // 2 + far_slots < far_count:
            grant(y_free, over_y)

    def stage_total(i):
        k = i % slots

        @pl.when(inner)
        def _():
            across(i).wait()
            add(z_pair.at[k], inner_slot.at[k], total_slot.at[k])
            if i + slots < count:
                grant(inner_free, middle)
            if i >= slots:
                pl.semaphore_wait(outer_free, 1)
            backward(i).start()
            result_inner(i).start()

    def stage_result(i):
        @pl.when(inner)
        def _():
            backward(i).wait_send()
            result_inner(i).wait()

        @pl.when(outer)
        def _():
            backward(i).wait_recv()
            result_outer(i).start()

    def stage_finish(i):
        @pl.when(outer)
        def _():
            result_outer(i).wait()
            if i + slots < count:
                grant(outer_free, mate)

    stages = (
        (0, stage_send),
        (2, stage_pair),
        (4, stage_outward),
        (6, stage_across),
        (8, stage_total),
        (10, stage_result),
        (11, stage_finish),
    )
    for step in range(count + 12):
        for lag, stage in reversed(stages):
            if 0 <= step - lag < count:
                stage(step - lag)


def reduce_all(down_parts, up_parts, out_parts, qkv_parts):
    bf16 = jnp.bfloat16
    parts = (*down_parts, *up_parts, *out_parts, *qkv_parts)
    hbm = pl.BlockSpec(memory_space=pl.ANY)
    down_rows, strip = down_parts[0].shape
    up_cols = up_parts[0].shape[1]
    features = out_parts[0].shape[0]

    def kernel(*refs):
        reduce_kernel(
            refs[0:4],
            refs[4:8],
            refs[8:12],
            refs[12:16],
            refs[16],
            refs[17],
            refs[18],
            refs[19:22],
            refs[22:],
        )

    slots, far_slots, rows, cols = 8, 8, 256, 512
    dma, regular = pltpu.SemaphoreType.DMA, pltpu.SemaphoreType.REGULAR

    def buffer(n):
        return pltpu.VMEM((n, rows, cols), bf16)

    return pl.pallas_call(
        kernel,
        out_shape=(
            jax.ShapeDtypeStruct((2 * down_rows, strip), bf16),
            jax.ShapeDtypeStruct((strip, 2 * up_cols), bf16),
            jax.ShapeDtypeStruct((2 * features, strip), bf16),
        )
        + (jax.ShapeDtypeStruct((strip, 2 * features), bf16),) * 3,
        in_specs=[hbm] * 16,
        out_specs=(hbm,) * 6,
        scratch_shapes=[
            buffer(slots),
            buffer(slots),
            buffer(slots),
            buffer(far_slots),
            buffer(slots),
            buffer(slots),
            buffer(slots),
            buffer(slots),
            dma((slots,)),
            dma((slots,)),
            dma((slots,)),
            dma((far_slots,)),
            dma((far_slots,)),
            dma((slots,)),
            dma((slots,)),
            dma((slots,)),
            dma((slots,)),
            dma((slots,)),
            regular,
            regular,
            regular,
            regular,
        ],
        compiler_params=pltpu.CompilerParams(
            collective_id=1, has_side_effects=True, vmem_limit_bytes=40 << 20
        ),
        cost_estimate=pl.CostEstimate(flops=0, bytes_accessed=64 << 20, transcendentals=0),
    )(*parts)


def split_body(
    layer_input,
    cotangent,
    seq_lengths,
    dealing,
    attn_gain,
    attn_shift,
    query_weight,
    query_bias,
    key_weight,
    value_weight,
    value_bias,
    out_weight,
    out_bias,
    mlp_gain,
    mlp_shift,
    up_weight,
    up_bias,
    down_weight,
    down_bias,
    clip_level,
):
    f32, bf16 = jnp.float32, jnp.bfloat16
    f = lax.axis_index("fsdp")
    z = lax.axis_index("ctx")
    t = lax.axis_index("tp")
    y, x = f // 2, f % 2
    depth = lax.axis_size("ctx")
    slots, block_rows, width = layer_input.shape
    local_heads = query_bias.shape[0] // 2
    head_size = 4 * query_bias.shape[1]
    features = local_heads * head_size
    hidden_units = up_weight.shape[1] // 2
    strip = query_weight.shape[0]
    own_rows = depth * block_rows

    over_x = [(0, 1), (1, 0), (2, 3), (3, 2)]
    over_y = [(0, 2), (2, 0), (1, 3), (3, 1)]
    x_core = [(0, 0), (1, 2), (2, 1), (3, 3), (4, 4), (5, 6), (6, 5), (7, 7)]

    def across_x(v):
        return lax.ppermute(v, "fsdp", over_x)

    def across_y(v):
        return lax.ppermute(v, "fsdp", over_y)

    def across_core(v):
        return lax.ppermute(v, "tp", [(0, 1), (1, 0)])

    def half(v, which, axis):
        size = v.shape[axis] // 2
        return lax.dynamic_slice_in_dim(v, which * size, size, axis)

    def return_rows(rows):
        part = rows.reshape(depth, block_rows, rows.shape[-1])
        part = lax.all_to_all(part, "ctx", split_axis=0, concat_axis=0, tiled=True)
        part = lax.ppermute(part, ("fsdp", "tp"), x_core)
        other = across_core(part)
        both = jnp.where(t == 0, jnp.stack([part, other]), jnp.stack([other, part]))
        return both.reshape(slots, block_rows, rows.shape[-1]).astype(f32)

    def gather_rows(own):
        peer = across_core(own)
        far = across_y(own)
        far_peer = across_core(far)
        return jnp.concatenate([own, peer], 0), jnp.concatenate([far, far_peer], 0)

    def scatter_rows(near, far):
        far_mine = far[:own_rows] + across_core(far[own_rows:].astype(bf16)).astype(f32)
        arrived = across_y(far_mine.astype(bf16)).astype(f32)
        return near[:own_rows] + across_core(near[own_rows:].astype(bf16)).astype(f32) + arrived

    def strip_of(v, home):
        return lax.dynamic_slice_in_dim(v, home * strip, strip, 1)

    homes = (2 * y + 1 - x, 2 * (1 - y) + 1 - x, f, 2 * (1 - y) + x)

    def products(product):
        return tuple(product(home).astype(bf16) for home in homes)

    slot = x * depth + z
    length = seq_lengths[dealing[slot]]
    own_rank = 2 * y + t
    near_rank = 2 * y + 1 - t
    far_rank = 2 * (1 - y) + t
    places = jnp.zeros((4,), jnp.int32)
    for k, rank in enumerate((own_rank, near_rank, far_rank, 2 * (1 - y) + 1 - t)):
        places = places.at[rank].set(k * own_rows)
    info = jnp.concatenate([places, length[None]])

    small = jnp.stack([attn_gain, attn_shift, out_bias, mlp_gain, mlp_shift, down_bias])
    small = lax.all_gather(small, "fsdp", axis=1, tiled=True).astype(f32)
    gain_one, shift_one, out_vec, gain_two, shift_two, down_vec = [small[k] for k in range(6)]
    vectors = jnp.concatenate([query_bias, value_bias, up_bias.reshape(-1, query_bias.shape[1])], 0)
    vectors = lax.all_gather(vectors, "fsdp", axis=0, tiled=False)
    nb = query_bias.shape[0]
    query_vec = half(vectors[:, :nb].transpose(1, 0, 2).reshape(-1), y, 0).astype(f32)
    value_vec = half(vectors[:, nb : 2 * nb].transpose(1, 0, 2).reshape(-1), y, 0).astype(f32)
    up_vec = half(
        vectors[:, 2 * nb :].reshape(4, up_bias.shape[0], -1).transpose(1, 0, 2).reshape(-1), y, 0
    ).astype(f32)

    arrived = pick_slots(layer_input, dealing, t * depth, depth)
    cot_part = lax.dynamic_slice_in_dim(cotangent, t * depth, depth, 0)
    down_bias_part = jnp.sum(cot_part, (0, 1))
    act_part = normalize(arrived, gain_one, shift_one)[0].astype(bf16)
    qkv_mat, out_mat, up_mat, down_mat, act_one, cot_low, resid = gather_all(
        query_weight,
        key_weight,
        value_weight,
        out_weight,
        up_weight,
        down_weight,
        act_part,
        cot_part.astype(bf16),
        arrived,
    )
    cot_own = cot_low[:own_rows]

    qkv_vec = jnp.concatenate([query_vec, jnp.zeros_like(query_vec), value_vec])
    qkv = (matmul(act_one, qkv_mat) + qkv_vec).astype(bf16)
    attended, peaks = attention_forward(info, qkv, head_size)
    chip_rows = 2 * own_rows
    attn_far = matmul(attended[chip_rows:], out_mat)
    attn_near = matmul(attended[:chip_rows], out_mat)
    hidden = resid + scatter_rows(attn_near, attn_far) + out_vec
    normed_b, unit_two, inverse_two = normalize(hidden, gain_two, shift_two)
    act_two = jnp.concatenate(gather_rows(normed_b.astype(bf16)), 0)

    pre = matmul(act_two, up_mat) + up_vec
    cdf = 0.5 * (1.0 + lax.erf(pre * INV_ROOT_TWO))
    gelu_low = (pre * cdf).astype(bf16)
    slope = cdf + pre * (jnp.exp(-0.5 * pre * pre) * INV_ROOT_TWO_PI)
    pre_grad = back_product(cot_low, down_mat) * slope
    pre_low = pre_grad.astype(bf16)
    up_bias_part = jnp.sum(pre_grad, 0)
    two_far = back_product(pre_low[chip_rows:], up_mat)
    two_near = back_product(pre_low[:chip_rows], up_mat)
    normed_two_grad = scatter_rows(two_near, two_far)
    hidden_in, mlp_gain_part, mlp_shift_part = norm_back(
        normed_two_grad, unit_two, inverse_two, gain_two
    )
    hidden_grad = cot_own.astype(f32) + hidden_in
    out_bias_part = jnp.sum(hidden_grad, 0)
    hidden_low = jnp.concatenate(gather_rows(hidden_grad.astype(bf16)), 0)
    attended_grad = back_product(hidden_low, out_mat).astype(bf16)
    qkv_low, bias_parts = attention_backward(info, qkv, attended_grad, head_size)

    down_parts = products(lambda home: weight_product(gelu_low, strip_of(cot_low, home)))
    up_parts = products(lambda home: weight_product(strip_of(act_two, home), pre_low))
    out_parts = products(lambda home: weight_product(attended, strip_of(hidden_low, home)))
    qkv_parts = products(lambda home: weight_product(strip_of(act_one, home), qkv_low))
    mlp_far = matmul(gelu_low[chip_rows:], down_mat)
    mlp_near = matmul(gelu_low[:chip_rows], down_mat)
    layer_output = hidden + scatter_rows(mlp_near, mlp_far) + down_vec
    final_output = return_rows(layer_output.astype(bf16))

    one_far = back_product(qkv_low[chip_rows:], qkv_mat)
    one_near = back_product(qkv_low[:chip_rows], qkv_mat)
    normed_one_grad = scatter_rows(one_near, one_far)
    _, unit_one, inverse_one = normalize(resid, gain_one, shift_one)
    input_in, attn_gain_part, attn_shift_part = norm_back(
        normed_one_grad, unit_one, inverse_one, gain_one
    )
    final_grad = return_rows((hidden_grad + input_in).astype(bf16))

    sums = reduce_all(down_parts, up_parts, out_parts, qkv_parts)
    down_weight_grad, up_weight_grad, out_weight_grad = [v.astype(f32) for v in sums[:3]]
    query_weight_grad, key_weight_grad, value_weight_grad = [v.astype(f32) for v in sums[3:]]

    def placed(v, which):
        whole = jnp.zeros((4,) + v.shape, f32)
        return lax.dynamic_update_slice_in_dim(whole, v[None], which, 0)

    column = 2 * t + y
    rows_sum = jnp.stack(
        [attn_gain_part, attn_shift_part, out_bias_part, mlp_gain_part, mlp_shift_part, down_bias_part]
    )
    head_sum = placed(jnp.stack([bias_parts[:, 0].reshape(-1), bias_parts[:, 1].reshape(-1)]), column)
    unit_sum = placed(up_bias_part, column)
    flat = jnp.concatenate([rows_sum.reshape(-1), head_sum.reshape(-1), unit_sum.reshape(-1)])
    flat = lax.psum(flat, ("fsdp", "ctx", "tp"))
    cut_one, cut_two = rows_sum.size, rows_sum.size + head_sum.size
    rows_sum = lax.dynamic_slice_in_dim(flat[:cut_one].reshape(6, width), f * strip, strip, 1)
    head_sum = lax.dynamic_slice_in_dim(flat[cut_one:cut_two].reshape(4, 2, features), 2 * t, 2, 0)
    head_sum = head_sum.transpose(1, 0, 2).reshape(2, 2 * local_heads, head_size)
    head_sum = lax.dynamic_slice_in_dim(head_sum, f * query_bias.shape[1], query_bias.shape[1], 2)
    unit_sum = lax.dynamic_slice_in_dim(
        flat[cut_two:].reshape(2, up_bias.shape[0], width), t, 1, 0
    )[0]
    unit_sum = lax.dynamic_slice_in_dim(unit_sum, f * strip, strip, 1)

    my_peaks = lax.dynamic_update_slice_in_dim(
        jnp.full((2, local_heads), NEG, f32), peaks[None], y, 0
    ).reshape(-1)
    peak_all = lax.pmax(my_peaks, ("fsdp", "ctx"))
    level = clip_level[0]
    factor = jnp.repeat(jnp.sqrt(level / jnp.maximum(peak_all, level)), head_size)
    query_clipped = (query_weight.astype(f32) * factor[None, :]).astype(bf16)
    key_clipped = (key_weight.astype(f32) * factor[None, :]).astype(bf16)
    return (
        final_output,
        final_grad,
        rows_sum[0],
        rows_sum[1],
        query_weight_grad,
        head_sum[0],
        key_weight_grad,
        value_weight_grad,
        head_sum[1],
        out_weight_grad,
        rows_sum[2],
        rows_sum[3],
        rows_sum[4],
        up_weight_grad,
        unit_sum,
        down_weight_grad,
        rows_sum[5],
        peak_all,
        query_clipped,
        key_clipped,
    )


def solution(mesh):
    sizes = dict(mesh.shape)
    small_slice = sizes == {"fsdp": 4, "ctx": 4, "tp": 2}
    return jax.shard_map(
        split_body if small_slice else gathered_body,
        mesh=mesh,
        in_specs=(
            P(None, ("fsdp", "ctx"), None),
            P(None, ("fsdp", "ctx"), None),
            P(),
            P(),
            P("fsdp"),
            P("fsdp"),
            P("fsdp", "tp"),
            P("tp", "fsdp"),
            P("fsdp", "tp"),
            P("fsdp", "tp"),
            P("tp", "fsdp"),
            P("tp", "fsdp"),
            P("fsdp"),
            P("fsdp"),
            P("fsdp"),
            P("fsdp", "tp"),
            P("tp", "fsdp"),
            P("tp", "fsdp"),
            P("fsdp"),
            P(),
        ),
        out_specs=(
            P(None, ("fsdp", "ctx"), None),
            P(None, ("fsdp", "ctx"), None),
            P("fsdp"),
            P("fsdp"),
            P("fsdp", "tp"),
            P("tp", "fsdp"),
            P("fsdp", "tp"),
            P("fsdp", "tp"),
            P("tp", "fsdp"),
            P("tp", "fsdp"),
            P("fsdp"),
            P("fsdp"),
            P("fsdp"),
            P("fsdp", "tp"),
            P("tp", "fsdp"),
            P("tp", "fsdp"),
            P("fsdp"),
            P("tp"),
            P("fsdp", "tp"),
            P("fsdp", "tp"),
        ),
        check_vma=False,
    )
```

```python
import functools
import math

import jax
import jax.numpy as jnp
from jax import lax
from jax.experimental import pallas as pl
from jax.experimental.pallas import tpu as pltpu
from jax.sharding import PartitionSpec as P

EPS = 1e-05
NEG = -1e30
INV_ROOT_TWO = 0.7071067811865476
INV_ROOT_TWO_PI = 0.3989422804014327


def normalize(values, scale_vec, offset_vec):
    center = values - jnp.mean(values, -1, keepdims=True)
    inverse = lax.rsqrt(jnp.mean(center * center, -1, keepdims=True) + EPS)
    normed = center * inverse
    return (normed * scale_vec + offset_vec, normed, inverse)


def norm_back(upstream, normed, inverse, scale_vec):
    scaled = upstream * scale_vec
    inner = (
        scaled
        - jnp.mean(scaled, -1, keepdims=True)
        - normed * jnp.mean(scaled * normed, -1, keepdims=True)
    )
    return (inverse * inner, jnp.sum(upstream * normed, 0), jnp.sum(upstream, 0))


def pick_slots(rows, dealing, first, count):
    return jnp.concatenate(
        [lax.dynamic_slice_in_dim(rows, dealing[first + j], 1, 0) for j in range(count)], 0
    )


def matmul(left, right):
    return jnp.dot(left, right, preferred_element_type=jnp.float32)


def weight_product(left, right):
    return jnp.einsum("td,te->de", left, right, preferred_element_type=jnp.float32)


def back_product(left, right):
    return jnp.einsum("te,de->td", left, right, preferred_element_type=jnp.float32)


def gathered_body(
    layer_input,
    cotangent,
    seq_lengths,
    dealing,
    attn_gain,
    attn_shift,
    query_weight,
    query_bias,
    key_weight,
    value_weight,
    value_bias,
    out_weight,
    out_bias,
    mlp_gain,
    mlp_shift,
    up_weight,
    up_bias,
    down_weight,
    down_bias,
    clip_level,
):
    shard_count = lax.axis_size("fsdp")
    ctx_count = lax.axis_size("ctx")
    my_group = lax.axis_index("fsdp")
    ctx_place = lax.axis_index("ctx")
    slot_count, block_rows, width = layer_input.shape
    per_group = slot_count // shard_count
    local_rows = shard_count * block_rows
    tokens = per_group * local_rows
    dealt_input = pick_slots(layer_input, dealing, 0, slot_count).reshape(
        shard_count, per_group, block_rows, width
    )
    dealt_grad = cotangent.reshape(shard_count, per_group, block_rows, width)
    arrived_input, arrived_grad = (
        lax.all_to_all(dealt_input, "fsdp", split_axis=0, concat_axis=2, tiled=True),
        lax.all_to_all(dealt_grad, "fsdp", split_axis=0, concat_axis=2, tiled=True),
    )
    resid = arrived_input.reshape(tokens, width)
    upstream = arrived_grad.reshape(tokens, width)
    seq_lens = lax.dynamic_slice_in_dim(
        jnp.take(seq_lengths, dealing), my_group * per_group, per_group
    )
    gathered = (
        lax.all_gather(attn_gain, "fsdp", axis=0, tiled=True),
        lax.all_gather(attn_shift, "fsdp", axis=0, tiled=True),
        lax.all_gather(query_weight, "fsdp", axis=0, tiled=True),
        lax.all_gather(query_bias, "fsdp", axis=1, tiled=True),
        lax.all_gather(key_weight, "fsdp", axis=0, tiled=True),
        lax.all_gather(value_weight, "fsdp", axis=0, tiled=True),
        lax.all_gather(value_bias, "fsdp", axis=1, tiled=True),
        lax.all_gather(out_weight, "fsdp", axis=1, tiled=True),
        lax.all_gather(out_bias, "fsdp", axis=0, tiled=True),
        lax.all_gather(mlp_gain, "fsdp", axis=0, tiled=True),
        lax.all_gather(mlp_shift, "fsdp", axis=0, tiled=True),
        lax.all_gather(up_weight, "fsdp", axis=0, tiled=True),
        lax.all_gather(up_bias, "fsdp", axis=1, tiled=True),
        lax.all_gather(down_weight, "fsdp", axis=1, tiled=True),
        lax.all_gather(down_bias, "fsdp", axis=0, tiled=True),
    )
    (
        gain_one,
        shift_one,
        query_mat,
        query_vec,
        key_mat,
        value_mat,
        value_vec,
        out_mat,
        out_vec,
        gain_two,
        shift_two,
        up_mat,
        up_vec,
        down_mat,
        down_vec,
    ) = gathered
    head_count, head_size = query_vec.shape
    features = head_count * head_size
    scale_of_scores = 1.0 / math.sqrt(head_size)
    row_ids = jnp.arange(local_rows, dtype=jnp.int32)
    query_pos = (row_ids // block_rows * ctx_count + ctx_place) * block_rows + row_ids % block_rows
    key_ids = jnp.arange(ctx_count * local_rows, dtype=jnp.int32)
    key_rows = key_ids % local_rows
    key_pos = (
        key_rows // block_rows * ctx_count + key_ids // local_rows
    ) * block_rows + key_rows % block_rows
    allowed = (key_pos[None, None, :] <= query_pos[None, :, None]) & (
        key_pos[None, None, :] < seq_lens[:, None, None]
    )
    query_live = query_pos[None, :] < seq_lens[:, None]
    normed_a, unit_one, inverse_one = normalize(
        resid, gain_one.astype(jnp.float32), shift_one.astype(jnp.float32)
    )
    act_one = normed_a.astype(jnp.bfloat16)
    queries = (
        (matmul(act_one, query_mat) + query_vec.reshape(features).astype(jnp.float32))
        .astype(jnp.bfloat16)
        .reshape(per_group, local_rows, features)
    )
    keys_mine = (
        matmul(act_one, key_mat).astype(jnp.bfloat16).reshape(per_group, local_rows, features)
    )
    values_mine = (
        (matmul(act_one, value_mat) + value_vec.reshape(features).astype(jnp.float32))
        .astype(jnp.bfloat16)
        .reshape(per_group, local_rows, features)
    )
    keys_all, values_all = (
        lax.all_gather(keys_mine, "ctx", axis=1, tiled=True),
        lax.all_gather(values_mine, "ctx", axis=1, tiled=True),
    )

    def head_cut(array, head_index):
        return lax.dynamic_slice_in_dim(array, head_index * head_size, head_size, 2)

    def head_scores(head_queries, head_keys):
        return (
            jnp.einsum("sqd,skd->sqk", head_queries, head_keys, preferred_element_type=jnp.float32)
            * scale_of_scores
        )

    def forward_head(head_index):
        logit_scores = head_scores(head_cut(queries, head_index), head_cut(keys_all, head_index))
        masked = jnp.where(allowed, logit_scores, NEG)
        row_top = jnp.max(masked, -1, keepdims=True)
        exp_terms = jnp.where(allowed, jnp.exp(masked - row_top), 0.0)
        total = jnp.sum(exp_terms, -1, keepdims=True)
        attention_probabilities = exp_terms / total
        attended_rows = jnp.einsum(
            "sqk,skd->sqd",
            attention_probabilities.astype(jnp.bfloat16),
            head_cut(values_all, head_index),
            preferred_element_type=jnp.float32,
        )
        log_total = row_top[..., 0] + jnp.log(total[..., 0])
        peak = jnp.max(jnp.where(query_live, row_top[..., 0], NEG))
        return (attended_rows, log_total, peak)

    attended_rows, log_totals, peaks = lax.map(forward_head, jnp.arange(head_count))
    attn_low = attended_rows.transpose(1, 2, 0, 3).reshape(tokens, features).astype(jnp.bfloat16)
    attn_sum = lax.psum(matmul(attn_low, out_mat), "tp")
    hidden = resid + attn_sum + out_vec.astype(jnp.float32)
    normed_b, unit_two, inverse_two = normalize(
        hidden, gain_two.astype(jnp.float32), shift_two.astype(jnp.float32)
    )
    act_two = normed_b.astype(jnp.bfloat16)
    pre = matmul(act_two, up_mat) + up_vec.reshape(-1).astype(jnp.float32)
    gelu_low = jax.nn.gelu(pre, approximate=False).astype(jnp.bfloat16)
    mlp_sum = lax.psum(matmul(gelu_low, down_mat).astype(jnp.bfloat16), "tp").astype(jnp.float32)
    layer_output = hidden + mlp_sum + down_vec.astype(jnp.float32)
    peak_all = lax.pmax(peaks, ("fsdp", "ctx"))
    level = clip_level[0]
    factor = jnp.repeat(jnp.sqrt(level / jnp.maximum(peak_all, level)), head_size)
    query_clipped = (query_weight.astype(jnp.float32) * factor[None, :]).astype(jnp.bfloat16)
    key_clipped = (key_weight.astype(jnp.float32) * factor[None, :]).astype(jnp.bfloat16)
    grad_low = upstream.astype(jnp.bfloat16)
    down_weight_grad = weight_product(gelu_low, grad_low)
    down_bias_grad = jnp.sum(upstream, 0)
    cdf = 0.5 * (1.0 + lax.erf(pre * INV_ROOT_TWO))
    density = jnp.exp(-0.5 * pre * pre) * INV_ROOT_TWO_PI
    pre_grad = back_product(grad_low, down_mat) * (cdf + pre * density)
    pre_low = pre_grad.astype(jnp.bfloat16)
    up_weight_grad = weight_product(act_two, pre_low)
    up_bias_grad = jnp.sum(pre_grad, 0).reshape(up_vec.shape)
    normed_two_grad = lax.psum(back_product(pre_low, up_mat), "tp")
    hidden_in, mlp_gain_grad, mlp_shift_grad = norm_back(
        normed_two_grad, unit_two, inverse_two, gain_two.astype(jnp.float32)
    )
    hidden_grad = upstream + hidden_in
    hidden_low = hidden_grad.astype(jnp.bfloat16)
    out_weight_grad = weight_product(attn_low, hidden_low)
    out_bias_grad = jnp.sum(hidden_grad, 0)
    attended_grad = (
        back_product(hidden_low, out_mat)
        .astype(jnp.bfloat16)
        .reshape(per_group, local_rows, features)
    )

    def backward_head(head_index):
        head_queries = head_cut(queries, head_index)
        head_keys = head_cut(keys_all, head_index)
        head_values = head_cut(values_all, head_index)
        grad_head = head_cut(attended_grad, head_index)
        logit_scores = head_scores(head_queries, head_keys)
        masked = jnp.where(allowed, logit_scores, NEG)
        attention_probabilities = jnp.where(
            allowed, jnp.exp(masked - log_totals[head_index][..., None]), 0.0
        )
        prob_grad = jnp.einsum(
            "sqd,skd->sqk", grad_head, head_values, preferred_element_type=jnp.float32
        )
        inner = jnp.sum(attention_probabilities * prob_grad, -1, keepdims=True)
        score_grad = (attention_probabilities * (prob_grad - inner)).astype(jnp.bfloat16)
        query_grad = (
            jnp.einsum("sqk,skd->sqd", score_grad, head_keys, preferred_element_type=jnp.float32)
            * scale_of_scores
        )
        key_grad = (
            jnp.einsum("sqk,sqd->skd", score_grad, head_queries, preferred_element_type=jnp.float32)
            * scale_of_scores
        )
        value_grad = jnp.einsum(
            "sqk,sqd->skd",
            attention_probabilities.astype(jnp.bfloat16),
            grad_head,
            preferred_element_type=jnp.float32,
        )
        return (query_grad, key_grad, value_grad)

    query_parts, key_parts, value_parts = lax.map(backward_head, jnp.arange(head_count))
    query_grads = query_parts.transpose(1, 2, 0, 3).reshape(tokens, features)
    key_whole = key_parts.transpose(1, 2, 0, 3).reshape(per_group, ctx_count * local_rows, features)
    value_whole = value_parts.transpose(1, 2, 0, 3).reshape(
        per_group, ctx_count * local_rows, features
    )
    key_summed, value_summed = (
        lax.psum_scatter(key_whole, "ctx", scatter_dimension=1, tiled=True),
        lax.psum_scatter(value_whole, "ctx", scatter_dimension=1, tiled=True),
    )
    key_grads = key_summed.reshape(tokens, features)
    value_grads = value_summed.reshape(tokens, features)
    query_bias_grad = jnp.sum(query_grads, 0).reshape(head_count, head_size)
    value_bias_grad = jnp.sum(value_grads, 0).reshape(head_count, head_size)
    query_low = query_grads.astype(jnp.bfloat16)
    key_low = key_grads.astype(jnp.bfloat16)
    value_low = value_grads.astype(jnp.bfloat16)
    query_weight_grad = weight_product(act_one, query_low)
    key_weight_grad = weight_product(act_one, key_low)
    value_weight_grad = weight_product(act_one, value_low)
    normed_one_grad = lax.psum(
        (
            back_product(query_low, query_mat)
            + back_product(key_low, key_mat)
            + back_product(value_low, value_mat)
        ).astype(jnp.bfloat16),
        "tp",
    ).astype(jnp.float32)
    input_in, attn_gain_grad, attn_shift_grad = norm_back(
        normed_one_grad, unit_one, inverse_one, gain_one.astype(jnp.float32)
    )
    input_grad = hidden_grad + input_in
    partial_sums = (
        lax.psum_scatter(
            attn_gain_grad.astype(jnp.bfloat16), "fsdp", scatter_dimension=0, tiled=True
        ).astype(jnp.float32),
        lax.psum_scatter(
            attn_shift_grad.astype(jnp.bfloat16), "fsdp", scatter_dimension=0, tiled=True
        ).astype(jnp.float32),
        lax.psum_scatter(
            query_weight_grad.astype(jnp.bfloat16), "fsdp", scatter_dimension=0, tiled=True
        ).astype(jnp.float32),
        lax.psum_scatter(
            query_bias_grad.astype(jnp.bfloat16), "fsdp", scatter_dimension=1, tiled=True
        ).astype(jnp.float32),
        lax.psum_scatter(
            key_weight_grad.astype(jnp.bfloat16), "fsdp", scatter_dimension=0, tiled=True
        ).astype(jnp.float32),
        lax.psum_scatter(
            value_weight_grad.astype(jnp.bfloat16), "fsdp", scatter_dimension=0, tiled=True
        ).astype(jnp.float32),
        lax.psum_scatter(
            value_bias_grad.astype(jnp.bfloat16), "fsdp", scatter_dimension=1, tiled=True
        ).astype(jnp.float32),
        lax.psum_scatter(
            out_weight_grad.astype(jnp.bfloat16), "fsdp", scatter_dimension=1, tiled=True
        ).astype(jnp.float32),
        lax.psum_scatter(
            out_bias_grad.astype(jnp.bfloat16), "fsdp", scatter_dimension=0, tiled=True
        ).astype(jnp.float32),
        lax.psum_scatter(
            mlp_gain_grad.astype(jnp.bfloat16), "fsdp", scatter_dimension=0, tiled=True
        ).astype(jnp.float32),
        lax.psum_scatter(
            mlp_shift_grad.astype(jnp.bfloat16), "fsdp", scatter_dimension=0, tiled=True
        ).astype(jnp.float32),
        lax.psum_scatter(
            up_weight_grad.astype(jnp.bfloat16), "fsdp", scatter_dimension=0, tiled=True
        ).astype(jnp.float32),
        lax.psum_scatter(
            up_bias_grad.astype(jnp.bfloat16), "fsdp", scatter_dimension=1, tiled=True
        ).astype(jnp.float32),
        lax.psum_scatter(
            down_weight_grad.astype(jnp.bfloat16), "fsdp", scatter_dimension=1, tiled=True
        ).astype(jnp.float32),
        lax.psum_scatter(
            down_bias_grad.astype(jnp.bfloat16), "fsdp", scatter_dimension=0, tiled=True
        ).astype(jnp.float32),
    )
    shards = (
        lax.psum(partial_sums[0].astype(jnp.bfloat16), "ctx").astype(jnp.float32),
        lax.psum(partial_sums[1].astype(jnp.bfloat16), "ctx").astype(jnp.float32),
        lax.psum(partial_sums[2].astype(jnp.bfloat16), "ctx").astype(jnp.float32),
        lax.psum(partial_sums[3].astype(jnp.bfloat16), "ctx").astype(jnp.float32),
        lax.psum(partial_sums[4].astype(jnp.bfloat16), "ctx").astype(jnp.float32),
        lax.psum(partial_sums[5].astype(jnp.bfloat16), "ctx").astype(jnp.float32),
        lax.psum(partial_sums[6].astype(jnp.bfloat16), "ctx").astype(jnp.float32),
        lax.psum(partial_sums[7].astype(jnp.bfloat16), "ctx").astype(jnp.float32),
        lax.psum(partial_sums[8].astype(jnp.bfloat16), "ctx").astype(jnp.float32),
        lax.psum(partial_sums[9].astype(jnp.bfloat16), "ctx").astype(jnp.float32),
        lax.psum(partial_sums[10].astype(jnp.bfloat16), "ctx").astype(jnp.float32),
        lax.psum(partial_sums[11].astype(jnp.bfloat16), "ctx").astype(jnp.float32),
        lax.psum(partial_sums[12].astype(jnp.bfloat16), "ctx").astype(jnp.float32),
        lax.psum(partial_sums[13].astype(jnp.bfloat16), "ctx").astype(jnp.float32),
        lax.psum(partial_sums[14].astype(jnp.bfloat16), "ctx").astype(jnp.float32),
    )
    sent_output = layer_output.reshape(1, per_group, local_rows, width)
    sent_grad = input_grad.reshape(1, per_group, local_rows, width)
    back_output, back_grad = (
        lax.all_to_all(
            sent_output.astype(jnp.bfloat16), "fsdp", split_axis=2, concat_axis=0, tiled=True
        ).astype(sent_output.dtype),
        lax.all_to_all(
            sent_grad.astype(jnp.bfloat16), "fsdp", split_axis=2, concat_axis=0, tiled=True
        ).astype(sent_grad.dtype),
    )
    final_output = back_output.reshape(slot_count, block_rows, width)
    final_grad = back_grad.reshape(slot_count, block_rows, width)
    return (
        final_output,
        final_grad,
        shards[0],
        shards[1],
        shards[2],
        shards[3],
        shards[4],
        shards[5],
        shards[6],
        shards[7],
        shards[8],
        shards[9],
        shards[10],
        shards[11],
        shards[12],
        shards[13],
        shards[14],
        peak_all,
        query_clipped,
        key_clipped,
    )


def attention_probs(query_block, key_rows, block, length):
    rows, cols = query_block.shape[0], key_rows.shape[0]
    scores = lax.dot_general(
        query_block, key_rows, (((1,), (1,)), ((), ())), preferred_element_type=jnp.float32
    ) * (1.0 / math.sqrt(query_block.shape[1]))
    row_pos = block * rows + lax.broadcasted_iota(jnp.int32, (rows, cols), 0)
    col_pos = lax.broadcasted_iota(jnp.int32, (rows, cols), 1)
    scores = jnp.where((col_pos <= row_pos) & (col_pos < length), scores, NEG)
    top = jnp.max(scores, -1, keepdims=True)
    terms = jnp.exp(scores - top)
    return terms / jnp.sum(terms, -1, keepdims=True), top


def attention_forward_kernel(ranks, info, q_ref, k_ref, v_ref, out_ref, peak_ref, keys, values):
    rows = keys.shape[0] // ranks
    length = info[ranks]
    for block in range(ranks):
        at = pl.ds(pl.multiple_of(info[block], rows), rows)
        keys[pl.ds(block * rows, rows), :] = k_ref[at, :]
        values[pl.ds(block * rows, rows), :] = v_ref[at, :]
    peak = jnp.full((1, 1), NEG, jnp.float32)
    for block in range(ranks):
        at = pl.ds(pl.multiple_of(info[block], rows), rows)
        extent = (block + 1) * rows
        probs, top = attention_probs(q_ref[at, :], keys[pl.ds(0, extent), :], block, length)
        out_ref[at, :] = jnp.dot(
            probs.astype(jnp.bfloat16),
            values[pl.ds(0, extent), :],
            preferred_element_type=jnp.float32,
        ).astype(out_ref.dtype)
        live = block * rows + lax.broadcasted_iota(jnp.int32, top.shape, 0) < length
        peak = jnp.maximum(peak, jnp.max(jnp.where(live, top, NEG), 0, keepdims=True))
    peak_ref[...] = jnp.broadcast_to(peak[None], peak_ref.shape)


def attention_forward(info, qkv, head_size):
    tokens, features = qkv.shape[0], qkv.shape[1] // 3
    heads, ranks = features // head_size, info.shape[0] - 1

    def part(k):
        return pl.BlockSpec((tokens, head_size), lambda h, info: (0, k * heads + h))

    attended, peaks = pl.pallas_call(
        functools.partial(attention_forward_kernel, ranks),
        out_shape=(
            jax.ShapeDtypeStruct((tokens, features), jnp.bfloat16),
            jax.ShapeDtypeStruct((heads, 8, 128), jnp.float32),
        ),
        grid_spec=pltpu.PrefetchScalarGridSpec(
            num_scalar_prefetch=1,
            grid=(heads,),
            in_specs=[part(0), part(1), part(2)],
            out_specs=(
                pl.BlockSpec((tokens, head_size), lambda h, info: (0, h)),
                pl.BlockSpec((1, 8, 128), lambda h, info: (h, 0, 0)),
            ),
            scratch_shapes=[pltpu.VMEM((tokens, head_size), jnp.bfloat16)] * 2,
        ),
        compiler_params=pltpu.CompilerParams(vmem_limit_bytes=40 << 20),
        cost_estimate=pl.CostEstimate(
            flops=4 * tokens * tokens * features, bytes_accessed=8 * tokens * features, transcendentals=0
        ),
    )(info, qkv, qkv, qkv)
    return attended, peaks[:, 0, 0]


def entry_barrier(targets):
    barrier = pltpu.get_barrier_semaphore()
    for target in targets:
        pl.semaphore_signal(barrier, inc=1, device_id=target, device_id_type=pl.DeviceIdType.MESH)
    pl.semaphore_wait(barrier, len(targets))


def gather_kernel(
    q_ref,
    k_ref,
    v_ref,
    o_ref,
    u_ref,
    d_ref,
    act_ref,
    cot_ref,
    res_ref,
    qkv_all,
    out_all,
    up_all,
    down_all,
    act_all,
    cot_all,
    res_own,
    local_sem,
    send_sem,
    recv_sem,
    row_send,
    row_recv,
    join_send,
    join_recv,
):
    f = lax.axis_index("fsdp")
    z = lax.axis_index("ctx")
    t = lax.axis_index("tp")
    y, x = f // 2, f % 2
    depth = act_ref.shape[0]
    block_rows = act_ref.shape[1]
    own_rows = depth * block_rows
    strip = q_ref.shape[0]
    features = q_ref.shape[1] // 2
    hidden = u_ref.shape[1] // 2
    even = z % 2 == 0
    mate_z = z + 1 - 2 * (z % 2)
    over_x = {"fsdp": 2 * y + 1 - x, "ctx": z, "tp": t}
    over_y = {"fsdp": 2 * (1 - y) + x, "ctx": z, "tp": t}
    over_z = {"fsdp": f, "ctx": mate_z, "tp": t}
    over_core = {"fsdp": f, "ctx": z, "tp": 1 - t}
    turned = x != t

    def row_target(k):
        return {"fsdp": 2 * y + t, "ctx": k, "tp": x}

    targets = [over_x, over_y, over_z, over_core]
    targets += [row_target(lax.rem(z + k, depth)) for k in range(1, depth)]
    targets.append({"fsdp": 2 * y + 1 - x, "ctx": z, "tp": 1 - t})
    entry_barrier(targets)

    def at(start, size):
        return pl.ds(pl.multiple_of(start, 128), size)

    chunks = []
    for k, ref in enumerate((q_ref, k_ref, v_ref)):
        chunks.append(
            (
                lambda w, ref=ref: ref.at[:, at(w * features, features)],
                lambda home, k=k: qkv_all.at[at(home * strip, strip), pl.ds(k * features, features)],
            )
        )
    chunks.append(
        (
            lambda w: o_ref.at[at(w * features, features), :],
            lambda home: out_all.at[:, at(home * strip, strip)],
        )
    )
    pieces = 4
    for k in range(pieces):
        size = strip // pieces
        chunks.append(
            (
                lambda w, k=k, size=size: u_ref.at[pl.ds(k * size, size), at(w * hidden, hidden)],
                lambda home, k=k, size=size: up_all.at[at(home * strip + k * size, size), :],
            )
        )
    for k in range(pieces):
        size = hidden // pieces
        chunks.append(
            (
                lambda w, k=k, size=size: d_ref.at[at(w * hidden + k * size, size), :],
                lambda home, k=k, size=size: down_all.at[pl.ds(k * size, size), at(home * strip, strip)],
            )
        )
    count = len(chunks)

    def remote(src, dst, send, recv, target):
        return pltpu.make_async_remote_copy(
            src_ref=src,
            dst_ref=dst,
            send_sem=send,
            recv_sem=recv,
            device_id=target,
            device_id_type=pl.DeviceIdType.MESH,
        )

    far_home = 2 * (1 - y) + x

    def own_copy(i):
        source, place = chunks[i]
        return pltpu.make_async_copy(source(y), place(f), local_sem.at[i])

    def y_copy(i):
        source, place = chunks[i]
        return remote(source(1 - y), place(f), send_sem.at[0, i], recv_sem.at[0, i], over_y)

    def x_copy(i, is_even):
        source, place = chunks[i]
        if is_even:
            return remote(source(y), place(f), send_sem.at[1, i], recv_sem.at[1, i], over_x)
        return remote(
            place(far_home), place(far_home), send_sem.at[1, i], recv_sem.at[1, i], over_x
        )

    def z_copy(i, is_even):
        source, place = chunks[i]
        home = 2 * y + 1 - x if is_even else 2 * (1 - y) + 1 - x
        return remote(place(home), place(home), send_sem.at[2, i], recv_sem.at[2, i], over_z)

    rows_of = ((act_ref, act_all), (cot_ref, cot_all), (res_ref, res_own))

    def row_copy(a, k):
        source, place = rows_of[a]
        return remote(
            source.at[k],
            place.at[pl.ds(pl.multiple_of(z * block_rows, block_rows), block_rows), :],
            row_send.at[a, k],
            row_recv.at[a, z],
            row_target(k),
        )

    def row_arrival(a, k):
        source, place = rows_of[a]
        return remote(
            source.at[k],
            place.at[pl.ds(k * block_rows, block_rows), :],
            row_send.at[a, k],
            row_recv.at[a, k],
            row_target(k),
        )

    def row_stay(a, k):
        source, place = rows_of[a]
        return pltpu.make_async_copy(
            source.at[k], place.at[pl.ds(k * block_rows, block_rows), :], row_send.at[a, k]
        )

    def rows_start(a):
        for k in range(depth):
            stays = (z == k) & (x == t)
            pl.when(stays)(lambda k=k: row_stay(a, k).start())
            pl.when(jnp.logical_not(stays))(lambda k=k: row_copy(a, k).start())

    def rows_wait(a):
        for k in range(depth):
            stays = (z == k) & (x == t)
            pl.when(stays)(lambda k=k: row_stay(a, k).wait())

            @pl.when(jnp.logical_not(stays))
            def _(k=k):
                row_copy(a, k).wait_send()
                row_arrival(a, k).wait_recv()

    def block(a, k):
        return rows_of[a][1].at[pl.ds(k * own_rows, own_rows), :]

    def join_copy(a, step):
        source, place, target = (
            (0, 1, over_core),
            (0, 2, over_y),
            (2, 3, over_core),
        )[step]
        return remote(
            block(a, source), block(a, place), join_send.at[a, step], join_recv.at[a, step], target
        )

    def join_start(a):
        rows_wait(a)
        join_copy(a, 0).start()
        join_copy(a, 1).start()

    def join_pass(a):
        join_copy(a, 1).wait_recv()
        join_copy(a, 2).start()

    events = {
        0: [lambda: rows_start(0)],
        2: [lambda: rows_start(1), lambda: join_start(0)],
        4: [lambda: rows_start(2), lambda: join_pass(0)],
        6: [lambda: join_start(1)],
        9: [lambda: join_pass(1)],
    }
    lag = 2
    for i in range(count + 2 * lag):
        for event in events.get(i, ()):
            event()
        if i < count:
            y_copy(i).start()
            pl.when(even)(lambda i=i: x_copy(i, True).start())
            own_copy(i).start()
        j = i - lag
        if 0 <= j < count:
            y_copy(j).wait_recv()

            @pl.when(even)
            def _(j=j):
                x_copy(j, True).wait_recv()
                z_copy(j, True).start()

            pl.when(jnp.logical_not(even))(lambda j=j: x_copy(j, False).start())
        j = i - 2 * lag
        if 0 <= j < count:

            @pl.when(jnp.logical_not(even))
            def _(j=j):
                x_copy(j, False).wait_recv()
                z_copy(j, False).start()

    for i in range(count):
        own_copy(i).wait()
        y_copy(i).wait_send()
        x_copy(i, True).wait_send()
        z_copy(i, True).wait()
    for a in range(2):
        join_copy(a, 0).wait()
        join_copy(a, 1).wait_send()
        join_copy(a, 2).wait()
    rows_wait(2)


def gather_all(query_weight, key_weight, value_weight, out_weight, up_weight, down_weight, act, cot, res):
    strip, features, hidden = query_weight.shape[0], query_weight.shape[1] // 2, up_weight.shape[1] // 2
    width = 4 * strip
    own_rows = act.shape[0] * act.shape[1]
    bf16 = jnp.bfloat16
    hbm = pl.BlockSpec(memory_space=pl.ANY)
    count = 12
    dma = pltpu.SemaphoreType.DMA
    return pl.pallas_call(
        gather_kernel,
        out_shape=(
            jax.ShapeDtypeStruct((width, 3 * features), bf16),
            jax.ShapeDtypeStruct((features, width), bf16),
            jax.ShapeDtypeStruct((width, hidden), bf16),
            jax.ShapeDtypeStruct((hidden, width), bf16),
            jax.ShapeDtypeStruct((4 * own_rows, width), bf16),
            jax.ShapeDtypeStruct((4 * own_rows, width), bf16),
            jax.ShapeDtypeStruct((own_rows, width), jnp.float32),
        ),
        in_specs=[hbm] * 9,
        out_specs=(hbm,) * 7,
        scratch_shapes=[
            dma((count,)),
            dma((3, count)),
            dma((3, count)),
            dma((3, act.shape[0])),
            dma((3, act.shape[0])),
            dma((2, 3)),
            dma((2, 3)),
        ],
        compiler_params=pltpu.CompilerParams(collective_id=0, has_side_effects=True),
        cost_estimate=pl.CostEstimate(flops=0, bytes_accessed=64 << 20, transcendentals=0),
    )(query_weight, key_weight, value_weight, out_weight, up_weight, down_weight, act, cot, res)


def remote_copy(src, dst, send, recv, target):
    return pltpu.make_async_remote_copy(
        src_ref=src,
        dst_ref=dst,
        send_sem=send,
        recv_sem=recv,
        device_id=target,
        device_id_type=pl.DeviceIdType.MESH,
    )


def grant(semaphore, target):
    pl.semaphore_signal(semaphore, inc=1, device_id=target, device_id_type=pl.DeviceIdType.MESH)


def aligned(start, size):
    return pl.ds(pl.multiple_of(start, 128), size)


class Place:
    def __init__(self, depth):
        self.depth = depth
        f = lax.axis_index("fsdp")
        z = lax.axis_index("ctx")
        t = lax.axis_index("tp")
        y, x = f // 2, f % 2
        self.f, self.z, self.t, self.y, self.x = f, z, t, y, x
        self.over_x = {"fsdp": 2 * y + 1 - x, "ctx": z, "tp": t}
        self.over_y = {"fsdp": 2 * (1 - y) + x, "ctx": z, "tp": t}
        self.over_core = {"fsdp": f, "ctx": z, "tp": 1 - t}
        self.mate = {"fsdp": f, "ctx": z + 1 - 2 * (z % 2), "tp": t}
        self.middle = {"fsdp": f, "ctx": 3 - z, "tp": t}
        self.hop = {"fsdp": f, "ctx": lax.rem(z + 2, 4), "tp": t}
        self.homes = (2 * y + 1 - x, 2 * (1 - y) + 1 - x, f, 2 * (1 - y) + x)

    def row_target(self, k):
        return {"fsdp": 2 * self.y + self.t, "ctx": k, "tp": self.x}

    def row_targets(self):
        others = [self.row_target(lax.rem(self.z + k, self.depth)) for k in range(1, self.depth)]
        return others + [{"fsdp": 2 * self.y + 1 - self.x, "ctx": self.z, "tp": 1 - self.t}]

    def block_place(self, block):
        return 2 * jnp.where(self.y == block // 2, 0, 1) + jnp.where(self.t == block % 2, 0, 1)


def reduce_stages(p, groups, scratch):
    (
        x_slot,
        own_slot,
        pair_slot,
        y_slot,
        z_slot,
        z_pair,
        inner_slot,
        total_slot,
        x_send,
        x_recv,
        own_sem,
        y_send,
        y_recv,
        outer_send,
        outer_recv,
        inner_send,
        inner_recv,
        out_sem,
        x_free,
        y_free,
        outer_free,
        inner_free,
    ) = scratch
    y, z = p.y, p.z
    outer = (z == 0) | (z == 3)
    inner = (z == 1) | (z == 2)
    slots, rows, cols = x_slot.shape
    items = []
    for parts, row_count, col_count, place in groups:
        near_send, far_send, near_own, far_own = parts
        for r in range(row_count):
            for c in range(col_count):
                cut = (pl.ds(r * rows, rows), pl.ds(c * cols, cols))
                items.append((True, far_send.at[cut], far_own.at[cut], place(1 - y, r, c)))
                items.append((False, near_send.at[cut], near_own.at[cut], place(y, r, c)))
    count = len(items)
    far_count = count // 2
    far_slots = y_slot.shape[0]

    def x_copy(i):
        k = i % slots
        return remote_copy(items[i][1], x_slot.at[k], x_send.at[k], x_recv.at[k], p.over_x)

    def own_copy(i):
        k = i % slots
        return pltpu.make_async_copy(items[i][2], own_slot.at[k], own_sem.at[k])

    def y_copy(i):
        k, g = i % slots, (i // 2) % far_slots
        return remote_copy(pair_slot.at[k], y_slot.at[g], y_send.at[g], y_recv.at[g], p.over_y)

    def summed(i):
        return y_slot.at[(i // 2) % far_slots] if items[i][0] else pair_slot.at[i % slots]

    def outward(i):
        k = i % slots
        return remote_copy(summed(i), z_slot.at[k], outer_send.at[k], outer_recv.at[k], p.mate)

    def across(i):
        k = i % slots
        return remote_copy(z_pair.at[k], inner_slot.at[k], inner_send.at[k], inner_recv.at[k], p.middle)

    def backward(i):
        k = i % slots
        return remote_copy(total_slot.at[k], z_slot.at[k], outer_send.at[k], outer_recv.at[k], p.mate)

    def result_inner(i):
        k = i % slots
        return pltpu.make_async_copy(total_slot.at[k], items[i][3], out_sem.at[k])

    def result_outer(i):
        k = i % slots
        return pltpu.make_async_copy(z_slot.at[k], items[i][3], out_sem.at[k])

    def add(left, right, target):
        target[...] = (left[...].astype(jnp.float32) + right[...].astype(jnp.float32)).astype(
            target.dtype
        )

    def stage_send(i):
        if i >= slots:
            pl.semaphore_wait(x_free, 1)
        x_copy(i).start()
        own_copy(i).start()

    def stage_pair(i):
        x_copy(i).wait()
        own_copy(i).wait()
        k = i % slots
        add(x_slot.at[k], own_slot.at[k], pair_slot.at[k])
        if i + slots < count:
            grant(x_free, p.over_x)
        if items[i][0]:
            if i // 2 >= far_slots:
                pl.semaphore_wait(y_free, 1)
            y_copy(i).start()

    def stage_outward(i):
        if items[i][0]:
            y_copy(i).wait()

        @pl.when(outer)
        def _():
            if i >= slots:
                pl.semaphore_wait(outer_free, 1)
            outward(i).start()

    def stage_across(i):
        k = i % slots

        @pl.when(outer)
        def _():
            outward(i).wait_send()

        @pl.when(inner)
        def _():
            outward(i).wait_recv()
            add(summed(i), z_slot.at[k], z_pair.at[k])
            if i + slots < count:
                grant(outer_free, p.mate)
            if i >= slots:
                pl.semaphore_wait(inner_free, 1)
            across(i).start()

        if items[i][0] and i // 2 + far_slots < far_count:
            grant(y_free, p.over_y)

    def stage_total(i):
        k = i % slots

        @pl.when(inner)
        def _():
            across(i).wait()
            add(z_pair.at[k], inner_slot.at[k], total_slot.at[k])
            if i + slots < count:
                grant(inner_free, p.middle)
            if i >= slots:
                pl.semaphore_wait(outer_free, 1)
            backward(i).start()
            result_inner(i).start()

    def stage_result(i):
        @pl.when(inner)
        def _():
            backward(i).wait_send()
            result_inner(i).wait()

        @pl.when(outer)
        def _():
            backward(i).wait_recv()
            result_outer(i).start()

    def stage_finish(i):
        @pl.when(outer)
        def _():
            result_outer(i).wait()
            if i + slots < count:
                grant(outer_free, p.mate)

    stages = (
        (11, stage_finish),
        (10, stage_result),
        (8, stage_total),
        (6, stage_across),
        (4, stage_outward),
        (2, stage_pair),
        (0, stage_send),
    )

    def run(step):
        for lag, stage in stages:
            if 0 <= step - lag < count:
                stage(step - lag)

    return run, count + 12


def reduce_scratch(slots, far_slots, rows, cols):
    dma, regular = pltpu.SemaphoreType.DMA, pltpu.SemaphoreType.REGULAR
    counts = (slots,) * 3 + (far_slots,) + (slots,) * 4
    return [pltpu.VMEM((n, rows, cols), jnp.bfloat16) for n in counts] + [
        dma((n,)) for n in (slots,) * 3 + (far_slots,) * 2 + (slots,) * 5
    ] + [regular] * 4


class RowSum:
    def __init__(self, p, rows, arrived, sent, loaded, send_sem, recv_sem, load_sem, core_free, y_free, uses):
        self.p, self.rows, self.uses = p, rows, uses
        self.arrived, self.sent, self.loaded = arrived, sent, loaded
        self.send_sem, self.recv_sem, self.load_sem = send_sem, recv_sem, load_sem
        self.core_free, self.y_free = core_free, y_free

    def block(self, ref, k):
        return ref.at[pl.ds(k * self.rows, self.rows), :]

    def hop(self, ref, k):
        source = (self.block(ref, 3), self.block(ref, 1), self.sent)[k]
        target = self.p.over_y if k == 2 else self.p.over_core
        return remote_copy(source, self.arrived.at[k], self.send_sem.at[k], self.recv_sem.at[k], target)

    def load(self, ref, k):
        return pltpu.make_async_copy(self.block(ref, k), self.loaded, self.load_sem)

    def start(self, use, ref, local):
        if use:
            pl.semaphore_wait(self.core_free, 1)
            pl.semaphore_wait(self.y_free, 1)
        self.hop(ref, 0).start()
        self.hop(ref, 1).start()
        if not local:
            self.load(ref, 2).start()

    def middle(self, ref, local):
        self.hop(ref, 0).wait()
        if not local:
            self.load(ref, 2).wait()
        base = self.block(ref, 2) if local else self.loaded

        @pl.loop(0, self.rows // 32)
        def _(k):
            at = pl.ds(pl.multiple_of(k * 32, 32), 32)
            self.sent[at, :] = (
                base[at, :].astype(jnp.float32) + self.arrived[0, at, :].astype(jnp.float32)
            ).astype(jnp.bfloat16)

        self.hop(ref, 2).start()
        if not local:
            self.load(ref, 0).start()

    def finish(self, ref, local):
        self.hop(ref, 1).wait()
        self.hop(ref, 2).wait()
        if not local:
            self.load(ref, 0).wait()

    def total(self, ref, local, at):
        base = self.block(ref, 0) if local else self.loaded
        return (
            base[at, :].astype(jnp.float32)
            + self.arrived[1, at, :].astype(jnp.float32)
            + self.arrived[2, at, :].astype(jnp.float32)
        )

    def release(self, use):
        if use + 1 < self.uses:
            grant(self.core_free, self.p.over_core)
            grant(self.y_free, self.p.over_y)


def unit_rows(values):
    center = values - jnp.mean(values, -1, keepdims=True)
    inverse = lax.rsqrt(jnp.mean(center * center, -1, keepdims=True) + EPS)
    return center * inverse, inverse


def unit_back(upstream, unit, inverse, gain):
    scaled = upstream * gain
    return inverse * (
        scaled
        - jnp.mean(scaled, -1, keepdims=True)
        - unit * jnp.mean(scaled * unit, -1, keepdims=True)
    )


GAIN_ONE, SHIFT_ONE, OUT_BIAS, GAIN_TWO, SHIFT_TWO, DOWN_BIAS, QUERY_BIAS, VALUE_BIAS, UP_BIAS, PEAKS = (
    0,
    1,
    2,
    3,
    4,
    5,
    6,
    7,
    8,
    12,
)


def backward_kernel(
    head_size,
    info,
    vector_ref,
    small_in,
    down_parts,
    up_parts,
    two_part,
    mlp_part,
    hidden_hbm,
    cot_hbm,
    resid_hbm,
    out_hbm,
    qkv_mat_hbm,
    qkv_hbm,
    attended_hbm,
    act_hbm,
    down_sum,
    up_sum,
    out_sum,
    qkv_sums,
    rows_out,
    rows_grad,
    small,
    out_products,
    qkv_products,
    engine,
    base,
    hidden_grad,
    low,
    out_mat,
    attended_grad,
    qkv,
    qkv_grad,
    act,
    attended,
    qkv_mat,
    keys,
    values,
    key_sum,
    value_sum,
    stage,
    packed,
    arrived,
    sent,
    loaded,
    small_arrived,
    load_sem,
    sum_send,
    sum_recv,
    sum_load,
    join_send,
    join_recv,
    stage_sem,
    row_send,
    row_recv,
    share_send,
    share_recv,
    small_send,
    small_recv,
    core_free,
    y_free,
):
    f32, bf16 = jnp.float32, jnp.bfloat16
    own_rows, width = base.shape
    tokens, features = attended.shape
    heads = features // head_size
    depth = rows_out.shape[0] // 2
    block_rows = rows_out.shape[1]
    p = Place(depth)
    x, y, z, t = p.x, p.y, p.z, p.t
    entry_barrier(
        [p.over_x, p.over_y, p.over_core, p.mate, p.middle, p.hop] + p.row_targets()
    )
    length = info[0]
    scale = 1.0 / math.sqrt(head_size)
    column = 2 * t + y

    rows, cols = engine[0].shape[1:]
    down_rows = down_sum.shape[0] // 2
    up_cols = up_sum.shape[1] // 2
    strip = out_sum.shape[1]

    def four(ref):
        return tuple(ref.at[k] for k in range(4))

    groups = (
        (
            down_parts,
            down_rows // rows,
            1,
            lambda h, r, c: down_sum.at[aligned(h * down_rows + r * rows, rows), :],
        ),
        (
            up_parts,
            strip // rows,
            up_cols // cols,
            lambda h, r, c: up_sum.at[pl.ds(r * rows, rows), aligned(h * up_cols + c * cols, cols)],
        ),
        (
            four(out_products),
            features // rows,
            1,
            lambda h, r, c: out_sum.at[aligned(h * features + r * rows, rows), :],
        ),
        (
            four(qkv_products),
            strip // rows,
            3,
            lambda h, r, c: qkv_sums[c].at[pl.ds(r * rows, rows), aligned(h * cols, cols)],
        ),
    )
    run, steps = reduce_stages(p, groups, engine)

    loads = [
        pltpu.make_async_copy(source, target, load_sem.at[k])
        for k, (source, target) in enumerate(
            (
                (hidden_hbm, base),
                (cot_hbm.at[pl.ds(0, own_rows), :], packed),
                (out_hbm, out_mat),
                (qkv_hbm, qkv),
                (attended_hbm, attended),
                (act_hbm, act),
                (qkv_mat_hbm, qkv_mat),
                (resid_hbm, base),
            )
        )
    ]
    sums = RowSum(
        p, own_rows, arrived, sent, loaded, sum_send, sum_recv, sum_load, core_free, y_free, 3
    )
    group_rows = 16
    quarter = own_rows // 4 // group_rows

    def start():
        for k in range(7):
            loads[k].start()
        small[...] = small_in[...]
        key_sum[...] = jnp.zeros_like(key_sum)
        value_sum[...] = jnp.zeros_like(value_sum)
        sums.start(0, two_part, False)

    def two_middle():
        sums.middle(two_part, False)

    def two_finish():
        sums.finish(two_part, False)
        loads[0].wait()
        loads[1].wait()

    def accumulate(row, value):
        small[pl.ds(row, 1), :] += jnp.sum(value, 0, keepdims=True)

    def two_rows(part):
        gain = vector_ref[pl.ds(GAIN_TWO, 1), :]

        @pl.loop(part * quarter, (part + 1) * quarter)
        def _(k):
            at = pl.ds(pl.multiple_of(k * group_rows, group_rows), group_rows)
            upstream = sums.total(two_part, False, at)
            unit, inverse = unit_rows(base[at, :])
            grad = packed[at, :].astype(f32) + unit_back(upstream, unit, inverse, gain)
            hidden_grad[at, :] = grad
            low[at, :] = grad.astype(bf16)
            accumulate(GAIN_TWO, upstream * unit)
            accumulate(SHIFT_TWO, upstream)
            accumulate(OUT_BIAS, grad)

    def low_block(k):
        return low.at[pl.ds(k * own_rows, own_rows), :]

    def join(k):
        source, place, target = ((0, 1, p.over_core), (0, 2, p.over_y), (2, 3, p.over_core))[k]
        return remote_copy(low_block(source), low_block(place), join_send.at[k], join_recv.at[k], target)

    def join_start():
        join(0).start()
        join(1).start()
        sums.release(0)

    def join_pass():
        join(1).wait_recv()
        join(2).start()

    def attend_block(k):
        at = pl.ds(k * own_rows, own_rows)
        attended_grad[at, :] = lax.dot_general(
            low[at, :], out_mat[...], (((1,), (1,)), ((), ())), preferred_element_type=f32
        ).astype(bf16)

    def attend_own():
        loads[2].wait()
        attend_block(0)

    def attend_peer():
        join(0).wait()
        attend_block(1)

    def attend_far():
        attend_block(2)

    def attend_last():
        join(1).wait_send()
        join(2).wait()
        attend_block(3)

    def mlp_start():
        sums.start(1, mlp_part, False)

    def mlp_middle():
        sums.middle(mlp_part, False)

    def mlp_finish():
        sums.finish(mlp_part, False)
        bias = vector_ref[pl.ds(DOWN_BIAS, 1), :]

        @pl.loop(0, own_rows // group_rows)
        def _(k):
            at = pl.ds(pl.multiple_of(k * group_rows, group_rows), group_rows)
            packed[at, :] = (base[at, :] + sums.total(mlp_part, False, at) + bias).astype(bf16)

        sums.release(1)

    def row_source(k):
        return packed.at[pl.ds(k * block_rows, block_rows), :]

    row_ends = (rows_out, rows_grad)

    def row_copy(a, k):
        end = row_ends[a].at[x * depth + z]
        return remote_copy(row_source(k), end, row_send.at[a, k], row_recv.at[a, z], p.row_target(k))

    def row_arrival(a, k):
        end = row_ends[a].at[t * depth + k]
        return remote_copy(row_source(k), end, row_send.at[a, k], row_recv.at[a, k], p.row_target(k))

    def row_stay(a, k):
        return pltpu.make_async_copy(row_source(k), row_ends[a].at[x * depth + z], row_send.at[a, k])

    def rows_start(a):
        for k in range(depth):
            stays = (z == k) & (x == t)
            pl.when(stays)(lambda k=k: row_stay(a, k).start())
            pl.when(jnp.logical_not(stays))(lambda k=k: row_copy(a, k).start())

    def share(a):
        group = row_ends[a].at[pl.ds(t * depth, depth)]
        return remote_copy(group, group, share_send.at[a], share_recv.at[a], p.over_core)

    def rows_share(a):
        for k in range(depth):
            stays = (z == k) & (x == t)
            pl.when(stays)(lambda k=k: row_stay(a, k).wait())

            @pl.when(jnp.logical_not(stays))
            def _(k=k):
                row_copy(a, k).wait_send()
                row_arrival(a, k).wait_recv()

        share(a).start()

    def head_rows():
        loads[3].wait()
        loads[4].wait()
        for block in range(4):
            at = pl.ds(pl.multiple_of(p.block_place(block) * own_rows, own_rows), own_rows)
            keys[pl.ds(block * own_rows, own_rows), :] = qkv[at, pl.ds(features, features)]
            values[pl.ds(block * own_rows, own_rows), :] = qkv[at, pl.ds(2 * features, features)]

    def attention_block(block):
        at = pl.ds(pl.multiple_of(p.block_place(block) * own_rows, own_rows), own_rows)
        part = pl.ds(0, (block + 1) * own_rows)

        @pl.loop(0, heads)
        def _(head):
            lanes = aligned(head * head_size, head_size)
            queries, grads = qkv[at, lanes], attended_grad[at, lanes]
            probs, _ = attention_probs(queries, keys[part, lanes], block, length)
            prob_grad = lax.dot_general(
                grads, values[part, lanes], (((1,), (1,)), ((), ())), preferred_element_type=f32
            )
            inner = jnp.sum(probs * prob_grad, -1, keepdims=True)
            score_grad = (probs * (prob_grad - inner)).astype(bf16)
            query_grad = (
                jnp.dot(score_grad, keys[part, lanes], preferred_element_type=f32) * scale
            )
            spot = aligned(column * features + head * head_size, head_size)
            small[pl.ds(QUERY_BIAS, 1), spot] += jnp.sum(query_grad, 0, keepdims=True)
            qkv_grad[at, lanes] = query_grad.astype(bf16)
            key_sum[part, lanes] += lax.dot_general(
                score_grad, queries, (((0,), (0,)), ((), ())), preferred_element_type=f32
            )
            value_sum[part, lanes] += lax.dot_general(
                probs.astype(bf16), grads, (((0,), (0,)), ((), ())), preferred_element_type=f32
            )

    def attention_end(block):
        at = pl.ds(pl.multiple_of(p.block_place(block) * own_rows, own_rows), own_rows)
        part = pl.ds(block * own_rows, own_rows)
        qkv_grad[at, pl.ds(features, features)] = (key_sum[part, :] * scale).astype(bf16)
        value_grad = value_sum[part, :]
        qkv_grad[at, pl.ds(2 * features, features)] = value_grad.astype(bf16)
        spot = aligned(column * features, features)
        small[pl.ds(VALUE_BIAS, 1), spot] += jnp.sum(value_grad, 0, keepdims=True)

    stored = []

    def store(value, target):
        k = len(stored) % 2
        if len(stored) >= 2:
            stored[-2].wait()
        stage[k] = value.astype(bf16)
        copy = pltpu.make_async_copy(stage.at[k], target, stage_sem.at[k])
        copy.start()
        stored.append(copy)

    def over_tokens(left, right):
        return lax.dot_general(left, right, (((0,), (0,)), ((), ())), preferred_element_type=f32)

    def out_product(k):
        store(
            over_tokens(attended[...], low[:, aligned(p.homes[k] * strip, strip)]),
            out_products.at[k],
        )

    def qkv_product(k, c):
        if k == 0 and c == 0:
            loads[5].wait()
        cut = pl.ds(c * features, features)
        store(
            over_tokens(act[:, aligned(p.homes[k] * strip, strip)], qkv_grad[:, cut]),
            qkv_products.at[k, :, cut],
        )

    def products_end():
        stored[-2].wait()
        stored[-1].wait()

    def one_block(k):
        if k == 3:
            loads[6].wait()
        at = pl.ds(k * own_rows, own_rows)

        @pl.loop(0, 4)
        def _(n):
            cut = aligned(n * strip, strip)
            low[at, cut] = lax.dot_general(
                qkv_grad[at, :], qkv_mat[cut, :], (((1,), (1,)), ((), ())), preferred_element_type=f32
            ).astype(bf16)

    def one_start():
        sums.start(2, low, True)

    def one_middle():
        sums.middle(low, True)

    def one_finish():
        sums.finish(low, True)
        loads[7].wait()

    def one_rows(part):
        gain = vector_ref[pl.ds(GAIN_ONE, 1), :]

        @pl.loop(part * quarter, (part + 1) * quarter)
        def _(k):
            at = pl.ds(pl.multiple_of(k * group_rows, group_rows), group_rows)
            upstream = sums.total(low, True, at)
            unit, inverse = unit_rows(base[at, :])
            grad = hidden_grad[at, :] + unit_back(upstream, unit, inverse, gain)
            packed[at, :] = grad.astype(bf16)
            accumulate(GAIN_ONE, upstream * unit)
            accumulate(SHIFT_ONE, upstream)

    def small_copy(k):
        target = (p.over_core, p.over_x, p.over_y, p.mate, p.hop)[k]
        return remote_copy(small, small_arrived.at[k], small_send.at[k], small_recv.at[k], target)

    def small_add(k):
        small_copy(k).wait()
        mine, other = small[...], small_arrived[k]
        row = lax.broadcasted_iota(jnp.int32, mine.shape, 0)
        small[...] = jnp.where(row == PEAKS, jnp.maximum(mine, other), mine + other)

    def call(function, *arguments):
        return lambda: function(*arguments)

    plan = {}

    def at_step(step, *tasks):
        plan.setdefault(step, []).extend(tasks)

    at_step(0, start)
    at_step(2, two_middle)
    at_step(7, two_finish, call(two_rows, 0))
    for k in range(1, 4):
        at_step(7 + k // 2, call(two_rows, k))
    at_step(8, join_start, mlp_start)
    at_step(9, attend_own)
    at_step(10, mlp_middle, attend_peer)
    at_step(12, head_rows)
    at_step(13, join_pass)
    at_step(14, attend_far)
    at_step(15, attend_last)
    at_step(16, call(attention_block, 0), call(attention_block, 1))
    at_step(17, call(attention_block, 2))
    at_step(18, call(attention_block, 3))
    at_step(19, *(call(attention_end, k) for k in range(4)))
    for k in range(4):
        at_step(19 + k, *(call(qkv_product, k, c) for c in range(3)))
        at_step(23, call(out_product, k))
    at_step(24, products_end, call(one_block, 3), call(one_block, 1), one_start)
    at_step(25, call(one_block, 2), call(one_block, 0))
    at_step(26, one_middle)
    at_step(20, mlp_finish, lambda: rows_start(0), loads[7].start)
    at_step(25, lambda: rows_share(0))
    at_step(31, one_finish, share(0).wait, call(one_rows, 0))
    for k in range(1, 4):
        at_step(31 + k // 2, call(one_rows, k))
    at_step(32, lambda: rows_start(1))
    at_step(33, small_copy(0).start)
    for k in range(4):
        at_step(35 + 2 * k, call(small_add, k), small_copy(k + 1).start)
    at_step(43, call(small_add, 4))
    at_step(38, lambda: rows_share(1))
    at_step(44, share(1).wait)
    for step in range(steps):
        run(step)
        for task in plan.get(step, ()):
            task()


def backward_all(
    head_size,
    length,
    vectors,
    small,
    down_parts,
    up_parts,
    two_part,
    mlp_part,
    hidden,
    cot_low,
    resid,
    out_mat,
    qkv_mat,
    qkv,
    attended,
    act_one,
    slots,
):
    bf16, f32 = jnp.bfloat16, jnp.float32
    hbm = pl.BlockSpec(memory_space=pl.ANY)
    vmem = pl.BlockSpec(memory_space=pltpu.VMEM)
    down_rows, strip = down_parts[0].shape
    up_cols = up_parts[0].shape[1]
    tokens, features = attended.shape
    own_rows, width = hidden.shape
    depth = slots // 2
    engine = reduce_scratch(6, 4, 256, 512)
    n_engine = len(engine)

    def kernel(*refs):
        ins, rest = refs[:21], refs[21:]
        outs, scratch = rest[:11], rest[11:]
        backward_kernel(
            head_size,
            ins[0],
            ins[1],
            ins[2],
            ins[3:7],
            ins[7:11],
            *ins[11:],
            outs[0],
            outs[1],
            outs[2],
            outs[3:6],
            *outs[6:],
            scratch[:n_engine],
            *scratch[n_engine:],
        )

    dma, regular = pltpu.SemaphoreType.DMA, pltpu.SemaphoreType.REGULAR

    def hold(shape, dtype=bf16):
        return pltpu.VMEM(shape, dtype)

    return pl.pallas_call(
        kernel,
        out_shape=(
            jax.ShapeDtypeStruct((2 * down_rows, strip), bf16),
            jax.ShapeDtypeStruct((strip, 2 * up_cols), bf16),
            jax.ShapeDtypeStruct((2 * features, strip), bf16),
            jax.ShapeDtypeStruct((strip, 2 * features), bf16),
            jax.ShapeDtypeStruct((strip, 2 * features), bf16),
            jax.ShapeDtypeStruct((strip, 2 * features), bf16),
            jax.ShapeDtypeStruct((slots, own_rows // depth, width), bf16),
            jax.ShapeDtypeStruct((slots, own_rows // depth, width), bf16),
            jax.ShapeDtypeStruct(small.shape, f32),
            jax.ShapeDtypeStruct((4, features, strip), bf16),
            jax.ShapeDtypeStruct((4, strip, 3 * features), bf16),
        ),
        in_specs=[pl.BlockSpec(memory_space=pltpu.SMEM), vmem, vmem] + [hbm] * 18,
        out_specs=(hbm,) * 8 + (vmem,) + (hbm,) * 2,
        scratch_shapes=engine
        + [
            hold((own_rows, width), f32),
            hold((own_rows, width), f32),
            hold((tokens, width)),
            hold((features, width)),
            hold((tokens, features)),
            hold((tokens, 3 * features)),
            hold((tokens, 3 * features)),
            hold((tokens, width)),
            hold((tokens, features)),
            hold((width, 3 * features)),
            hold((tokens, features)),
            hold((tokens, features)),
            hold((tokens, features), f32),
            hold((tokens, features), f32),
            hold((2, features, strip)),
            hold((own_rows, width)),
            hold((3, own_rows, width)),
            hold((own_rows, width)),
            hold((own_rows, width)),
            hold((5,) + small.shape, f32),
            dma((8,)),
            dma((3,)),
            dma((3,)),
            dma(()),
            dma((3,)),
            dma((3,)),
            dma((2,)),
            dma((2, depth)),
            dma((2, depth)),
            dma((2,)),
            dma((2,)),
            dma((5,)),
            dma((5,)),
            regular,
            regular,
        ],
        compiler_params=pltpu.CompilerParams(
            collective_id=1, has_side_effects=True, vmem_limit_bytes=58 << 20
        ),
        cost_estimate=pl.CostEstimate(flops=0, bytes_accessed=64 << 20, transcendentals=0),
    )(
        length,
        vectors,
        small,
        *down_parts,
        *up_parts,
        two_part,
        mlp_part,
        hidden,
        cot_low,
        resid,
        out_mat,
        qkv_mat,
        qkv,
        attended,
        act_one,
    )


def split_body(
    layer_input,
    cotangent,
    seq_lengths,
    dealing,
    attn_gain,
    attn_shift,
    query_weight,
    query_bias,
    key_weight,
    value_weight,
    value_bias,
    out_weight,
    out_bias,
    mlp_gain,
    mlp_shift,
    up_weight,
    up_bias,
    down_weight,
    down_bias,
    clip_level,
):
    f32, bf16 = jnp.float32, jnp.bfloat16
    f = lax.axis_index("fsdp")
    z = lax.axis_index("ctx")
    t = lax.axis_index("tp")
    y, x = f // 2, f % 2
    depth = lax.axis_size("ctx")
    slots, block_rows, width = layer_input.shape
    local_heads = query_bias.shape[0] // 2
    head_size = 4 * query_bias.shape[1]
    features = local_heads * head_size
    hidden_units = up_weight.shape[1] // 2
    strip = query_weight.shape[0]
    own_rows = depth * block_rows

    over_x = [(0, 1), (1, 0), (2, 3), (3, 2)]
    over_y = [(0, 2), (2, 0), (1, 3), (3, 1)]
    x_core = [(0, 0), (1, 2), (2, 1), (3, 3), (4, 4), (5, 6), (6, 5), (7, 7)]

    def across_x(v):
        return lax.ppermute(v, "fsdp", over_x)

    def across_y(v):
        return lax.ppermute(v, "fsdp", over_y)

    def across_core(v):
        return lax.ppermute(v, "tp", [(0, 1), (1, 0)])

    def half(v, which, axis):
        size = v.shape[axis] // 2
        return lax.dynamic_slice_in_dim(v, which * size, size, axis)

    def gather_rows(own):
        peer = across_core(own)
        far = across_y(own)
        far_peer = across_core(far)
        return jnp.concatenate([own, peer], 0), jnp.concatenate([far, far_peer], 0)

    def scatter_rows(near, far):
        far_mine = far[:own_rows] + across_core(far[own_rows:].astype(bf16)).astype(f32)
        arrived = across_y(far_mine.astype(bf16)).astype(f32)
        return near[:own_rows] + across_core(near[own_rows:].astype(bf16)).astype(f32) + arrived

    def strip_of(v, home):
        return lax.dynamic_slice_in_dim(v, home * strip, strip, 1)

    homes = (2 * y + 1 - x, 2 * (1 - y) + 1 - x, f, 2 * (1 - y) + x)

    def products(product):
        return tuple(product(home).astype(bf16) for home in homes)

    slot = x * depth + z
    length = seq_lengths[dealing[slot]]
    own_rank = 2 * y + t
    near_rank = 2 * y + 1 - t
    far_rank = 2 * (1 - y) + t
    places = jnp.zeros((4,), jnp.int32)
    for k, rank in enumerate((own_rank, near_rank, far_rank, 2 * (1 - y) + 1 - t)):
        places = places.at[rank].set(k * own_rows)
    info = jnp.concatenate([places, length[None]])

    small = jnp.stack([attn_gain, attn_shift, out_bias, mlp_gain, mlp_shift, down_bias])
    small = lax.all_gather(small, "fsdp", axis=1, tiled=True).astype(f32)
    vectors_whole = small
    gain_one, shift_one, out_vec, gain_two, shift_two, down_vec = [small[k] for k in range(6)]
    vectors = jnp.concatenate([query_bias, value_bias, up_bias.reshape(-1, query_bias.shape[1])], 0)
    vectors = lax.all_gather(vectors, "fsdp", axis=0, tiled=False)
    nb = query_bias.shape[0]
    query_vec = half(vectors[:, :nb].transpose(1, 0, 2).reshape(-1), y, 0).astype(f32)
    value_vec = half(vectors[:, nb : 2 * nb].transpose(1, 0, 2).reshape(-1), y, 0).astype(f32)
    up_vec = half(
        vectors[:, 2 * nb :].reshape(4, up_bias.shape[0], -1).transpose(1, 0, 2).reshape(-1), y, 0
    ).astype(f32)

    arrived = pick_slots(layer_input, dealing, t * depth, depth)
    cot_part = lax.dynamic_slice_in_dim(cotangent, t * depth, depth, 0)
    down_bias_part = jnp.sum(cot_part, (0, 1))
    act_part = normalize(arrived, gain_one, shift_one)[0].astype(bf16)
    qkv_mat, out_mat, up_mat, down_mat, act_one, cot_low, resid = gather_all(
        query_weight,
        key_weight,
        value_weight,
        out_weight,
        up_weight,
        down_weight,
        act_part,
        cot_part.astype(bf16),
        arrived,
    )
    cot_own = cot_low[:own_rows]

    qkv_vec = jnp.concatenate([query_vec, jnp.zeros_like(query_vec), value_vec])
    qkv = (matmul(act_one, qkv_mat) + qkv_vec).astype(bf16)
    attended, peaks = attention_forward(info, qkv, head_size)
    chip_rows = 2 * own_rows
    attn_far = matmul(attended[chip_rows:], out_mat)
    attn_near = matmul(attended[:chip_rows], out_mat)
    hidden = resid + scatter_rows(attn_near, attn_far) + out_vec
    normed_b = normalize(hidden, gain_two, shift_two)[0]
    act_two = jnp.concatenate(gather_rows(normed_b.astype(bf16)), 0)

    pre = matmul(act_two, up_mat) + up_vec
    cdf = 0.5 * (1.0 + lax.erf(pre * INV_ROOT_TWO))
    gelu_low = (pre * cdf).astype(bf16)
    slope = cdf + pre * (jnp.exp(-0.5 * pre * pre) * INV_ROOT_TWO_PI)
    pre_grad = back_product(cot_low, down_mat) * slope
    pre_low = pre_grad.astype(bf16)
    up_bias_part = jnp.sum(pre_grad, 0)
    down_parts = products(lambda home: weight_product(gelu_low, strip_of(cot_low, home)))
    up_parts = products(lambda home: weight_product(strip_of(act_two, home), pre_low))
    two_part = back_product(pre_low, up_mat).astype(bf16)
    mlp_part = matmul(gelu_low, down_mat).astype(bf16)
    column = 2 * t + y
    small = jnp.zeros((16, width), f32).at[DOWN_BIAS].set(down_bias_part)
    small = lax.dynamic_update_slice(small, up_bias_part[None], (UP_BIAS + column, 0))
    small = small.at[PEAKS].set(NEG)
    small = lax.dynamic_update_slice(small, peaks[None], (PEAKS, local_heads * (2 * t + y)))
    (
        down_sum,
        up_sum,
        out_sum,
        query_sum,
        key_sum,
        value_sum,
        rows_out,
        rows_grad,
        totals,
        _,
        _,
    ) = backward_all(
        head_size,
        length[None],
        vectors_whole,
        small,
        down_parts,
        up_parts,
        two_part,
        mlp_part,
        hidden,
        cot_low,
        resid,
        out_mat,
        qkv_mat,
        qkv,
        attended,
        act_one,
        slots,
    )
    rows_sum = lax.dynamic_slice(totals, (0, f * strip), (6, strip))
    head_sum = lax.dynamic_slice(totals, (QUERY_BIAS, 2 * t * features), (2, 2 * features))
    head_sum = head_sum.reshape(2, 2 * local_heads, head_size)
    head_sum = lax.dynamic_slice_in_dim(head_sum, f * query_bias.shape[1], query_bias.shape[1], 2)
    unit_sum = lax.dynamic_slice(
        totals, (UP_BIAS + up_bias.shape[0] * t, f * strip), (up_bias.shape[0], strip)
    )
    peak_all = lax.dynamic_slice(totals, (PEAKS, 2 * local_heads * t), (1, 2 * local_heads))[0]
    level = clip_level[0]
    factor = jnp.repeat(jnp.sqrt(level / jnp.maximum(peak_all, level)), head_size)
    query_clipped = (query_weight.astype(f32) * factor[None, :]).astype(bf16)
    key_clipped = (key_weight.astype(f32) * factor[None, :]).astype(bf16)
    return (
        rows_out.astype(f32),
        rows_grad.astype(f32),
        rows_sum[GAIN_ONE],
        rows_sum[SHIFT_ONE],
        query_sum.astype(f32),
        head_sum[0],
        key_sum.astype(f32),
        value_sum.astype(f32),
        head_sum[1],
        out_sum.astype(f32),
        rows_sum[OUT_BIAS],
        rows_sum[GAIN_TWO],
        rows_sum[SHIFT_TWO],
        up_sum.astype(f32),
        unit_sum,
        down_sum.astype(f32),
        rows_sum[DOWN_BIAS],
        peak_all,
        query_clipped,
        key_clipped,
    )


def solution(mesh):
    sizes = dict(mesh.shape)
    small_slice = sizes == {"fsdp": 4, "ctx": 4, "tp": 2}
    return jax.shard_map(
        split_body if small_slice else gathered_body,
        mesh=mesh,
        in_specs=(
            P(None, ("fsdp", "ctx"), None),
            P(None, ("fsdp", "ctx"), None),
            P(),
            P(),
            P("fsdp"),
            P("fsdp"),
            P("fsdp", "tp"),
            P("tp", "fsdp"),
            P("fsdp", "tp"),
            P("fsdp", "tp"),
            P("tp", "fsdp"),
            P("tp", "fsdp"),
            P("fsdp"),
            P("fsdp"),
            P("fsdp"),
            P("fsdp", "tp"),
            P("tp", "fsdp"),
            P("tp", "fsdp"),
            P("fsdp"),
            P(),
        ),
        out_specs=(
            P(None, ("fsdp", "ctx"), None),
            P(None, ("fsdp", "ctx"), None),
            P("fsdp"),
            P("fsdp"),
            P("fsdp", "tp"),
            P("tp", "fsdp"),
            P("fsdp", "tp"),
            P("fsdp", "tp"),
            P("tp", "fsdp"),
            P("tp", "fsdp"),
            P("fsdp"),
            P("fsdp"),
            P("fsdp"),
            P("fsdp", "tp"),
            P("tp", "fsdp"),
            P("tp", "fsdp"),
            P("fsdp"),
            P("tp"),
            P("fsdp", "tp"),
            P("fsdp", "tp"),
        ),
        check_vma=False,
    )
```

```python
import functools
import math

import jax
import jax.numpy as jnp
from jax import lax
from jax.experimental import pallas as pl
from jax.experimental.pallas import tpu as pltpu
from jax.sharding import PartitionSpec as P

EPS = 1e-05
NEG = -1e30
INV_ROOT_TWO = 0.7071067811865476
INV_ROOT_TWO_PI = 0.3989422804014327


def normalize(values, scale_vec, offset_vec):
    center = values - jnp.mean(values, -1, keepdims=True)
    inverse = lax.rsqrt(jnp.mean(center * center, -1, keepdims=True) + EPS)
    normed = center * inverse
    return (normed * scale_vec + offset_vec, normed, inverse)


def norm_back(upstream, normed, inverse, scale_vec):
    scaled = upstream * scale_vec
    inner = (
        scaled
        - jnp.mean(scaled, -1, keepdims=True)
        - normed * jnp.mean(scaled * normed, -1, keepdims=True)
    )
    return (inverse * inner, jnp.sum(upstream * normed, 0), jnp.sum(upstream, 0))


def pick_slots(rows, dealing, first, count):
    return jnp.concatenate(
        [lax.dynamic_slice_in_dim(rows, dealing[first + j], 1, 0) for j in range(count)], 0
    )


def matmul(left, right):
    return jnp.dot(left, right, preferred_element_type=jnp.float32)


def weight_product(left, right):
    return jnp.einsum("td,te->de", left, right, preferred_element_type=jnp.float32)


def back_product(left, right):
    return jnp.einsum("te,de->td", left, right, preferred_element_type=jnp.float32)


def gathered_body(
    layer_input,
    cotangent,
    seq_lengths,
    dealing,
    attn_gain,
    attn_shift,
    query_weight,
    query_bias,
    key_weight,
    value_weight,
    value_bias,
    out_weight,
    out_bias,
    mlp_gain,
    mlp_shift,
    up_weight,
    up_bias,
    down_weight,
    down_bias,
    clip_level,
):
    shard_count = lax.axis_size("fsdp")
    ctx_count = lax.axis_size("ctx")
    my_group = lax.axis_index("fsdp")
    ctx_place = lax.axis_index("ctx")
    slot_count, block_rows, width = layer_input.shape
    per_group = slot_count // shard_count
    local_rows = shard_count * block_rows
    tokens = per_group * local_rows
    dealt_input = pick_slots(layer_input, dealing, 0, slot_count).reshape(
        shard_count, per_group, block_rows, width
    )
    dealt_grad = cotangent.reshape(shard_count, per_group, block_rows, width)
    arrived_input, arrived_grad = (
        lax.all_to_all(dealt_input, "fsdp", split_axis=0, concat_axis=2, tiled=True),
        lax.all_to_all(dealt_grad, "fsdp", split_axis=0, concat_axis=2, tiled=True),
    )
    resid = arrived_input.reshape(tokens, width)
    upstream = arrived_grad.reshape(tokens, width)
    seq_lens = lax.dynamic_slice_in_dim(
        jnp.take(seq_lengths, dealing), my_group * per_group, per_group
    )
    gathered = (
        lax.all_gather(attn_gain, "fsdp", axis=0, tiled=True),
        lax.all_gather(attn_shift, "fsdp", axis=0, tiled=True),
        lax.all_gather(query_weight, "fsdp", axis=0, tiled=True),
        lax.all_gather(query_bias, "fsdp", axis=1, tiled=True),
        lax.all_gather(key_weight, "fsdp", axis=0, tiled=True),
        lax.all_gather(value_weight, "fsdp", axis=0, tiled=True),
        lax.all_gather(value_bias, "fsdp", axis=1, tiled=True),
        lax.all_gather(out_weight, "fsdp", axis=1, tiled=True),
        lax.all_gather(out_bias, "fsdp", axis=0, tiled=True),
        lax.all_gather(mlp_gain, "fsdp", axis=0, tiled=True),
        lax.all_gather(mlp_shift, "fsdp", axis=0, tiled=True),
        lax.all_gather(up_weight, "fsdp", axis=0, tiled=True),
        lax.all_gather(up_bias, "fsdp", axis=1, tiled=True),
        lax.all_gather(down_weight, "fsdp", axis=1, tiled=True),
        lax.all_gather(down_bias, "fsdp", axis=0, tiled=True),
    )
    (
        gain_one,
        shift_one,
        query_mat,
        query_vec,
        key_mat,
        value_mat,
        value_vec,
        out_mat,
        out_vec,
        gain_two,
        shift_two,
        up_mat,
        up_vec,
        down_mat,
        down_vec,
    ) = gathered
    head_count, head_size = query_vec.shape
    features = head_count * head_size
    scale_of_scores = 1.0 / math.sqrt(head_size)
    row_ids = jnp.arange(local_rows, dtype=jnp.int32)
    query_pos = (row_ids // block_rows * ctx_count + ctx_place) * block_rows + row_ids % block_rows
    key_ids = jnp.arange(ctx_count * local_rows, dtype=jnp.int32)
    key_rows = key_ids % local_rows
    key_pos = (
        key_rows // block_rows * ctx_count + key_ids // local_rows
    ) * block_rows + key_rows % block_rows
    allowed = (key_pos[None, None, :] <= query_pos[None, :, None]) & (
        key_pos[None, None, :] < seq_lens[:, None, None]
    )
    query_live = query_pos[None, :] < seq_lens[:, None]
    normed_a, unit_one, inverse_one = normalize(
        resid, gain_one.astype(jnp.float32), shift_one.astype(jnp.float32)
    )
    act_one = normed_a.astype(jnp.bfloat16)
    queries = (
        (matmul(act_one, query_mat) + query_vec.reshape(features).astype(jnp.float32))
        .astype(jnp.bfloat16)
        .reshape(per_group, local_rows, features)
    )
    keys_mine = (
        matmul(act_one, key_mat).astype(jnp.bfloat16).reshape(per_group, local_rows, features)
    )
    values_mine = (
        (matmul(act_one, value_mat) + value_vec.reshape(features).astype(jnp.float32))
        .astype(jnp.bfloat16)
        .reshape(per_group, local_rows, features)
    )
    keys_all, values_all = (
        lax.all_gather(keys_mine, "ctx", axis=1, tiled=True),
        lax.all_gather(values_mine, "ctx", axis=1, tiled=True),
    )

    def head_cut(array, head_index):
        return lax.dynamic_slice_in_dim(array, head_index * head_size, head_size, 2)

    def head_scores(head_queries, head_keys):
        return (
            jnp.einsum("sqd,skd->sqk", head_queries, head_keys, preferred_element_type=jnp.float32)
            * scale_of_scores
        )

    def forward_head(head_index):
        logit_scores = head_scores(head_cut(queries, head_index), head_cut(keys_all, head_index))
        masked = jnp.where(allowed, logit_scores, NEG)
        row_top = jnp.max(masked, -1, keepdims=True)
        exp_terms = jnp.where(allowed, jnp.exp(masked - row_top), 0.0)
        total = jnp.sum(exp_terms, -1, keepdims=True)
        attention_probabilities = exp_terms / total
        attended_rows = jnp.einsum(
            "sqk,skd->sqd",
            attention_probabilities.astype(jnp.bfloat16),
            head_cut(values_all, head_index),
            preferred_element_type=jnp.float32,
        )
        log_total = row_top[..., 0] + jnp.log(total[..., 0])
        peak = jnp.max(jnp.where(query_live, row_top[..., 0], NEG))
        return (attended_rows, log_total, peak)

    attended_rows, log_totals, peaks = lax.map(forward_head, jnp.arange(head_count))
    attn_low = attended_rows.transpose(1, 2, 0, 3).reshape(tokens, features).astype(jnp.bfloat16)
    attn_sum = lax.psum(matmul(attn_low, out_mat), "tp")
    hidden = resid + attn_sum + out_vec.astype(jnp.float32)
    normed_b, unit_two, inverse_two = normalize(
        hidden, gain_two.astype(jnp.float32), shift_two.astype(jnp.float32)
    )
    act_two = normed_b.astype(jnp.bfloat16)
    pre = matmul(act_two, up_mat) + up_vec.reshape(-1).astype(jnp.float32)
    gelu_low = jax.nn.gelu(pre, approximate=False).astype(jnp.bfloat16)
    mlp_sum = lax.psum(matmul(gelu_low, down_mat).astype(jnp.bfloat16), "tp").astype(jnp.float32)
    layer_output = hidden + mlp_sum + down_vec.astype(jnp.float32)
    peak_all = lax.pmax(peaks, ("fsdp", "ctx"))
    level = clip_level[0]
    factor = jnp.repeat(jnp.sqrt(level / jnp.maximum(peak_all, level)), head_size)
    query_clipped = (query_weight.astype(jnp.float32) * factor[None, :]).astype(jnp.bfloat16)
    key_clipped = (key_weight.astype(jnp.float32) * factor[None, :]).astype(jnp.bfloat16)
    grad_low = upstream.astype(jnp.bfloat16)
    down_weight_grad = weight_product(gelu_low, grad_low)
    down_bias_grad = jnp.sum(upstream, 0)
    cdf = 0.5 * (1.0 + lax.erf(pre * INV_ROOT_TWO))
    density = jnp.exp(-0.5 * pre * pre) * INV_ROOT_TWO_PI
    pre_grad = back_product(grad_low, down_mat) * (cdf + pre * density)
    pre_low = pre_grad.astype(jnp.bfloat16)
    up_weight_grad = weight_product(act_two, pre_low)
    up_bias_grad = jnp.sum(pre_grad, 0).reshape(up_vec.shape)
    normed_two_grad = lax.psum(back_product(pre_low, up_mat), "tp")
    hidden_in, mlp_gain_grad, mlp_shift_grad = norm_back(
        normed_two_grad, unit_two, inverse_two, gain_two.astype(jnp.float32)
    )
    hidden_grad = upstream + hidden_in
    hidden_low = hidden_grad.astype(jnp.bfloat16)
    out_weight_grad = weight_product(attn_low, hidden_low)
    out_bias_grad = jnp.sum(hidden_grad, 0)
    attended_grad = (
        back_product(hidden_low, out_mat)
        .astype(jnp.bfloat16)
        .reshape(per_group, local_rows, features)
    )

    def backward_head(head_index):
        head_queries = head_cut(queries, head_index)
        head_keys = head_cut(keys_all, head_index)
        head_values = head_cut(values_all, head_index)
        grad_head = head_cut(attended_grad, head_index)
        logit_scores = head_scores(head_queries, head_keys)
        masked = jnp.where(allowed, logit_scores, NEG)
        attention_probabilities = jnp.where(
            allowed, jnp.exp(masked - log_totals[head_index][..., None]), 0.0
        )
        prob_grad = jnp.einsum(
            "sqd,skd->sqk", grad_head, head_values, preferred_element_type=jnp.float32
        )
        inner = jnp.sum(attention_probabilities * prob_grad, -1, keepdims=True)
        score_grad = (attention_probabilities * (prob_grad - inner)).astype(jnp.bfloat16)
        query_grad = (
            jnp.einsum("sqk,skd->sqd", score_grad, head_keys, preferred_element_type=jnp.float32)
            * scale_of_scores
        )
        key_grad = (
            jnp.einsum("sqk,sqd->skd", score_grad, head_queries, preferred_element_type=jnp.float32)
            * scale_of_scores
        )
        value_grad = jnp.einsum(
            "sqk,sqd->skd",
            attention_probabilities.astype(jnp.bfloat16),
            grad_head,
            preferred_element_type=jnp.float32,
        )
        return (query_grad, key_grad, value_grad)

    query_parts, key_parts, value_parts = lax.map(backward_head, jnp.arange(head_count))
    query_grads = query_parts.transpose(1, 2, 0, 3).reshape(tokens, features)
    key_whole = key_parts.transpose(1, 2, 0, 3).reshape(per_group, ctx_count * local_rows, features)
    value_whole = value_parts.transpose(1, 2, 0, 3).reshape(
        per_group, ctx_count * local_rows, features
    )
    key_summed, value_summed = (
        lax.psum_scatter(key_whole, "ctx", scatter_dimension=1, tiled=True),
        lax.psum_scatter(value_whole, "ctx", scatter_dimension=1, tiled=True),
    )
    key_grads = key_summed.reshape(tokens, features)
    value_grads = value_summed.reshape(tokens, features)
    query_bias_grad = jnp.sum(query_grads, 0).reshape(head_count, head_size)
    value_bias_grad = jnp.sum(value_grads, 0).reshape(head_count, head_size)
    query_low = query_grads.astype(jnp.bfloat16)
    key_low = key_grads.astype(jnp.bfloat16)
    value_low = value_grads.astype(jnp.bfloat16)
    query_weight_grad = weight_product(act_one, query_low)
    key_weight_grad = weight_product(act_one, key_low)
    value_weight_grad = weight_product(act_one, value_low)
    normed_one_grad = lax.psum(
        (
            back_product(query_low, query_mat)
            + back_product(key_low, key_mat)
            + back_product(value_low, value_mat)
        ).astype(jnp.bfloat16),
        "tp",
    ).astype(jnp.float32)
    input_in, attn_gain_grad, attn_shift_grad = norm_back(
        normed_one_grad, unit_one, inverse_one, gain_one.astype(jnp.float32)
    )
    input_grad = hidden_grad + input_in
    partial_sums = (
        lax.psum_scatter(
            attn_gain_grad.astype(jnp.bfloat16), "fsdp", scatter_dimension=0, tiled=True
        ).astype(jnp.float32),
        lax.psum_scatter(
            attn_shift_grad.astype(jnp.bfloat16), "fsdp", scatter_dimension=0, tiled=True
        ).astype(jnp.float32),
        lax.psum_scatter(
            query_weight_grad.astype(jnp.bfloat16), "fsdp", scatter_dimension=0, tiled=True
        ).astype(jnp.float32),
        lax.psum_scatter(
            query_bias_grad.astype(jnp.bfloat16), "fsdp", scatter_dimension=1, tiled=True
        ).astype(jnp.float32),
        lax.psum_scatter(
            key_weight_grad.astype(jnp.bfloat16), "fsdp", scatter_dimension=0, tiled=True
        ).astype(jnp.float32),
        lax.psum_scatter(
            value_weight_grad.astype(jnp.bfloat16), "fsdp", scatter_dimension=0, tiled=True
        ).astype(jnp.float32),
        lax.psum_scatter(
            value_bias_grad.astype(jnp.bfloat16), "fsdp", scatter_dimension=1, tiled=True
        ).astype(jnp.float32),
        lax.psum_scatter(
            out_weight_grad.astype(jnp.bfloat16), "fsdp", scatter_dimension=1, tiled=True
        ).astype(jnp.float32),
        lax.psum_scatter(
            out_bias_grad.astype(jnp.bfloat16), "fsdp", scatter_dimension=0, tiled=True
        ).astype(jnp.float32),
        lax.psum_scatter(
            mlp_gain_grad.astype(jnp.bfloat16), "fsdp", scatter_dimension=0, tiled=True
        ).astype(jnp.float32),
        lax.psum_scatter(
            mlp_shift_grad.astype(jnp.bfloat16), "fsdp", scatter_dimension=0, tiled=True
        ).astype(jnp.float32),
        lax.psum_scatter(
            up_weight_grad.astype(jnp.bfloat16), "fsdp", scatter_dimension=0, tiled=True
        ).astype(jnp.float32),
        lax.psum_scatter(
            up_bias_grad.astype(jnp.bfloat16), "fsdp", scatter_dimension=1, tiled=True
        ).astype(jnp.float32),
        lax.psum_scatter(
            down_weight_grad.astype(jnp.bfloat16), "fsdp", scatter_dimension=1, tiled=True
        ).astype(jnp.float32),
        lax.psum_scatter(
            down_bias_grad.astype(jnp.bfloat16), "fsdp", scatter_dimension=0, tiled=True
        ).astype(jnp.float32),
    )
    shards = (
        lax.psum(partial_sums[0].astype(jnp.bfloat16), "ctx").astype(jnp.float32),
        lax.psum(partial_sums[1].astype(jnp.bfloat16), "ctx").astype(jnp.float32),
        lax.psum(partial_sums[2].astype(jnp.bfloat16), "ctx").astype(jnp.float32),
        lax.psum(partial_sums[3].astype(jnp.bfloat16), "ctx").astype(jnp.float32),
        lax.psum(partial_sums[4].astype(jnp.bfloat16), "ctx").astype(jnp.float32),
        lax.psum(partial_sums[5].astype(jnp.bfloat16), "ctx").astype(jnp.float32),
        lax.psum(partial_sums[6].astype(jnp.bfloat16), "ctx").astype(jnp.float32),
        lax.psum(partial_sums[7].astype(jnp.bfloat16), "ctx").astype(jnp.float32),
        lax.psum(partial_sums[8].astype(jnp.bfloat16), "ctx").astype(jnp.float32),
        lax.psum(partial_sums[9].astype(jnp.bfloat16), "ctx").astype(jnp.float32),
        lax.psum(partial_sums[10].astype(jnp.bfloat16), "ctx").astype(jnp.float32),
        lax.psum(partial_sums[11].astype(jnp.bfloat16), "ctx").astype(jnp.float32),
        lax.psum(partial_sums[12].astype(jnp.bfloat16), "ctx").astype(jnp.float32),
        lax.psum(partial_sums[13].astype(jnp.bfloat16), "ctx").astype(jnp.float32),
        lax.psum(partial_sums[14].astype(jnp.bfloat16), "ctx").astype(jnp.float32),
    )
    sent_output = layer_output.reshape(1, per_group, local_rows, width)
    sent_grad = input_grad.reshape(1, per_group, local_rows, width)
    back_output, back_grad = (
        lax.all_to_all(
            sent_output.astype(jnp.bfloat16), "fsdp", split_axis=2, concat_axis=0, tiled=True
        ).astype(sent_output.dtype),
        lax.all_to_all(
            sent_grad.astype(jnp.bfloat16), "fsdp", split_axis=2, concat_axis=0, tiled=True
        ).astype(sent_grad.dtype),
    )
    final_output = back_output.reshape(slot_count, block_rows, width)
    final_grad = back_grad.reshape(slot_count, block_rows, width)
    return (
        final_output,
        final_grad,
        shards[0],
        shards[1],
        shards[2],
        shards[3],
        shards[4],
        shards[5],
        shards[6],
        shards[7],
        shards[8],
        shards[9],
        shards[10],
        shards[11],
        shards[12],
        shards[13],
        shards[14],
        peak_all,
        query_clipped,
        key_clipped,
    )


def attention_probs(query_block, key_rows, block, length):
    rows, cols = query_block.shape[0], key_rows.shape[0]
    scores = lax.dot_general(
        query_block, key_rows, (((1,), (1,)), ((), ())), preferred_element_type=jnp.float32
    ) * (1.0 / math.sqrt(query_block.shape[1]))
    row_pos = block * rows + lax.broadcasted_iota(jnp.int32, (rows, cols), 0)
    col_pos = lax.broadcasted_iota(jnp.int32, (rows, cols), 1)
    scores = jnp.where((col_pos <= row_pos) & (col_pos < length), scores, NEG)
    top = jnp.max(scores, -1, keepdims=True)
    terms = jnp.exp(scores - top)
    return terms / jnp.sum(terms, -1, keepdims=True), top


def entry_barrier(targets):
    barrier = pltpu.get_barrier_semaphore()
    for target in targets:
        pl.semaphore_signal(barrier, inc=1, device_id=target, device_id_type=pl.DeviceIdType.MESH)
    pl.semaphore_wait(barrier, len(targets))


def remote_copy(src, dst, send, recv, target):
    return pltpu.make_async_remote_copy(
        src_ref=src,
        dst_ref=dst,
        send_sem=send,
        recv_sem=recv,
        device_id=target,
        device_id_type=pl.DeviceIdType.MESH,
    )


def grant(semaphore, target):
    pl.semaphore_signal(semaphore, inc=1, device_id=target, device_id_type=pl.DeviceIdType.MESH)


def aligned(start, size):
    return pl.ds(pl.multiple_of(start, 128), size)


class Place:
    def __init__(self, depth):
        self.depth = depth
        f = lax.axis_index("fsdp")
        z = lax.axis_index("ctx")
        t = lax.axis_index("tp")
        y, x = f // 2, f % 2
        self.f, self.z, self.t, self.y, self.x = f, z, t, y, x
        self.over_x = {"fsdp": 2 * y + 1 - x, "ctx": z, "tp": t}
        self.over_y = {"fsdp": 2 * (1 - y) + x, "ctx": z, "tp": t}
        self.over_core = {"fsdp": f, "ctx": z, "tp": 1 - t}
        self.mate = {"fsdp": f, "ctx": z + 1 - 2 * (z % 2), "tp": t}
        self.middle = {"fsdp": f, "ctx": 3 - z, "tp": t}
        self.hop = {"fsdp": f, "ctx": lax.rem(z + 2, 4), "tp": t}
        self.homes = (2 * y + 1 - x, 2 * (1 - y) + 1 - x, f, 2 * (1 - y) + x)

    def row_target(self, k):
        return {"fsdp": 2 * self.y + self.t, "ctx": k, "tp": self.x}

    def row_targets(self):
        others = [self.row_target(lax.rem(self.z + k, self.depth)) for k in range(1, self.depth)]
        return others + [{"fsdp": 2 * self.y + 1 - self.x, "ctx": self.z, "tp": 1 - self.t}]

    def block_place(self, block):
        return 2 * jnp.where(self.y == block // 2, 0, 1) + jnp.where(self.t == block % 2, 0, 1)


def reduce_stages(p, groups, scratch):
    (
        x_slot,
        own_slot,
        pair_slot,
        y_slot,
        z_slot,
        z_pair,
        inner_slot,
        total_slot,
        x_send,
        x_recv,
        own_sem,
        y_send,
        y_recv,
        outer_send,
        outer_recv,
        inner_send,
        inner_recv,
        out_sem,
        x_free,
        y_free,
        outer_free,
        inner_free,
    ) = scratch
    y, z = p.y, p.z
    outer = (z == 0) | (z == 3)
    inner = (z == 1) | (z == 2)
    slots, rows, cols = x_slot.shape
    items = []
    for parts, row_count, col_count, place in groups:
        near_send, far_send, near_own, far_own = parts
        for r in range(row_count):
            for c in range(col_count):
                cut = (pl.ds(r * rows, rows), pl.ds(c * cols, cols))
                items.append((True, far_send.at[cut], far_own.at[cut], place(1 - y, r, c)))
                items.append((False, near_send.at[cut], near_own.at[cut], place(y, r, c)))
    count = len(items)
    far_count = count // 2
    far_slots = y_slot.shape[0]

    def x_copy(i):
        k = i % slots
        return remote_copy(items[i][1], x_slot.at[k], x_send.at[k], x_recv.at[k], p.over_x)

    def own_copy(i):
        k = i % slots
        return pltpu.make_async_copy(items[i][2], own_slot.at[k], own_sem.at[k])

    def y_copy(i):
        k, g = i % slots, (i // 2) % far_slots
        return remote_copy(pair_slot.at[k], y_slot.at[g], y_send.at[g], y_recv.at[g], p.over_y)

    def summed(i):
        return y_slot.at[(i // 2) % far_slots] if items[i][0] else pair_slot.at[i % slots]

    def outward(i):
        k = i % slots
        return remote_copy(summed(i), z_slot.at[k], outer_send.at[k], outer_recv.at[k], p.mate)

    def across(i):
        k = i % slots
        return remote_copy(z_pair.at[k], inner_slot.at[k], inner_send.at[k], inner_recv.at[k], p.middle)

    def backward(i):
        k = i % slots
        return remote_copy(total_slot.at[k], z_slot.at[k], outer_send.at[k], outer_recv.at[k], p.mate)

    def result_inner(i):
        k = i % slots
        return pltpu.make_async_copy(total_slot.at[k], items[i][3], out_sem.at[k])

    def result_outer(i):
        k = i % slots
        return pltpu.make_async_copy(z_slot.at[k], items[i][3], out_sem.at[k])

    def add(left, right, target):
        target[...] = (left[...].astype(jnp.float32) + right[...].astype(jnp.float32)).astype(
            target.dtype
        )

    def stage_send(i):
        if i >= slots:
            pl.semaphore_wait(x_free, 1)
        x_copy(i).start()
        own_copy(i).start()

    def stage_pair(i):
        x_copy(i).wait()
        own_copy(i).wait()
        k = i % slots
        add(x_slot.at[k], own_slot.at[k], pair_slot.at[k])
        if i + slots < count:
            grant(x_free, p.over_x)
        if items[i][0]:
            if i // 2 >= far_slots:
                pl.semaphore_wait(y_free, 1)
            y_copy(i).start()

    def stage_outward(i):
        if items[i][0]:
            y_copy(i).wait()

        @pl.when(outer)
        def _():
            if i >= slots:
                pl.semaphore_wait(outer_free, 1)
            outward(i).start()

    def stage_across(i):
        k = i % slots

        @pl.when(outer)
        def _():
            outward(i).wait_send()

        @pl.when(inner)
        def _():
            outward(i).wait_recv()
            add(summed(i), z_slot.at[k], z_pair.at[k])
            if i + slots < count:
                grant(outer_free, p.mate)
            if i >= slots:
                pl.semaphore_wait(inner_free, 1)
            across(i).start()

        if items[i][0] and i // 2 + far_slots < far_count:
            grant(y_free, p.over_y)

    def stage_total(i):
        k = i % slots

        @pl.when(inner)
        def _():
            across(i).wait()
            add(z_pair.at[k], inner_slot.at[k], total_slot.at[k])
            if i + slots < count:
                grant(inner_free, p.middle)
            if i >= slots:
                pl.semaphore_wait(outer_free, 1)
            backward(i).start()
            result_inner(i).start()

    def stage_result(i):
        @pl.when(inner)
        def _():
            backward(i).wait_send()
            result_inner(i).wait()

        @pl.when(outer)
        def _():
            backward(i).wait_recv()
            result_outer(i).start()

    def stage_finish(i):
        @pl.when(outer)
        def _():
            result_outer(i).wait()
            if i + slots < count:
                grant(outer_free, p.mate)

    stages = (
        (11, stage_finish),
        (10, stage_result),
        (8, stage_total),
        (6, stage_across),
        (4, stage_outward),
        (2, stage_pair),
        (0, stage_send),
    )

    def run(step):
        for lag, stage in stages:
            if 0 <= step - lag < count:
                stage(step - lag)

    return run, count + 12


def reduce_scratch(slots, far_slots, rows, cols):
    dma, regular = pltpu.SemaphoreType.DMA, pltpu.SemaphoreType.REGULAR
    counts = (slots,) * 3 + (far_slots,) + (slots,) * 4
    return [pltpu.VMEM((n, rows, cols), jnp.bfloat16) for n in counts] + [
        dma((n,)) for n in (slots,) * 3 + (far_slots,) * 2 + (slots,) * 5
    ] + [regular] * 4


class RowSum:
    def __init__(self, p, rows, arrived, sent, loaded, send_sem, recv_sem, load_sem, core_free, y_free, uses):
        self.p, self.rows, self.uses = p, rows, uses
        self.arrived, self.sent, self.loaded = arrived, sent, loaded
        self.send_sem, self.recv_sem, self.load_sem = send_sem, recv_sem, load_sem
        self.core_free, self.y_free = core_free, y_free

    def block(self, ref, k):
        return ref.at[pl.ds(k * self.rows, self.rows), :]

    def hop(self, ref, k):
        source = (self.block(ref, 3), self.block(ref, 1), self.sent)[k]
        target = self.p.over_y if k == 2 else self.p.over_core
        return remote_copy(source, self.arrived.at[k], self.send_sem.at[k], self.recv_sem.at[k], target)

    def load(self, ref, k):
        return pltpu.make_async_copy(self.block(ref, k), self.loaded, self.load_sem)

    def start(self, use, ref, local):
        if use:
            pl.semaphore_wait(self.core_free, 1)
            pl.semaphore_wait(self.y_free, 1)
        self.hop(ref, 0).start()
        self.hop(ref, 1).start()
        if not local:
            self.load(ref, 2).start()

    def middle(self, ref, local):
        self.hop(ref, 0).wait()
        if not local:
            self.load(ref, 2).wait()
        base = self.block(ref, 2) if local else self.loaded

        @pl.loop(0, self.rows // 32)
        def _(k):
            at = pl.ds(pl.multiple_of(k * 32, 32), 32)
            self.sent[at, :] = (
                base[at, :].astype(jnp.float32) + self.arrived[0, at, :].astype(jnp.float32)
            ).astype(jnp.bfloat16)

        self.hop(ref, 2).start()
        if not local:
            self.load(ref, 0).start()

    def finish(self, ref, local):
        self.hop(ref, 1).wait()
        self.hop(ref, 2).wait()
        if not local:
            self.load(ref, 0).wait()

    def total(self, ref, local, at):
        base = self.block(ref, 0) if local else self.loaded
        return (
            base[at, :].astype(jnp.float32)
            + self.arrived[1, at, :].astype(jnp.float32)
            + self.arrived[2, at, :].astype(jnp.float32)
        )

    def release(self, use):
        if use + 1 < self.uses:
            grant(self.core_free, self.p.over_core)
            grant(self.y_free, self.p.over_y)


def unit_rows(values):
    center = values - jnp.mean(values, -1, keepdims=True)
    inverse = lax.rsqrt(jnp.mean(center * center, -1, keepdims=True) + EPS)
    return center * inverse, inverse


def unit_back(upstream, unit, inverse, gain):
    scaled = upstream * gain
    return inverse * (
        scaled
        - jnp.mean(scaled, -1, keepdims=True)
        - unit * jnp.mean(scaled * unit, -1, keepdims=True)
    )


GAIN_ONE, SHIFT_ONE, OUT_BIAS, GAIN_TWO, SHIFT_TWO, DOWN_BIAS, QUERY_BIAS, VALUE_BIAS, UP_BIAS, PEAKS = (
    0,
    1,
    2,
    3,
    4,
    5,
    6,
    7,
    8,
    12,
)


def forward_kernel(
    head_size,
    info,
    vec_hbm,
    head_hbm,
    q_ref,
    k_ref,
    v_ref,
    o_ref,
    u_ref,
    d_ref,
    arrived_hbm,
    cot_hbm,
    qkv_mat_out,
    out_mat_out,
    up_all,
    down_all,
    act_out,
    cot_all,
    qkv_out,
    attended_out,
    hidden_out,
    resid_out,
    two_out,
    vec_all,
    peaks,
    qkv_mat,
    out_mat,
    fresh,
    part,
    act,
    hidden,
    qkv,
    keys,
    values,
    attended,
    partial,
    arrived,
    sent,
    two,
    vec_own,
    head_own,
    head_got,
    qkv_bias,
    local_sem,
    send_sem,
    recv_sem,
    row_send,
    row_recv,
    join_send,
    join_recv,
    vec_send,
    vec_recv,
    load_sem,
    sum_send,
    sum_recv,
    out_sem,
):
    f32, bf16 = jnp.float32, jnp.bfloat16
    depth, block_rows, width = arrived_hbm.shape
    own_rows = depth * block_rows
    strip = q_ref.shape[0]
    features = q_ref.shape[1] // 2
    units = u_ref.shape[1] // 2
    heads = features // head_size
    p = Place(depth)
    f, x, y, z, t = p.f, p.x, p.y, p.z, p.t
    even = z % 2 == 0
    odd = jnp.logical_not(even)
    diagonal = {"fsdp": 3 - f, "ctx": z, "tp": t}
    entry_barrier([p.over_x, p.over_y, p.mate, p.over_core, diagonal] + p.row_targets())
    length = info[0]

    chunks = []
    rows = strip // 2
    for k, ref in enumerate((q_ref, k_ref, v_ref)):
        for r in range(2):
            chunks.append(
                (
                    lambda w, ref=ref, r=r: ref.at[pl.ds(r * rows, rows), aligned(w * features, features)],
                    lambda home, k=k, r=r: qkv_mat.at[
                        aligned(home * strip + r * rows, rows), pl.ds(k * features, features)
                    ],
                )
            )
    for r in range(2):
        chunks.append(
            (
                lambda w, r=r: o_ref.at[aligned(w * features + r * rows, rows), :],
                lambda home, r=r: out_mat.at[pl.ds(r * rows, rows), aligned(home * strip, strip)],
            )
        )
    pieces = 8
    for r in range(pieces):
        size = strip // pieces
        chunks.append(
            (
                lambda w, r=r, size=size: u_ref.at[pl.ds(r * size, size), aligned(w * units, units)],
                lambda home, r=r, size=size: up_all.at[
                    pl.ds(pl.multiple_of(home * strip + r * size, size), size), :
                ],
            )
        )
    for r in range(pieces):
        size = units // pieces
        chunks.append(
            (
                lambda w, r=r, size=size: d_ref.at[aligned(w * units + r * size, size), :],
                lambda home, r=r, size=size: down_all.at[pl.ds(r * size, size), aligned(home * strip, strip)],
            )
        )
    count = len(chunks)
    far_home = 2 * (1 - y) + x

    def own_copy(i):
        source, place = chunks[i]
        return pltpu.make_async_copy(source(y), place(f), local_sem.at[i])

    def y_copy(i):
        source, place = chunks[i]
        return remote_copy(source(1 - y), place(f), send_sem.at[0, i], recv_sem.at[0, i], p.over_y)

    def x_copy(i, is_even):
        source, place = chunks[i]
        start = source(y) if is_even else place(far_home)
        home = f if is_even else far_home
        return remote_copy(start, place(home), send_sem.at[1, i], recv_sem.at[1, i], p.over_x)

    def z_copy(i, is_even):
        place = chunks[i][1]
        home = 2 * y + 1 - x if is_even else 2 * (1 - y) + 1 - x
        return remote_copy(place(home), place(home), send_sem.at[2, i], recv_sem.at[2, i], p.mate)

    rows_of = ((part, act), (cot_hbm, cot_all), (arrived_hbm, hidden))

    def row_copy(a, k):
        source, place = rows_of[a]
        return remote_copy(
            source.at[k],
            place.at[pl.ds(pl.multiple_of(z * block_rows, block_rows), block_rows), :],
            row_send.at[a, k],
            row_recv.at[a, z],
            p.row_target(k),
        )

    def row_arrival(a, k):
        source, place = rows_of[a]
        return remote_copy(
            source.at[k],
            place.at[pl.ds(k * block_rows, block_rows), :],
            row_send.at[a, k],
            row_recv.at[a, k],
            p.row_target(k),
        )

    def row_stay(a, k):
        source, place = rows_of[a]
        return pltpu.make_async_copy(
            source.at[k], place.at[pl.ds(k * block_rows, block_rows), :], row_send.at[a, k]
        )

    def rows_start(a):
        for k in range(depth):
            stays = (z == k) & (x == t)
            pl.when(stays)(lambda k=k: row_stay(a, k).start())
            pl.when(jnp.logical_not(stays))(lambda k=k: row_copy(a, k).start())

    def rows_wait(a):
        for k in range(depth):
            stays = (z == k) & (x == t)
            pl.when(stays)(lambda k=k: row_stay(a, k).wait())

            @pl.when(jnp.logical_not(stays))
            def _(k=k):
                row_copy(a, k).wait_send()
                row_arrival(a, k).wait_recv()

    joined = (act, cot_all, two)

    def block(ref, k):
        return ref.at[pl.ds(k * own_rows, own_rows), :]

    def join(a, step):
        source, place, target = ((0, 1, p.over_core), (0, 2, p.over_y), (2, 3, p.over_core))[step]
        ref = joined[a]
        return remote_copy(
            block(ref, source), block(ref, place), join_send.at[a, step], join_recv.at[a, step], target
        )

    def join_start(a):
        join(a, 0).start()
        join(a, 1).start()

    def join_pass(a):
        join(a, 1).wait_recv()
        join(a, 2).start()

    def join_end(a):
        join(a, 0).wait()
        join(a, 1).wait_send()
        join(a, 2).wait()

    def vec_place(ref):
        return ref.at[:, aligned(f * strip, strip)]

    vec_targets = (p.over_x, p.over_y, diagonal)

    def vec_copy(k):
        return remote_copy(vec_own, vec_place(vec_all), vec_send.at[0, k], vec_recv.at[0, k], vec_targets[k])

    def head_copy(k):
        return remote_copy(head_own, head_got.at[k], vec_send.at[1, k], vec_recv.at[1, k], vec_targets[k])

    loads = [
        pltpu.make_async_copy(source, target, load_sem.at[k])
        for k, (source, target) in enumerate(
            ((vec_hbm, vec_own), (head_hbm, head_own), (arrived_hbm, fresh))
        )
    ]

    def begin():
        for load in loads:
            load.start()
        loads[0].wait()
        loads[1].wait()
        for k in range(3):
            vec_copy(k).start()
            head_copy(k).start()
        vec_place(vec_all)[...] = vec_own[...]
        peaks[...] = jnp.full_like(peaks, NEG)

    def vector_row(k):
        return vec_all[pl.ds(k, 1), :]

    group_rows = 16

    def first_norm():
        for k in range(3):
            vec_copy(k).wait()
            head_copy(k).wait()
        loads[2].wait()
        for k in range(3):
            head_own[...] += head_got[k]
        qkv_bias[...] = jnp.zeros_like(qkv_bias)
        for h in range(heads):
            lanes = pl.ds(h * head_size, head_size)
            qkv_bias[pl.ds(0, 1), lanes] = head_own[pl.ds(heads * y + h, 1), :]
            lanes = pl.ds(2 * features + h * head_size, head_size)
            qkv_bias[pl.ds(0, 1), lanes] = head_own[pl.ds(2 * heads + heads * y + h, 1), :]
        gain, shift = vector_row(GAIN_ONE), vector_row(SHIFT_ONE)
        for s in range(depth):

            @pl.loop(0, block_rows // group_rows)
            def _(k, s=s):
                at = pl.ds(pl.multiple_of(k * group_rows, group_rows), group_rows)
                unit, _ = unit_rows(fresh[s, at, :])
                part[s, at, :] = (unit * gain + shift).astype(bf16)

        rows_start(0)

    def weights_wait(start, stop):
        for i in range(start, stop):
            own_copy(i).wait()
            z_copy(i, True).wait_recv()

    kept, used = [], [0]

    def keep(source, target):
        copy = pltpu.make_async_copy(source, target, out_sem.at[used[0]])
        used[0] += 1
        copy.start()
        kept.append(copy)

    def project(k):
        at = pl.ds(k * own_rows, own_rows)

        @pl.loop(0, 3)
        def _(c):
            cut = aligned(c * features, features)
            qkv[at, cut] = (
                jnp.dot(act[at, :], qkv_mat[:, cut], preferred_element_type=f32)
                + qkv_bias[pl.ds(0, 1), cut]
            ).astype(bf16)

    def head_rows():
        for b in range(4):
            at = pl.ds(pl.multiple_of(p.block_place(b) * own_rows, own_rows), own_rows)
            keys[pl.ds(b * own_rows, own_rows), :] = qkv[at, pl.ds(features, features)]
            values[pl.ds(b * own_rows, own_rows), :] = qkv[at, pl.ds(2 * features, features)]

    def attention_block(b):
        at = pl.ds(pl.multiple_of(p.block_place(b) * own_rows, own_rows), own_rows)
        past = pl.ds(0, (b + 1) * own_rows)

        @pl.loop(0, heads)
        def _(head):
            lanes = aligned(head * head_size, head_size)
            probs, top = attention_probs(qkv[at, lanes], keys[past, lanes], b, length)
            attended[at, lanes] = jnp.dot(
                probs.astype(bf16), values[past, lanes], preferred_element_type=f32
            ).astype(bf16)
            live = b * own_rows + lax.broadcasted_iota(jnp.int32, top.shape, 0) < length
            peak = jnp.max(jnp.where(live, top, NEG), 0, keepdims=True)
            row = pl.ds(head, 1)
            peaks[row, :] = jnp.maximum(peaks[row, :], jnp.broadcast_to(peak, (1, peaks.shape[1])))

    sums = RowSum(p, own_rows, arrived, sent, None, sum_send, sum_recv, None, None, None, 1)

    def out_block(k):
        at = pl.ds(k * own_rows, own_rows)

        @pl.loop(0, 4)
        def _(n):
            cut = aligned(n * strip, strip)
            partial[at, cut] = jnp.dot(
                attended[at, :], out_mat[:, cut], preferred_element_type=f32
            ).astype(bf16)

    def second_norm():
        sums.finish(partial, True)
        kept[-1].wait()
        kept.pop()
        bias, gain, shift = vector_row(OUT_BIAS), vector_row(GAIN_TWO), vector_row(SHIFT_TWO)

        @pl.loop(0, own_rows // group_rows)
        def _(k):
            at = pl.ds(pl.multiple_of(k * group_rows, group_rows), group_rows)
            value = hidden[at, :] + sums.total(partial, True, at) + bias
            hidden[at, :] = value
            unit, _ = unit_rows(value)
            two[at, :] = (unit * gain + shift).astype(bf16)

        join_start(2)
        keep(hidden, hidden_out)

    def call(function, *arguments):
        return lambda: function(*arguments)

    plan = {}

    def at_step(step, *tasks):
        plan.setdefault(step, []).extend(tasks)

    at_step(0, begin)
    at_step(1, first_norm)
    at_step(2, call(rows_start, 1))
    at_step(3, call(rows_wait, 0), call(join_start, 0))
    at_step(4, call(rows_start, 2))
    at_step(7, call(join_pass, 0))
    at_step(9, call(join_end, 0), lambda: keep(act, act_out))
    at_step(10, call(weights_wait, 0, 6), call(project, 0), lambda: keep(qkv_mat, qkv_mat_out))
    at_step(10, call(project, 1))
    at_step(11, call(project, 2), call(project, 3), head_rows, lambda: keep(qkv, qkv_out))
    at_step(12, *(call(attention_block, b) for b in range(4)))
    at_step(13, lambda: keep(attended, attended_out), call(weights_wait, 6, 8), call(out_block, 3))
    at_step(13, call(out_block, 1), call(sums.start, 0, partial, True), call(out_block, 2))
    at_step(13, call(sums.middle, partial, True), call(out_block, 0))
    at_step(14, lambda: keep(out_mat, out_mat_out), call(rows_wait, 2), lambda: keep(hidden, resid_out))
    at_step(17, second_norm)
    at_step(18, call(rows_wait, 1), call(join_start, 1))
    at_step(21, call(join_pass, 2))
    at_step(22, call(join_end, 2), lambda: keep(two, two_out))
    at_step(24, call(join_pass, 1))
    lag = 2
    for i in range(count + 2 * lag):
        if i < count:
            y_copy(i).start()
            pl.when(even)(lambda i=i: x_copy(i, True).start())
            own_copy(i).start()
        j = i - lag
        if 0 <= j < count:
            y_copy(j).wait_recv()

            @pl.when(even)
            def _(j=j):
                x_copy(j, True).wait_recv()
                z_copy(j, True).start()

            pl.when(odd)(lambda j=j: x_copy(j, False).start())
        j = i - 2 * lag
        if 0 <= j < count:

            @pl.when(odd)
            def _(j=j):
                x_copy(j, False).wait_recv()
                z_copy(j, False).start()

        for task in plan.get(i, ()):
            task()

    weights_wait(8, count)
    for i in range(count):
        y_copy(i).wait_send()
        x_copy(i, True).wait_send()
        z_copy(i, True).wait_send()
    join_end(1)
    for copy in kept:
        copy.wait()


def forward_all(
    head_size,
    length,
    vectors,
    head_vectors,
    query_weight,
    key_weight,
    value_weight,
    out_weight,
    up_weight,
    down_weight,
    arrived,
    cot,
):
    strip, features, units = query_weight.shape[0], query_weight.shape[1] // 2, up_weight.shape[1] // 2
    width = 4 * strip
    depth, block_rows = arrived.shape[:2]
    own_rows = depth * block_rows
    tokens = 4 * own_rows
    bf16, f32 = jnp.bfloat16, jnp.float32
    hbm = pl.BlockSpec(memory_space=pl.ANY)
    vmem = pl.BlockSpec(memory_space=pltpu.VMEM)
    count = 24
    dma = pltpu.SemaphoreType.DMA

    def made(shape, dtype=bf16):
        return jax.ShapeDtypeStruct(shape, dtype)

    def hold(shape, dtype=bf16):
        return pltpu.VMEM(shape, dtype)

    return pl.pallas_call(
        functools.partial(forward_kernel, head_size),
        out_shape=(
            made((width, 3 * features)),
            made((features, width)),
            made((width, units)),
            made((units, width)),
            made((tokens, width)),
            made((tokens, width)),
            made((tokens, 3 * features)),
            made((tokens, features)),
            made((own_rows, width), f32),
            made((own_rows, width), f32),
            made((tokens, width)),
            made((8, width), f32),
            made((8, 128), f32),
        ),
        in_specs=[pl.BlockSpec(memory_space=pltpu.SMEM)] + [hbm] * 10,
        out_specs=(hbm,) * 11 + (vmem,) * 2,
        scratch_shapes=[
            hold((width, 3 * features)),
            hold((features, width)),
            hold((depth, block_rows, width), f32),
            hold((depth, block_rows, width)),
            hold((tokens, width)),
            hold((own_rows, width), f32),
            hold((tokens, 3 * features)),
            hold((tokens, features)),
            hold((tokens, features)),
            hold((tokens, features)),
            hold((tokens, width)),
            hold((3, own_rows, width)),
            hold((own_rows, width)),
            hold((tokens, width)),
            hold((8, strip), f32),
            hold(head_vectors.shape, f32),
            hold((3,) + head_vectors.shape, f32),
            hold((8, 3 * features), f32),
            dma((count,)),
            dma((3, count)),
            dma((3, count)),
            dma((3, depth)),
            dma((3, depth)),
            dma((3, 3)),
            dma((3, 3)),
            dma((2, 3)),
            dma((2, 3)),
            dma((3,)),
            dma((3,)),
            dma((3,)),
            dma((8,)),
        ],
        compiler_params=pltpu.CompilerParams(
            collective_id=0, has_side_effects=True, vmem_limit_bytes=56 << 20
        ),
        cost_estimate=pl.CostEstimate(flops=0, bytes_accessed=64 << 20, transcendentals=0),
    )(
        length,
        vectors,
        head_vectors,
        query_weight,
        key_weight,
        value_weight,
        out_weight,
        up_weight,
        down_weight,
        arrived,
        cot,
    )


def backward_kernel(
    head_size,
    info,
    vector_ref,
    small_in,
    down_parts,
    up_parts,
    two_part,
    mlp_part,
    hidden_hbm,
    cot_hbm,
    resid_hbm,
    out_hbm,
    qkv_mat_hbm,
    qkv_hbm,
    attended_hbm,
    act_hbm,
    down_sum,
    up_sum,
    out_sum,
    qkv_sums,
    rows_out,
    rows_grad,
    small,
    out_products,
    qkv_products,
    engine,
    base,
    hidden_grad,
    low,
    out_mat,
    attended_grad,
    qkv,
    qkv_grad,
    act,
    attended,
    qkv_mat,
    keys,
    values,
    key_sum,
    value_sum,
    stage,
    packed,
    arrived,
    sent,
    loaded,
    small_arrived,
    load_sem,
    sum_send,
    sum_recv,
    sum_load,
    join_send,
    join_recv,
    stage_sem,
    row_send,
    row_recv,
    share_send,
    share_recv,
    small_send,
    small_recv,
    core_free,
    y_free,
):
    f32, bf16 = jnp.float32, jnp.bfloat16
    own_rows, width = base.shape
    tokens, features = attended.shape
    heads = features // head_size
    depth = rows_out.shape[0] // 2
    block_rows = rows_out.shape[1]
    p = Place(depth)
    x, y, z, t = p.x, p.y, p.z, p.t
    entry_barrier(
        [p.over_x, p.over_y, p.over_core, p.mate, p.middle, p.hop] + p.row_targets()
    )
    length = info[0]
    scale = 1.0 / math.sqrt(head_size)
    column = 2 * t + y

    rows, cols = engine[0].shape[1:]
    down_rows = down_sum.shape[0] // 2
    up_cols = up_sum.shape[1] // 2
    strip = out_sum.shape[1]

    def four(ref):
        return tuple(ref.at[k] for k in range(4))

    groups = (
        (
            down_parts,
            down_rows // rows,
            1,
            lambda h, r, c: down_sum.at[aligned(h * down_rows + r * rows, rows), :],
        ),
        (
            up_parts,
            strip // rows,
            up_cols // cols,
            lambda h, r, c: up_sum.at[pl.ds(r * rows, rows), aligned(h * up_cols + c * cols, cols)],
        ),
        (
            four(out_products),
            features // rows,
            1,
            lambda h, r, c: out_sum.at[aligned(h * features + r * rows, rows), :],
        ),
        (
            four(qkv_products),
            strip // rows,
            3,
            lambda h, r, c: qkv_sums[c].at[pl.ds(r * rows, rows), aligned(h * cols, cols)],
        ),
    )
    run, steps = reduce_stages(p, groups, engine)

    loads = [
        pltpu.make_async_copy(source, target, load_sem.at[k])
        for k, (source, target) in enumerate(
            (
                (hidden_hbm, base),
                (cot_hbm.at[pl.ds(0, own_rows), :], packed),
                (out_hbm, out_mat),
                (qkv_hbm, qkv),
                (attended_hbm, attended),
                (act_hbm, act),
                (qkv_mat_hbm, qkv_mat),
                (resid_hbm, base),
            )
        )
    ]
    sums = RowSum(
        p, own_rows, arrived, sent, loaded, sum_send, sum_recv, sum_load, core_free, y_free, 3
    )
    group_rows = 16
    quarter = own_rows // 4 // group_rows

    def start():
        for k in range(7):
            loads[k].start()
        small[...] = small_in[...]
        key_sum[...] = jnp.zeros_like(key_sum)
        value_sum[...] = jnp.zeros_like(value_sum)
        sums.start(0, two_part, False)

    def two_middle():
        sums.middle(two_part, False)

    def two_finish():
        sums.finish(two_part, False)
        loads[0].wait()
        loads[1].wait()

    def accumulate(row, value):
        small[pl.ds(row, 1), :] += jnp.sum(value, 0, keepdims=True)

    def two_rows(part):
        gain = vector_ref[pl.ds(GAIN_TWO, 1), :]

        @pl.loop(part * quarter, (part + 1) * quarter)
        def _(k):
            at = pl.ds(pl.multiple_of(k * group_rows, group_rows), group_rows)
            upstream = sums.total(two_part, False, at)
            unit, inverse = unit_rows(base[at, :])
            grad = packed[at, :].astype(f32) + unit_back(upstream, unit, inverse, gain)
            hidden_grad[at, :] = grad
            low[at, :] = grad.astype(bf16)
            accumulate(GAIN_TWO, upstream * unit)
            accumulate(SHIFT_TWO, upstream)
            accumulate(OUT_BIAS, grad)

    def low_block(k):
        return low.at[pl.ds(k * own_rows, own_rows), :]

    def join(k):
        source, place, target = ((0, 1, p.over_core), (0, 2, p.over_y), (2, 3, p.over_core))[k]
        return remote_copy(low_block(source), low_block(place), join_send.at[k], join_recv.at[k], target)

    def join_start():
        join(0).start()
        join(1).start()
        sums.release(0)

    def join_pass():
        join(1).wait_recv()
        join(2).start()

    def attend_block(k):
        at = pl.ds(k * own_rows, own_rows)
        attended_grad[at, :] = lax.dot_general(
            low[at, :], out_mat[...], (((1,), (1,)), ((), ())), preferred_element_type=f32
        ).astype(bf16)

    def attend_own():
        loads[2].wait()
        attend_block(0)

    def attend_peer():
        join(0).wait()
        attend_block(1)

    def attend_far():
        attend_block(2)

    def attend_last():
        join(1).wait_send()
        join(2).wait()
        attend_block(3)

    def mlp_start():
        sums.start(1, mlp_part, False)

    def mlp_middle():
        sums.middle(mlp_part, False)

    def mlp_finish():
        sums.finish(mlp_part, False)
        bias = vector_ref[pl.ds(DOWN_BIAS, 1), :]

        @pl.loop(0, own_rows // group_rows)
        def _(k):
            at = pl.ds(pl.multiple_of(k * group_rows, group_rows), group_rows)
            packed[at, :] = (base[at, :] + sums.total(mlp_part, False, at) + bias).astype(bf16)

        sums.release(1)

    def row_source(k):
        return packed.at[pl.ds(k * block_rows, block_rows), :]

    row_ends = (rows_out, rows_grad)

    def row_copy(a, k):
        end = row_ends[a].at[x * depth + z]
        return remote_copy(row_source(k), end, row_send.at[a, k], row_recv.at[a, z], p.row_target(k))

    def row_arrival(a, k):
        end = row_ends[a].at[t * depth + k]
        return remote_copy(row_source(k), end, row_send.at[a, k], row_recv.at[a, k], p.row_target(k))

    def row_stay(a, k):
        return pltpu.make_async_copy(row_source(k), row_ends[a].at[x * depth + z], row_send.at[a, k])

    def rows_start(a):
        for k in range(depth):
            stays = (z == k) & (x == t)
            pl.when(stays)(lambda k=k: row_stay(a, k).start())
            pl.when(jnp.logical_not(stays))(lambda k=k: row_copy(a, k).start())

    def share(a):
        group = row_ends[a].at[pl.ds(t * depth, depth)]
        return remote_copy(group, group, share_send.at[a], share_recv.at[a], p.over_core)

    def rows_share(a):
        for k in range(depth):
            stays = (z == k) & (x == t)
            pl.when(stays)(lambda k=k: row_stay(a, k).wait())

            @pl.when(jnp.logical_not(stays))
            def _(k=k):
                row_copy(a, k).wait_send()
                row_arrival(a, k).wait_recv()

        share(a).start()

    def head_rows():
        loads[3].wait()
        loads[4].wait()
        for block in range(4):
            at = pl.ds(pl.multiple_of(p.block_place(block) * own_rows, own_rows), own_rows)
            keys[pl.ds(block * own_rows, own_rows), :] = qkv[at, pl.ds(features, features)]
            values[pl.ds(block * own_rows, own_rows), :] = qkv[at, pl.ds(2 * features, features)]

    def attention_block(block):
        at = pl.ds(pl.multiple_of(p.block_place(block) * own_rows, own_rows), own_rows)
        part = pl.ds(0, (block + 1) * own_rows)

        @pl.loop(0, heads)
        def _(head):
            lanes = aligned(head * head_size, head_size)
            queries, grads = qkv[at, lanes], attended_grad[at, lanes]
            probs, _ = attention_probs(queries, keys[part, lanes], block, length)
            prob_grad = lax.dot_general(
                grads, values[part, lanes], (((1,), (1,)), ((), ())), preferred_element_type=f32
            )
            inner = jnp.sum(probs * prob_grad, -1, keepdims=True)
            score_grad = (probs * (prob_grad - inner)).astype(bf16)
            query_grad = (
                jnp.dot(score_grad, keys[part, lanes], preferred_element_type=f32) * scale
            )
            spot = aligned(column * features + head * head_size, head_size)
            small[pl.ds(QUERY_BIAS, 1), spot] += jnp.sum(query_grad, 0, keepdims=True)
            qkv_grad[at, lanes] = query_grad.astype(bf16)
            key_sum[part, lanes] += lax.dot_general(
                score_grad, queries, (((0,), (0,)), ((), ())), preferred_element_type=f32
            )
            value_sum[part, lanes] += lax.dot_general(
                probs.astype(bf16), grads, (((0,), (0,)), ((), ())), preferred_element_type=f32
            )

    def attention_end(block):
        at = pl.ds(pl.multiple_of(p.block_place(block) * own_rows, own_rows), own_rows)
        part = pl.ds(block * own_rows, own_rows)
        qkv_grad[at, pl.ds(features, features)] = (key_sum[part, :] * scale).astype(bf16)
        value_grad = value_sum[part, :]
        qkv_grad[at, pl.ds(2 * features, features)] = value_grad.astype(bf16)
        spot = aligned(column * features, features)
        small[pl.ds(VALUE_BIAS, 1), spot] += jnp.sum(value_grad, 0, keepdims=True)

    stored = []

    def store(value, target):
        k = len(stored) % 2
        if len(stored) >= 2:
            stored[-2].wait()
        stage[k] = value.astype(bf16)
        copy = pltpu.make_async_copy(stage.at[k], target, stage_sem.at[k])
        copy.start()
        stored.append(copy)

    def over_tokens(left, right):
        return lax.dot_general(left, right, (((0,), (0,)), ((), ())), preferred_element_type=f32)

    def out_product(k):
        store(
            over_tokens(attended[...], low[:, aligned(p.homes[k] * strip, strip)]),
            out_products.at[k],
        )

    def qkv_product(k, c):
        if k == 0 and c == 0:
            loads[5].wait()
        cut = pl.ds(c * features, features)
        store(
            over_tokens(act[:, aligned(p.homes[k] * strip, strip)], qkv_grad[:, cut]),
            qkv_products.at[k, :, cut],
        )

    def products_end():
        stored[-2].wait()
        stored[-1].wait()

    def one_block(k):
        if k == 3:
            loads[6].wait()
        at = pl.ds(k * own_rows, own_rows)

        @pl.loop(0, 4)
        def _(n):
            cut = aligned(n * strip, strip)
            low[at, cut] = lax.dot_general(
                qkv_grad[at, :], qkv_mat[cut, :], (((1,), (1,)), ((), ())), preferred_element_type=f32
            ).astype(bf16)

    def one_start():
        sums.start(2, low, True)

    def one_middle():
        sums.middle(low, True)

    def one_finish():
        sums.finish(low, True)
        loads[7].wait()

    def one_rows(part):
        gain = vector_ref[pl.ds(GAIN_ONE, 1), :]

        @pl.loop(part * quarter, (part + 1) * quarter)
        def _(k):
            at = pl.ds(pl.multiple_of(k * group_rows, group_rows), group_rows)
            upstream = sums.total(low, True, at)
            unit, inverse = unit_rows(base[at, :])
            grad = hidden_grad[at, :] + unit_back(upstream, unit, inverse, gain)
            packed[at, :] = grad.astype(bf16)
            accumulate(GAIN_ONE, upstream * unit)
            accumulate(SHIFT_ONE, upstream)

    def small_copy(k):
        target = (p.over_core, p.over_x, p.over_y, p.mate, p.hop)[k]
        return remote_copy(small, small_arrived.at[k], small_send.at[k], small_recv.at[k], target)

    def small_add(k):
        small_copy(k).wait()
        mine, other = small[...], small_arrived[k]
        row = lax.broadcasted_iota(jnp.int32, mine.shape, 0)
        small[...] = jnp.where(row == PEAKS, jnp.maximum(mine, other), mine + other)

    def call(function, *arguments):
        return lambda: function(*arguments)

    plan = {}

    def at_step(step, *tasks):
        plan.setdefault(step, []).extend(tasks)

    at_step(0, start)
    at_step(2, two_middle)
    at_step(7, two_finish, call(two_rows, 0))
    for k in range(1, 4):
        at_step(7 + k // 2, call(two_rows, k))
    at_step(8, join_start, mlp_start)
    at_step(9, attend_own)
    at_step(10, mlp_middle, attend_peer)
    at_step(12, head_rows)
    at_step(13, join_pass)
    at_step(14, attend_far)
    at_step(15, attend_last)
    at_step(16, call(attention_block, 0), call(attention_block, 1))
    at_step(17, call(attention_block, 2))
    at_step(18, call(attention_block, 3))
    at_step(19, *(call(attention_end, k) for k in range(4)))
    for k in range(4):
        at_step(19 + k, *(call(qkv_product, k, c) for c in range(3)))
        at_step(23, call(out_product, k))
    at_step(24, products_end, call(one_block, 3), call(one_block, 1), one_start)
    at_step(25, call(one_block, 2), call(one_block, 0))
    at_step(26, one_middle)
    at_step(20, mlp_finish, lambda: rows_start(0), loads[7].start)
    at_step(25, lambda: rows_share(0))
    at_step(31, one_finish, share(0).wait, call(one_rows, 0))
    for k in range(1, 4):
        at_step(31 + k // 2, call(one_rows, k))
    at_step(32, lambda: rows_start(1))
    at_step(33, small_copy(0).start)
    for k in range(4):
        at_step(35 + 2 * k, call(small_add, k), small_copy(k + 1).start)
    at_step(43, call(small_add, 4))
    at_step(38, lambda: rows_share(1))
    at_step(44, share(1).wait)
    for step in range(steps):
        run(step)
        for task in plan.get(step, ()):
            task()


def backward_all(
    head_size,
    length,
    vectors,
    small,
    down_parts,
    up_parts,
    two_part,
    mlp_part,
    hidden,
    cot_low,
    resid,
    out_mat,
    qkv_mat,
    qkv,
    attended,
    act_one,
    slots,
):
    bf16, f32 = jnp.bfloat16, jnp.float32
    hbm = pl.BlockSpec(memory_space=pl.ANY)
    vmem = pl.BlockSpec(memory_space=pltpu.VMEM)
    down_rows, strip = down_parts[0].shape
    up_cols = up_parts[0].shape[1]
    tokens, features = attended.shape
    own_rows, width = hidden.shape
    depth = slots // 2
    engine = reduce_scratch(6, 4, 256, 512)
    n_engine = len(engine)

    def kernel(*refs):
        ins, rest = refs[:21], refs[21:]
        outs, scratch = rest[:11], rest[11:]
        backward_kernel(
            head_size,
            ins[0],
            ins[1],
            ins[2],
            ins[3:7],
            ins[7:11],
            *ins[11:],
            outs[0],
            outs[1],
            outs[2],
            outs[3:6],
            *outs[6:],
            scratch[:n_engine],
            *scratch[n_engine:],
        )

    dma, regular = pltpu.SemaphoreType.DMA, pltpu.SemaphoreType.REGULAR

    def hold(shape, dtype=bf16):
        return pltpu.VMEM(shape, dtype)

    return pl.pallas_call(
        kernel,
        out_shape=(
            jax.ShapeDtypeStruct((2 * down_rows, strip), bf16),
            jax.ShapeDtypeStruct((strip, 2 * up_cols), bf16),
            jax.ShapeDtypeStruct((2 * features, strip), bf16),
            jax.ShapeDtypeStruct((strip, 2 * features), bf16),
            jax.ShapeDtypeStruct((strip, 2 * features), bf16),
            jax.ShapeDtypeStruct((strip, 2 * features), bf16),
            jax.ShapeDtypeStruct((slots, own_rows // depth, width), bf16),
            jax.ShapeDtypeStruct((slots, own_rows // depth, width), bf16),
            jax.ShapeDtypeStruct(small.shape, f32),
            jax.ShapeDtypeStruct((4, features, strip), bf16),
            jax.ShapeDtypeStruct((4, strip, 3 * features), bf16),
        ),
        in_specs=[pl.BlockSpec(memory_space=pltpu.SMEM), vmem, vmem] + [hbm] * 18,
        out_specs=(hbm,) * 8 + (vmem,) + (hbm,) * 2,
        scratch_shapes=engine
        + [
            hold((own_rows, width), f32),
            hold((own_rows, width), f32),
            hold((tokens, width)),
            hold((features, width)),
            hold((tokens, features)),
            hold((tokens, 3 * features)),
            hold((tokens, 3 * features)),
            hold((tokens, width)),
            hold((tokens, features)),
            hold((width, 3 * features)),
            hold((tokens, features)),
            hold((tokens, features)),
            hold((tokens, features), f32),
            hold((tokens, features), f32),
            hold((2, features, strip)),
            hold((own_rows, width)),
            hold((3, own_rows, width)),
            hold((own_rows, width)),
            hold((own_rows, width)),
            hold((5,) + small.shape, f32),
            dma((8,)),
            dma((3,)),
            dma((3,)),
            dma(()),
            dma((3,)),
            dma((3,)),
            dma((2,)),
            dma((2, depth)),
            dma((2, depth)),
            dma((2,)),
            dma((2,)),
            dma((5,)),
            dma((5,)),
            regular,
            regular,
        ],
        compiler_params=pltpu.CompilerParams(
            collective_id=1, has_side_effects=True, vmem_limit_bytes=58 << 20
        ),
        cost_estimate=pl.CostEstimate(flops=0, bytes_accessed=64 << 20, transcendentals=0),
    )(
        length,
        vectors,
        small,
        *down_parts,
        *up_parts,
        two_part,
        mlp_part,
        hidden,
        cot_low,
        resid,
        out_mat,
        qkv_mat,
        qkv,
        attended,
        act_one,
    )


def split_body(
    layer_input,
    cotangent,
    seq_lengths,
    dealing,
    attn_gain,
    attn_shift,
    query_weight,
    query_bias,
    key_weight,
    value_weight,
    value_bias,
    out_weight,
    out_bias,
    mlp_gain,
    mlp_shift,
    up_weight,
    up_bias,
    down_weight,
    down_bias,
    clip_level,
):
    f32, bf16 = jnp.float32, jnp.bfloat16
    f = lax.axis_index("fsdp")
    z = lax.axis_index("ctx")
    t = lax.axis_index("tp")
    y, x = f // 2, f % 2
    depth = lax.axis_size("ctx")
    slots, block_rows, width = layer_input.shape
    local_heads = query_bias.shape[0] // 2
    head_size = 4 * query_bias.shape[1]
    features = local_heads * head_size
    hidden_units = up_weight.shape[1] // 2
    strip = query_weight.shape[0]
    own_rows = depth * block_rows

    def strip_of(v, home):
        return lax.dynamic_slice_in_dim(v, home * strip, strip, 1)

    homes = (2 * y + 1 - x, 2 * (1 - y) + 1 - x, f, 2 * (1 - y) + x)

    def products(product):
        return tuple(product(home).astype(bf16) for home in homes)

    slot = x * depth + z
    length = seq_lengths[dealing[slot]]
    arrived = pick_slots(layer_input, dealing, t * depth, depth)
    cot_part = lax.dynamic_slice_in_dim(cotangent, t * depth, depth, 0)
    down_bias_part = jnp.sum(cot_part, (0, 1))
    vectors = jnp.concatenate(
        [jnp.stack([attn_gain, attn_shift, out_bias, mlp_gain, mlp_shift, down_bias]), up_bias], 0
    ).astype(f32)
    head_vectors = jnp.concatenate([query_bias, value_bias], 0).astype(f32)
    head_vectors = lax.dynamic_update_slice(
        jnp.zeros((head_vectors.shape[0], head_size), f32), head_vectors, (0, f * query_bias.shape[1])
    )
    (
        qkv_mat,
        out_mat,
        up_mat,
        down_mat,
        act_one,
        cot_low,
        qkv,
        attended,
        hidden,
        resid,
        act_two,
        vectors_whole,
        peaks,
    ) = forward_all(
        head_size,
        length[None],
        vectors,
        head_vectors,
        query_weight,
        key_weight,
        value_weight,
        out_weight,
        up_weight,
        down_weight,
        arrived,
        cot_part.astype(bf16),
    )
    peaks = peaks[:local_heads, 0]
    up_vec = lax.dynamic_slice_in_dim(vectors_whole, 6 + y, 1, 0)

    pre = matmul(act_two, up_mat) + up_vec
    cdf = 0.5 * (1.0 + lax.erf(pre * INV_ROOT_TWO))
    gelu_low = (pre * cdf).astype(bf16)
    slope = cdf + pre * (jnp.exp(-0.5 * pre * pre) * INV_ROOT_TWO_PI)
    pre_grad = back_product(cot_low, down_mat) * slope
    pre_low = pre_grad.astype(bf16)
    up_bias_part = jnp.sum(pre_grad, 0)
    down_parts = products(lambda home: weight_product(gelu_low, strip_of(cot_low, home)))
    up_parts = products(lambda home: weight_product(strip_of(act_two, home), pre_low))
    two_part = back_product(pre_low, up_mat).astype(bf16)
    mlp_part = matmul(gelu_low, down_mat).astype(bf16)
    column = 2 * t + y
    small = jnp.zeros((16, width), f32).at[DOWN_BIAS].set(down_bias_part)
    small = lax.dynamic_update_slice(small, up_bias_part[None], (UP_BIAS + column, 0))
    small = small.at[PEAKS].set(NEG)
    small = lax.dynamic_update_slice(small, peaks[None], (PEAKS, local_heads * (2 * t + y)))
    (
        down_sum,
        up_sum,
        out_sum,
        query_sum,
        key_sum,
        value_sum,
        rows_out,
        rows_grad,
        totals,
        _,
        _,
    ) = backward_all(
        head_size,
        length[None],
        vectors_whole,
        small,
        down_parts,
        up_parts,
        two_part,
        mlp_part,
        hidden,
        cot_low,
        resid,
        out_mat,
        qkv_mat,
        qkv,
        attended,
        act_one,
        slots,
    )
    rows_sum = lax.dynamic_slice(totals, (0, f * strip), (6, strip))
    head_sum = lax.dynamic_slice(totals, (QUERY_BIAS, 2 * t * features), (2, 2 * features))
    head_sum = head_sum.reshape(2, 2 * local_heads, head_size)
    head_sum = lax.dynamic_slice_in_dim(head_sum, f * query_bias.shape[1], query_bias.shape[1], 2)
    unit_sum = lax.dynamic_slice(
        totals, (UP_BIAS + up_bias.shape[0] * t, f * strip), (up_bias.shape[0], strip)
    )
    peak_all = lax.dynamic_slice(totals, (PEAKS, 2 * local_heads * t), (1, 2 * local_heads))[0]
    level = clip_level[0]
    factor = jnp.repeat(jnp.sqrt(level / jnp.maximum(peak_all, level)), head_size)
    query_clipped = (query_weight.astype(f32) * factor[None, :]).astype(bf16)
    key_clipped = (key_weight.astype(f32) * factor[None, :]).astype(bf16)
    return (
        rows_out.astype(f32),
        rows_grad.astype(f32),
        rows_sum[GAIN_ONE],
        rows_sum[SHIFT_ONE],
        query_sum.astype(f32),
        head_sum[0],
        key_sum.astype(f32),
        value_sum.astype(f32),
        head_sum[1],
        out_sum.astype(f32),
        rows_sum[OUT_BIAS],
        rows_sum[GAIN_TWO],
        rows_sum[SHIFT_TWO],
        up_sum.astype(f32),
        unit_sum,
        down_sum.astype(f32),
        rows_sum[DOWN_BIAS],
        peak_all,
        query_clipped,
        key_clipped,
    )


def solution(mesh):
    sizes = dict(mesh.shape)
    small_slice = sizes == {"fsdp": 4, "ctx": 4, "tp": 2}
    return jax.shard_map(
        split_body if small_slice else gathered_body,
        mesh=mesh,
        in_specs=(
            P(None, ("fsdp", "ctx"), None),
            P(None, ("fsdp", "ctx"), None),
            P(),
            P(),
            P("fsdp"),
            P("fsdp"),
            P("fsdp", "tp"),
            P("tp", "fsdp"),
            P("fsdp", "tp"),
            P("fsdp", "tp"),
            P("tp", "fsdp"),
            P("tp", "fsdp"),
            P("fsdp"),
            P("fsdp"),
            P("fsdp"),
            P("fsdp", "tp"),
            P("tp", "fsdp"),
            P("tp", "fsdp"),
            P("fsdp"),
            P(),
        ),
        out_specs=(
            P(None, ("fsdp", "ctx"), None),
            P(None, ("fsdp", "ctx"), None),
            P("fsdp"),
            P("fsdp"),
            P("fsdp", "tp"),
            P("tp", "fsdp"),
            P("fsdp", "tp"),
            P("fsdp", "tp"),
            P("tp", "fsdp"),
            P("tp", "fsdp"),
            P("fsdp"),
            P("fsdp"),
            P("fsdp"),
            P("fsdp", "tp"),
            P("tp", "fsdp"),
            P("tp", "fsdp"),
            P("fsdp"),
            P("tp"),
            P("fsdp", "tp"),
            P("fsdp", "tp"),
        ),
        check_vma=False,
    )
```

```python
import functools
import math

import jax
import jax.numpy as jnp
from jax import lax
from jax.experimental import pallas as pl
from jax.experimental.pallas import tpu as pltpu
from jax.sharding import PartitionSpec as P

EPS = 1e-05
NEG = -1e30
INV_ROOT_TWO = 0.7071067811865476
INV_ROOT_TWO_PI = 0.3989422804014327


def normalize(values, scale_vec, offset_vec):
    center = values - jnp.mean(values, -1, keepdims=True)
    inverse = lax.rsqrt(jnp.mean(center * center, -1, keepdims=True) + EPS)
    normed = center * inverse
    return (normed * scale_vec + offset_vec, normed, inverse)


def norm_back(upstream, normed, inverse, scale_vec):
    scaled = upstream * scale_vec
    inner = (
        scaled
        - jnp.mean(scaled, -1, keepdims=True)
        - normed * jnp.mean(scaled * normed, -1, keepdims=True)
    )
    return (inverse * inner, jnp.sum(upstream * normed, 0), jnp.sum(upstream, 0))


def pick_slots(rows, dealing, first, count):
    return jnp.concatenate(
        [lax.dynamic_slice_in_dim(rows, dealing[first + j], 1, 0) for j in range(count)], 0
    )


def matmul(left, right):
    return jnp.dot(left, right, preferred_element_type=jnp.float32)


def weight_product(left, right):
    return jnp.einsum("td,te->de", left, right, preferred_element_type=jnp.float32)


def back_product(left, right):
    return jnp.einsum("te,de->td", left, right, preferred_element_type=jnp.float32)


def gathered_body(
    layer_input,
    cotangent,
    seq_lengths,
    dealing,
    attn_gain,
    attn_shift,
    query_weight,
    query_bias,
    key_weight,
    value_weight,
    value_bias,
    out_weight,
    out_bias,
    mlp_gain,
    mlp_shift,
    up_weight,
    up_bias,
    down_weight,
    down_bias,
    clip_level,
):
    shard_count = lax.axis_size("fsdp")
    ctx_count = lax.axis_size("ctx")
    my_group = lax.axis_index("fsdp")
    ctx_place = lax.axis_index("ctx")
    slot_count, block_rows, width = layer_input.shape
    per_group = slot_count // shard_count
    local_rows = shard_count * block_rows
    tokens = per_group * local_rows
    dealt_input = pick_slots(layer_input, dealing, 0, slot_count).reshape(
        shard_count, per_group, block_rows, width
    )
    dealt_grad = cotangent.reshape(shard_count, per_group, block_rows, width)
    arrived_input, arrived_grad = (
        lax.all_to_all(dealt_input, "fsdp", split_axis=0, concat_axis=2, tiled=True),
        lax.all_to_all(dealt_grad, "fsdp", split_axis=0, concat_axis=2, tiled=True),
    )
    resid = arrived_input.reshape(tokens, width)
    upstream = arrived_grad.reshape(tokens, width)
    seq_lens = lax.dynamic_slice_in_dim(
        jnp.take(seq_lengths, dealing), my_group * per_group, per_group
    )
    gathered = (
        lax.all_gather(attn_gain, "fsdp", axis=0, tiled=True),
        lax.all_gather(attn_shift, "fsdp", axis=0, tiled=True),
        lax.all_gather(query_weight, "fsdp", axis=0, tiled=True),
        lax.all_gather(query_bias, "fsdp", axis=1, tiled=True),
        lax.all_gather(key_weight, "fsdp", axis=0, tiled=True),
        lax.all_gather(value_weight, "fsdp", axis=0, tiled=True),
        lax.all_gather(value_bias, "fsdp", axis=1, tiled=True),
        lax.all_gather(out_weight, "fsdp", axis=1, tiled=True),
        lax.all_gather(out_bias, "fsdp", axis=0, tiled=True),
        lax.all_gather(mlp_gain, "fsdp", axis=0, tiled=True),
        lax.all_gather(mlp_shift, "fsdp", axis=0, tiled=True),
        lax.all_gather(up_weight, "fsdp", axis=0, tiled=True),
        lax.all_gather(up_bias, "fsdp", axis=1, tiled=True),
        lax.all_gather(down_weight, "fsdp", axis=1, tiled=True),
        lax.all_gather(down_bias, "fsdp", axis=0, tiled=True),
    )
    (
        gain_one,
        shift_one,
        query_mat,
        query_vec,
        key_mat,
        value_mat,
        value_vec,
        out_mat,
        out_vec,
        gain_two,
        shift_two,
        up_mat,
        up_vec,
        down_mat,
        down_vec,
    ) = gathered
    head_count, head_size = query_vec.shape
    features = head_count * head_size
    scale_of_scores = 1.0 / math.sqrt(head_size)
    row_ids = jnp.arange(local_rows, dtype=jnp.int32)
    query_pos = (row_ids // block_rows * ctx_count + ctx_place) * block_rows + row_ids % block_rows
    key_ids = jnp.arange(ctx_count * local_rows, dtype=jnp.int32)
    key_rows = key_ids % local_rows
    key_pos = (
        key_rows // block_rows * ctx_count + key_ids // local_rows
    ) * block_rows + key_rows % block_rows
    allowed = (key_pos[None, None, :] <= query_pos[None, :, None]) & (
        key_pos[None, None, :] < seq_lens[:, None, None]
    )
    query_live = query_pos[None, :] < seq_lens[:, None]
    normed_a, unit_one, inverse_one = normalize(
        resid, gain_one.astype(jnp.float32), shift_one.astype(jnp.float32)
    )
    act_one = normed_a.astype(jnp.bfloat16)
    queries = (
        (matmul(act_one, query_mat) + query_vec.reshape(features).astype(jnp.float32))
        .astype(jnp.bfloat16)
        .reshape(per_group, local_rows, features)
    )
    keys_mine = (
        matmul(act_one, key_mat).astype(jnp.bfloat16).reshape(per_group, local_rows, features)
    )
    values_mine = (
        (matmul(act_one, value_mat) + value_vec.reshape(features).astype(jnp.float32))
        .astype(jnp.bfloat16)
        .reshape(per_group, local_rows, features)
    )
    keys_all, values_all = (
        lax.all_gather(keys_mine, "ctx", axis=1, tiled=True),
        lax.all_gather(values_mine, "ctx", axis=1, tiled=True),
    )

    def head_cut(array, head_index):
        return lax.dynamic_slice_in_dim(array, head_index * head_size, head_size, 2)

    def head_scores(head_queries, head_keys):
        return (
            jnp.einsum("sqd,skd->sqk", head_queries, head_keys, preferred_element_type=jnp.float32)
            * scale_of_scores
        )

    def forward_head(head_index):
        logit_scores = head_scores(head_cut(queries, head_index), head_cut(keys_all, head_index))
        masked = jnp.where(allowed, logit_scores, NEG)
        row_top = jnp.max(masked, -1, keepdims=True)
        exp_terms = jnp.where(allowed, jnp.exp(masked - row_top), 0.0)
        total = jnp.sum(exp_terms, -1, keepdims=True)
        attention_probabilities = exp_terms / total
        attended_rows = jnp.einsum(
            "sqk,skd->sqd",
            attention_probabilities.astype(jnp.bfloat16),
            head_cut(values_all, head_index),
            preferred_element_type=jnp.float32,
        )
        log_total = row_top[..., 0] + jnp.log(total[..., 0])
        peak = jnp.max(jnp.where(query_live, row_top[..., 0], NEG))
        return (attended_rows, log_total, peak)

    attended_rows, log_totals, peaks = lax.map(forward_head, jnp.arange(head_count))
    attn_low = attended_rows.transpose(1, 2, 0, 3).reshape(tokens, features).astype(jnp.bfloat16)
    attn_sum = lax.psum(matmul(attn_low, out_mat), "tp")
    hidden = resid + attn_sum + out_vec.astype(jnp.float32)
    normed_b, unit_two, inverse_two = normalize(
        hidden, gain_two.astype(jnp.float32), shift_two.astype(jnp.float32)
    )
    act_two = normed_b.astype(jnp.bfloat16)
    pre = matmul(act_two, up_mat) + up_vec.reshape(-1).astype(jnp.float32)
    gelu_low = jax.nn.gelu(pre, approximate=False).astype(jnp.bfloat16)
    mlp_sum = lax.psum(matmul(gelu_low, down_mat).astype(jnp.bfloat16), "tp").astype(jnp.float32)
    layer_output = hidden + mlp_sum + down_vec.astype(jnp.float32)
    peak_all = lax.pmax(peaks, ("fsdp", "ctx"))
    level = clip_level[0]
    factor = jnp.repeat(jnp.sqrt(level / jnp.maximum(peak_all, level)), head_size)
    query_clipped = (query_weight.astype(jnp.float32) * factor[None, :]).astype(jnp.bfloat16)
    key_clipped = (key_weight.astype(jnp.float32) * factor[None, :]).astype(jnp.bfloat16)
    grad_low = upstream.astype(jnp.bfloat16)
    down_weight_grad = weight_product(gelu_low, grad_low)
    down_bias_grad = jnp.sum(upstream, 0)
    cdf = 0.5 * (1.0 + lax.erf(pre * INV_ROOT_TWO))
    density = jnp.exp(-0.5 * pre * pre) * INV_ROOT_TWO_PI
    pre_grad = back_product(grad_low, down_mat) * (cdf + pre * density)
    pre_low = pre_grad.astype(jnp.bfloat16)
    up_weight_grad = weight_product(act_two, pre_low)
    up_bias_grad = jnp.sum(pre_grad, 0).reshape(up_vec.shape)
    normed_two_grad = lax.psum(back_product(pre_low, up_mat), "tp")
    hidden_in, mlp_gain_grad, mlp_shift_grad = norm_back(
        normed_two_grad, unit_two, inverse_two, gain_two.astype(jnp.float32)
    )
    hidden_grad = upstream + hidden_in
    hidden_low = hidden_grad.astype(jnp.bfloat16)
    out_weight_grad = weight_product(attn_low, hidden_low)
    out_bias_grad = jnp.sum(hidden_grad, 0)
    attended_grad = (
        back_product(hidden_low, out_mat)
        .astype(jnp.bfloat16)
        .reshape(per_group, local_rows, features)
    )

    def backward_head(head_index):
        head_queries = head_cut(queries, head_index)
        head_keys = head_cut(keys_all, head_index)
        head_values = head_cut(values_all, head_index)
        grad_head = head_cut(attended_grad, head_index)
        logit_scores = head_scores(head_queries, head_keys)
        masked = jnp.where(allowed, logit_scores, NEG)
        attention_probabilities = jnp.where(
            allowed, jnp.exp(masked - log_totals[head_index][..., None]), 0.0
        )
        prob_grad = jnp.einsum(
            "sqd,skd->sqk", grad_head, head_values, preferred_element_type=jnp.float32
        )
        inner = jnp.sum(attention_probabilities * prob_grad, -1, keepdims=True)
        score_grad = (attention_probabilities * (prob_grad - inner)).astype(jnp.bfloat16)
        query_grad = (
            jnp.einsum("sqk,skd->sqd", score_grad, head_keys, preferred_element_type=jnp.float32)
            * scale_of_scores
        )
        key_grad = (
            jnp.einsum("sqk,sqd->skd", score_grad, head_queries, preferred_element_type=jnp.float32)
            * scale_of_scores
        )
        value_grad = jnp.einsum(
            "sqk,sqd->skd",
            attention_probabilities.astype(jnp.bfloat16),
            grad_head,
            preferred_element_type=jnp.float32,
        )
        return (query_grad, key_grad, value_grad)

    query_parts, key_parts, value_parts = lax.map(backward_head, jnp.arange(head_count))
    query_grads = query_parts.transpose(1, 2, 0, 3).reshape(tokens, features)
    key_whole = key_parts.transpose(1, 2, 0, 3).reshape(per_group, ctx_count * local_rows, features)
    value_whole = value_parts.transpose(1, 2, 0, 3).reshape(
        per_group, ctx_count * local_rows, features
    )
    key_summed, value_summed = (
        lax.psum_scatter(key_whole, "ctx", scatter_dimension=1, tiled=True),
        lax.psum_scatter(value_whole, "ctx", scatter_dimension=1, tiled=True),
    )
    key_grads = key_summed.reshape(tokens, features)
    value_grads = value_summed.reshape(tokens, features)
    query_bias_grad = jnp.sum(query_grads, 0).reshape(head_count, head_size)
    value_bias_grad = jnp.sum(value_grads, 0).reshape(head_count, head_size)
    query_low = query_grads.astype(jnp.bfloat16)
    key_low = key_grads.astype(jnp.bfloat16)
    value_low = value_grads.astype(jnp.bfloat16)
    query_weight_grad = weight_product(act_one, query_low)
    key_weight_grad = weight_product(act_one, key_low)
    value_weight_grad = weight_product(act_one, value_low)
    normed_one_grad = lax.psum(
        (
            back_product(query_low, query_mat)
            + back_product(key_low, key_mat)
            + back_product(value_low, value_mat)
        ).astype(jnp.bfloat16),
        "tp",
    ).astype(jnp.float32)
    input_in, attn_gain_grad, attn_shift_grad = norm_back(
        normed_one_grad, unit_one, inverse_one, gain_one.astype(jnp.float32)
    )
    input_grad = hidden_grad + input_in
    partial_sums = (
        lax.psum_scatter(
            attn_gain_grad.astype(jnp.bfloat16), "fsdp", scatter_dimension=0, tiled=True
        ).astype(jnp.float32),
        lax.psum_scatter(
            attn_shift_grad.astype(jnp.bfloat16), "fsdp", scatter_dimension=0, tiled=True
        ).astype(jnp.float32),
        lax.psum_scatter(
            query_weight_grad.astype(jnp.bfloat16), "fsdp", scatter_dimension=0, tiled=True
        ).astype(jnp.float32),
        lax.psum_scatter(
            query_bias_grad.astype(jnp.bfloat16), "fsdp", scatter_dimension=1, tiled=True
        ).astype(jnp.float32),
        lax.psum_scatter(
            key_weight_grad.astype(jnp.bfloat16), "fsdp", scatter_dimension=0, tiled=True
        ).astype(jnp.float32),
        lax.psum_scatter(
            value_weight_grad.astype(jnp.bfloat16), "fsdp", scatter_dimension=0, tiled=True
        ).astype(jnp.float32),
        lax.psum_scatter(
            value_bias_grad.astype(jnp.bfloat16), "fsdp", scatter_dimension=1, tiled=True
        ).astype(jnp.float32),
        lax.psum_scatter(
            out_weight_grad.astype(jnp.bfloat16), "fsdp", scatter_dimension=1, tiled=True
        ).astype(jnp.float32),
        lax.psum_scatter(
            out_bias_grad.astype(jnp.bfloat16), "fsdp", scatter_dimension=0, tiled=True
        ).astype(jnp.float32),
        lax.psum_scatter(
            mlp_gain_grad.astype(jnp.bfloat16), "fsdp", scatter_dimension=0, tiled=True
        ).astype(jnp.float32),
        lax.psum_scatter(
            mlp_shift_grad.astype(jnp.bfloat16), "fsdp", scatter_dimension=0, tiled=True
        ).astype(jnp.float32),
        lax.psum_scatter(
            up_weight_grad.astype(jnp.bfloat16), "fsdp", scatter_dimension=0, tiled=True
        ).astype(jnp.float32),
        lax.psum_scatter(
            up_bias_grad.astype(jnp.bfloat16), "fsdp", scatter_dimension=1, tiled=True
        ).astype(jnp.float32),
        lax.psum_scatter(
            down_weight_grad.astype(jnp.bfloat16), "fsdp", scatter_dimension=1, tiled=True
        ).astype(jnp.float32),
        lax.psum_scatter(
            down_bias_grad.astype(jnp.bfloat16), "fsdp", scatter_dimension=0, tiled=True
        ).astype(jnp.float32),
    )
    shards = (
        lax.psum(partial_sums[0].astype(jnp.bfloat16), "ctx").astype(jnp.float32),
        lax.psum(partial_sums[1].astype(jnp.bfloat16), "ctx").astype(jnp.float32),
        lax.psum(partial_sums[2].astype(jnp.bfloat16), "ctx").astype(jnp.float32),
        lax.psum(partial_sums[3].astype(jnp.bfloat16), "ctx").astype(jnp.float32),
        lax.psum(partial_sums[4].astype(jnp.bfloat16), "ctx").astype(jnp.float32),
        lax.psum(partial_sums[5].astype(jnp.bfloat16), "ctx").astype(jnp.float32),
        lax.psum(partial_sums[6].astype(jnp.bfloat16), "ctx").astype(jnp.float32),
        lax.psum(partial_sums[7].astype(jnp.bfloat16), "ctx").astype(jnp.float32),
        lax.psum(partial_sums[8].astype(jnp.bfloat16), "ctx").astype(jnp.float32),
        lax.psum(partial_sums[9].astype(jnp.bfloat16), "ctx").astype(jnp.float32),
        lax.psum(partial_sums[10].astype(jnp.bfloat16), "ctx").astype(jnp.float32),
        lax.psum(partial_sums[11].astype(jnp.bfloat16), "ctx").astype(jnp.float32),
        lax.psum(partial_sums[12].astype(jnp.bfloat16), "ctx").astype(jnp.float32),
        lax.psum(partial_sums[13].astype(jnp.bfloat16), "ctx").astype(jnp.float32),
        lax.psum(partial_sums[14].astype(jnp.bfloat16), "ctx").astype(jnp.float32),
    )
    sent_output = layer_output.reshape(1, per_group, local_rows, width)
    sent_grad = input_grad.reshape(1, per_group, local_rows, width)
    back_output, back_grad = (
        lax.all_to_all(
            sent_output.astype(jnp.bfloat16), "fsdp", split_axis=2, concat_axis=0, tiled=True
        ).astype(sent_output.dtype),
        lax.all_to_all(
            sent_grad.astype(jnp.bfloat16), "fsdp", split_axis=2, concat_axis=0, tiled=True
        ).astype(sent_grad.dtype),
    )
    final_output = back_output.reshape(slot_count, block_rows, width)
    final_grad = back_grad.reshape(slot_count, block_rows, width)
    return (
        final_output,
        final_grad,
        shards[0],
        shards[1],
        shards[2],
        shards[3],
        shards[4],
        shards[5],
        shards[6],
        shards[7],
        shards[8],
        shards[9],
        shards[10],
        shards[11],
        shards[12],
        shards[13],
        shards[14],
        peak_all,
        query_clipped,
        key_clipped,
    )


def attention_probs(query_block, key_rows, block, length):
    rows, cols = query_block.shape[0], key_rows.shape[0]
    scores = lax.dot_general(
        query_block, key_rows, (((1,), (1,)), ((), ())), preferred_element_type=jnp.float32
    ) * (1.0 / math.sqrt(query_block.shape[1]))
    row_pos = block * rows + lax.broadcasted_iota(jnp.int32, (rows, cols), 0)
    col_pos = lax.broadcasted_iota(jnp.int32, (rows, cols), 1)
    scores = jnp.where((col_pos <= row_pos) & (col_pos < length), scores, NEG)
    top = jnp.max(scores, -1, keepdims=True)
    terms = jnp.exp(scores - top)
    return terms / jnp.sum(terms, -1, keepdims=True), top


def entry_barrier(targets):
    barrier = pltpu.get_barrier_semaphore()
    for target in targets:
        pl.semaphore_signal(barrier, inc=1, device_id=target, device_id_type=pl.DeviceIdType.MESH)
    pl.semaphore_wait(barrier, len(targets))


def remote_copy(src, dst, send, recv, target):
    return pltpu.make_async_remote_copy(
        src_ref=src,
        dst_ref=dst,
        send_sem=send,
        recv_sem=recv,
        device_id=target,
        device_id_type=pl.DeviceIdType.MESH,
    )


def grant(semaphore, target):
    pl.semaphore_signal(semaphore, inc=1, device_id=target, device_id_type=pl.DeviceIdType.MESH)


def aligned(start, size):
    return pl.ds(pl.multiple_of(start, 128), size)


class Place:
    def __init__(self, depth):
        self.depth = depth
        f = lax.axis_index("fsdp")
        z = lax.axis_index("ctx")
        t = lax.axis_index("tp")
        y, x = f // 2, f % 2
        self.f, self.z, self.t, self.y, self.x = f, z, t, y, x
        self.over_x = {"fsdp": 2 * y + 1 - x, "ctx": z, "tp": t}
        self.over_y = {"fsdp": 2 * (1 - y) + x, "ctx": z, "tp": t}
        self.over_core = {"fsdp": f, "ctx": z, "tp": 1 - t}
        self.mate = {"fsdp": f, "ctx": z + 1 - 2 * (z % 2), "tp": t}
        self.middle = {"fsdp": f, "ctx": 3 - z, "tp": t}
        self.hop = {"fsdp": f, "ctx": lax.rem(z + 2, 4), "tp": t}
        self.homes = (2 * y + 1 - x, 2 * (1 - y) + 1 - x, f, 2 * (1 - y) + x)

    def row_target(self, k):
        return {"fsdp": 2 * self.y + self.t, "ctx": k, "tp": self.x}

    def row_targets(self):
        others = [self.row_target(lax.rem(self.z + k, self.depth)) for k in range(1, self.depth)]
        return others + [{"fsdp": 2 * self.y + 1 - self.x, "ctx": self.z, "tp": 1 - self.t}]

    def block_place(self, block):
        return 2 * jnp.where(self.y == block // 2, 0, 1) + jnp.where(self.t == block % 2, 0, 1)


def reduce_stages(p, items, scratch):
    (
        x_slot,
        made_slot,
        own_slot,
        pair_slot,
        y_slot,
        z_slot,
        z_pair,
        inner_slot,
        total_slot,
        x_send,
        x_recv,
        y_send,
        y_recv,
        outer_send,
        outer_recv,
        inner_send,
        inner_recv,
        out_sem,
        x_free,
        y_free,
        outer_free,
        inner_free,
    ) = scratch
    y, z = p.y, p.z
    outer = (z == 0) | (z == 3)
    inner = (z == 1) | (z == 2)
    slots = x_slot.shape[0]
    count = len(items)
    far_count = count // 2
    far_slots = y_slot.shape[0]

    def x_copy(i):
        k = i % slots
        return remote_copy(made_slot.at[k], x_slot.at[k], x_send.at[k], x_recv.at[k], p.over_x)

    def y_copy(i):
        k, g = i % slots, (i // 2) % far_slots
        return remote_copy(pair_slot.at[k], y_slot.at[g], y_send.at[g], y_recv.at[g], p.over_y)

    def summed(i):
        return y_slot.at[(i // 2) % far_slots] if items[i][0] else pair_slot.at[i % slots]

    def outward(i):
        k = i % slots
        return remote_copy(summed(i), z_slot.at[k], outer_send.at[k], outer_recv.at[k], p.mate)

    def across(i):
        k = i % slots
        return remote_copy(z_pair.at[k], inner_slot.at[k], inner_send.at[k], inner_recv.at[k], p.middle)

    def backward(i):
        k = i % slots
        return remote_copy(total_slot.at[k], z_slot.at[k], outer_send.at[k], outer_recv.at[k], p.mate)

    def result_inner(i):
        k = i % slots
        return pltpu.make_async_copy(total_slot.at[k], items[i][1], out_sem.at[k])

    def result_outer(i):
        k = i % slots
        return pltpu.make_async_copy(z_slot.at[k], items[i][1], out_sem.at[k])

    def add(left, right, target):
        target[...] = (left[...].astype(jnp.float32) + right[...].astype(jnp.float32)).astype(
            target.dtype
        )

    def stage_send(i):
        k = i % slots
        items[i][2](made_slot.at[k], own_slot.at[k])
        if i >= slots:
            pl.semaphore_wait(x_free, 1)
        x_copy(i).start()

    def stage_pair(i):
        x_copy(i).wait()
        k = i % slots
        add(x_slot.at[k], own_slot.at[k], pair_slot.at[k])
        if i + slots < count:
            grant(x_free, p.over_x)
        if items[i][0]:
            if i // 2 >= far_slots:
                pl.semaphore_wait(y_free, 1)
            y_copy(i).start()

    def stage_outward(i):
        if items[i][0]:
            y_copy(i).wait()

        @pl.when(outer)
        def _():
            if i >= slots:
                pl.semaphore_wait(outer_free, 1)
            outward(i).start()

    def stage_across(i):
        k = i % slots

        @pl.when(outer)
        def _():
            outward(i).wait_send()

        @pl.when(inner)
        def _():
            outward(i).wait_recv()
            add(summed(i), z_slot.at[k], z_pair.at[k])
            if i + slots < count:
                grant(outer_free, p.mate)
            if i >= slots:
                pl.semaphore_wait(inner_free, 1)
            across(i).start()

        if items[i][0] and i // 2 + far_slots < far_count:
            grant(y_free, p.over_y)

    def stage_total(i):
        k = i % slots

        @pl.when(inner)
        def _():
            across(i).wait()
            add(z_pair.at[k], inner_slot.at[k], total_slot.at[k])
            if i + slots < count:
                grant(inner_free, p.middle)
            if i >= slots:
                pl.semaphore_wait(outer_free, 1)
            backward(i).start()
            result_inner(i).start()

    def stage_result(i):
        @pl.when(inner)
        def _():
            backward(i).wait_send()
            result_inner(i).wait()

        @pl.when(outer)
        def _():
            backward(i).wait_recv()
            result_outer(i).start()

    def stage_finish(i):
        @pl.when(outer)
        def _():
            result_outer(i).wait()
            if i + slots < count:
                grant(outer_free, p.mate)

    stages = (
        (11, stage_finish),
        (10, stage_result),
        (8, stage_total),
        (6, stage_across),
        (4, stage_outward),
        (2, stage_pair),
        (0, stage_send),
    )

    def run(step):
        for lag, stage in stages:
            if 0 <= step - lag < count:
                stage(step - lag)

    return run, count + 12


def reduce_scratch(slots, far_slots, rows, cols):
    dma, regular = pltpu.SemaphoreType.DMA, pltpu.SemaphoreType.REGULAR
    counts = (slots,) * 4 + (far_slots,) + (slots,) * 4
    return [pltpu.VMEM((n, rows, cols), jnp.bfloat16) for n in counts] + [
        dma((n,)) for n in (slots,) * 2 + (far_slots,) * 2 + (slots,) * 5
    ] + [regular] * 4


PARTS = 4


class RowSum:
    def __init__(self, p, rows, arrived, sent, loaded, send_sem, recv_sem, load_sem, core_free, y_free, uses):
        self.p, self.rows, self.uses = p, rows, uses
        self.arrived, self.sent, self.loaded = arrived, sent, loaded
        self.send_sem, self.recv_sem, self.load_sem = send_sem, recv_sem, load_sem
        self.core_free, self.y_free = core_free, y_free

    def block(self, ref, k):
        return ref.at[pl.ds(k * self.rows, self.rows), :]

    def hop(self, ref, k):
        return remote_copy(
            self.block(ref, 3 - 2 * k),
            self.arrived.at[k],
            self.send_sem.at[k],
            self.recv_sem.at[k],
            self.p.over_core,
        )

    def hop_y(self, part):
        size = self.rows // PARTS
        cut = pl.ds(part * size, size)
        return remote_copy(
            self.sent.at[cut, :],
            self.arrived.at[2, cut, :],
            self.send_sem.at[2 + part],
            self.recv_sem.at[2 + part],
            self.p.over_y,
        )

    def load(self, ref, k):
        return pltpu.make_async_copy(self.block(ref, k), self.loaded, self.load_sem)

    def start(self, use, ref, local):
        if use:
            pl.semaphore_wait(self.core_free, 1)
            pl.semaphore_wait(self.y_free, 1)
        self.hop(ref, 0).start()
        self.hop(ref, 1).start()
        if not local:
            self.load(ref, 2).start()

    def middle(self, ref, local, part):
        if part == 0:
            self.hop(ref, 0).wait()
            if not local:
                self.load(ref, 2).wait()
        base = self.block(ref, 2) if local else self.loaded
        size = self.rows // PARTS

        @pl.loop(part * size // 32, (part + 1) * size // 32)
        def _(k):
            at = pl.ds(pl.multiple_of(k * 32, 32), 32)
            self.sent[at, :] = (
                base[at, :].astype(jnp.float32) + self.arrived[0, at, :].astype(jnp.float32)
            ).astype(jnp.bfloat16)

        self.hop_y(part).start()
        if part == PARTS - 1 and not local:
            self.load(ref, 0).start()

    def finish(self, ref, local):
        self.hop(ref, 1).wait()
        for part in range(PARTS):
            self.hop_y(part).wait()
        if not local:
            self.load(ref, 0).wait()

    def total(self, ref, local, at):
        base = self.block(ref, 0) if local else self.loaded
        return (
            base[at, :].astype(jnp.float32)
            + self.arrived[1, at, :].astype(jnp.float32)
            + self.arrived[2, at, :].astype(jnp.float32)
        )

    def release(self, use):
        if use + 1 < self.uses:
            grant(self.core_free, self.p.over_core)
            grant(self.y_free, self.p.over_y)


def unit_rows(values):
    center = values - jnp.mean(values, -1, keepdims=True)
    inverse = lax.rsqrt(jnp.mean(center * center, -1, keepdims=True) + EPS)
    return center * inverse, inverse


def unit_back(upstream, unit, inverse, gain):
    scaled = upstream * gain
    return inverse * (
        scaled
        - jnp.mean(scaled, -1, keepdims=True)
        - unit * jnp.mean(scaled * unit, -1, keepdims=True)
    )


GAIN_ONE, SHIFT_ONE, OUT_BIAS, GAIN_TWO, SHIFT_TWO, DOWN_BIAS, QUERY_BIAS, VALUE_BIAS, UP_BIAS, PEAKS = (
    0,
    1,
    2,
    3,
    4,
    5,
    6,
    7,
    8,
    12,
)


def forward_kernel(
    head_size,
    info,
    vec_hbm,
    head_hbm,
    q_ref,
    k_ref,
    v_ref,
    o_ref,
    u_ref,
    d_ref,
    arrived_hbm,
    cot_hbm,
    qkv_mat_out,
    out_mat_out,
    up_all,
    down_all,
    act_out,
    cot_all,
    qkv_out,
    attended_out,
    hidden_out,
    resid_out,
    two_out,
    vec_all,
    peaks,
    qkv_mat,
    out_mat,
    fresh,
    part,
    act,
    hidden,
    qkv,
    keys,
    values,
    attended,
    partial,
    arrived,
    sent,
    two,
    vec_own,
    head_own,
    head_got,
    qkv_bias,
    local_sem,
    send_sem,
    recv_sem,
    row_send,
    row_recv,
    join_send,
    join_recv,
    vec_send,
    vec_recv,
    load_sem,
    sum_send,
    sum_recv,
    out_sem,
):
    f32, bf16 = jnp.float32, jnp.bfloat16
    depth, block_rows, width = arrived_hbm.shape
    own_rows = depth * block_rows
    strip = q_ref.shape[0]
    features = q_ref.shape[1] // 2
    units = u_ref.shape[1] // 2
    heads = features // head_size
    p = Place(depth)
    f, x, y, z, t = p.f, p.x, p.y, p.z, p.t
    even = z % 2 == 0
    odd = jnp.logical_not(even)
    diagonal = {"fsdp": 3 - f, "ctx": z, "tp": t}
    entry_barrier([p.over_x, p.over_y, p.mate, p.over_core, diagonal] + p.row_targets())
    length = info[0]

    chunks = []
    rows = strip // 2
    for k, ref in enumerate((q_ref, k_ref, v_ref)):
        for r in range(2):
            chunks.append(
                (
                    lambda w, ref=ref, r=r: ref.at[pl.ds(r * rows, rows), aligned(w * features, features)],
                    lambda home, k=k, r=r: qkv_mat.at[
                        aligned(home * strip + r * rows, rows), pl.ds(k * features, features)
                    ],
                )
            )
    for r in range(2):
        chunks.append(
            (
                lambda w, r=r: o_ref.at[aligned(w * features + r * rows, rows), :],
                lambda home, r=r: out_mat.at[pl.ds(r * rows, rows), aligned(home * strip, strip)],
            )
        )
    pieces = 8
    for r in range(pieces):
        size = strip // pieces
        chunks.append(
            (
                lambda w, r=r, size=size: u_ref.at[pl.ds(r * size, size), aligned(w * units, units)],
                lambda home, r=r, size=size: up_all.at[
                    pl.ds(pl.multiple_of(home * strip + r * size, size), size), :
                ],
            )
        )
    for r in range(pieces):
        size = units // pieces
        chunks.append(
            (
                lambda w, r=r, size=size: d_ref.at[aligned(w * units + r * size, size), :],
                lambda home, r=r, size=size: down_all.at[pl.ds(r * size, size), aligned(home * strip, strip)],
            )
        )
    count = len(chunks)
    far_home = 2 * (1 - y) + x

    def own_copy(i):
        source, place = chunks[i]
        return pltpu.make_async_copy(source(y), place(f), local_sem.at[i])

    def y_copy(i):
        source, place = chunks[i]
        return remote_copy(source(1 - y), place(f), send_sem.at[0, i], recv_sem.at[0, i], p.over_y)

    def x_copy(i, is_even):
        source, place = chunks[i]
        start = source(y) if is_even else place(far_home)
        home = f if is_even else far_home
        return remote_copy(start, place(home), send_sem.at[1, i], recv_sem.at[1, i], p.over_x)

    def z_copy(i, is_even):
        place = chunks[i][1]
        home = 2 * y + 1 - x if is_even else 2 * (1 - y) + 1 - x
        return remote_copy(place(home), place(home), send_sem.at[2, i], recv_sem.at[2, i], p.mate)

    rows_of = ((part, act), (cot_hbm, cot_all), (arrived_hbm, hidden))

    def row_copy(a, k):
        source, place = rows_of[a]
        return remote_copy(
            source.at[k],
            place.at[pl.ds(pl.multiple_of(z * block_rows, block_rows), block_rows), :],
            row_send.at[a, k],
            row_recv.at[a, z],
            p.row_target(k),
        )

    def row_arrival(a, k):
        source, place = rows_of[a]
        return remote_copy(
            source.at[k],
            place.at[pl.ds(k * block_rows, block_rows), :],
            row_send.at[a, k],
            row_recv.at[a, k],
            p.row_target(k),
        )

    def row_stay(a, k):
        source, place = rows_of[a]
        return pltpu.make_async_copy(
            source.at[k], place.at[pl.ds(k * block_rows, block_rows), :], row_send.at[a, k]
        )

    def rows_start(a):
        for k in range(depth):
            stays = (z == k) & (x == t)
            pl.when(stays)(lambda k=k: row_stay(a, k).start())
            pl.when(jnp.logical_not(stays))(lambda k=k: row_copy(a, k).start())

    def rows_wait(a):
        for k in range(depth):
            stays = (z == k) & (x == t)
            pl.when(stays)(lambda k=k: row_stay(a, k).wait())

            @pl.when(jnp.logical_not(stays))
            def _(k=k):
                row_copy(a, k).wait_send()
                row_arrival(a, k).wait_recv()

    joined = (act, cot_all, two)

    def block(ref, k):
        return ref.at[pl.ds(k * own_rows, own_rows), :]

    def join(a, step):
        source, place, target = ((0, 1, p.over_core), (0, 2, p.over_y), (2, 3, p.over_core))[step]
        ref = joined[a]
        return remote_copy(
            block(ref, source), block(ref, place), join_send.at[a, step], join_recv.at[a, step], target
        )

    def join_start(a):
        join(a, 0).start()
        join(a, 1).start()

    def join_pass(a):
        join(a, 1).wait_recv()
        join(a, 2).start()

    def join_end(a):
        join(a, 0).wait()
        join(a, 1).wait_send()
        join(a, 2).wait()

    def vec_place(ref):
        return ref.at[:, aligned(f * strip, strip)]

    vec_targets = (p.over_x, p.over_y, diagonal)

    def vec_copy(k):
        return remote_copy(vec_own, vec_place(vec_all), vec_send.at[0, k], vec_recv.at[0, k], vec_targets[k])

    def head_copy(k):
        return remote_copy(head_own, head_got.at[k], vec_send.at[1, k], vec_recv.at[1, k], vec_targets[k])

    loads = [
        pltpu.make_async_copy(source, target, load_sem.at[k])
        for k, (source, target) in enumerate(
            ((vec_hbm, vec_own), (head_hbm, head_own), (arrived_hbm, fresh))
        )
    ]

    def begin():
        for load in loads:
            load.start()
        loads[0].wait()
        loads[1].wait()
        for k in range(3):
            vec_copy(k).start()
            head_copy(k).start()
        vec_place(vec_all)[...] = vec_own[...]
        peaks[...] = jnp.full_like(peaks, NEG)

    def vector_row(k):
        return vec_all[pl.ds(k, 1), :]

    group_rows = 16

    def first_norm():
        for k in range(3):
            vec_copy(k).wait()
            head_copy(k).wait()
        loads[2].wait()
        for k in range(3):
            head_own[...] += head_got[k]
        qkv_bias[...] = jnp.zeros_like(qkv_bias)
        for h in range(heads):
            lanes = pl.ds(h * head_size, head_size)
            qkv_bias[pl.ds(0, 1), lanes] = head_own[pl.ds(heads * y + h, 1), :]
            lanes = pl.ds(2 * features + h * head_size, head_size)
            qkv_bias[pl.ds(0, 1), lanes] = head_own[pl.ds(2 * heads + heads * y + h, 1), :]
        gain, shift = vector_row(GAIN_ONE), vector_row(SHIFT_ONE)
        for s in range(depth):

            @pl.loop(0, block_rows // group_rows)
            def _(k, s=s):
                at = pl.ds(pl.multiple_of(k * group_rows, group_rows), group_rows)
                unit, _ = unit_rows(fresh[s, at, :])
                part[s, at, :] = (unit * gain + shift).astype(bf16)

        rows_start(0)

    def weights_wait(start, stop):
        for i in range(start, stop):
            own_copy(i).wait()
            z_copy(i, True).wait_recv()

    kept, used = [], [0]

    def keep(source, target):
        copy = pltpu.make_async_copy(source, target, out_sem.at[used[0]])
        used[0] += 1
        copy.start()
        kept.append(copy)

    def project(k):
        at = pl.ds(k * own_rows, own_rows)

        @pl.loop(0, 3)
        def _(c):
            cut = aligned(c * features, features)
            qkv[at, cut] = (
                jnp.dot(act[at, :], qkv_mat[:, cut], preferred_element_type=f32)
                + qkv_bias[pl.ds(0, 1), cut]
            ).astype(bf16)

    def head_rows():
        for b in range(4):
            at = pl.ds(pl.multiple_of(p.block_place(b) * own_rows, own_rows), own_rows)
            keys[pl.ds(b * own_rows, own_rows), :] = qkv[at, pl.ds(features, features)]
            values[pl.ds(b * own_rows, own_rows), :] = qkv[at, pl.ds(2 * features, features)]

    def attention_block(b):
        at = pl.ds(pl.multiple_of(p.block_place(b) * own_rows, own_rows), own_rows)
        past = pl.ds(0, (b + 1) * own_rows)

        @pl.loop(0, heads)
        def _(head):
            lanes = aligned(head * head_size, head_size)
            probs, top = attention_probs(qkv[at, lanes], keys[past, lanes], b, length)
            attended[at, lanes] = jnp.dot(
                probs.astype(bf16), values[past, lanes], preferred_element_type=f32
            ).astype(bf16)
            live = b * own_rows + lax.broadcasted_iota(jnp.int32, top.shape, 0) < length
            peak = jnp.max(jnp.where(live, top, NEG), 0, keepdims=True)
            row = pl.ds(head, 1)
            peaks[row, :] = jnp.maximum(peaks[row, :], jnp.broadcast_to(peak, (1, peaks.shape[1])))

    sums = RowSum(p, own_rows, arrived, sent, None, sum_send, sum_recv, None, None, None, 1)

    def out_block(k):
        at = pl.ds(k * own_rows, own_rows)

        @pl.loop(0, 4)
        def _(n):
            cut = aligned(n * strip, strip)
            partial[at, cut] = jnp.dot(
                attended[at, :], out_mat[:, cut], preferred_element_type=f32
            ).astype(bf16)

    def second_norm():
        sums.finish(partial, True)
        kept[-1].wait()
        kept.pop()
        bias, gain, shift = vector_row(OUT_BIAS), vector_row(GAIN_TWO), vector_row(SHIFT_TWO)

        @pl.loop(0, own_rows // group_rows)
        def _(k):
            at = pl.ds(pl.multiple_of(k * group_rows, group_rows), group_rows)
            value = hidden[at, :] + sums.total(partial, True, at) + bias
            hidden[at, :] = value
            unit, _ = unit_rows(value)
            two[at, :] = (unit * gain + shift).astype(bf16)

        join_start(2)
        keep(hidden, hidden_out)

    def call(function, *arguments):
        return lambda: function(*arguments)

    plan = {}

    def at_step(step, *tasks):
        plan.setdefault(step, []).extend(tasks)

    at_step(0, begin)
    at_step(1, first_norm)
    at_step(5, call(rows_wait, 0), call(join_start, 0), call(rows_start, 1))
    at_step(7, call(rows_start, 2))
    at_step(10, call(rows_wait, 1), call(join_start, 1), call(join_pass, 0))
    at_step(16, call(join_pass, 1))
    at_step(11, call(weights_wait, 0, 6), call(project, 0))
    at_step(12, join(0, 0).wait, call(project, 1), lambda: keep(qkv_mat, qkv_mat_out))
    at_step(13, join(0, 1).wait_send, join(0, 2).wait, call(project, 2), lambda: keep(act, act_out))
    at_step(14, call(project, 3), head_rows, lambda: keep(qkv, qkv_out))
    at_step(15, call(attention_block, 0), call(attention_block, 1))
    at_step(16, call(attention_block, 2))
    at_step(17, call(attention_block, 3), lambda: keep(attended, attended_out))
    at_step(18, call(weights_wait, 6, 8), call(out_block, 3), call(out_block, 1))
    at_step(18, call(sums.start, 0, partial, True))
    at_step(19, call(out_block, 2), *(call(sums.middle, partial, True, part) for part in range(PARTS)))
    at_step(19, call(out_block, 0), lambda: keep(out_mat, out_mat_out))
    at_step(19, call(rows_wait, 2), lambda: keep(hidden, resid_out))
    at_step(24, second_norm)
    at_step(27, call(join_pass, 2), call(join_end, 2), lambda: keep(two, two_out))
    lag = 2
    for i in range(count + 2 * lag):
        if i < count:
            y_copy(i).start()
            pl.when(even)(lambda i=i: x_copy(i, True).start())
            own_copy(i).start()
        j = i - lag
        if 0 <= j < count:
            y_copy(j).wait_recv()

            @pl.when(even)
            def _(j=j):
                x_copy(j, True).wait_recv()
                z_copy(j, True).start()

            pl.when(odd)(lambda j=j: x_copy(j, False).start())
        j = i - 2 * lag
        if 0 <= j < count:

            @pl.when(odd)
            def _(j=j):
                x_copy(j, False).wait_recv()
                z_copy(j, False).start()

        for task in plan.get(i, ()):
            task()

    weights_wait(8, count)
    for i in range(count):
        y_copy(i).wait_send()
        x_copy(i, True).wait_send()
        z_copy(i, True).wait_send()
    join_end(1)
    for copy in kept:
        copy.wait()


def forward_all(
    head_size,
    length,
    vectors,
    head_vectors,
    query_weight,
    key_weight,
    value_weight,
    out_weight,
    up_weight,
    down_weight,
    arrived,
    cot,
):
    strip, features, units = query_weight.shape[0], query_weight.shape[1] // 2, up_weight.shape[1] // 2
    width = 4 * strip
    depth, block_rows = arrived.shape[:2]
    own_rows = depth * block_rows
    tokens = 4 * own_rows
    bf16, f32 = jnp.bfloat16, jnp.float32
    hbm = pl.BlockSpec(memory_space=pl.ANY)
    vmem = pl.BlockSpec(memory_space=pltpu.VMEM)
    count = 24
    dma = pltpu.SemaphoreType.DMA

    def made(shape, dtype=bf16):
        return jax.ShapeDtypeStruct(shape, dtype)

    def hold(shape, dtype=bf16):
        return pltpu.VMEM(shape, dtype)

    return pl.pallas_call(
        functools.partial(forward_kernel, head_size),
        out_shape=(
            made((width, 3 * features)),
            made((features, width)),
            made((width, units)),
            made((units, width)),
            made((tokens, width)),
            made((tokens, width)),
            made((tokens, 3 * features)),
            made((tokens, features)),
            made((own_rows, width), f32),
            made((own_rows, width), f32),
            made((tokens, width)),
            made((8, width), f32),
            made((8, 128), f32),
        ),
        in_specs=[pl.BlockSpec(memory_space=pltpu.SMEM)] + [hbm] * 10,
        out_specs=(hbm,) * 11 + (vmem,) * 2,
        scratch_shapes=[
            hold((width, 3 * features)),
            hold((features, width)),
            hold((depth, block_rows, width), f32),
            hold((depth, block_rows, width)),
            hold((tokens, width)),
            hold((own_rows, width), f32),
            hold((tokens, 3 * features)),
            hold((tokens, features)),
            hold((tokens, features)),
            hold((tokens, features)),
            hold((tokens, width)),
            hold((3, own_rows, width)),
            hold((own_rows, width)),
            hold((tokens, width)),
            hold((8, strip), f32),
            hold(head_vectors.shape, f32),
            hold((3,) + head_vectors.shape, f32),
            hold((8, 3 * features), f32),
            dma((count,)),
            dma((3, count)),
            dma((3, count)),
            dma((3, depth)),
            dma((3, depth)),
            dma((3, 3)),
            dma((3, 3)),
            dma((2, 3)),
            dma((2, 3)),
            dma((3,)),
            dma((2 + PARTS,)),
            dma((2 + PARTS,)),
            dma((8,)),
        ],
        compiler_params=pltpu.CompilerParams(
            collective_id=0, has_side_effects=True, vmem_limit_bytes=56 << 20
        ),
        cost_estimate=pl.CostEstimate(flops=0, bytes_accessed=64 << 20, transcendentals=0),
    )(
        length,
        vectors,
        head_vectors,
        query_weight,
        key_weight,
        value_weight,
        out_weight,
        up_weight,
        down_weight,
        arrived,
        cot,
    )


def backward_kernel(
    head_size,
    info,
    vector_ref,
    small_in,
    gelu_hbm,
    pre_hbm,
    act_two_hbm,
    two_part,
    mlp_part,
    hidden_hbm,
    cot_hbm,
    resid_hbm,
    out_hbm,
    qkv_mat_hbm,
    qkv_hbm,
    attended_hbm,
    act_hbm,
    down_sum,
    up_sum,
    out_sum,
    qkv_sums,
    rows_out,
    rows_grad,
    small,
    engine,
    base,
    hidden_grad,
    low,
    out_mat,
    attended_grad,
    qkv,
    qkv_grad,
    act,
    attended,
    qkv_mat,
    keys,
    values,
    key_sum,
    value_sum,
    strips,
    packed,
    arrived,
    sent,
    loaded,
    small_arrived,
    load_sem,
    sum_send,
    sum_recv,
    sum_load,
    join_send,
    join_recv,
    strip_sem,
    row_send,
    row_recv,
    share_send,
    share_recv,
    small_send,
    small_recv,
    core_free,
    y_free,
):
    f32, bf16 = jnp.float32, jnp.bfloat16
    own_rows, width = base.shape
    tokens, features = attended.shape
    heads = features // head_size
    depth = rows_out.shape[0] // 2
    block_rows = rows_out.shape[1]
    p = Place(depth)
    x, y, z, t = p.x, p.y, p.z, p.t
    entry_barrier(
        [p.over_x, p.over_y, p.over_core, p.mate, p.middle, p.hop] + p.row_targets()
    )
    length = info[0]
    scale = 1.0 / math.sqrt(head_size)
    column = 2 * t + y

    rows, cols = engine[0].shape[1:]
    down_rows = down_sum.shape[0] // 2
    up_cols = up_sum.shape[1] // 2
    strip = out_sum.shape[1]

    def over_tokens(left, right, target):
        target[...] = lax.dot_general(
            left, right, (((0,), (0,)), ((), ())), preferred_element_type=f32
        ).astype(target.dtype)

    per_down, per_up = down_rows // strip, up_cols // cols
    strip_count = per_down + per_up

    def strip_load(n):
        source = gelu_hbm if n < per_down else pre_hbm
        cut = pl.ds((n % per_down) * strip, strip)
        return pltpu.make_async_copy(source.at[:, cut], strips.at[n % 2], strip_sem.at[n % 2])

    def resident_load(k):
        source = (cot_hbm, act_two_hbm, act_hbm)[k]
        return pltpu.make_async_copy(source, act, load_sem.at[5])

    def strip_ready(n):
        strip_load(n).wait()
        if n + 1 < strip_count:
            strip_load(n + 1).start()

    def homes_of(far):
        return (p.homes[1], p.homes[3]) if far else (p.homes[0], p.homes[2])

    def down_item(r, far):
        def make(send, own):
            if far and r % 2 == 0:
                if r == 0:
                    resident_load(0).wait()
                strip_ready(r // 2)
            left = strips.at[(r // 2) % 2, :, pl.ds((r % 2) * rows, rows)]
            for home, target in zip(homes_of(far), (send, own)):
                over_tokens(left[...], act[:, aligned(home * strip, strip)], target)

        side = 1 - y if far else y
        return far, down_sum.at[aligned(side * down_rows + r * rows, rows), :], make

    def up_item(c, r, far):
        def make(send, own):
            if far and r == 0:
                if c == 0:
                    resident_load(1).start()
                    resident_load(1).wait()
                strip_ready(per_down + c)
            for home, target in zip(homes_of(far), (send, own)):
                over_tokens(
                    act[:, aligned(home * strip + r * rows, rows)], strips[c % 2], target
                )

        side = 1 - y if far else y
        place = up_sum.at[pl.ds(r * rows, rows), aligned(side * up_cols + c * cols, cols)]
        return far, place, make

    def out_item(r, far):
        def make(send, own):
            for home, target in zip(homes_of(far), (send, own)):
                over_tokens(
                    attended[:, pl.ds(r * rows, rows)], low[:, aligned(home * strip, strip)], target
                )

        side = 1 - y if far else y
        return far, out_sum.at[aligned(side * features + r * rows, rows), :], make

    def qkv_item(r, c, far):
        def make(send, own):
            if far and r == 0 and c == 0:
                resident_load(2).start()
                resident_load(2).wait()
            for home, target in zip(homes_of(far), (send, own)):
                over_tokens(
                    act[:, aligned(home * strip + r * rows, rows)],
                    qkv_grad[:, pl.ds(c * cols, cols)],
                    target,
                )

        side = 1 - y if far else y
        return far, qkv_sums[c].at[pl.ds(r * rows, rows), aligned(side * cols, cols)], make

    sides = (True, False)
    items = [down_item(r, far) for r in range(down_rows // rows) for far in sides]
    items += [up_item(c, r, far) for c in range(per_up) for r in range(strip // rows) for far in sides]
    items += [out_item(r, far) for r in range(features // rows) for far in sides]
    items += [qkv_item(r, c, far) for r in range(strip // rows) for c in range(3) for far in sides]
    run, steps = reduce_stages(p, items, engine)

    loads = [
        pltpu.make_async_copy(source, target, load_sem.at[k])
        for k, (source, target) in enumerate(
            (
                (hidden_hbm, base),
                (cot_hbm.at[pl.ds(0, own_rows), :], packed),
                (out_hbm, out_mat),
                (qkv_hbm, qkv),
                (attended_hbm, attended),
                (cot_hbm, act),
                (qkv_mat_hbm, qkv_mat),
                (resid_hbm, base),
            )
        )
    ]
    sums = RowSum(
        p, own_rows, arrived, sent, loaded, sum_send, sum_recv, sum_load, core_free, y_free, 3
    )
    group_rows = 16
    quarter = own_rows // 4 // group_rows

    def start():
        loads[5].start()
        strip_load(0).start()
        sums.start(0, two_part, False)
        for k in (0, 1, 2, 3, 4, 6):
            loads[k].start()
        small[...] = small_in[...]
        key_sum[...] = jnp.zeros_like(key_sum)
        value_sum[...] = jnp.zeros_like(value_sum)

    def two_middle(part):
        sums.middle(two_part, False, part)

    def two_finish():
        sums.finish(two_part, False)
        loads[0].wait()
        loads[1].wait()

    def accumulate(row, value):
        small[pl.ds(row, 1), :] += jnp.sum(value, 0, keepdims=True)

    def two_rows(part):
        gain = vector_ref[pl.ds(GAIN_TWO, 1), :]

        @pl.loop(part * quarter, (part + 1) * quarter)
        def _(k):
            at = pl.ds(pl.multiple_of(k * group_rows, group_rows), group_rows)
            upstream = sums.total(two_part, False, at)
            unit, inverse = unit_rows(base[at, :])
            grad = packed[at, :].astype(f32) + unit_back(upstream, unit, inverse, gain)
            hidden_grad[at, :] = grad
            low[at, :] = grad.astype(bf16)
            accumulate(GAIN_TWO, upstream * unit)
            accumulate(SHIFT_TWO, upstream)
            accumulate(OUT_BIAS, grad)

    def low_block(k):
        return low.at[pl.ds(k * own_rows, own_rows), :]

    def join(k):
        source, place = ((0, 1), (None, None), (2, 3))[k]
        return remote_copy(
            low_block(source), low_block(place), join_send.at[k], join_recv.at[k], p.over_core
        )

    def join_y(part):
        size = own_rows // PARTS
        return remote_copy(
            low.at[pl.ds(part * size, size), :],
            low.at[pl.ds(2 * own_rows + part * size, size), :],
            join_send.at[3 + part],
            join_recv.at[3 + part],
            p.over_y,
        )

    def join_start():
        join(0).start()
        join_y(0).start()
        sums.release(0)

    def join_pass():
        for part in range(PARTS):
            join_y(part).wait_recv()
        join(2).start()

    def attend_block(k):
        at = pl.ds(k * own_rows, own_rows)
        attended_grad[at, :] = lax.dot_general(
            low[at, :], out_mat[...], (((1,), (1,)), ((), ())), preferred_element_type=f32
        ).astype(bf16)

    def attend_own():
        loads[2].wait()
        attend_block(0)

    def attend_peer():
        join(0).wait()
        attend_block(1)

    def attend_far():
        attend_block(2)

    def attend_last():
        for part in range(PARTS):
            join_y(part).wait_send()
        join(2).wait()
        attend_block(3)

    def mlp_start():
        sums.start(1, mlp_part, False)

    def mlp_middle(part):
        sums.middle(mlp_part, False, part)

    def mlp_finish():
        sums.finish(mlp_part, False)
        bias = vector_ref[pl.ds(DOWN_BIAS, 1), :]

        @pl.loop(0, own_rows // group_rows)
        def _(k):
            at = pl.ds(pl.multiple_of(k * group_rows, group_rows), group_rows)
            packed[at, :] = (base[at, :] + sums.total(mlp_part, False, at) + bias).astype(bf16)

        sums.release(1)

    def row_source(k):
        return packed.at[pl.ds(k * block_rows, block_rows), :]

    row_ends = (rows_out, rows_grad)

    def row_copy(a, k):
        end = row_ends[a].at[x * depth + z]
        return remote_copy(row_source(k), end, row_send.at[a, k], row_recv.at[a, z], p.row_target(k))

    def row_arrival(a, k):
        end = row_ends[a].at[t * depth + k]
        return remote_copy(row_source(k), end, row_send.at[a, k], row_recv.at[a, k], p.row_target(k))

    def row_stay(a, k):
        return pltpu.make_async_copy(row_source(k), row_ends[a].at[x * depth + z], row_send.at[a, k])

    def rows_start(a):
        for k in range(depth):
            stays = (z == k) & (x == t)
            pl.when(stays)(lambda k=k: row_stay(a, k).start())
            pl.when(jnp.logical_not(stays))(lambda k=k: row_copy(a, k).start())

    def share(a):
        group = row_ends[a].at[pl.ds(t * depth, depth)]
        return remote_copy(group, group, share_send.at[a], share_recv.at[a], p.over_core)

    def rows_share(a):
        for k in range(depth):
            stays = (z == k) & (x == t)
            pl.when(stays)(lambda k=k: row_stay(a, k).wait())

            @pl.when(jnp.logical_not(stays))
            def _(k=k):
                row_copy(a, k).wait_send()
                row_arrival(a, k).wait_recv()

        share(a).start()

    def head_rows():
        loads[3].wait()
        loads[4].wait()
        for block in range(4):
            at = pl.ds(pl.multiple_of(p.block_place(block) * own_rows, own_rows), own_rows)
            keys[pl.ds(block * own_rows, own_rows), :] = qkv[at, pl.ds(features, features)]
            values[pl.ds(block * own_rows, own_rows), :] = qkv[at, pl.ds(2 * features, features)]

    def attention_block(block):
        at = pl.ds(pl.multiple_of(p.block_place(block) * own_rows, own_rows), own_rows)
        part = pl.ds(0, (block + 1) * own_rows)

        @pl.loop(0, heads)
        def _(head):
            lanes = aligned(head * head_size, head_size)
            queries, grads = qkv[at, lanes], attended_grad[at, lanes]
            probs, _ = attention_probs(queries, keys[part, lanes], block, length)
            prob_grad = lax.dot_general(
                grads, values[part, lanes], (((1,), (1,)), ((), ())), preferred_element_type=f32
            )
            inner = jnp.sum(probs * prob_grad, -1, keepdims=True)
            score_grad = (probs * (prob_grad - inner)).astype(bf16)
            query_grad = (
                jnp.dot(score_grad, keys[part, lanes], preferred_element_type=f32) * scale
            )
            spot = aligned(column * features + head * head_size, head_size)
            small[pl.ds(QUERY_BIAS, 1), spot] += jnp.sum(query_grad, 0, keepdims=True)
            qkv_grad[at, lanes] = query_grad.astype(bf16)
            key_sum[part, lanes] += lax.dot_general(
                score_grad, queries, (((0,), (0,)), ((), ())), preferred_element_type=f32
            )
            value_sum[part, lanes] += lax.dot_general(
                probs.astype(bf16), grads, (((0,), (0,)), ((), ())), preferred_element_type=f32
            )

    def attention_end(block):
        at = pl.ds(pl.multiple_of(p.block_place(block) * own_rows, own_rows), own_rows)
        part = pl.ds(block * own_rows, own_rows)
        qkv_grad[at, pl.ds(features, features)] = (key_sum[part, :] * scale).astype(bf16)
        value_grad = value_sum[part, :]
        qkv_grad[at, pl.ds(2 * features, features)] = value_grad.astype(bf16)
        spot = aligned(column * features, features)
        small[pl.ds(VALUE_BIAS, 1), spot] += jnp.sum(value_grad, 0, keepdims=True)

    def one_block(k):
        if k == 3:
            loads[6].wait()
        at = pl.ds(k * own_rows, own_rows)

        @pl.loop(0, 4)
        def _(n):
            cut = aligned(n * strip, strip)
            low[at, cut] = lax.dot_general(
                qkv_grad[at, :], qkv_mat[cut, :], (((1,), (1,)), ((), ())), preferred_element_type=f32
            ).astype(bf16)

    def one_start():
        sums.start(2, low, True)

    def one_middle(part):
        sums.middle(low, True, part)

    def one_finish():
        sums.finish(low, True)
        loads[7].wait()

    def one_rows(part):
        gain = vector_ref[pl.ds(GAIN_ONE, 1), :]

        @pl.loop(part * quarter, (part + 1) * quarter)
        def _(k):
            at = pl.ds(pl.multiple_of(k * group_rows, group_rows), group_rows)
            upstream = sums.total(low, True, at)
            unit, inverse = unit_rows(base[at, :])
            grad = hidden_grad[at, :] + unit_back(upstream, unit, inverse, gain)
            packed[at, :] = grad.astype(bf16)
            accumulate(GAIN_ONE, upstream * unit)
            accumulate(SHIFT_ONE, upstream)

    def small_copy(k):
        target = (p.over_core, p.over_x, p.over_y, p.mate, p.hop)[k]
        return remote_copy(small, small_arrived.at[k], small_send.at[k], small_recv.at[k], target)

    def small_add(k):
        small_copy(k).wait()
        mine, other = small[...], small_arrived[k]
        row = lax.broadcasted_iota(jnp.int32, mine.shape, 0)
        small[...] = jnp.where(row == PEAKS, jnp.maximum(mine, other), mine + other)

    def call(function, *arguments):
        return lambda: function(*arguments)

    plan = {}

    def at_step(step, *tasks):
        plan.setdefault(step, []).extend(tasks)

    at_step(2, call(two_middle, 0))
    at_step(3, call(two_middle, 1))
    at_step(4, call(two_middle, 2))
    at_step(5, call(two_middle, 3))
    at_step(9, two_finish, call(two_rows, 0))
    for k in range(1, 4):
        at_step(9 + k // 2, call(two_rows, k))
    at_step(10, join_start)
    for k in range(1, 4):
        at_step(10 + k, join_y(k).start)
    at_step(11, attend_own)
    at_step(12, attend_peer)
    at_step(14, head_rows)
    at_step(17, join_pass)
    at_step(18, attend_far)
    at_step(19, attend_last)
    at_step(20, call(attention_block, 0), call(attention_block, 1))
    at_step(21, call(attention_block, 2))
    at_step(22, call(attention_block, 3))
    at_step(23, *(call(attention_end, k) for k in range(4)))
    at_step(14, mlp_start)
    for k in range(4):
        at_step(16 + k, call(mlp_middle, k))
    at_step(25, mlp_finish, loads[7].start, lambda: rows_start(0))
    at_step(33, lambda: rows_share(0))
    at_step(36, call(one_block, 3), call(one_block, 1), one_start)
    at_step(37, call(one_block, 2), call(one_block, 0))
    for k in range(4):
        at_step(38 + k, call(one_middle, k))
    at_step(45, one_finish, share(0).wait, call(one_rows, 0))
    for k in range(1, 4):
        at_step(45 + k // 2, call(one_rows, k))
    at_step(46, lambda: rows_start(1))
    at_step(47, small_copy(0).start)
    for k in range(4):
        at_step(49 + 2 * k, call(small_add, k), small_copy(k + 1).start)
    at_step(57, call(small_add, 4))
    at_step(55, lambda: rows_share(1))
    at_step(58, share(1).wait)
    start()
    for step in range(steps):
        run(step)
        for task in plan.get(step, ()):
            task()


def backward_all(
    head_size,
    length,
    vectors,
    small,
    gelu_low,
    pre_low,
    act_two,
    two_part,
    mlp_part,
    hidden,
    cot_low,
    resid,
    out_mat,
    qkv_mat,
    qkv,
    attended,
    act_one,
    slots,
):
    bf16, f32 = jnp.bfloat16, jnp.float32
    hbm = pl.BlockSpec(memory_space=pl.ANY)
    vmem = pl.BlockSpec(memory_space=pltpu.VMEM)
    down_rows, up_cols = gelu_low.shape[1], pre_low.shape[1]
    tokens, features = attended.shape
    own_rows, width = hidden.shape
    strip = width // 4
    depth = slots // 2
    engine = reduce_scratch(6, 4, 256, 512)
    n_engine = len(engine)

    def kernel(*refs):
        ins, rest = refs[:16], refs[16:]
        outs, scratch = rest[:9], rest[9:]
        backward_kernel(
            head_size,
            *ins,
            outs[0],
            outs[1],
            outs[2],
            outs[3:6],
            *outs[6:],
            scratch[:n_engine],
            *scratch[n_engine:],
        )

    dma, regular = pltpu.SemaphoreType.DMA, pltpu.SemaphoreType.REGULAR

    def hold(shape, dtype=bf16):
        return pltpu.VMEM(shape, dtype)

    return pl.pallas_call(
        kernel,
        out_shape=(
            jax.ShapeDtypeStruct((2 * down_rows, strip), bf16),
            jax.ShapeDtypeStruct((strip, 2 * up_cols), bf16),
            jax.ShapeDtypeStruct((2 * features, strip), bf16),
            jax.ShapeDtypeStruct((strip, 2 * features), bf16),
            jax.ShapeDtypeStruct((strip, 2 * features), bf16),
            jax.ShapeDtypeStruct((strip, 2 * features), bf16),
            jax.ShapeDtypeStruct((slots, own_rows // depth, width), bf16),
            jax.ShapeDtypeStruct((slots, own_rows // depth, width), bf16),
            jax.ShapeDtypeStruct(small.shape, f32),
        ),
        in_specs=[pl.BlockSpec(memory_space=pltpu.SMEM), vmem, vmem] + [hbm] * 13,
        out_specs=(hbm,) * 8 + (vmem,),
        scratch_shapes=engine
        + [
            hold((own_rows, width), f32),
            hold((own_rows, width), f32),
            hold((tokens, width)),
            hold((features, width)),
            hold((tokens, features)),
            hold((tokens, 3 * features)),
            hold((tokens, 3 * features)),
            hold((tokens, width)),
            hold((tokens, features)),
            hold((width, 3 * features)),
            hold((tokens, features)),
            hold((tokens, features)),
            hold((tokens, features), f32),
            hold((tokens, features), f32),
            hold((2, tokens, strip)),
            hold((own_rows, width)),
            hold((3, own_rows, width)),
            hold((own_rows, width)),
            hold((own_rows, width)),
            hold((5,) + small.shape, f32),
            dma((8,)),
            dma((2 + PARTS,)),
            dma((2 + PARTS,)),
            dma(()),
            dma((3 + PARTS,)),
            dma((3 + PARTS,)),
            dma((2,)),
            dma((2, depth)),
            dma((2, depth)),
            dma((2,)),
            dma((2,)),
            dma((5,)),
            dma((5,)),
            regular,
            regular,
        ],
        compiler_params=pltpu.CompilerParams(
            collective_id=1, has_side_effects=True, vmem_limit_bytes=60 << 20
        ),
        cost_estimate=pl.CostEstimate(flops=0, bytes_accessed=64 << 20, transcendentals=0),
    )(
        length,
        vectors,
        small,
        gelu_low,
        pre_low,
        act_two,
        two_part,
        mlp_part,
        hidden,
        cot_low,
        resid,
        out_mat,
        qkv_mat,
        qkv,
        attended,
        act_one,
    )


def split_body(
    layer_input,
    cotangent,
    seq_lengths,
    dealing,
    attn_gain,
    attn_shift,
    query_weight,
    query_bias,
    key_weight,
    value_weight,
    value_bias,
    out_weight,
    out_bias,
    mlp_gain,
    mlp_shift,
    up_weight,
    up_bias,
    down_weight,
    down_bias,
    clip_level,
):
    f32, bf16 = jnp.float32, jnp.bfloat16
    f = lax.axis_index("fsdp")
    z = lax.axis_index("ctx")
    t = lax.axis_index("tp")
    y, x = f // 2, f % 2
    depth = lax.axis_size("ctx")
    slots, block_rows, width = layer_input.shape
    local_heads = query_bias.shape[0] // 2
    head_size = 4 * query_bias.shape[1]
    features = local_heads * head_size
    hidden_units = up_weight.shape[1] // 2
    strip = query_weight.shape[0]
    own_rows = depth * block_rows

    slot = x * depth + z
    length = seq_lengths[dealing[slot]]
    arrived = pick_slots(layer_input, dealing, t * depth, depth)
    cot_part = lax.dynamic_slice_in_dim(cotangent, t * depth, depth, 0)
    down_bias_part = jnp.sum(cot_part, (0, 1))
    vectors = jnp.concatenate(
        [jnp.stack([attn_gain, attn_shift, out_bias, mlp_gain, mlp_shift, down_bias]), up_bias], 0
    ).astype(f32)
    head_vectors = jnp.concatenate([query_bias, value_bias], 0).astype(f32)
    head_vectors = lax.dynamic_update_slice(
        jnp.zeros((head_vectors.shape[0], head_size), f32), head_vectors, (0, f * query_bias.shape[1])
    )
    (
        qkv_mat,
        out_mat,
        up_mat,
        down_mat,
        act_one,
        cot_low,
        qkv,
        attended,
        hidden,
        resid,
        act_two,
        vectors_whole,
        peaks,
    ) = forward_all(
        head_size,
        length[None],
        vectors,
        head_vectors,
        query_weight,
        key_weight,
        value_weight,
        out_weight,
        up_weight,
        down_weight,
        arrived,
        cot_part.astype(bf16),
    )
    peaks = peaks[:local_heads, 0]
    up_vec = lax.dynamic_slice_in_dim(vectors_whole, 6 + y, 1, 0)

    pre = matmul(act_two, up_mat) + up_vec
    cdf = 0.5 * (1.0 + lax.erf(pre * INV_ROOT_TWO))
    gelu_low = (pre * cdf).astype(bf16)
    slope = cdf + pre * (jnp.exp(-0.5 * pre * pre) * INV_ROOT_TWO_PI)
    pre_grad = back_product(cot_low, down_mat) * slope
    pre_low = pre_grad.astype(bf16)
    up_bias_part = jnp.sum(pre_grad, 0)
    two_part = back_product(pre_low, up_mat).astype(bf16)
    mlp_part = matmul(gelu_low, down_mat).astype(bf16)
    column = 2 * t + y
    small = jnp.zeros((16, width), f32).at[DOWN_BIAS].set(down_bias_part)
    small = lax.dynamic_update_slice(small, up_bias_part[None], (UP_BIAS + column, 0))
    small = small.at[PEAKS].set(NEG)
    small = lax.dynamic_update_slice(small, peaks[None], (PEAKS, local_heads * (2 * t + y)))
    (
        down_sum,
        up_sum,
        out_sum,
        query_sum,
        key_sum,
        value_sum,
        rows_out,
        rows_grad,
        totals,
    ) = backward_all(
        head_size,
        length[None],
        vectors_whole,
        small,
        gelu_low,
        pre_low,
        act_two,
        two_part,
        mlp_part,
        hidden,
        cot_low,
        resid,
        out_mat,
        qkv_mat,
        qkv,
        attended,
        act_one,
        slots,
    )
    rows_sum = lax.dynamic_slice(totals, (0, f * strip), (6, strip))
    head_sum = lax.dynamic_slice(totals, (QUERY_BIAS, 2 * t * features), (2, 2 * features))
    head_sum = head_sum.reshape(2, 2 * local_heads, head_size)
    head_sum = lax.dynamic_slice_in_dim(head_sum, f * query_bias.shape[1], query_bias.shape[1], 2)
    unit_sum = lax.dynamic_slice(
        totals, (UP_BIAS + up_bias.shape[0] * t, f * strip), (up_bias.shape[0], strip)
    )
    peak_all = lax.dynamic_slice(totals, (PEAKS, 2 * local_heads * t), (1, 2 * local_heads))[0]
    level = clip_level[0]
    factor = jnp.repeat(jnp.sqrt(level / jnp.maximum(peak_all, level)), head_size)
    query_clipped = (query_weight.astype(f32) * factor[None, :]).astype(bf16)
    key_clipped = (key_weight.astype(f32) * factor[None, :]).astype(bf16)
    return (
        rows_out.astype(f32),
        rows_grad.astype(f32),
        rows_sum[GAIN_ONE],
        rows_sum[SHIFT_ONE],
        query_sum.astype(f32),
        head_sum[0],
        key_sum.astype(f32),
        value_sum.astype(f32),
        head_sum[1],
        out_sum.astype(f32),
        rows_sum[OUT_BIAS],
        rows_sum[GAIN_TWO],
        rows_sum[SHIFT_TWO],
        up_sum.astype(f32),
        unit_sum,
        down_sum.astype(f32),
        rows_sum[DOWN_BIAS],
        peak_all,
        query_clipped,
        key_clipped,
    )


def solution(mesh):
    sizes = dict(mesh.shape)
    small_slice = sizes == {"fsdp": 4, "ctx": 4, "tp": 2}
    return jax.shard_map(
        split_body if small_slice else gathered_body,
        mesh=mesh,
        in_specs=(
            P(None, ("fsdp", "ctx"), None),
            P(None, ("fsdp", "ctx"), None),
            P(),
            P(),
            P("fsdp"),
            P("fsdp"),
            P("fsdp", "tp"),
            P("tp", "fsdp"),
            P("fsdp", "tp"),
            P("fsdp", "tp"),
            P("tp", "fsdp"),
            P("tp", "fsdp"),
            P("fsdp"),
            P("fsdp"),
            P("fsdp"),
            P("fsdp", "tp"),
            P("tp", "fsdp"),
            P("tp", "fsdp"),
            P("fsdp"),
            P(),
        ),
        out_specs=(
            P(None, ("fsdp", "ctx"), None),
            P(None, ("fsdp", "ctx"), None),
            P("fsdp"),
            P("fsdp"),
            P("fsdp", "tp"),
            P("tp", "fsdp"),
            P("fsdp", "tp"),
            P("fsdp", "tp"),
            P("tp", "fsdp"),
            P("tp", "fsdp"),
            P("fsdp"),
            P("fsdp"),
            P("fsdp"),
            P("fsdp", "tp"),
            P("tp", "fsdp"),
            P("tp", "fsdp"),
            P("fsdp"),
            P("tp"),
            P("fsdp", "tp"),
            P("fsdp", "tp"),
        ),
        check_vma=False,
    )
```

```python
import functools
import math

import jax
import jax.numpy as jnp
from jax import lax
from jax.experimental import pallas as pl
from jax.experimental.pallas import tpu as pltpu
from jax.sharding import PartitionSpec as P

EPS = 1e-05
NEG = -1e30
INV_ROOT_TWO = 0.7071067811865476
INV_ROOT_TWO_PI = 0.3989422804014327


def normalize(values, scale_vec, offset_vec):
    center = values - jnp.mean(values, -1, keepdims=True)
    inverse = lax.rsqrt(jnp.mean(center * center, -1, keepdims=True) + EPS)
    normed = center * inverse
    return (normed * scale_vec + offset_vec, normed, inverse)


def norm_back(upstream, normed, inverse, scale_vec):
    scaled = upstream * scale_vec
    inner = (
        scaled
        - jnp.mean(scaled, -1, keepdims=True)
        - normed * jnp.mean(scaled * normed, -1, keepdims=True)
    )
    return (inverse * inner, jnp.sum(upstream * normed, 0), jnp.sum(upstream, 0))


def pick_slots(rows, dealing, first, count):
    return jnp.concatenate(
        [lax.dynamic_slice_in_dim(rows, dealing[first + j], 1, 0) for j in range(count)], 0
    )


def matmul(left, right):
    return jnp.dot(left, right, preferred_element_type=jnp.float32)


def weight_product(left, right):
    return jnp.einsum("td,te->de", left, right, preferred_element_type=jnp.float32)


def back_product(left, right):
    return jnp.einsum("te,de->td", left, right, preferred_element_type=jnp.float32)


def gathered_body(
    layer_input,
    cotangent,
    seq_lengths,
    dealing,
    attn_gain,
    attn_shift,
    query_weight,
    query_bias,
    key_weight,
    value_weight,
    value_bias,
    out_weight,
    out_bias,
    mlp_gain,
    mlp_shift,
    up_weight,
    up_bias,
    down_weight,
    down_bias,
    clip_level,
):
    shard_count = lax.axis_size("fsdp")
    ctx_count = lax.axis_size("ctx")
    my_group = lax.axis_index("fsdp")
    ctx_place = lax.axis_index("ctx")
    slot_count, block_rows, width = layer_input.shape
    per_group = slot_count // shard_count
    local_rows = shard_count * block_rows
    tokens = per_group * local_rows
    dealt_input = pick_slots(layer_input, dealing, 0, slot_count).reshape(
        shard_count, per_group, block_rows, width
    )
    dealt_grad = cotangent.reshape(shard_count, per_group, block_rows, width)
    arrived_input, arrived_grad = (
        lax.all_to_all(dealt_input, "fsdp", split_axis=0, concat_axis=2, tiled=True),
        lax.all_to_all(dealt_grad, "fsdp", split_axis=0, concat_axis=2, tiled=True),
    )
    resid = arrived_input.reshape(tokens, width)
    upstream = arrived_grad.reshape(tokens, width)
    seq_lens = lax.dynamic_slice_in_dim(
        jnp.take(seq_lengths, dealing), my_group * per_group, per_group
    )
    gathered = (
        lax.all_gather(attn_gain, "fsdp", axis=0, tiled=True),
        lax.all_gather(attn_shift, "fsdp", axis=0, tiled=True),
        lax.all_gather(query_weight, "fsdp", axis=0, tiled=True),
        lax.all_gather(query_bias, "fsdp", axis=1, tiled=True),
        lax.all_gather(key_weight, "fsdp", axis=0, tiled=True),
        lax.all_gather(value_weight, "fsdp", axis=0, tiled=True),
        lax.all_gather(value_bias, "fsdp", axis=1, tiled=True),
        lax.all_gather(out_weight, "fsdp", axis=1, tiled=True),
        lax.all_gather(out_bias, "fsdp", axis=0, tiled=True),
        lax.all_gather(mlp_gain, "fsdp", axis=0, tiled=True),
        lax.all_gather(mlp_shift, "fsdp", axis=0, tiled=True),
        lax.all_gather(up_weight, "fsdp", axis=0, tiled=True),
        lax.all_gather(up_bias, "fsdp", axis=1, tiled=True),
        lax.all_gather(down_weight, "fsdp", axis=1, tiled=True),
        lax.all_gather(down_bias, "fsdp", axis=0, tiled=True),
    )
    (
        gain_one,
        shift_one,
        query_mat,
        query_vec,
        key_mat,
        value_mat,
        value_vec,
        out_mat,
        out_vec,
        gain_two,
        shift_two,
        up_mat,
        up_vec,
        down_mat,
        down_vec,
    ) = gathered
    head_count, head_size = query_vec.shape
    features = head_count * head_size
    scale_of_scores = 1.0 / math.sqrt(head_size)
    row_ids = jnp.arange(local_rows, dtype=jnp.int32)
    query_pos = (row_ids // block_rows * ctx_count + ctx_place) * block_rows + row_ids % block_rows
    key_ids = jnp.arange(ctx_count * local_rows, dtype=jnp.int32)
    key_rows = key_ids % local_rows
    key_pos = (
        key_rows // block_rows * ctx_count + key_ids // local_rows
    ) * block_rows + key_rows % block_rows
    allowed = (key_pos[None, None, :] <= query_pos[None, :, None]) & (
        key_pos[None, None, :] < seq_lens[:, None, None]
    )
    query_live = query_pos[None, :] < seq_lens[:, None]
    normed_a, unit_one, inverse_one = normalize(
        resid, gain_one.astype(jnp.float32), shift_one.astype(jnp.float32)
    )
    act_one = normed_a.astype(jnp.bfloat16)
    queries = (
        (matmul(act_one, query_mat) + query_vec.reshape(features).astype(jnp.float32))
        .astype(jnp.bfloat16)
        .reshape(per_group, local_rows, features)
    )
    keys_mine = (
        matmul(act_one, key_mat).astype(jnp.bfloat16).reshape(per_group, local_rows, features)
    )
    values_mine = (
        (matmul(act_one, value_mat) + value_vec.reshape(features).astype(jnp.float32))
        .astype(jnp.bfloat16)
        .reshape(per_group, local_rows, features)
    )
    keys_all, values_all = (
        lax.all_gather(keys_mine, "ctx", axis=1, tiled=True),
        lax.all_gather(values_mine, "ctx", axis=1, tiled=True),
    )

    def head_cut(array, head_index):
        return lax.dynamic_slice_in_dim(array, head_index * head_size, head_size, 2)

    def head_scores(head_queries, head_keys):
        return (
            jnp.einsum("sqd,skd->sqk", head_queries, head_keys, preferred_element_type=jnp.float32)
            * scale_of_scores
        )

    def forward_head(head_index):
        logit_scores = head_scores(head_cut(queries, head_index), head_cut(keys_all, head_index))
        masked = jnp.where(allowed, logit_scores, NEG)
        row_top = jnp.max(masked, -1, keepdims=True)
        exp_terms = jnp.where(allowed, jnp.exp(masked - row_top), 0.0)
        total = jnp.sum(exp_terms, -1, keepdims=True)
        attention_probabilities = exp_terms / total
        attended_rows = jnp.einsum(
            "sqk,skd->sqd",
            attention_probabilities.astype(jnp.bfloat16),
            head_cut(values_all, head_index),
            preferred_element_type=jnp.float32,
        )
        log_total = row_top[..., 0] + jnp.log(total[..., 0])
        peak = jnp.max(jnp.where(query_live, row_top[..., 0], NEG))
        return (attended_rows, log_total, peak)

    attended_rows, log_totals, peaks = lax.map(forward_head, jnp.arange(head_count))
    attn_low = attended_rows.transpose(1, 2, 0, 3).reshape(tokens, features).astype(jnp.bfloat16)
    attn_sum = lax.psum(matmul(attn_low, out_mat), "tp")
    hidden = resid + attn_sum + out_vec.astype(jnp.float32)
    normed_b, unit_two, inverse_two = normalize(
        hidden, gain_two.astype(jnp.float32), shift_two.astype(jnp.float32)
    )
    act_two = normed_b.astype(jnp.bfloat16)
    pre = matmul(act_two, up_mat) + up_vec.reshape(-1).astype(jnp.float32)
    gelu_low = jax.nn.gelu(pre, approximate=False).astype(jnp.bfloat16)
    mlp_sum = lax.psum(matmul(gelu_low, down_mat).astype(jnp.bfloat16), "tp").astype(jnp.float32)
    layer_output = hidden + mlp_sum + down_vec.astype(jnp.float32)
    peak_all = lax.pmax(peaks, ("fsdp", "ctx"))
    level = clip_level[0]
    factor = jnp.repeat(jnp.sqrt(level / jnp.maximum(peak_all, level)), head_size)
    query_clipped = (query_weight.astype(jnp.float32) * factor[None, :]).astype(jnp.bfloat16)
    key_clipped = (key_weight.astype(jnp.float32) * factor[None, :]).astype(jnp.bfloat16)
    grad_low = upstream.astype(jnp.bfloat16)
    down_weight_grad = weight_product(gelu_low, grad_low)
    down_bias_grad = jnp.sum(upstream, 0)
    cdf = 0.5 * (1.0 + lax.erf(pre * INV_ROOT_TWO))
    density = jnp.exp(-0.5 * pre * pre) * INV_ROOT_TWO_PI
    pre_grad = back_product(grad_low, down_mat) * (cdf + pre * density)
    pre_low = pre_grad.astype(jnp.bfloat16)
    up_weight_grad = weight_product(act_two, pre_low)
    up_bias_grad = jnp.sum(pre_grad, 0).reshape(up_vec.shape)
    normed_two_grad = lax.psum(back_product(pre_low, up_mat), "tp")
    hidden_in, mlp_gain_grad, mlp_shift_grad = norm_back(
        normed_two_grad, unit_two, inverse_two, gain_two.astype(jnp.float32)
    )
    hidden_grad = upstream + hidden_in
    hidden_low = hidden_grad.astype(jnp.bfloat16)
    out_weight_grad = weight_product(attn_low, hidden_low)
    out_bias_grad = jnp.sum(hidden_grad, 0)
    attended_grad = (
        back_product(hidden_low, out_mat)
        .astype(jnp.bfloat16)
        .reshape(per_group, local_rows, features)
    )

    def backward_head(head_index):
        head_queries = head_cut(queries, head_index)
        head_keys = head_cut(keys_all, head_index)
        head_values = head_cut(values_all, head_index)
        grad_head = head_cut(attended_grad, head_index)
        logit_scores = head_scores(head_queries, head_keys)
        masked = jnp.where(allowed, logit_scores, NEG)
        attention_probabilities = jnp.where(
            allowed, jnp.exp(masked - log_totals[head_index][..., None]), 0.0
        )
        prob_grad = jnp.einsum(
            "sqd,skd->sqk", grad_head, head_values, preferred_element_type=jnp.float32
        )
        inner = jnp.sum(attention_probabilities * prob_grad, -1, keepdims=True)
        score_grad = (attention_probabilities * (prob_grad - inner)).astype(jnp.bfloat16)
        query_grad = (
            jnp.einsum("sqk,skd->sqd", score_grad, head_keys, preferred_element_type=jnp.float32)
            * scale_of_scores
        )
        key_grad = (
            jnp.einsum("sqk,sqd->skd", score_grad, head_queries, preferred_element_type=jnp.float32)
            * scale_of_scores
        )
        value_grad = jnp.einsum(
            "sqk,sqd->skd",
            attention_probabilities.astype(jnp.bfloat16),
            grad_head,
            preferred_element_type=jnp.float32,
        )
        return (query_grad, key_grad, value_grad)

    query_parts, key_parts, value_parts = lax.map(backward_head, jnp.arange(head_count))
    query_grads = query_parts.transpose(1, 2, 0, 3).reshape(tokens, features)
    key_whole = key_parts.transpose(1, 2, 0, 3).reshape(per_group, ctx_count * local_rows, features)
    value_whole = value_parts.transpose(1, 2, 0, 3).reshape(
        per_group, ctx_count * local_rows, features
    )
    key_summed, value_summed = (
        lax.psum_scatter(key_whole, "ctx", scatter_dimension=1, tiled=True),
        lax.psum_scatter(value_whole, "ctx", scatter_dimension=1, tiled=True),
    )
    key_grads = key_summed.reshape(tokens, features)
    value_grads = value_summed.reshape(tokens, features)
    query_bias_grad = jnp.sum(query_grads, 0).reshape(head_count, head_size)
    value_bias_grad = jnp.sum(value_grads, 0).reshape(head_count, head_size)
    query_low = query_grads.astype(jnp.bfloat16)
    key_low = key_grads.astype(jnp.bfloat16)
    value_low = value_grads.astype(jnp.bfloat16)
    query_weight_grad = weight_product(act_one, query_low)
    key_weight_grad = weight_product(act_one, key_low)
    value_weight_grad = weight_product(act_one, value_low)
    normed_one_grad = lax.psum(
        (
            back_product(query_low, query_mat)
            + back_product(key_low, key_mat)
            + back_product(value_low, value_mat)
        ).astype(jnp.bfloat16),
        "tp",
    ).astype(jnp.float32)
    input_in, attn_gain_grad, attn_shift_grad = norm_back(
        normed_one_grad, unit_one, inverse_one, gain_one.astype(jnp.float32)
    )
    input_grad = hidden_grad + input_in
    partial_sums = (
        lax.psum_scatter(
            attn_gain_grad.astype(jnp.bfloat16), "fsdp", scatter_dimension=0, tiled=True
        ).astype(jnp.float32),
        lax.psum_scatter(
            attn_shift_grad.astype(jnp.bfloat16), "fsdp", scatter_dimension=0, tiled=True
        ).astype(jnp.float32),
        lax.psum_scatter(
            query_weight_grad.astype(jnp.bfloat16), "fsdp", scatter_dimension=0, tiled=True
        ).astype(jnp.float32),
        lax.psum_scatter(
            query_bias_grad.astype(jnp.bfloat16), "fsdp", scatter_dimension=1, tiled=True
        ).astype(jnp.float32),
        lax.psum_scatter(
            key_weight_grad.astype(jnp.bfloat16), "fsdp", scatter_dimension=0, tiled=True
        ).astype(jnp.float32),
        lax.psum_scatter(
            value_weight_grad.astype(jnp.bfloat16), "fsdp", scatter_dimension=0, tiled=True
        ).astype(jnp.float32),
        lax.psum_scatter(
            value_bias_grad.astype(jnp.bfloat16), "fsdp", scatter_dimension=1, tiled=True
        ).astype(jnp.float32),
        lax.psum_scatter(
            out_weight_grad.astype(jnp.bfloat16), "fsdp", scatter_dimension=1, tiled=True
        ).astype(jnp.float32),
        lax.psum_scatter(
            out_bias_grad.astype(jnp.bfloat16), "fsdp", scatter_dimension=0, tiled=True
        ).astype(jnp.float32),
        lax.psum_scatter(
            mlp_gain_grad.astype(jnp.bfloat16), "fsdp", scatter_dimension=0, tiled=True
        ).astype(jnp.float32),
        lax.psum_scatter(
            mlp_shift_grad.astype(jnp.bfloat16), "fsdp", scatter_dimension=0, tiled=True
        ).astype(jnp.float32),
        lax.psum_scatter(
            up_weight_grad.astype(jnp.bfloat16), "fsdp", scatter_dimension=0, tiled=True
        ).astype(jnp.float32),
        lax.psum_scatter(
            up_bias_grad.astype(jnp.bfloat16), "fsdp", scatter_dimension=1, tiled=True
        ).astype(jnp.float32),
        lax.psum_scatter(
            down_weight_grad.astype(jnp.bfloat16), "fsdp", scatter_dimension=1, tiled=True
        ).astype(jnp.float32),
        lax.psum_scatter(
            down_bias_grad.astype(jnp.bfloat16), "fsdp", scatter_dimension=0, tiled=True
        ).astype(jnp.float32),
    )
    shards = (
        lax.psum(partial_sums[0].astype(jnp.bfloat16), "ctx").astype(jnp.float32),
        lax.psum(partial_sums[1].astype(jnp.bfloat16), "ctx").astype(jnp.float32),
        lax.psum(partial_sums[2].astype(jnp.bfloat16), "ctx").astype(jnp.float32),
        lax.psum(partial_sums[3].astype(jnp.bfloat16), "ctx").astype(jnp.float32),
        lax.psum(partial_sums[4].astype(jnp.bfloat16), "ctx").astype(jnp.float32),
        lax.psum(partial_sums[5].astype(jnp.bfloat16), "ctx").astype(jnp.float32),
        lax.psum(partial_sums[6].astype(jnp.bfloat16), "ctx").astype(jnp.float32),
        lax.psum(partial_sums[7].astype(jnp.bfloat16), "ctx").astype(jnp.float32),
        lax.psum(partial_sums[8].astype(jnp.bfloat16), "ctx").astype(jnp.float32),
        lax.psum(partial_sums[9].astype(jnp.bfloat16), "ctx").astype(jnp.float32),
        lax.psum(partial_sums[10].astype(jnp.bfloat16), "ctx").astype(jnp.float32),
        lax.psum(partial_sums[11].astype(jnp.bfloat16), "ctx").astype(jnp.float32),
        lax.psum(partial_sums[12].astype(jnp.bfloat16), "ctx").astype(jnp.float32),
        lax.psum(partial_sums[13].astype(jnp.bfloat16), "ctx").astype(jnp.float32),
        lax.psum(partial_sums[14].astype(jnp.bfloat16), "ctx").astype(jnp.float32),
    )
    sent_output = layer_output.reshape(1, per_group, local_rows, width)
    sent_grad = input_grad.reshape(1, per_group, local_rows, width)
    back_output, back_grad = (
        lax.all_to_all(
            sent_output.astype(jnp.bfloat16), "fsdp", split_axis=2, concat_axis=0, tiled=True
        ).astype(sent_output.dtype),
        lax.all_to_all(
            sent_grad.astype(jnp.bfloat16), "fsdp", split_axis=2, concat_axis=0, tiled=True
        ).astype(sent_grad.dtype),
    )
    final_output = back_output.reshape(slot_count, block_rows, width)
    final_grad = back_grad.reshape(slot_count, block_rows, width)
    return (
        final_output,
        final_grad,
        shards[0],
        shards[1],
        shards[2],
        shards[3],
        shards[4],
        shards[5],
        shards[6],
        shards[7],
        shards[8],
        shards[9],
        shards[10],
        shards[11],
        shards[12],
        shards[13],
        shards[14],
        peak_all,
        query_clipped,
        key_clipped,
    )


def attention_probs(query_block, key_rows, block, length):
    rows, cols = query_block.shape[0], key_rows.shape[0]
    scores = lax.dot_general(
        query_block, key_rows, (((1,), (1,)), ((), ())), preferred_element_type=jnp.float32
    ) * (1.0 / math.sqrt(query_block.shape[1]))
    row_pos = block * rows + lax.broadcasted_iota(jnp.int32, (rows, cols), 0)
    col_pos = lax.broadcasted_iota(jnp.int32, (rows, cols), 1)
    scores = jnp.where((col_pos <= row_pos) & (col_pos < length), scores, NEG)
    top = jnp.max(scores, -1, keepdims=True)
    terms = jnp.exp(scores - top)
    return terms / jnp.sum(terms, -1, keepdims=True), top


def entry_barrier(targets):
    barrier = pltpu.get_barrier_semaphore()
    for target in targets:
        pl.semaphore_signal(barrier, inc=1, device_id=target, device_id_type=pl.DeviceIdType.MESH)
    pl.semaphore_wait(barrier, len(targets))


def remote_copy(src, dst, send, recv, target):
    return pltpu.make_async_remote_copy(
        src_ref=src,
        dst_ref=dst,
        send_sem=send,
        recv_sem=recv,
        device_id=target,
        device_id_type=pl.DeviceIdType.MESH,
    )


def grant(semaphore, target):
    pl.semaphore_signal(semaphore, inc=1, device_id=target, device_id_type=pl.DeviceIdType.MESH)


def aligned(start, size):
    return pl.ds(pl.multiple_of(start, 128), size)


class Place:
    def __init__(self, depth):
        self.depth = depth
        f = lax.axis_index("fsdp")
        z = lax.axis_index("ctx")
        t = lax.axis_index("tp")
        y, x = f // 2, f % 2
        self.f, self.z, self.t, self.y, self.x = f, z, t, y, x
        self.over_x = {"fsdp": 2 * y + 1 - x, "ctx": z, "tp": t}
        self.over_y = {"fsdp": 2 * (1 - y) + x, "ctx": z, "tp": t}
        self.over_core = {"fsdp": f, "ctx": z, "tp": 1 - t}
        self.mate = {"fsdp": f, "ctx": z + 1 - 2 * (z % 2), "tp": t}
        self.middle = {"fsdp": f, "ctx": 3 - z, "tp": t}
        self.hop = {"fsdp": f, "ctx": lax.rem(z + 2, 4), "tp": t}
        self.homes = (2 * y + 1 - x, 2 * (1 - y) + 1 - x, f, 2 * (1 - y) + x)

    def row_target(self, k):
        return {"fsdp": 2 * self.y + self.t, "ctx": k, "tp": self.x}

    def row_targets(self):
        others = [self.row_target(lax.rem(self.z + k, self.depth)) for k in range(1, self.depth)]
        return others + [{"fsdp": 2 * self.y + 1 - self.x, "ctx": self.z, "tp": 1 - self.t}]

    def block_place(self, block):
        return 2 * jnp.where(self.y == block // 2, 0, 1) + jnp.where(self.t == block % 2, 0, 1)


def reduce_stages(p, items, scratch):
    (
        x_slot,
        made_slot,
        own_slot,
        pair_slot,
        y_slot,
        z_slot,
        z_pair,
        inner_slot,
        total_slot,
        x_send,
        x_recv,
        y_send,
        y_recv,
        outer_send,
        outer_recv,
        inner_send,
        inner_recv,
        out_sem,
        x_free,
        y_free,
        outer_free,
        inner_free,
    ) = scratch
    y, z = p.y, p.z
    outer = (z == 0) | (z == 3)
    inner = (z == 1) | (z == 2)
    slots = x_slot.shape[0]
    count = len(items)
    far_count = count // 2
    far_slots = y_slot.shape[0]

    def x_copy(i):
        k = i % slots
        return remote_copy(made_slot.at[k], x_slot.at[k], x_send.at[k], x_recv.at[k], p.over_x)

    def y_copy(i):
        k, g = i % slots, (i // 2) % far_slots
        return remote_copy(pair_slot.at[k], y_slot.at[g], y_send.at[g], y_recv.at[g], p.over_y)

    def summed(i):
        return y_slot.at[(i // 2) % far_slots] if items[i][0] else pair_slot.at[i % slots]

    def outward(i):
        k = i % slots
        return remote_copy(summed(i), z_slot.at[k], outer_send.at[k], outer_recv.at[k], p.mate)

    def across(i):
        k = i % slots
        return remote_copy(z_pair.at[k], inner_slot.at[k], inner_send.at[k], inner_recv.at[k], p.middle)

    def backward(i):
        k = i % slots
        return remote_copy(total_slot.at[k], z_slot.at[k], outer_send.at[k], outer_recv.at[k], p.mate)

    def result_inner(i):
        k = i % slots
        return pltpu.make_async_copy(total_slot.at[k], items[i][1], out_sem.at[k])

    def result_outer(i):
        k = i % slots
        return pltpu.make_async_copy(z_slot.at[k], items[i][1], out_sem.at[k])

    def add(left, right, target):
        target[...] = (left[...].astype(jnp.float32) + right[...].astype(jnp.float32)).astype(
            target.dtype
        )

    def stage_send(i):
        k = i % slots
        items[i][2](made_slot.at[k], own_slot.at[k])
        if i >= slots:
            pl.semaphore_wait(x_free, 1)
        x_copy(i).start()

    def stage_pair(i):
        x_copy(i).wait()
        k = i % slots
        add(x_slot.at[k], own_slot.at[k], pair_slot.at[k])
        if i + slots < count:
            grant(x_free, p.over_x)
        if items[i][0]:
            if i // 2 >= far_slots:
                pl.semaphore_wait(y_free, 1)
            y_copy(i).start()

    def stage_outward(i):
        if items[i][0]:
            y_copy(i).wait()

        @pl.when(outer)
        def _():
            if i >= slots:
                pl.semaphore_wait(outer_free, 1)
            outward(i).start()

    def stage_across(i):
        k = i % slots

        @pl.when(outer)
        def _():
            outward(i).wait_send()

        @pl.when(inner)
        def _():
            outward(i).wait_recv()
            add(summed(i), z_slot.at[k], z_pair.at[k])
            if i + slots < count:
                grant(outer_free, p.mate)
            if i >= slots:
                pl.semaphore_wait(inner_free, 1)
            across(i).start()

        if items[i][0] and i // 2 + far_slots < far_count:
            grant(y_free, p.over_y)

    def stage_total(i):
        k = i % slots

        @pl.when(inner)
        def _():
            across(i).wait()
            add(z_pair.at[k], inner_slot.at[k], total_slot.at[k])
            if i + slots < count:
                grant(inner_free, p.middle)
            if i >= slots:
                pl.semaphore_wait(outer_free, 1)
            backward(i).start()
            result_inner(i).start()

    def stage_result(i):
        @pl.when(inner)
        def _():
            backward(i).wait_send()
            result_inner(i).wait()

        @pl.when(outer)
        def _():
            backward(i).wait_recv()
            result_outer(i).start()

    def stage_finish(i):
        @pl.when(outer)
        def _():
            result_outer(i).wait()
            if i + slots < count:
                grant(outer_free, p.mate)

    stages = (
        (11, stage_finish),
        (10, stage_result),
        (8, stage_total),
        (6, stage_across),
        (4, stage_outward),
        (2, stage_pair),
        (0, stage_send),
    )

    def run(step):
        for lag, stage in stages:
            if 0 <= step - lag < count:
                stage(step - lag)

    return run, count + 12


def reduce_scratch(slots, far_slots, rows, cols):
    dma, regular = pltpu.SemaphoreType.DMA, pltpu.SemaphoreType.REGULAR
    counts = (slots,) * 4 + (far_slots,) + (slots,) * 4
    return [pltpu.VMEM((n, rows, cols), jnp.bfloat16) for n in counts] + [
        dma((n,)) for n in (slots,) * 2 + (far_slots,) * 2 + (slots,) * 5
    ] + [regular] * 4


PARTS = 4


class RowSum:
    def __init__(self, p, rows, arrived, sent, loaded, send_sem, recv_sem, load_sem, core_free, y_free, uses):
        self.p, self.rows, self.uses = p, rows, uses
        self.arrived, self.sent, self.loaded = arrived, sent, loaded
        self.send_sem, self.recv_sem, self.load_sem = send_sem, recv_sem, load_sem
        self.core_free, self.y_free = core_free, y_free

    def block(self, ref, k):
        return ref.at[pl.ds(k * self.rows, self.rows), :]

    def hop(self, ref, k):
        return remote_copy(
            self.block(ref, 3 - 2 * k),
            self.arrived.at[k],
            self.send_sem.at[k],
            self.recv_sem.at[k],
            self.p.over_core,
        )

    def hop_y(self, part):
        size = self.rows // PARTS
        cut = pl.ds(part * size, size)
        return remote_copy(
            self.sent.at[cut, :],
            self.arrived.at[2, cut, :],
            self.send_sem.at[2 + part],
            self.recv_sem.at[2 + part],
            self.p.over_y,
        )

    def load(self, ref, k):
        return pltpu.make_async_copy(self.block(ref, k), self.loaded, self.load_sem)

    def start(self, use, ref, local):
        if use:
            pl.semaphore_wait(self.core_free, 1)
            pl.semaphore_wait(self.y_free, 1)
        self.hop(ref, 0).start()
        self.hop(ref, 1).start()
        if not local:
            self.load(ref, 2).start()

    def middle(self, ref, local, part):
        if part == 0:
            self.hop(ref, 0).wait()
            if not local:
                self.load(ref, 2).wait()
        base = self.block(ref, 2) if local else self.loaded
        size = self.rows // PARTS

        @pl.loop(part * size // 32, (part + 1) * size // 32)
        def _(k):
            at = pl.ds(pl.multiple_of(k * 32, 32), 32)
            self.sent[at, :] = (
                base[at, :].astype(jnp.float32) + self.arrived[0, at, :].astype(jnp.float32)
            ).astype(jnp.bfloat16)

        self.hop_y(part).start()
        if part == PARTS - 1 and not local:
            self.load(ref, 0).start()

    def finish(self, ref, local):
        self.hop(ref, 1).wait()
        for part in range(PARTS):
            self.hop_y(part).wait()
        if not local:
            self.load(ref, 0).wait()

    def total(self, ref, local, at):
        base = self.block(ref, 0) if local else self.loaded
        return (
            base[at, :].astype(jnp.float32)
            + self.arrived[1, at, :].astype(jnp.float32)
            + self.arrived[2, at, :].astype(jnp.float32)
        )

    def release(self, use):
        if use + 1 < self.uses:
            grant(self.core_free, self.p.over_core)
            grant(self.y_free, self.p.over_y)


def unit_rows(values):
    center = values - jnp.mean(values, -1, keepdims=True)
    inverse = lax.rsqrt(jnp.mean(center * center, -1, keepdims=True) + EPS)
    return center * inverse, inverse


def unit_back(upstream, unit, inverse, gain):
    scaled = upstream * gain
    return inverse * (
        scaled
        - jnp.mean(scaled, -1, keepdims=True)
        - unit * jnp.mean(scaled * unit, -1, keepdims=True)
    )


GAIN_ONE, SHIFT_ONE, OUT_BIAS, GAIN_TWO, SHIFT_TWO, DOWN_BIAS, QUERY_BIAS, VALUE_BIAS, UP_BIAS, PEAKS = (
    0,
    1,
    2,
    3,
    4,
    5,
    6,
    7,
    8,
    12,
)


def prepare_kernel(dealing, lengths, place, rows_ref, cot_ref, rows_out, cot_out, bias_ref):
    step = pl.program_id(0)
    rows_out[...] = rows_ref[...]
    cot = cot_ref[...]
    cot_out[...] = cot.astype(cot_out.dtype)

    @pl.when(step == 0)
    def _():
        bias_ref[...] = jnp.zeros_like(bias_ref)

    bias_ref[pl.ds(0, 1), :] += jnp.sum(cot[0], 0, keepdims=True)


def prepare(dealing, seq_lengths, place, layer_input, cotangent, count):
    block = (1,) + layer_input.shape[1:]
    width = layer_input.shape[2]
    return pl.pallas_call(
        prepare_kernel,
        out_shape=(
            jax.ShapeDtypeStruct((count,) + block[1:], jnp.float32),
            jax.ShapeDtypeStruct((count,) + block[1:], jnp.bfloat16),
            jax.ShapeDtypeStruct((8, width), jnp.float32),
        ),
        grid_spec=pltpu.PrefetchScalarGridSpec(
            num_scalar_prefetch=3,
            grid=(count,),
            in_specs=[
                pl.BlockSpec(block, lambda j, dealing, lengths, place: (dealing[place[0] * count + j], 0, 0)),
                pl.BlockSpec(block, lambda j, dealing, lengths, place: (place[0] * count + j, 0, 0)),
            ],
            out_specs=(
                pl.BlockSpec(block, lambda j, *_: (j, 0, 0)),
                pl.BlockSpec(block, lambda j, *_: (j, 0, 0)),
                pl.BlockSpec((8, width), lambda j, *_: (0, 0)),
            ),
        ),
    )(dealing, seq_lengths, place, layer_input, cotangent)


def finish_kernel(head_size, place, level_ref, totals_ref, query_ref, key_ref, *refs):
    count = (len(refs) - 3) // 2
    for source, target in zip(refs[:count], refs[count : 2 * count]):
        target[...] = source[...].astype(target.dtype)
    query_out, key_out, factor = refs[2 * count :]
    level = level_ref[0]
    heads = factor.shape[1] // head_size

    @pl.when(pl.program_id(0) == 0)
    def _():
        peaks = totals_ref[pl.ds(PEAKS, 1), :]
        lane = lax.broadcasted_iota(jnp.int32, peaks.shape, 1)
        for h in range(heads):
            mine = jnp.where(lane == place[0] * heads + h, peaks, NEG)
            peak = jnp.max(mine, -1, keepdims=True)
            value = jnp.sqrt(level / jnp.maximum(peak, level))
            factor[:, pl.ds(h * head_size, head_size)] = jnp.broadcast_to(value, (8, head_size))

    scale = factor[pl.ds(0, 1), :]
    query_out[...] = (query_ref[...].astype(jnp.float32) * scale).astype(query_out.dtype)
    key_out[...] = (key_ref[...].astype(jnp.float32) * scale).astype(key_out.dtype)


def finish_all(head_size, place, level, totals, query_weight, key_weight, arrays):
    steps = 8

    def spec(v):
        block = (v.shape[0] // steps,) + v.shape[1:]
        return pl.BlockSpec(block, lambda i: (i,) + (0,) * (v.ndim - 1))

    smem = pl.BlockSpec(memory_space=pltpu.SMEM)
    weights = (query_weight, key_weight)
    return pl.pallas_call(
        functools.partial(finish_kernel, head_size),
        out_shape=tuple(jax.ShapeDtypeStruct(v.shape, jnp.float32) for v in arrays)
        + tuple(jax.ShapeDtypeStruct(v.shape, v.dtype) for v in weights),
        grid=(steps,),
        in_specs=[smem, smem, pl.BlockSpec(totals.shape, lambda i: (0, 0))]
        + [spec(v) for v in weights]
        + [spec(v) for v in arrays],
        out_specs=tuple(spec(v) for v in arrays) + tuple(spec(v) for v in weights),
        scratch_shapes=[pltpu.VMEM((8, query_weight.shape[1]), jnp.float32)],
        compiler_params=pltpu.CompilerParams(vmem_limit_bytes=48 << 20),
    )(place, level, totals, *weights, *arrays)


def forward_kernel(
    head_size,
    info,
    vec_hbm,
    head_hbm,
    q_ref,
    k_ref,
    v_ref,
    o_ref,
    u_ref,
    d_ref,
    arrived_hbm,
    cot_hbm,
    qkv_mat_out,
    out_mat_out,
    up_all,
    down_out,
    act_out,
    cot_out,
    qkv_out,
    attended_out,
    hidden_out,
    resid_out,
    two_out,
    back_out,
    vec_all,
    peaks,
    cot_all,
    down_all,
    back_stage,
    qkv_mat,
    out_mat,
    fresh,
    part,
    act,
    hidden,
    qkv,
    keys,
    values,
    attended,
    partial,
    arrived,
    sent,
    two,
    vec_own,
    head_own,
    head_got,
    qkv_bias,
    local_sem,
    send_sem,
    recv_sem,
    row_send,
    row_recv,
    join_send,
    join_recv,
    vec_send,
    vec_recv,
    load_sem,
    sum_send,
    sum_recv,
    out_sem,
):
    f32, bf16 = jnp.float32, jnp.bfloat16
    depth, block_rows, width = arrived_hbm.shape
    own_rows = depth * block_rows
    strip = q_ref.shape[0]
    features = q_ref.shape[1] // 2
    units = u_ref.shape[1] // 2
    heads = features // head_size
    p = Place(depth)
    f, x, y, z, t = p.f, p.x, p.y, p.z, p.t
    even = z % 2 == 0
    odd = jnp.logical_not(even)
    diagonal = {"fsdp": 3 - f, "ctx": z, "tp": t}
    entry_barrier([p.over_x, p.over_y, p.mate, p.over_core, diagonal] + p.row_targets())
    length = info[0]

    chunks = []
    rows = strip // 2
    for k, ref in enumerate((q_ref, k_ref, v_ref)):
        for r in range(2):
            chunks.append(
                (
                    lambda w, ref=ref, r=r: ref.at[pl.ds(r * rows, rows), aligned(w * features, features)],
                    lambda home, k=k, r=r: qkv_mat.at[
                        aligned(home * strip + r * rows, rows), pl.ds(k * features, features)
                    ],
                )
            )
    for r in range(2):
        chunks.append(
            (
                lambda w, r=r: o_ref.at[aligned(w * features + r * rows, rows), :],
                lambda home, r=r: out_mat.at[pl.ds(r * rows, rows), aligned(home * strip, strip)],
            )
        )
    pieces = 8
    for r in range(pieces):
        size = strip // pieces
        chunks.append(
            (
                lambda w, r=r, size=size: u_ref.at[pl.ds(r * size, size), aligned(w * units, units)],
                lambda home, r=r, size=size: up_all.at[
                    pl.ds(pl.multiple_of(home * strip + r * size, size), size), :
                ],
            )
        )
    for r in range(pieces):
        size = units // pieces
        chunks.append(
            (
                lambda w, r=r, size=size: d_ref.at[aligned(w * units + r * size, size), :],
                lambda home, r=r, size=size: down_all.at[pl.ds(r * size, size), aligned(home * strip, strip)],
            )
        )
    count = len(chunks)
    far_home = 2 * (1 - y) + x

    def own_copy(i):
        source, place = chunks[i]
        return pltpu.make_async_copy(source(y), place(f), local_sem.at[i])

    def y_copy(i):
        source, place = chunks[i]
        return remote_copy(source(1 - y), place(f), send_sem.at[0, i], recv_sem.at[0, i], p.over_y)

    def x_copy(i, is_even):
        source, place = chunks[i]
        start = source(y) if is_even else place(far_home)
        home = f if is_even else far_home
        return remote_copy(start, place(home), send_sem.at[1, i], recv_sem.at[1, i], p.over_x)

    def z_copy(i, is_even):
        place = chunks[i][1]
        home = 2 * y + 1 - x if is_even else 2 * (1 - y) + 1 - x
        return remote_copy(place(home), place(home), send_sem.at[2, i], recv_sem.at[2, i], p.mate)

    rows_of = ((part, act), (cot_hbm, cot_all), (arrived_hbm, hidden))

    def row_copy(a, k):
        source, place = rows_of[a]
        return remote_copy(
            source.at[k],
            place.at[pl.ds(pl.multiple_of(z * block_rows, block_rows), block_rows), :],
            row_send.at[a, k],
            row_recv.at[a, z],
            p.row_target(k),
        )

    def row_arrival(a, k):
        source, place = rows_of[a]
        return remote_copy(
            source.at[k],
            place.at[pl.ds(k * block_rows, block_rows), :],
            row_send.at[a, k],
            row_recv.at[a, k],
            p.row_target(k),
        )

    def row_stay(a, k):
        source, place = rows_of[a]
        return pltpu.make_async_copy(
            source.at[k], place.at[pl.ds(k * block_rows, block_rows), :], row_send.at[a, k]
        )

    def rows_start(a):
        for k in range(depth):
            stays = (z == k) & (x == t)
            pl.when(stays)(lambda k=k: row_stay(a, k).start())
            pl.when(jnp.logical_not(stays))(lambda k=k: row_copy(a, k).start())

    def rows_wait(a):
        for k in range(depth):
            stays = (z == k) & (x == t)
            pl.when(stays)(lambda k=k: row_stay(a, k).wait())

            @pl.when(jnp.logical_not(stays))
            def _(k=k):
                row_copy(a, k).wait_send()
                row_arrival(a, k).wait_recv()

    joined = (act, cot_all, two)

    def block(ref, k):
        return ref.at[pl.ds(k * own_rows, own_rows), :]

    def join(a, step):
        source, place, target = ((0, 1, p.over_core), (0, 2, p.over_y), (2, 3, p.over_core))[step]
        ref = joined[a]
        return remote_copy(
            block(ref, source), block(ref, place), join_send.at[a, step], join_recv.at[a, step], target
        )

    def join_start(a):
        join(a, 0).start()
        join(a, 1).start()

    def join_pass(a):
        join(a, 1).wait_recv()
        join(a, 2).start()

    def join_end(a):
        join(a, 0).wait()
        join(a, 1).wait_send()
        join(a, 2).wait()

    def vec_place(ref):
        return ref.at[:, aligned(f * strip, strip)]

    vec_targets = (p.over_x, p.over_y, diagonal)

    def vec_copy(k):
        return remote_copy(vec_own, vec_place(vec_all), vec_send.at[0, k], vec_recv.at[0, k], vec_targets[k])

    def head_copy(k):
        return remote_copy(head_own, head_got.at[k], vec_send.at[1, k], vec_recv.at[1, k], vec_targets[k])

    loads = [
        pltpu.make_async_copy(source, target, load_sem.at[k])
        for k, (source, target) in enumerate(
            ((vec_hbm, vec_own), (head_hbm, head_own), (arrived_hbm, fresh))
        )
    ]

    def begin():
        for load in loads:
            load.start()
        loads[0].wait()
        loads[1].wait()
        for k in range(3):
            vec_copy(k).start()
            head_copy(k).start()
        vec_place(vec_all)[...] = vec_own[...]
        peaks[...] = jnp.full_like(peaks, NEG)

    def vector_row(k):
        return vec_all[pl.ds(k, 1), :]

    group_rows = 16

    def first_norm():
        for k in range(3):
            vec_copy(k).wait()
            head_copy(k).wait()
        loads[2].wait()
        for k in range(3):
            head_own[...] += head_got[k]
        qkv_bias[...] = jnp.zeros_like(qkv_bias)
        for h in range(heads):
            lanes = pl.ds(h * head_size, head_size)
            qkv_bias[pl.ds(0, 1), lanes] = head_own[pl.ds(heads * y + h, 1), :]
            lanes = pl.ds(2 * features + h * head_size, head_size)
            qkv_bias[pl.ds(0, 1), lanes] = head_own[pl.ds(2 * heads + heads * y + h, 1), :]
        gain, shift = vector_row(GAIN_ONE), vector_row(SHIFT_ONE)
        for s in range(depth):

            @pl.loop(0, block_rows // group_rows)
            def _(k, s=s):
                at = pl.ds(pl.multiple_of(k * group_rows, group_rows), group_rows)
                unit, _ = unit_rows(fresh[s, at, :])
                part[s, at, :] = (unit * gain + shift).astype(bf16)

        rows_start(0)

    def weights_wait(start, stop):
        for i in range(start, stop):
            own_copy(i).wait()
            z_copy(i, True).wait_recv()

    kept, used = [], [0]

    def keep(source, target):
        copy = pltpu.make_async_copy(source, target, out_sem.at[used[0]])
        used[0] += 1
        copy.start()
        kept.append(copy)

    def project(k):
        at = pl.ds(k * own_rows, own_rows)

        @pl.loop(0, 3)
        def _(c):
            cut = aligned(c * features, features)
            qkv[at, cut] = (
                jnp.dot(act[at, :], qkv_mat[:, cut], preferred_element_type=f32)
                + qkv_bias[pl.ds(0, 1), cut]
            ).astype(bf16)

    def head_rows():
        for b in range(4):
            at = pl.ds(pl.multiple_of(p.block_place(b) * own_rows, own_rows), own_rows)
            keys[pl.ds(b * own_rows, own_rows), :] = qkv[at, pl.ds(features, features)]
            values[pl.ds(b * own_rows, own_rows), :] = qkv[at, pl.ds(2 * features, features)]

    def attention_block(b):
        at = pl.ds(pl.multiple_of(p.block_place(b) * own_rows, own_rows), own_rows)
        past = pl.ds(0, (b + 1) * own_rows)

        @pl.loop(0, heads)
        def _(head):
            lanes = aligned(head * head_size, head_size)
            probs, top = attention_probs(qkv[at, lanes], keys[past, lanes], b, length)
            attended[at, lanes] = jnp.dot(
                probs.astype(bf16), values[past, lanes], preferred_element_type=f32
            ).astype(bf16)
            live = b * own_rows + lax.broadcasted_iota(jnp.int32, top.shape, 0) < length
            peak = jnp.max(jnp.where(live, top, NEG), 0, keepdims=True)
            row = pl.ds(head, 1)
            peaks[row, :] = jnp.maximum(peaks[row, :], jnp.broadcast_to(peak, (1, peaks.shape[1])))

    sums = RowSum(p, own_rows, arrived, sent, None, sum_send, sum_recv, None, None, None, 1)

    def out_block(k):
        at = pl.ds(k * own_rows, own_rows)

        @pl.loop(0, 4)
        def _(n):
            cut = aligned(n * strip, strip)
            partial[at, cut] = jnp.dot(
                attended[at, :], out_mat[:, cut], preferred_element_type=f32
            ).astype(bf16)

    spot = []

    def keep_resid():
        spot.append(len(kept))
        keep(hidden, resid_out)

    back_sem = [out_sem.at[10], out_sem.at[11]]
    unit_rows_per_chunk = units // pieces

    def back_store(r):
        cut = pl.ds(r * unit_rows_per_chunk, unit_rows_per_chunk)
        return pltpu.make_async_copy(back_stage.at[r % 2], back_out.at[:, cut], back_sem[r % 2])

    def back_chunk(r):
        weights_wait(8 + pieces + r, 9 + pieces + r)
        if r >= 2:
            back_store(r - 2).wait()

        @pl.loop(0, 4)
        def _(b):
            at = pl.ds(pl.multiple_of(b * own_rows, own_rows), own_rows)
            back_stage[r % 2, at, :] = lax.dot_general(
                cot_all[at, :],
                down_all[pl.ds(r * unit_rows_per_chunk, unit_rows_per_chunk), :],
                (((1,), (1,)), ((), ())),
                preferred_element_type=f32,
            ).astype(bf16)

        back_store(r).start()

    def second_norm():
        sums.finish(partial, True)
        kept.pop(spot[0]).wait()
        bias, gain, shift = vector_row(OUT_BIAS), vector_row(GAIN_TWO), vector_row(SHIFT_TWO)

        @pl.loop(0, own_rows // group_rows)
        def _(k):
            at = pl.ds(pl.multiple_of(k * group_rows, group_rows), group_rows)
            value = hidden[at, :] + sums.total(partial, True, at) + bias
            hidden[at, :] = value
            unit, _ = unit_rows(value)
            two[at, :] = (unit * gain + shift).astype(bf16)

        join_start(2)
        keep(hidden, hidden_out)

    def call(function, *arguments):
        return lambda: function(*arguments)

    plan = {}

    def at_step(step, *tasks):
        plan.setdefault(step, []).extend(tasks)

    at_step(0, begin)
    at_step(1, first_norm)
    at_step(5, call(rows_wait, 0), call(join_start, 0), call(rows_start, 1))
    at_step(7, call(rows_start, 2))
    at_step(10, call(rows_wait, 1), call(join_start, 1), call(join_pass, 0))
    at_step(16, call(join_pass, 1))
    at_step(11, call(weights_wait, 0, 6), call(project, 0))
    at_step(12, join(0, 0).wait, call(project, 1), lambda: keep(qkv_mat, qkv_mat_out))
    at_step(13, join(0, 1).wait_send, join(0, 2).wait, call(project, 2), lambda: keep(act, act_out))
    at_step(14, call(project, 3), head_rows, lambda: keep(qkv, qkv_out))
    at_step(15, call(attention_block, 0), call(attention_block, 1))
    at_step(16, call(attention_block, 2))
    at_step(17, call(attention_block, 3), lambda: keep(attended, attended_out))
    at_step(18, call(weights_wait, 6, 8), call(out_block, 3), call(out_block, 1))
    at_step(18, call(sums.start, 0, partial, True))
    at_step(19, call(out_block, 2), *(call(sums.middle, partial, True, part) for part in range(PARTS)))
    at_step(19, call(out_block, 0), lambda: keep(out_mat, out_mat_out))
    at_step(19, call(rows_wait, 2), keep_resid)
    at_step(21, call(join_end, 1), lambda: keep(cot_all, cot_out))
    at_step(23, call(back_chunk, 0))
    at_step(24, second_norm)
    at_step(24, call(back_chunk, 1))
    at_step(25, call(back_chunk, 2))
    at_step(26, call(back_chunk, 3))
    at_step(27, call(join_pass, 2), call(back_chunk, 4))
    lag = 2
    for i in range(count + 2 * lag):
        if i < count:
            y_copy(i).start()
            pl.when(even)(lambda i=i: x_copy(i, True).start())
            own_copy(i).start()
        j = i - lag
        if 0 <= j < count:
            y_copy(j).wait_recv()

            @pl.when(even)
            def _(j=j):
                x_copy(j, True).wait_recv()
                z_copy(j, True).start()

            pl.when(odd)(lambda j=j: x_copy(j, False).start())
        j = i - 2 * lag
        if 0 <= j < count:

            @pl.when(odd)
            def _(j=j):
                x_copy(j, False).wait_recv()
                z_copy(j, False).start()

        for task in plan.get(i, ()):
            task()

    for r in range(5, pieces):
        back_chunk(r)
    keep(down_all, down_out)
    join_end(2)
    keep(two, two_out)
    weights_wait(8, 8 + pieces)
    back_store(pieces - 2).wait()
    back_store(pieces - 1).wait()
    for i in range(count):
        y_copy(i).wait_send()
        x_copy(i, True).wait_send()
        z_copy(i, True).wait_send()
    for copy in kept:
        copy.wait()


def forward_all(
    head_size,
    length,
    vectors,
    head_vectors,
    query_weight,
    key_weight,
    value_weight,
    out_weight,
    up_weight,
    down_weight,
    arrived,
    cot,
):
    strip, features, units = query_weight.shape[0], query_weight.shape[1] // 2, up_weight.shape[1] // 2
    width = 4 * strip
    depth, block_rows = arrived.shape[:2]
    own_rows = depth * block_rows
    tokens = 4 * own_rows
    bf16, f32 = jnp.bfloat16, jnp.float32
    hbm = pl.BlockSpec(memory_space=pl.ANY)
    vmem = pl.BlockSpec(memory_space=pltpu.VMEM)
    count = 24
    dma = pltpu.SemaphoreType.DMA

    def made(shape, dtype=bf16):
        return jax.ShapeDtypeStruct(shape, dtype)

    def hold(shape, dtype=bf16):
        return pltpu.VMEM(shape, dtype)

    return pl.pallas_call(
        functools.partial(forward_kernel, head_size),
        out_shape=(
            made((width, 3 * features)),
            made((features, width)),
            made((width, units)),
            made((units, width)),
            made((tokens, width)),
            made((tokens, width)),
            made((tokens, 3 * features)),
            made((tokens, features)),
            made((own_rows, width), f32),
            made((own_rows, width), f32),
            made((tokens, width)),
            made((tokens, units)),
            made((8, width), f32),
            made((8, 128), f32),
        ),
        in_specs=[pl.BlockSpec(memory_space=pltpu.SMEM)] + [hbm] * 10,
        out_specs=(hbm,) * 12 + (vmem,) * 2,
        scratch_shapes=[
            hold((tokens, width)),
            hold((units, width)),
            hold((2, tokens, units // 8)),
            hold((width, 3 * features)),
            hold((features, width)),
            hold((depth, block_rows, width), f32),
            hold((depth, block_rows, width)),
            hold((tokens, width)),
            hold((own_rows, width), f32),
            hold((tokens, 3 * features)),
            hold((tokens, features)),
            hold((tokens, features)),
            hold((tokens, features)),
            hold((tokens, width)),
            hold((3, own_rows, width)),
            hold((own_rows, width)),
            hold((tokens, width)),
            hold((8, strip), f32),
            hold(head_vectors.shape, f32),
            hold((3,) + head_vectors.shape, f32),
            hold((8, 3 * features), f32),
            dma((count,)),
            dma((3, count)),
            dma((3, count)),
            dma((3, depth)),
            dma((3, depth)),
            dma((3, 3)),
            dma((3, 3)),
            dma((2, 3)),
            dma((2, 3)),
            dma((3,)),
            dma((2 + PARTS,)),
            dma((2 + PARTS,)),
            dma((12,)),
        ],
        compiler_params=pltpu.CompilerParams(
            collective_id=0, has_side_effects=True, vmem_limit_bytes=56 << 20
        ),
        cost_estimate=pl.CostEstimate(flops=0, bytes_accessed=64 << 20, transcendentals=0),
    )(
        length,
        vectors,
        head_vectors,
        query_weight,
        key_weight,
        value_weight,
        out_weight,
        up_weight,
        down_weight,
        arrived,
        cot,
    )


def backward_kernel(
    head_size,
    info,
    vector_ref,
    small_in,
    gelu_hbm,
    pre_hbm,
    act_two_hbm,
    two_part,
    mlp_part,
    hidden_hbm,
    cot_hbm,
    resid_hbm,
    out_hbm,
    qkv_mat_hbm,
    qkv_hbm,
    attended_hbm,
    act_hbm,
    down_sum,
    up_sum,
    out_sum,
    qkv_sums,
    rows_out,
    rows_grad,
    small,
    engine,
    base,
    hidden_grad,
    low,
    out_mat,
    attended_grad,
    qkv,
    qkv_grad,
    act,
    attended,
    qkv_mat,
    keys,
    values,
    key_sum,
    value_sum,
    strips,
    packed,
    arrived,
    sent,
    loaded,
    small_arrived,
    load_sem,
    sum_send,
    sum_recv,
    sum_load,
    join_send,
    join_recv,
    strip_sem,
    row_send,
    row_recv,
    share_send,
    share_recv,
    small_send,
    small_recv,
    core_free,
    y_free,
):
    f32, bf16 = jnp.float32, jnp.bfloat16
    own_rows, width = base.shape
    tokens, features = attended.shape
    heads = features // head_size
    depth = rows_out.shape[0] // 2
    block_rows = rows_out.shape[1]
    p = Place(depth)
    x, y, z, t = p.x, p.y, p.z, p.t
    entry_barrier(
        [p.over_x, p.over_y, p.over_core, p.mate, p.middle, p.hop] + p.row_targets()
    )
    length = info[0]
    scale = 1.0 / math.sqrt(head_size)
    column = 2 * t + y

    rows, cols = engine[0].shape[1:]
    down_rows = down_sum.shape[0] // 2
    up_cols = up_sum.shape[1] // 2
    strip = out_sum.shape[1]

    def over_tokens(left, right, target):
        target[...] = lax.dot_general(
            left, right, (((0,), (0,)), ((), ())), preferred_element_type=f32
        ).astype(target.dtype)

    per_down, per_up = down_rows // strip, up_cols // cols
    strip_count = per_down + per_up

    def strip_load(n):
        source = gelu_hbm if n < per_down else pre_hbm
        cut = pl.ds((n % per_down) * strip, strip)
        return pltpu.make_async_copy(source.at[:, cut], strips.at[n % 2], strip_sem.at[n % 2])

    def resident_load(k):
        source = (cot_hbm, act_two_hbm, act_hbm)[k]
        return pltpu.make_async_copy(source, act, load_sem.at[5])

    def strip_ready(n):
        strip_load(n).wait()
        if n + 1 < strip_count:
            strip_load(n + 1).start()

    def homes_of(far):
        return (p.homes[1], p.homes[3]) if far else (p.homes[0], p.homes[2])

    def down_item(r, far):
        def make(send, own):
            if far and r % 2 == 0:
                if r == 0:
                    resident_load(0).wait()
                strip_ready(r // 2)
            left = strips.at[(r // 2) % 2, :, pl.ds((r % 2) * rows, rows)]
            for home, target in zip(homes_of(far), (send, own)):
                over_tokens(left[...], act[:, aligned(home * strip, strip)], target)

        side = 1 - y if far else y
        return far, down_sum.at[aligned(side * down_rows + r * rows, rows), :], make

    def up_item(c, r, far):
        def make(send, own):
            if far and r == 0:
                if c == 0:
                    resident_load(1).start()
                    resident_load(1).wait()
                strip_ready(per_down + c)
            for home, target in zip(homes_of(far), (send, own)):
                over_tokens(
                    act[:, aligned(home * strip + r * rows, rows)], strips[c % 2], target
                )

        side = 1 - y if far else y
        place = up_sum.at[pl.ds(r * rows, rows), aligned(side * up_cols + c * cols, cols)]
        return far, place, make

    def out_item(r, far):
        def make(send, own):
            for home, target in zip(homes_of(far), (send, own)):
                over_tokens(
                    attended[:, pl.ds(r * rows, rows)], low[:, aligned(home * strip, strip)], target
                )

        side = 1 - y if far else y
        return far, out_sum.at[aligned(side * features + r * rows, rows), :], make

    def qkv_item(r, c, far):
        def make(send, own):
            if far and r == 0 and c == 0:
                resident_load(2).start()
                resident_load(2).wait()
            for home, target in zip(homes_of(far), (send, own)):
                over_tokens(
                    act[:, aligned(home * strip + r * rows, rows)],
                    qkv_grad[:, pl.ds(c * cols, cols)],
                    target,
                )

        side = 1 - y if far else y
        return far, qkv_sums[c].at[pl.ds(r * rows, rows), aligned(side * cols, cols)], make

    sides = (True, False)
    items = [down_item(r, far) for r in range(down_rows // rows) for far in sides]
    items += [up_item(c, r, far) for c in range(per_up) for r in range(strip // rows) for far in sides]
    items += [out_item(r, far) for r in range(features // rows) for far in sides]
    items += [qkv_item(r, c, far) for r in range(strip // rows) for c in range(3) for far in sides]
    run, steps = reduce_stages(p, items, engine)

    loads = [
        pltpu.make_async_copy(source, target, load_sem.at[k])
        for k, (source, target) in enumerate(
            (
                (hidden_hbm, base),
                (cot_hbm.at[pl.ds(0, own_rows), :], packed),
                (out_hbm, out_mat),
                (qkv_hbm, qkv),
                (attended_hbm, attended),
                (cot_hbm, act),
                (qkv_mat_hbm, qkv_mat),
                (resid_hbm, base),
            )
        )
    ]
    sums = RowSum(
        p, own_rows, arrived, sent, loaded, sum_send, sum_recv, sum_load, core_free, y_free, 3
    )
    group_rows = 16
    quarter = own_rows // 4 // group_rows

    def start():
        loads[5].start()
        strip_load(0).start()
        sums.start(0, two_part, False)
        for k in (0, 1, 2, 3, 4, 6):
            loads[k].start()
        small[...] = small_in[...]
        key_sum[...] = jnp.zeros_like(key_sum)
        value_sum[...] = jnp.zeros_like(value_sum)

    def two_middle(part):
        sums.middle(two_part, False, part)

    def two_finish():
        sums.finish(two_part, False)
        loads[0].wait()
        loads[1].wait()

    def accumulate(row, value):
        small[pl.ds(row, 1), :] += jnp.sum(value, 0, keepdims=True)

    def two_rows(part):
        gain = vector_ref[pl.ds(GAIN_TWO, 1), :]

        @pl.loop(part * quarter, (part + 1) * quarter)
        def _(k):
            at = pl.ds(pl.multiple_of(k * group_rows, group_rows), group_rows)
            upstream = sums.total(two_part, False, at)
            unit, inverse = unit_rows(base[at, :])
            grad = packed[at, :].astype(f32) + unit_back(upstream, unit, inverse, gain)
            hidden_grad[at, :] = grad
            low[at, :] = grad.astype(bf16)
            accumulate(GAIN_TWO, upstream * unit)
            accumulate(SHIFT_TWO, upstream)
            accumulate(OUT_BIAS, grad)

    def low_block(k):
        return low.at[pl.ds(k * own_rows, own_rows), :]

    def join(k):
        source, place = ((0, 1), (None, None), (2, 3))[k]
        return remote_copy(
            low_block(source), low_block(place), join_send.at[k], join_recv.at[k], p.over_core
        )

    def join_y(part):
        size = own_rows // PARTS
        return remote_copy(
            low.at[pl.ds(part * size, size), :],
            low.at[pl.ds(2 * own_rows + part * size, size), :],
            join_send.at[3 + part],
            join_recv.at[3 + part],
            p.over_y,
        )

    def join_start():
        join(0).start()
        join_y(0).start()
        sums.release(0)

    def join_pass():
        for part in range(PARTS):
            join_y(part).wait_recv()
        join(2).start()

    def attend_block(k):
        at = pl.ds(k * own_rows, own_rows)
        attended_grad[at, :] = lax.dot_general(
            low[at, :], out_mat[...], (((1,), (1,)), ((), ())), preferred_element_type=f32
        ).astype(bf16)

    def attend_own():
        loads[2].wait()
        attend_block(0)

    def attend_peer():
        join(0).wait()
        attend_block(1)

    def attend_far():
        attend_block(2)

    def attend_last():
        for part in range(PARTS):
            join_y(part).wait_send()
        join(2).wait()
        attend_block(3)

    def mlp_start():
        sums.start(1, mlp_part, False)

    def mlp_middle(part):
        sums.middle(mlp_part, False, part)

    def mlp_finish():
        sums.finish(mlp_part, False)
        bias = vector_ref[pl.ds(DOWN_BIAS, 1), :]

        @pl.loop(0, own_rows // group_rows)
        def _(k):
            at = pl.ds(pl.multiple_of(k * group_rows, group_rows), group_rows)
            packed[at, :] = (base[at, :] + sums.total(mlp_part, False, at) + bias).astype(bf16)

        sums.release(1)

    def row_source(k):
        return packed.at[pl.ds(k * block_rows, block_rows), :]

    row_ends = (rows_out, rows_grad)

    def row_copy(a, k):
        end = row_ends[a].at[x * depth + z]
        return remote_copy(row_source(k), end, row_send.at[a, k], row_recv.at[a, z], p.row_target(k))

    def row_arrival(a, k):
        end = row_ends[a].at[t * depth + k]
        return remote_copy(row_source(k), end, row_send.at[a, k], row_recv.at[a, k], p.row_target(k))

    def row_stay(a, k):
        return pltpu.make_async_copy(row_source(k), row_ends[a].at[x * depth + z], row_send.at[a, k])

    def rows_start(a):
        for k in range(depth):
            stays = (z == k) & (x == t)
            pl.when(stays)(lambda k=k: row_stay(a, k).start())
            pl.when(jnp.logical_not(stays))(lambda k=k: row_copy(a, k).start())

    def share(a):
        group = row_ends[a].at[pl.ds(t * depth, depth)]
        return remote_copy(group, group, share_send.at[a], share_recv.at[a], p.over_core)

    def rows_share(a):
        for k in range(depth):
            stays = (z == k) & (x == t)
            pl.when(stays)(lambda k=k: row_stay(a, k).wait())

            @pl.when(jnp.logical_not(stays))
            def _(k=k):
                row_copy(a, k).wait_send()
                row_arrival(a, k).wait_recv()

        share(a).start()

    def head_rows():
        loads[3].wait()
        loads[4].wait()
        for block in range(4):
            at = pl.ds(pl.multiple_of(p.block_place(block) * own_rows, own_rows), own_rows)
            keys[pl.ds(block * own_rows, own_rows), :] = qkv[at, pl.ds(features, features)]
            values[pl.ds(block * own_rows, own_rows), :] = qkv[at, pl.ds(2 * features, features)]

    def attention_block(block):
        at = pl.ds(pl.multiple_of(p.block_place(block) * own_rows, own_rows), own_rows)
        part = pl.ds(0, (block + 1) * own_rows)

        @pl.loop(0, heads)
        def _(head):
            lanes = aligned(head * head_size, head_size)
            queries, grads = qkv[at, lanes], attended_grad[at, lanes]
            probs, _ = attention_probs(queries, keys[part, lanes], block, length)
            prob_grad = lax.dot_general(
                grads, values[part, lanes], (((1,), (1,)), ((), ())), preferred_element_type=f32
            )
            inner = jnp.sum(probs * prob_grad, -1, keepdims=True)
            score_grad = (probs * (prob_grad - inner)).astype(bf16)
            query_grad = (
                jnp.dot(score_grad, keys[part, lanes], preferred_element_type=f32) * scale
            )
            spot = aligned(column * features + head * head_size, head_size)
            small[pl.ds(QUERY_BIAS, 1), spot] += jnp.sum(query_grad, 0, keepdims=True)
            qkv_grad[at, lanes] = query_grad.astype(bf16)
            key_sum[part, lanes] += lax.dot_general(
                score_grad, queries, (((0,), (0,)), ((), ())), preferred_element_type=f32
            )
            value_sum[part, lanes] += lax.dot_general(
                probs.astype(bf16), grads, (((0,), (0,)), ((), ())), preferred_element_type=f32
            )

    def attention_end(block):
        at = pl.ds(pl.multiple_of(p.block_place(block) * own_rows, own_rows), own_rows)
        part = pl.ds(block * own_rows, own_rows)
        qkv_grad[at, pl.ds(features, features)] = (key_sum[part, :] * scale).astype(bf16)
        value_grad = value_sum[part, :]
        qkv_grad[at, pl.ds(2 * features, features)] = value_grad.astype(bf16)
        spot = aligned(column * features, features)
        small[pl.ds(VALUE_BIAS, 1), spot] += jnp.sum(value_grad, 0, keepdims=True)

    def one_block(k):
        if k == 3:
            loads[6].wait()
        at = pl.ds(k * own_rows, own_rows)

        @pl.loop(0, 4)
        def _(n):
            cut = aligned(n * strip, strip)
            low[at, cut] = lax.dot_general(
                qkv_grad[at, :], qkv_mat[cut, :], (((1,), (1,)), ((), ())), preferred_element_type=f32
            ).astype(bf16)

    def one_start():
        sums.start(2, low, True)

    def one_middle(part):
        sums.middle(low, True, part)

    def one_finish():
        sums.finish(low, True)
        loads[7].wait()

    def one_rows(part):
        gain = vector_ref[pl.ds(GAIN_ONE, 1), :]

        @pl.loop(part * quarter, (part + 1) * quarter)
        def _(k):
            at = pl.ds(pl.multiple_of(k * group_rows, group_rows), group_rows)
            upstream = sums.total(low, True, at)
            unit, inverse = unit_rows(base[at, :])
            grad = hidden_grad[at, :] + unit_back(upstream, unit, inverse, gain)
            packed[at, :] = grad.astype(bf16)
            accumulate(GAIN_ONE, upstream * unit)
            accumulate(SHIFT_ONE, upstream)

    def small_copy(k):
        target = (p.over_core, p.over_x, p.over_y, p.mate, p.hop)[k]
        return remote_copy(small, small_arrived.at[k], small_send.at[k], small_recv.at[k], target)

    def small_add(k):
        small_copy(k).wait()
        mine, other = small[...], small_arrived[k]
        row = lax.broadcasted_iota(jnp.int32, mine.shape, 0)
        small[...] = jnp.where(row == PEAKS, jnp.maximum(mine, other), mine + other)

    def call(function, *arguments):
        return lambda: function(*arguments)

    plan = {}

    def at_step(step, *tasks):
        plan.setdefault(step, []).extend(tasks)

    for k in range(4):
        at_step(3 + k, call(two_middle, k))
    at_step(11, two_finish, call(two_rows, 0))
    for k in range(1, 4):
        at_step(11 + k // 2, call(two_rows, k))
    at_step(12, join_start)
    for k in range(1, 4):
        at_step(12 + k, join_y(k).start)
    at_step(13, attend_own)
    at_step(14, attend_peer)
    at_step(14, head_rows)
    at_step(19, join_pass)
    at_step(20, attend_far)
    at_step(21, attend_last)
    at_step(22, call(attention_block, 0), call(attention_block, 1))
    at_step(22 + 1, call(attention_block, 2))
    at_step(22 + 2, call(attention_block, 3))
    at_step(22 + 3, *(call(attention_end, k) for k in range(4)))
    at_step(16, mlp_start)
    for k in range(4):
        at_step(19 + 1 * k, call(mlp_middle, k))
    at_step(29, mlp_finish, loads[7].start, lambda: rows_start(0))
    at_step(38, lambda: rows_share(0))
    at_step(36, call(one_block, 3), call(one_block, 1), one_start)
    at_step(36 + 1, call(one_block, 2), call(one_block, 0))
    for k in range(4):
        at_step(38 + k, call(one_middle, k))
    at_step(47, one_finish, share(0).wait, call(one_rows, 0))
    for k in range(1, 4):
        at_step(47 + k // 2, call(one_rows, k))
    at_step(48, lambda: rows_start(1))
    at_step(49, small_copy(0).start)
    for k in range(4):
        at_step(49 + 2 + 2 * k, call(small_add, k), small_copy(k + 1).start)
    at_step(49 + 5 * 2, call(small_add, 4))
    at_step(57, lambda: rows_share(1))
    at_step(59, share(1).wait)
    start()
    for step in range(steps):
        run(step)
        for task in plan.get(step, ()):
            task()


def backward_all(
    head_size,
    length,
    vectors,
    small,
    gelu_low,
    pre_low,
    act_two,
    two_part,
    mlp_part,
    hidden,
    cot_low,
    resid,
    out_mat,
    qkv_mat,
    qkv,
    attended,
    act_one,
    slots,
):
    bf16, f32 = jnp.bfloat16, jnp.float32
    hbm = pl.BlockSpec(memory_space=pl.ANY)
    vmem = pl.BlockSpec(memory_space=pltpu.VMEM)
    down_rows, up_cols = gelu_low.shape[1], pre_low.shape[1]
    tokens, features = attended.shape
    own_rows, width = hidden.shape
    strip = width // 4
    depth = slots // 2
    engine = reduce_scratch(6, 4, 256, 512)
    n_engine = len(engine)

    def kernel(*refs):
        ins, rest = refs[:16], refs[16:]
        outs, scratch = rest[:9], rest[9:]
        backward_kernel(
            head_size,
            *ins,
            outs[0],
            outs[1],
            outs[2],
            outs[3:6],
            *outs[6:],
            scratch[:n_engine],
            *scratch[n_engine:],
        )

    dma, regular = pltpu.SemaphoreType.DMA, pltpu.SemaphoreType.REGULAR

    def hold(shape, dtype=bf16):
        return pltpu.VMEM(shape, dtype)

    return pl.pallas_call(
        kernel,
        out_shape=(
            jax.ShapeDtypeStruct((2 * down_rows, strip), bf16),
            jax.ShapeDtypeStruct((strip, 2 * up_cols), bf16),
            jax.ShapeDtypeStruct((2 * features, strip), bf16),
            jax.ShapeDtypeStruct((strip, 2 * features), bf16),
            jax.ShapeDtypeStruct((strip, 2 * features), bf16),
            jax.ShapeDtypeStruct((strip, 2 * features), bf16),
            jax.ShapeDtypeStruct((slots, own_rows // depth, width), bf16),
            jax.ShapeDtypeStruct((slots, own_rows // depth, width), bf16),
            jax.ShapeDtypeStruct(small.shape, f32),
        ),
        in_specs=[pl.BlockSpec(memory_space=pltpu.SMEM), vmem, vmem] + [hbm] * 13,
        out_specs=(hbm,) * 8 + (vmem,),
        scratch_shapes=engine
        + [
            hold((own_rows, width), f32),
            hold((own_rows, width), f32),
            hold((tokens, width)),
            hold((features, width)),
            hold((tokens, features)),
            hold((tokens, 3 * features)),
            hold((tokens, 3 * features)),
            hold((tokens, width)),
            hold((tokens, features)),
            hold((width, 3 * features)),
            hold((tokens, features)),
            hold((tokens, features)),
            hold((tokens, features), f32),
            hold((tokens, features), f32),
            hold((2, tokens, strip)),
            hold((own_rows, width)),
            hold((3, own_rows, width)),
            hold((own_rows, width)),
            hold((own_rows, width)),
            hold((5,) + small.shape, f32),
            dma((8,)),
            dma((2 + PARTS,)),
            dma((2 + PARTS,)),
            dma(()),
            dma((3 + PARTS,)),
            dma((3 + PARTS,)),
            dma((2,)),
            dma((2, depth)),
            dma((2, depth)),
            dma((2,)),
            dma((2,)),
            dma((5,)),
            dma((5,)),
            regular,
            regular,
        ],
        compiler_params=pltpu.CompilerParams(
            collective_id=1, has_side_effects=True, vmem_limit_bytes=60 << 20
        ),
        cost_estimate=pl.CostEstimate(flops=0, bytes_accessed=64 << 20, transcendentals=0),
    )(
        length,
        vectors,
        small,
        gelu_low,
        pre_low,
        act_two,
        two_part,
        mlp_part,
        hidden,
        cot_low,
        resid,
        out_mat,
        qkv_mat,
        qkv,
        attended,
        act_one,
    )


def split_body(
    layer_input,
    cotangent,
    seq_lengths,
    dealing,
    attn_gain,
    attn_shift,
    query_weight,
    query_bias,
    key_weight,
    value_weight,
    value_bias,
    out_weight,
    out_bias,
    mlp_gain,
    mlp_shift,
    up_weight,
    up_bias,
    down_weight,
    down_bias,
    clip_level,
):
    f32, bf16 = jnp.float32, jnp.bfloat16
    f = lax.axis_index("fsdp")
    z = lax.axis_index("ctx")
    t = lax.axis_index("tp")
    y, x = f // 2, f % 2
    depth = lax.axis_size("ctx")
    slots, block_rows, width = layer_input.shape
    local_heads = query_bias.shape[0] // 2
    head_size = 4 * query_bias.shape[1]
    features = local_heads * head_size
    hidden_units = up_weight.shape[1] // 2
    strip = query_weight.shape[0]
    own_rows = depth * block_rows

    place = t[None]
    length = seq_lengths[dealing[x * depth + z]]
    arrived, cot_part, down_bias_part = prepare(
        dealing, seq_lengths, place, layer_input, cotangent, depth
    )
    vectors = jnp.concatenate(
        [attn_gain, attn_shift, out_bias, mlp_gain, mlp_shift, down_bias, up_bias.reshape(-1)]
    )
    vectors = vectors.reshape(8, strip).astype(f32)
    head_vectors = jnp.concatenate([query_bias, value_bias], 0).astype(f32)
    head_vectors = lax.dynamic_update_slice(
        jnp.zeros((head_vectors.shape[0], head_size), f32), head_vectors, (0, f * query_bias.shape[1])
    )
    (
        qkv_mat,
        out_mat,
        up_mat,
        down_mat,
        act_one,
        cot_low,
        qkv,
        attended,
        hidden,
        resid,
        act_two,
        back,
        vectors_whole,
        peaks,
    ) = forward_all(
        head_size,
        length[None],
        vectors,
        head_vectors,
        query_weight,
        key_weight,
        value_weight,
        out_weight,
        up_weight,
        down_weight,
        arrived,
        cot_part,
    )
    peaks = peaks[:local_heads, 0]
    up_vec = lax.dynamic_slice_in_dim(vectors_whole, 6 + y, 1, 0)

    pre = matmul(act_two, up_mat) + up_vec
    cdf = 0.5 * (1.0 + lax.erf(pre * INV_ROOT_TWO))
    gelu_low = (pre * cdf).astype(bf16)
    slope = cdf + pre * (jnp.exp(-0.5 * pre * pre) * INV_ROOT_TWO_PI)
    pre_grad = back.astype(f32) * slope
    pre_low = pre_grad.astype(bf16)
    up_bias_part = jnp.sum(pre_grad, 0)
    two_part = back_product(pre_low, up_mat).astype(bf16)
    mlp_part = matmul(gelu_low, down_mat).astype(bf16)
    column = 2 * t + y
    small = jnp.zeros((16, width), f32).at[DOWN_BIAS].set(down_bias_part[0])
    small = lax.dynamic_update_slice(small, up_bias_part[None], (UP_BIAS + column, 0))
    small = small.at[PEAKS].set(NEG)
    small = lax.dynamic_update_slice(small, peaks[None], (PEAKS, local_heads * (2 * t + y)))
    (
        down_sum,
        up_sum,
        out_sum,
        query_sum,
        key_sum,
        value_sum,
        rows_out,
        rows_grad,
        totals,
    ) = backward_all(
        head_size,
        length[None],
        vectors_whole,
        small,
        gelu_low,
        pre_low,
        act_two,
        two_part,
        mlp_part,
        hidden,
        cot_low,
        resid,
        out_mat,
        qkv_mat,
        qkv,
        attended,
        act_one,
        slots,
    )
    rows_sum = lax.dynamic_slice(totals, (0, f * strip), (6, strip))
    head_sum = lax.dynamic_slice(totals, (QUERY_BIAS, 2 * t * features), (2, 2 * features))
    head_sum = head_sum.reshape(2, 2 * local_heads, head_size)
    head_sum = lax.dynamic_slice_in_dim(head_sum, f * query_bias.shape[1], query_bias.shape[1], 2)
    unit_sum = lax.dynamic_slice(
        totals, (UP_BIAS + up_bias.shape[0] * t, f * strip), (up_bias.shape[0], strip)
    )
    peak_all = lax.dynamic_slice(totals, (PEAKS, 2 * local_heads * t), (1, 2 * local_heads))[0]
    (
        final_output,
        final_grad,
        query_weight_grad,
        key_weight_grad,
        value_weight_grad,
        out_weight_grad,
        up_weight_grad,
        down_weight_grad,
        query_clipped,
        key_clipped,
    ) = finish_all(
        head_size,
        place,
        clip_level,
        totals,
        query_weight,
        key_weight,
        (rows_out, rows_grad, query_sum, key_sum, value_sum, out_sum, up_sum, down_sum),
    )
    return (
        final_output,
        final_grad,
        rows_sum[GAIN_ONE],
        rows_sum[SHIFT_ONE],
        query_weight_grad,
        head_sum[0],
        key_weight_grad,
        value_weight_grad,
        head_sum[1],
        out_weight_grad,
        rows_sum[OUT_BIAS],
        rows_sum[GAIN_TWO],
        rows_sum[SHIFT_TWO],
        up_weight_grad,
        unit_sum,
        down_weight_grad,
        rows_sum[DOWN_BIAS],
        peak_all,
        query_clipped,
        key_clipped,
    )


def solution(mesh):
    sizes = dict(mesh.shape)
    small_slice = sizes == {"fsdp": 4, "ctx": 4, "tp": 2}
    return jax.shard_map(
        split_body if small_slice else gathered_body,
        mesh=mesh,
        in_specs=(
            P(None, ("fsdp", "ctx"), None),
            P(None, ("fsdp", "ctx"), None),
            P(),
            P(),
            P("fsdp"),
            P("fsdp"),
            P("fsdp", "tp"),
            P("tp", "fsdp"),
            P("fsdp", "tp"),
            P("fsdp", "tp"),
            P("tp", "fsdp"),
            P("tp", "fsdp"),
            P("fsdp"),
            P("fsdp"),
            P("fsdp"),
            P("fsdp", "tp"),
            P("tp", "fsdp"),
            P("tp", "fsdp"),
            P("fsdp"),
            P(),
        ),
        out_specs=(
            P(None, ("fsdp", "ctx"), None),
            P(None, ("fsdp", "ctx"), None),
            P("fsdp"),
            P("fsdp"),
            P("fsdp", "tp"),
            P("tp", "fsdp"),
            P("fsdp", "tp"),
            P("fsdp", "tp"),
            P("tp", "fsdp"),
            P("tp", "fsdp"),
            P("fsdp"),
            P("fsdp"),
            P("fsdp"),
            P("fsdp", "tp"),
            P("tp", "fsdp"),
            P("tp", "fsdp"),
            P("fsdp"),
            P("tp"),
            P("fsdp", "tp"),
            P("fsdp", "tp"),
        ),
        check_vma=False,
    )
```

```python
import functools
import math

import jax
import jax.numpy as jnp
from jax import lax
from jax.experimental import pallas as pl
from jax.experimental.pallas import tpu as pltpu
from jax.sharding import PartitionSpec as P

EPS = 1e-05
NEG = -1e30
INV_ROOT_TWO = 0.7071067811865476
INV_ROOT_TWO_PI = 0.3989422804014327


def normalize(values, scale_vec, offset_vec):
    center = values - jnp.mean(values, -1, keepdims=True)
    inverse = lax.rsqrt(jnp.mean(center * center, -1, keepdims=True) + EPS)
    normed = center * inverse
    return (normed * scale_vec + offset_vec, normed, inverse)


def norm_back(upstream, normed, inverse, scale_vec):
    scaled = upstream * scale_vec
    inner = (
        scaled
        - jnp.mean(scaled, -1, keepdims=True)
        - normed * jnp.mean(scaled * normed, -1, keepdims=True)
    )
    return (inverse * inner, jnp.sum(upstream * normed, 0), jnp.sum(upstream, 0))


def pick_slots(rows, dealing, first, count):
    return jnp.concatenate(
        [lax.dynamic_slice_in_dim(rows, dealing[first + j], 1, 0) for j in range(count)], 0
    )


def matmul(left, right):
    return jnp.dot(left, right, preferred_element_type=jnp.float32)


def weight_product(left, right):
    return jnp.einsum("td,te->de", left, right, preferred_element_type=jnp.float32)


def back_product(left, right):
    return jnp.einsum("te,de->td", left, right, preferred_element_type=jnp.float32)


def gathered_body(
    layer_input,
    cotangent,
    seq_lengths,
    dealing,
    attn_gain,
    attn_shift,
    query_weight,
    query_bias,
    key_weight,
    value_weight,
    value_bias,
    out_weight,
    out_bias,
    mlp_gain,
    mlp_shift,
    up_weight,
    up_bias,
    down_weight,
    down_bias,
    clip_level,
):
    shard_count = lax.axis_size("fsdp")
    ctx_count = lax.axis_size("ctx")
    my_group = lax.axis_index("fsdp")
    ctx_place = lax.axis_index("ctx")
    slot_count, block_rows, width = layer_input.shape
    per_group = slot_count // shard_count
    local_rows = shard_count * block_rows
    tokens = per_group * local_rows
    dealt_input = pick_slots(layer_input, dealing, 0, slot_count).reshape(
        shard_count, per_group, block_rows, width
    )
    dealt_grad = cotangent.reshape(shard_count, per_group, block_rows, width)
    arrived_input, arrived_grad = (
        lax.all_to_all(dealt_input, "fsdp", split_axis=0, concat_axis=2, tiled=True),
        lax.all_to_all(dealt_grad, "fsdp", split_axis=0, concat_axis=2, tiled=True),
    )
    resid = arrived_input.reshape(tokens, width)
    upstream = arrived_grad.reshape(tokens, width)
    seq_lens = lax.dynamic_slice_in_dim(
        jnp.take(seq_lengths, dealing), my_group * per_group, per_group
    )
    gathered = (
        lax.all_gather(attn_gain, "fsdp", axis=0, tiled=True),
        lax.all_gather(attn_shift, "fsdp", axis=0, tiled=True),
        lax.all_gather(query_weight, "fsdp", axis=0, tiled=True),
        lax.all_gather(query_bias, "fsdp", axis=1, tiled=True),
        lax.all_gather(key_weight, "fsdp", axis=0, tiled=True),
        lax.all_gather(value_weight, "fsdp", axis=0, tiled=True),
        lax.all_gather(value_bias, "fsdp", axis=1, tiled=True),
        lax.all_gather(out_weight, "fsdp", axis=1, tiled=True),
        lax.all_gather(out_bias, "fsdp", axis=0, tiled=True),
        lax.all_gather(mlp_gain, "fsdp", axis=0, tiled=True),
        lax.all_gather(mlp_shift, "fsdp", axis=0, tiled=True),
        lax.all_gather(up_weight, "fsdp", axis=0, tiled=True),
        lax.all_gather(up_bias, "fsdp", axis=1, tiled=True),
        lax.all_gather(down_weight, "fsdp", axis=1, tiled=True),
        lax.all_gather(down_bias, "fsdp", axis=0, tiled=True),
    )
    (
        gain_one,
        shift_one,
        query_mat,
        query_vec,
        key_mat,
        value_mat,
        value_vec,
        out_mat,
        out_vec,
        gain_two,
        shift_two,
        up_mat,
        up_vec,
        down_mat,
        down_vec,
    ) = gathered
    head_count, head_size = query_vec.shape
    features = head_count * head_size
    scale_of_scores = 1.0 / math.sqrt(head_size)
    row_ids = jnp.arange(local_rows, dtype=jnp.int32)
    query_pos = (row_ids // block_rows * ctx_count + ctx_place) * block_rows + row_ids % block_rows
    key_ids = jnp.arange(ctx_count * local_rows, dtype=jnp.int32)
    key_rows = key_ids % local_rows
    key_pos = (
        key_rows // block_rows * ctx_count + key_ids // local_rows
    ) * block_rows + key_rows % block_rows
    allowed = (key_pos[None, None, :] <= query_pos[None, :, None]) & (
        key_pos[None, None, :] < seq_lens[:, None, None]
    )
    query_live = query_pos[None, :] < seq_lens[:, None]
    normed_a, unit_one, inverse_one = normalize(
        resid, gain_one.astype(jnp.float32), shift_one.astype(jnp.float32)
    )
    act_one = normed_a.astype(jnp.bfloat16)
    queries = (
        (matmul(act_one, query_mat) + query_vec.reshape(features).astype(jnp.float32))
        .astype(jnp.bfloat16)
        .reshape(per_group, local_rows, features)
    )
    keys_mine = (
        matmul(act_one, key_mat).astype(jnp.bfloat16).reshape(per_group, local_rows, features)
    )
    values_mine = (
        (matmul(act_one, value_mat) + value_vec.reshape(features).astype(jnp.float32))
        .astype(jnp.bfloat16)
        .reshape(per_group, local_rows, features)
    )
    keys_all, values_all = (
        lax.all_gather(keys_mine, "ctx", axis=1, tiled=True),
        lax.all_gather(values_mine, "ctx", axis=1, tiled=True),
    )

    def head_cut(array, head_index):
        return lax.dynamic_slice_in_dim(array, head_index * head_size, head_size, 2)

    def head_scores(head_queries, head_keys):
        return (
            jnp.einsum("sqd,skd->sqk", head_queries, head_keys, preferred_element_type=jnp.float32)
            * scale_of_scores
        )

    def forward_head(head_index):
        logit_scores = head_scores(head_cut(queries, head_index), head_cut(keys_all, head_index))
        masked = jnp.where(allowed, logit_scores, NEG)
        row_top = jnp.max(masked, -1, keepdims=True)
        exp_terms = jnp.where(allowed, jnp.exp(masked - row_top), 0.0)
        total = jnp.sum(exp_terms, -1, keepdims=True)
        attention_probabilities = exp_terms / total
        attended_rows = jnp.einsum(
            "sqk,skd->sqd",
            attention_probabilities.astype(jnp.bfloat16),
            head_cut(values_all, head_index),
            preferred_element_type=jnp.float32,
        )
        log_total = row_top[..., 0] + jnp.log(total[..., 0])
        peak = jnp.max(jnp.where(query_live, row_top[..., 0], NEG))
        return (attended_rows, log_total, peak)

    attended_rows, log_totals, peaks = lax.map(forward_head, jnp.arange(head_count))
    attn_low = attended_rows.transpose(1, 2, 0, 3).reshape(tokens, features).astype(jnp.bfloat16)
    attn_sum = lax.psum(matmul(attn_low, out_mat), "tp")
    hidden = resid + attn_sum + out_vec.astype(jnp.float32)
    normed_b, unit_two, inverse_two = normalize(
        hidden, gain_two.astype(jnp.float32), shift_two.astype(jnp.float32)
    )
    act_two = normed_b.astype(jnp.bfloat16)
    pre = matmul(act_two, up_mat) + up_vec.reshape(-1).astype(jnp.float32)
    gelu_low = jax.nn.gelu(pre, approximate=False).astype(jnp.bfloat16)
    mlp_sum = lax.psum(matmul(gelu_low, down_mat).astype(jnp.bfloat16), "tp").astype(jnp.float32)
    layer_output = hidden + mlp_sum + down_vec.astype(jnp.float32)
    peak_all = lax.pmax(peaks, ("fsdp", "ctx"))
    level = clip_level[0]
    factor = jnp.repeat(jnp.sqrt(level / jnp.maximum(peak_all, level)), head_size)
    query_clipped = (query_weight.astype(jnp.float32) * factor[None, :]).astype(jnp.bfloat16)
    key_clipped = (key_weight.astype(jnp.float32) * factor[None, :]).astype(jnp.bfloat16)
    grad_low = upstream.astype(jnp.bfloat16)
    down_weight_grad = weight_product(gelu_low, grad_low)
    down_bias_grad = jnp.sum(upstream, 0)
    cdf = 0.5 * (1.0 + lax.erf(pre * INV_ROOT_TWO))
    density = jnp.exp(-0.5 * pre * pre) * INV_ROOT_TWO_PI
    pre_grad = back_product(grad_low, down_mat) * (cdf + pre * density)
    pre_low = pre_grad.astype(jnp.bfloat16)
    up_weight_grad = weight_product(act_two, pre_low)
    up_bias_grad = jnp.sum(pre_grad, 0).reshape(up_vec.shape)
    normed_two_grad = lax.psum(back_product(pre_low, up_mat), "tp")
    hidden_in, mlp_gain_grad, mlp_shift_grad = norm_back(
        normed_two_grad, unit_two, inverse_two, gain_two.astype(jnp.float32)
    )
    hidden_grad = upstream + hidden_in
    hidden_low = hidden_grad.astype(jnp.bfloat16)
    out_weight_grad = weight_product(attn_low, hidden_low)
    out_bias_grad = jnp.sum(hidden_grad, 0)
    attended_grad = (
        back_product(hidden_low, out_mat)
        .astype(jnp.bfloat16)
        .reshape(per_group, local_rows, features)
    )

    def backward_head(head_index):
        head_queries = head_cut(queries, head_index)
        head_keys = head_cut(keys_all, head_index)
        head_values = head_cut(values_all, head_index)
        grad_head = head_cut(attended_grad, head_index)
        logit_scores = head_scores(head_queries, head_keys)
        masked = jnp.where(allowed, logit_scores, NEG)
        attention_probabilities = jnp.where(
            allowed, jnp.exp(masked - log_totals[head_index][..., None]), 0.0
        )
        prob_grad = jnp.einsum(
            "sqd,skd->sqk", grad_head, head_values, preferred_element_type=jnp.float32
        )
        inner = jnp.sum(attention_probabilities * prob_grad, -1, keepdims=True)
        score_grad = (attention_probabilities * (prob_grad - inner)).astype(jnp.bfloat16)
        query_grad = (
            jnp.einsum("sqk,skd->sqd", score_grad, head_keys, preferred_element_type=jnp.float32)
            * scale_of_scores
        )
        key_grad = (
            jnp.einsum("sqk,sqd->skd", score_grad, head_queries, preferred_element_type=jnp.float32)
            * scale_of_scores
        )
        value_grad = jnp.einsum(
            "sqk,sqd->skd",
            attention_probabilities.astype(jnp.bfloat16),
            grad_head,
            preferred_element_type=jnp.float32,
        )
        return (query_grad, key_grad, value_grad)

    query_parts, key_parts, value_parts = lax.map(backward_head, jnp.arange(head_count))
    query_grads = query_parts.transpose(1, 2, 0, 3).reshape(tokens, features)
    key_whole = key_parts.transpose(1, 2, 0, 3).reshape(per_group, ctx_count * local_rows, features)
    value_whole = value_parts.transpose(1, 2, 0, 3).reshape(
        per_group, ctx_count * local_rows, features
    )
    key_summed, value_summed = (
        lax.psum_scatter(key_whole, "ctx", scatter_dimension=1, tiled=True),
        lax.psum_scatter(value_whole, "ctx", scatter_dimension=1, tiled=True),
    )
    key_grads = key_summed.reshape(tokens, features)
    value_grads = value_summed.reshape(tokens, features)
    query_bias_grad = jnp.sum(query_grads, 0).reshape(head_count, head_size)
    value_bias_grad = jnp.sum(value_grads, 0).reshape(head_count, head_size)
    query_low = query_grads.astype(jnp.bfloat16)
    key_low = key_grads.astype(jnp.bfloat16)
    value_low = value_grads.astype(jnp.bfloat16)
    query_weight_grad = weight_product(act_one, query_low)
    key_weight_grad = weight_product(act_one, key_low)
    value_weight_grad = weight_product(act_one, value_low)
    normed_one_grad = lax.psum(
        (
            back_product(query_low, query_mat)
            + back_product(key_low, key_mat)
            + back_product(value_low, value_mat)
        ).astype(jnp.bfloat16),
        "tp",
    ).astype(jnp.float32)
    input_in, attn_gain_grad, attn_shift_grad = norm_back(
        normed_one_grad, unit_one, inverse_one, gain_one.astype(jnp.float32)
    )
    input_grad = hidden_grad + input_in
    partial_sums = (
        lax.psum_scatter(
            attn_gain_grad.astype(jnp.bfloat16), "fsdp", scatter_dimension=0, tiled=True
        ).astype(jnp.float32),
        lax.psum_scatter(
            attn_shift_grad.astype(jnp.bfloat16), "fsdp", scatter_dimension=0, tiled=True
        ).astype(jnp.float32),
        lax.psum_scatter(
            query_weight_grad.astype(jnp.bfloat16), "fsdp", scatter_dimension=0, tiled=True
        ).astype(jnp.float32),
        lax.psum_scatter(
            query_bias_grad.astype(jnp.bfloat16), "fsdp", scatter_dimension=1, tiled=True
        ).astype(jnp.float32),
        lax.psum_scatter(
            key_weight_grad.astype(jnp.bfloat16), "fsdp", scatter_dimension=0, tiled=True
        ).astype(jnp.float32),
        lax.psum_scatter(
            value_weight_grad.astype(jnp.bfloat16), "fsdp", scatter_dimension=0, tiled=True
        ).astype(jnp.float32),
        lax.psum_scatter(
            value_bias_grad.astype(jnp.bfloat16), "fsdp", scatter_dimension=1, tiled=True
        ).astype(jnp.float32),
        lax.psum_scatter(
            out_weight_grad.astype(jnp.bfloat16), "fsdp", scatter_dimension=1, tiled=True
        ).astype(jnp.float32),
        lax.psum_scatter(
            out_bias_grad.astype(jnp.bfloat16), "fsdp", scatter_dimension=0, tiled=True
        ).astype(jnp.float32),
        lax.psum_scatter(
            mlp_gain_grad.astype(jnp.bfloat16), "fsdp", scatter_dimension=0, tiled=True
        ).astype(jnp.float32),
        lax.psum_scatter(
            mlp_shift_grad.astype(jnp.bfloat16), "fsdp", scatter_dimension=0, tiled=True
        ).astype(jnp.float32),
        lax.psum_scatter(
            up_weight_grad.astype(jnp.bfloat16), "fsdp", scatter_dimension=0, tiled=True
        ).astype(jnp.float32),
        lax.psum_scatter(
            up_bias_grad.astype(jnp.bfloat16), "fsdp", scatter_dimension=1, tiled=True
        ).astype(jnp.float32),
        lax.psum_scatter(
            down_weight_grad.astype(jnp.bfloat16), "fsdp", scatter_dimension=1, tiled=True
        ).astype(jnp.float32),
        lax.psum_scatter(
            down_bias_grad.astype(jnp.bfloat16), "fsdp", scatter_dimension=0, tiled=True
        ).astype(jnp.float32),
    )
    shards = (
        lax.psum(partial_sums[0].astype(jnp.bfloat16), "ctx").astype(jnp.float32),
        lax.psum(partial_sums[1].astype(jnp.bfloat16), "ctx").astype(jnp.float32),
        lax.psum(partial_sums[2].astype(jnp.bfloat16), "ctx").astype(jnp.float32),
        lax.psum(partial_sums[3].astype(jnp.bfloat16), "ctx").astype(jnp.float32),
        lax.psum(partial_sums[4].astype(jnp.bfloat16), "ctx").astype(jnp.float32),
        lax.psum(partial_sums[5].astype(jnp.bfloat16), "ctx").astype(jnp.float32),
        lax.psum(partial_sums[6].astype(jnp.bfloat16), "ctx").astype(jnp.float32),
        lax.psum(partial_sums[7].astype(jnp.bfloat16), "ctx").astype(jnp.float32),
        lax.psum(partial_sums[8].astype(jnp.bfloat16), "ctx").astype(jnp.float32),
        lax.psum(partial_sums[9].astype(jnp.bfloat16), "ctx").astype(jnp.float32),
        lax.psum(partial_sums[10].astype(jnp.bfloat16), "ctx").astype(jnp.float32),
        lax.psum(partial_sums[11].astype(jnp.bfloat16), "ctx").astype(jnp.float32),
        lax.psum(partial_sums[12].astype(jnp.bfloat16), "ctx").astype(jnp.float32),
        lax.psum(partial_sums[13].astype(jnp.bfloat16), "ctx").astype(jnp.float32),
        lax.psum(partial_sums[14].astype(jnp.bfloat16), "ctx").astype(jnp.float32),
    )
    sent_output = layer_output.reshape(1, per_group, local_rows, width)
    sent_grad = input_grad.reshape(1, per_group, local_rows, width)
    back_output, back_grad = (
        lax.all_to_all(
            sent_output.astype(jnp.bfloat16), "fsdp", split_axis=2, concat_axis=0, tiled=True
        ).astype(sent_output.dtype),
        lax.all_to_all(
            sent_grad.astype(jnp.bfloat16), "fsdp", split_axis=2, concat_axis=0, tiled=True
        ).astype(sent_grad.dtype),
    )
    final_output = back_output.reshape(slot_count, block_rows, width)
    final_grad = back_grad.reshape(slot_count, block_rows, width)
    return (
        final_output,
        final_grad,
        shards[0],
        shards[1],
        shards[2],
        shards[3],
        shards[4],
        shards[5],
        shards[6],
        shards[7],
        shards[8],
        shards[9],
        shards[10],
        shards[11],
        shards[12],
        shards[13],
        shards[14],
        peak_all,
        query_clipped,
        key_clipped,
    )


def attention_probs(query_block, key_rows, block, length):
    rows, cols = query_block.shape[0], key_rows.shape[0]
    scores = lax.dot_general(
        query_block, key_rows, (((1,), (1,)), ((), ())), preferred_element_type=jnp.float32
    ) * (1.0 / math.sqrt(query_block.shape[1]))
    row_pos = block * rows + lax.broadcasted_iota(jnp.int32, (rows, cols), 0)
    col_pos = lax.broadcasted_iota(jnp.int32, (rows, cols), 1)
    scores = jnp.where((col_pos <= row_pos) & (col_pos < length), scores, NEG)
    top = jnp.max(scores, -1, keepdims=True)
    terms = jnp.exp(scores - top)
    return terms / jnp.sum(terms, -1, keepdims=True), top


def entry_barrier(targets):
    barrier = pltpu.get_barrier_semaphore()
    for target in targets:
        pl.semaphore_signal(barrier, inc=1, device_id=target, device_id_type=pl.DeviceIdType.MESH)
    pl.semaphore_wait(barrier, len(targets))


def remote_copy(src, dst, send, recv, target):
    return pltpu.make_async_remote_copy(
        src_ref=src,
        dst_ref=dst,
        send_sem=send,
        recv_sem=recv,
        device_id=target,
        device_id_type=pl.DeviceIdType.MESH,
    )


def grant(semaphore, target):
    pl.semaphore_signal(semaphore, inc=1, device_id=target, device_id_type=pl.DeviceIdType.MESH)


def aligned(start, size):
    return pl.ds(pl.multiple_of(start, 128), size)


class Place:
    def __init__(self, depth):
        self.depth = depth
        f = lax.axis_index("fsdp")
        z = lax.axis_index("ctx")
        t = lax.axis_index("tp")
        y, x = f // 2, f % 2
        self.f, self.z, self.t, self.y, self.x = f, z, t, y, x
        self.over_x = {"fsdp": 2 * y + 1 - x, "ctx": z, "tp": t}
        self.over_y = {"fsdp": 2 * (1 - y) + x, "ctx": z, "tp": t}
        self.over_core = {"fsdp": f, "ctx": z, "tp": 1 - t}
        self.mate = {"fsdp": f, "ctx": z + 1 - 2 * (z % 2), "tp": t}
        self.middle = {"fsdp": f, "ctx": 3 - z, "tp": t}
        self.hop = {"fsdp": f, "ctx": lax.rem(z + 2, 4), "tp": t}
        self.homes = (2 * y + 1 - x, 2 * (1 - y) + 1 - x, f, 2 * (1 - y) + x)

    def row_target(self, k):
        return {"fsdp": 2 * self.y + self.t, "ctx": k, "tp": self.x}

    def row_targets(self):
        others = [self.row_target(lax.rem(self.z + k, self.depth)) for k in range(1, self.depth)]
        return others + [{"fsdp": 2 * self.y + 1 - self.x, "ctx": self.z, "tp": 1 - self.t}]

    def block_place(self, block):
        return 2 * jnp.where(self.y == block // 2, 0, 1) + jnp.where(self.t == block % 2, 0, 1)


def reduce_stages(p, items, scratch):
    (
        x_slot,
        made_slot,
        own_slot,
        pair_slot,
        y_slot,
        z_slot,
        z_pair,
        inner_slot,
        total_slot,
        x_send,
        x_recv,
        y_send,
        y_recv,
        outer_send,
        outer_recv,
        inner_send,
        inner_recv,
        out_sem,
        x_free,
        y_free,
        outer_free,
        inner_free,
    ) = scratch
    y, z = p.y, p.z
    outer = (z == 0) | (z == 3)
    inner = (z == 1) | (z == 2)
    slots = x_slot.shape[0]
    count = len(items)
    far_count = count // 2
    far_slots = y_slot.shape[0]

    def x_copy(i):
        k = i % slots
        return remote_copy(made_slot.at[k], x_slot.at[k], x_send.at[k], x_recv.at[k], p.over_x)

    def y_copy(i):
        k, g = i % slots, (i // 2) % far_slots
        return remote_copy(pair_slot.at[k], y_slot.at[g], y_send.at[g], y_recv.at[g], p.over_y)

    def summed(i):
        return y_slot.at[(i // 2) % far_slots] if items[i][0] else pair_slot.at[i % slots]

    def outward(i):
        k = i % slots
        return remote_copy(summed(i), z_slot.at[k], outer_send.at[k], outer_recv.at[k], p.mate)

    def across(i):
        k = i % slots
        return remote_copy(z_pair.at[k], inner_slot.at[k], inner_send.at[k], inner_recv.at[k], p.middle)

    def backward(i):
        k = i % slots
        return remote_copy(total_slot.at[k], z_slot.at[k], outer_send.at[k], outer_recv.at[k], p.mate)

    def result_inner(i):
        k = i % slots
        return pltpu.make_async_copy(total_slot.at[k], items[i][1], out_sem.at[k])

    def result_outer(i):
        k = i % slots
        return pltpu.make_async_copy(z_slot.at[k], items[i][1], out_sem.at[k])

    def add(left, right, target):
        target[...] = (left[...].astype(jnp.float32) + right[...].astype(jnp.float32)).astype(
            target.dtype
        )

    def stage_send(i):
        k = i % slots
        items[i][2](made_slot.at[k], own_slot.at[k])
        if i >= slots:
            pl.semaphore_wait(x_free, 1)
        x_copy(i).start()

    def stage_pair(i):
        x_copy(i).wait()
        k = i % slots
        add(x_slot.at[k], own_slot.at[k], pair_slot.at[k])
        if i + slots < count:
            grant(x_free, p.over_x)
        if items[i][0]:
            if i // 2 >= far_slots:
                pl.semaphore_wait(y_free, 1)
            y_copy(i).start()

    def stage_outward(i):
        if items[i][0]:
            y_copy(i).wait()

        @pl.when(outer)
        def _():
            if i >= slots:
                pl.semaphore_wait(outer_free, 1)
            outward(i).start()

    def stage_across(i):
        k = i % slots

        @pl.when(outer)
        def _():
            outward(i).wait_send()

        @pl.when(inner)
        def _():
            outward(i).wait_recv()
            add(summed(i), z_slot.at[k], z_pair.at[k])
            if i + slots < count:
                grant(outer_free, p.mate)
            if i >= slots:
                pl.semaphore_wait(inner_free, 1)
            across(i).start()

        if items[i][0] and i // 2 + far_slots < far_count:
            grant(y_free, p.over_y)

    def stage_total(i):
        k = i % slots

        @pl.when(inner)
        def _():
            across(i).wait()
            add(z_pair.at[k], inner_slot.at[k], total_slot.at[k])
            if i + slots < count:
                grant(inner_free, p.middle)
            if i >= slots:
                pl.semaphore_wait(outer_free, 1)
            backward(i).start()
            result_inner(i).start()

    def stage_result(i):
        @pl.when(inner)
        def _():
            backward(i).wait_send()
            result_inner(i).wait()

        @pl.when(outer)
        def _():
            backward(i).wait_recv()
            result_outer(i).start()

    def stage_finish(i):
        @pl.when(outer)
        def _():
            result_outer(i).wait()
            if i + slots < count:
                grant(outer_free, p.mate)

    stages = (
        (11, stage_finish),
        (10, stage_result),
        (8, stage_total),
        (6, stage_across),
        (4, stage_outward),
        (2, stage_pair),
        (0, stage_send),
    )

    def run(step):
        for lag, stage in stages:
            if 0 <= step - lag < count:
                stage(step - lag)

    return run, count + 12


def reduce_scratch(slots, far_slots, rows, cols):
    dma, regular = pltpu.SemaphoreType.DMA, pltpu.SemaphoreType.REGULAR
    counts = (slots,) * 4 + (far_slots,) + (slots,) * 4
    return [pltpu.VMEM((n, rows, cols), jnp.bfloat16) for n in counts] + [
        dma((n,)) for n in (slots,) * 2 + (far_slots,) * 2 + (slots,) * 5
    ] + [regular] * 4


PARTS = 4


class RowSum:
    def __init__(self, p, rows, arrived, sent, loaded, send_sem, recv_sem, load_sem, core_free, y_free, uses):
        self.p, self.rows, self.uses = p, rows, uses
        self.arrived, self.sent, self.loaded = arrived, sent, loaded
        self.send_sem, self.recv_sem, self.load_sem = send_sem, recv_sem, load_sem
        self.core_free, self.y_free = core_free, y_free

    def block(self, ref, k):
        return ref.at[pl.ds(k * self.rows, self.rows), :]

    def hop(self, ref, k):
        return remote_copy(
            self.block(ref, 3 - 2 * k),
            self.arrived.at[k],
            self.send_sem.at[k],
            self.recv_sem.at[k],
            self.p.over_core,
        )

    def hop_y(self, part):
        size = self.rows // PARTS
        cut = pl.ds(part * size, size)
        return remote_copy(
            self.sent.at[cut, :],
            self.arrived.at[2, cut, :],
            self.send_sem.at[2 + part],
            self.recv_sem.at[2 + part],
            self.p.over_y,
        )

    def load(self, ref, k):
        return pltpu.make_async_copy(self.block(ref, k), self.loaded, self.load_sem)

    def start(self, use, ref, local):
        if use:
            pl.semaphore_wait(self.core_free, 1)
            pl.semaphore_wait(self.y_free, 1)
        self.hop(ref, 0).start()
        self.hop(ref, 1).start()
        if not local:
            self.load(ref, 2).start()

    def middle(self, ref, local, part):
        if part == 0:
            self.hop(ref, 0).wait()
            if not local:
                self.load(ref, 2).wait()
        base = self.block(ref, 2) if local else self.loaded
        size = self.rows // PARTS

        @pl.loop(part * size // 32, (part + 1) * size // 32)
        def _(k):
            at = pl.ds(pl.multiple_of(k * 32, 32), 32)
            self.sent[at, :] = (
                base[at, :].astype(jnp.float32) + self.arrived[0, at, :].astype(jnp.float32)
            ).astype(jnp.bfloat16)

        self.hop_y(part).start()
        if part == PARTS - 1 and not local:
            self.load(ref, 0).start()

    def finish(self, ref, local):
        self.hop(ref, 1).wait()
        for part in range(PARTS):
            self.hop_y(part).wait()
        if not local:
            self.load(ref, 0).wait()

    def total(self, ref, local, at):
        base = self.block(ref, 0) if local else self.loaded
        return (
            base[at, :].astype(jnp.float32)
            + self.arrived[1, at, :].astype(jnp.float32)
            + self.arrived[2, at, :].astype(jnp.float32)
        )

    def release(self, use):
        if use + 1 < self.uses:
            grant(self.core_free, self.p.over_core)
            grant(self.y_free, self.p.over_y)


def unit_rows(values):
    center = values - jnp.mean(values, -1, keepdims=True)
    inverse = lax.rsqrt(jnp.mean(center * center, -1, keepdims=True) + EPS)
    return center * inverse, inverse


def unit_back(upstream, unit, inverse, gain):
    scaled = upstream * gain
    return inverse * (
        scaled
        - jnp.mean(scaled, -1, keepdims=True)
        - unit * jnp.mean(scaled * unit, -1, keepdims=True)
    )


GAIN_ONE, SHIFT_ONE, OUT_BIAS, GAIN_TWO, SHIFT_TWO, DOWN_BIAS, QUERY_BIAS, VALUE_BIAS, UP_BIAS, PEAKS = (
    0,
    1,
    2,
    3,
    4,
    5,
    6,
    7,
    8,
    12,
)


def prepare_kernel(dealing, lengths, place, rows_ref, cot_ref, rows_out, cot_out, bias_ref):
    step = pl.program_id(0)
    rows_out[...] = rows_ref[...]
    cot = cot_ref[...]
    cot_out[...] = cot.astype(cot_out.dtype)

    @pl.when(step == 0)
    def _():
        bias_ref[...] = jnp.zeros_like(bias_ref)

    bias_ref[pl.ds(0, 1), :] += jnp.sum(cot[0], 0, keepdims=True)


def prepare(dealing, seq_lengths, place, layer_input, cotangent, count):
    block = (1,) + layer_input.shape[1:]
    width = layer_input.shape[2]
    return pl.pallas_call(
        prepare_kernel,
        out_shape=(
            jax.ShapeDtypeStruct((count,) + block[1:], jnp.float32),
            jax.ShapeDtypeStruct((count,) + block[1:], jnp.bfloat16),
            jax.ShapeDtypeStruct((8, width), jnp.float32),
        ),
        grid_spec=pltpu.PrefetchScalarGridSpec(
            num_scalar_prefetch=3,
            grid=(count,),
            in_specs=[
                pl.BlockSpec(block, lambda j, dealing, lengths, place: (dealing[place[0] * count + j], 0, 0)),
                pl.BlockSpec(block, lambda j, dealing, lengths, place: (place[0] * count + j, 0, 0)),
            ],
            out_specs=(
                pl.BlockSpec(block, lambda j, *_: (j, 0, 0)),
                pl.BlockSpec(block, lambda j, *_: (j, 0, 0)),
                pl.BlockSpec((8, width), lambda j, *_: (0, 0)),
            ),
        ),
    )(dealing, seq_lengths, place, layer_input, cotangent)


def finish_kernel(head_size, place, level_ref, totals_ref, query_ref, key_ref, *refs):
    count = (len(refs) - 3) // 2
    for source, target in zip(refs[:count], refs[count : 2 * count]):
        target[...] = source[...].astype(target.dtype)
    query_out, key_out, factor = refs[2 * count :]
    level = level_ref[0]
    heads = factor.shape[1] // head_size

    @pl.when(pl.program_id(0) == 0)
    def _():
        peaks = totals_ref[pl.ds(PEAKS, 1), :]
        lane = lax.broadcasted_iota(jnp.int32, peaks.shape, 1)
        for h in range(heads):
            mine = jnp.where(lane == place[0] * heads + h, peaks, NEG)
            peak = jnp.max(mine, -1, keepdims=True)
            value = jnp.sqrt(level / jnp.maximum(peak, level))
            factor[:, pl.ds(h * head_size, head_size)] = jnp.broadcast_to(value, (8, head_size))

    scale = factor[pl.ds(0, 1), :]
    query_out[...] = (query_ref[...].astype(jnp.float32) * scale).astype(query_out.dtype)
    key_out[...] = (key_ref[...].astype(jnp.float32) * scale).astype(key_out.dtype)


def finish_all(head_size, place, level, totals, query_weight, key_weight, arrays):
    steps = 8

    def spec(v):
        block = (v.shape[0] // steps,) + v.shape[1:]
        return pl.BlockSpec(block, lambda i: (i,) + (0,) * (v.ndim - 1))

    smem = pl.BlockSpec(memory_space=pltpu.SMEM)
    weights = (query_weight, key_weight)
    return pl.pallas_call(
        functools.partial(finish_kernel, head_size),
        out_shape=tuple(jax.ShapeDtypeStruct(v.shape, jnp.float32) for v in arrays)
        + tuple(jax.ShapeDtypeStruct(v.shape, v.dtype) for v in weights),
        grid=(steps,),
        in_specs=[smem, smem, pl.BlockSpec(totals.shape, lambda i: (0, 0))]
        + [spec(v) for v in weights]
        + [spec(v) for v in arrays],
        out_specs=tuple(spec(v) for v in arrays) + tuple(spec(v) for v in weights),
        scratch_shapes=[pltpu.VMEM((8, query_weight.shape[1]), jnp.float32)],
        compiler_params=pltpu.CompilerParams(vmem_limit_bytes=60 << 20),
    )(place, level, totals, *weights, *arrays)


def forward_kernel(
    head_size,
    info,
    vec_hbm,
    head_hbm,
    q_ref,
    k_ref,
    v_ref,
    o_ref,
    u_ref,
    d_ref,
    arrived_hbm,
    cot_hbm,
    qkv_mat_out,
    out_mat_out,
    up_all,
    down_out,
    act_out,
    cot_out,
    qkv_out,
    attended_out,
    hidden_out,
    resid_out,
    two_out,
    back_out,
    vec_all,
    peaks,
    cot_all,
    down_all,
    back_stage,
    qkv_mat,
    out_mat,
    fresh,
    part,
    act,
    hidden,
    qkv,
    keys,
    values,
    attended,
    partial,
    arrived,
    sent,
    two,
    vec_own,
    head_own,
    head_got,
    qkv_bias,
    local_sem,
    send_sem,
    recv_sem,
    row_send,
    row_recv,
    join_send,
    join_recv,
    vec_send,
    vec_recv,
    load_sem,
    sum_send,
    sum_recv,
    out_sem,
):
    f32, bf16 = jnp.float32, jnp.bfloat16
    depth, block_rows, width = arrived_hbm.shape
    own_rows = depth * block_rows
    strip = q_ref.shape[0]
    features = q_ref.shape[1] // 2
    units = u_ref.shape[1] // 2
    heads = features // head_size
    p = Place(depth)
    f, x, y, z, t = p.f, p.x, p.y, p.z, p.t
    even = z % 2 == 0
    odd = jnp.logical_not(even)
    diagonal = {"fsdp": 3 - f, "ctx": z, "tp": t}
    entry_barrier([p.over_x, p.over_y, p.mate, p.over_core, diagonal] + p.row_targets())
    length = info[0]

    chunks = []
    rows = strip // 2
    for k, ref in enumerate((q_ref, k_ref, v_ref)):
        for r in range(2):
            chunks.append(
                (
                    lambda w, ref=ref, r=r: ref.at[pl.ds(r * rows, rows), aligned(w * features, features)],
                    lambda home, k=k, r=r: qkv_mat.at[
                        aligned(home * strip + r * rows, rows), pl.ds(k * features, features)
                    ],
                )
            )
    for r in range(2):
        chunks.append(
            (
                lambda w, r=r: o_ref.at[aligned(w * features + r * rows, rows), :],
                lambda home, r=r: out_mat.at[pl.ds(r * rows, rows), aligned(home * strip, strip)],
            )
        )
    pieces = 8
    for r in range(pieces):
        size = strip // pieces
        chunks.append(
            (
                lambda w, r=r, size=size: u_ref.at[pl.ds(r * size, size), aligned(w * units, units)],
                lambda home, r=r, size=size: up_all.at[
                    pl.ds(pl.multiple_of(home * strip + r * size, size), size), :
                ],
            )
        )
    for r in range(pieces):
        size = units // pieces
        chunks.append(
            (
                lambda w, r=r, size=size: d_ref.at[aligned(w * units + r * size, size), :],
                lambda home, r=r, size=size: down_all.at[pl.ds(r * size, size), aligned(home * strip, strip)],
            )
        )
    count = len(chunks)
    far_home = 2 * (1 - y) + x

    def own_copy(i):
        source, place = chunks[i]
        return pltpu.make_async_copy(source(y), place(f), local_sem.at[i])

    def y_copy(i):
        source, place = chunks[i]
        return remote_copy(source(1 - y), place(f), send_sem.at[0, i], recv_sem.at[0, i], p.over_y)

    def x_copy(i, is_even):
        source, place = chunks[i]
        start = source(y) if is_even else place(far_home)
        home = f if is_even else far_home
        return remote_copy(start, place(home), send_sem.at[1, i], recv_sem.at[1, i], p.over_x)

    def z_copy(i, is_even):
        place = chunks[i][1]
        home = 2 * y + 1 - x if is_even else 2 * (1 - y) + 1 - x
        return remote_copy(place(home), place(home), send_sem.at[2, i], recv_sem.at[2, i], p.mate)

    rows_of = ((part, act), (cot_hbm, cot_all), (arrived_hbm, hidden))

    def row_copy(a, k):
        source, place = rows_of[a]
        return remote_copy(
            source.at[k],
            place.at[pl.ds(pl.multiple_of(z * block_rows, block_rows), block_rows), :],
            row_send.at[a, k],
            row_recv.at[a, z],
            p.row_target(k),
        )

    def row_arrival(a, k):
        source, place = rows_of[a]
        return remote_copy(
            source.at[k],
            place.at[pl.ds(k * block_rows, block_rows), :],
            row_send.at[a, k],
            row_recv.at[a, k],
            p.row_target(k),
        )

    def row_stay(a, k):
        source, place = rows_of[a]
        return pltpu.make_async_copy(
            source.at[k], place.at[pl.ds(k * block_rows, block_rows), :], row_send.at[a, k]
        )

    def rows_start(a):
        for k in range(depth):
            stays = (z == k) & (x == t)
            pl.when(stays)(lambda k=k: row_stay(a, k).start())
            pl.when(jnp.logical_not(stays))(lambda k=k: row_copy(a, k).start())

    def rows_wait(a):
        for k in range(depth):
            stays = (z == k) & (x == t)
            pl.when(stays)(lambda k=k: row_stay(a, k).wait())

            @pl.when(jnp.logical_not(stays))
            def _(k=k):
                row_copy(a, k).wait_send()
                row_arrival(a, k).wait_recv()

    joined = (act, cot_all, two)

    def block(ref, k):
        return ref.at[pl.ds(k * own_rows, own_rows), :]

    def join(a, step):
        source, place, target = ((0, 1, p.over_core), (0, 2, p.over_y), (2, 3, p.over_core))[step]
        ref = joined[a]
        return remote_copy(
            block(ref, source), block(ref, place), join_send.at[a, step], join_recv.at[a, step], target
        )

    def join_start(a):
        join(a, 0).start()
        join(a, 1).start()

    def join_pass(a):
        join(a, 1).wait_recv()
        join(a, 2).start()

    def join_end(a):
        join(a, 0).wait()
        join(a, 1).wait_send()
        join(a, 2).wait()

    def vec_place(ref):
        return ref.at[:, aligned(f * strip, strip)]

    vec_targets = (p.over_x, p.over_y, diagonal)

    def vec_copy(k):
        return remote_copy(vec_own, vec_place(vec_all), vec_send.at[0, k], vec_recv.at[0, k], vec_targets[k])

    def head_copy(k):
        return remote_copy(head_own, head_got.at[k], vec_send.at[1, k], vec_recv.at[1, k], vec_targets[k])

    loads = [
        pltpu.make_async_copy(source, target, load_sem.at[k])
        for k, (source, target) in enumerate(
            ((vec_hbm, vec_own), (head_hbm, head_own), (arrived_hbm, fresh))
        )
    ]

    def begin():
        for load in loads:
            load.start()
        loads[0].wait()
        loads[1].wait()
        for k in range(3):
            vec_copy(k).start()
            head_copy(k).start()
        vec_place(vec_all)[...] = vec_own[...]
        peaks[...] = jnp.full_like(peaks, NEG)

    def vector_row(k):
        return vec_all[pl.ds(k, 1), :]

    group_rows = 16

    def first_norm():
        for k in range(3):
            vec_copy(k).wait()
            head_copy(k).wait()
        loads[2].wait()
        for k in range(3):
            head_own[...] += head_got[k]
        qkv_bias[...] = jnp.zeros_like(qkv_bias)
        for h in range(heads):
            lanes = pl.ds(h * head_size, head_size)
            qkv_bias[pl.ds(0, 1), lanes] = head_own[pl.ds(heads * y + h, 1), :]
            lanes = pl.ds(2 * features + h * head_size, head_size)
            qkv_bias[pl.ds(0, 1), lanes] = head_own[pl.ds(2 * heads + heads * y + h, 1), :]
        gain, shift = vector_row(GAIN_ONE), vector_row(SHIFT_ONE)
        for s in range(depth):

            @pl.loop(0, block_rows // group_rows)
            def _(k, s=s):
                at = pl.ds(pl.multiple_of(k * group_rows, group_rows), group_rows)
                unit, _ = unit_rows(fresh[s, at, :])
                part[s, at, :] = (unit * gain + shift).astype(bf16)

        rows_start(0)

    def weights_wait(start, stop):
        for i in range(start, stop):
            own_copy(i).wait()
            z_copy(i, True).wait_recv()

    kept, used = [], [0]

    def keep(source, target):
        copy = pltpu.make_async_copy(source, target, out_sem.at[used[0]])
        used[0] += 1
        copy.start()
        kept.append(copy)

    def project(k):
        at = pl.ds(k * own_rows, own_rows)

        @pl.loop(0, 3)
        def _(c):
            cut = aligned(c * features, features)
            qkv[at, cut] = (
                jnp.dot(act[at, :], qkv_mat[:, cut], preferred_element_type=f32)
                + qkv_bias[pl.ds(0, 1), cut]
            ).astype(bf16)

    def head_rows():
        for b in range(4):
            at = pl.ds(pl.multiple_of(p.block_place(b) * own_rows, own_rows), own_rows)
            keys[pl.ds(b * own_rows, own_rows), :] = qkv[at, pl.ds(features, features)]
            values[pl.ds(b * own_rows, own_rows), :] = qkv[at, pl.ds(2 * features, features)]

    def attention_block(b):
        at = pl.ds(pl.multiple_of(p.block_place(b) * own_rows, own_rows), own_rows)
        past = pl.ds(0, (b + 1) * own_rows)

        @pl.loop(0, heads)
        def _(head):
            lanes = aligned(head * head_size, head_size)
            probs, top = attention_probs(qkv[at, lanes], keys[past, lanes], b, length)
            attended[at, lanes] = jnp.dot(
                probs.astype(bf16), values[past, lanes], preferred_element_type=f32
            ).astype(bf16)
            live = b * own_rows + lax.broadcasted_iota(jnp.int32, top.shape, 0) < length
            peak = jnp.max(jnp.where(live, top, NEG), 0, keepdims=True)
            row = pl.ds(head, 1)
            peaks[row, :] = jnp.maximum(peaks[row, :], jnp.broadcast_to(peak, (1, peaks.shape[1])))

    sums = RowSum(p, own_rows, arrived, sent, None, sum_send, sum_recv, None, None, None, 1)

    def out_block(k):
        at = pl.ds(k * own_rows, own_rows)

        @pl.loop(0, 4)
        def _(n):
            cut = aligned(n * strip, strip)
            partial[at, cut] = jnp.dot(
                attended[at, :], out_mat[:, cut], preferred_element_type=f32
            ).astype(bf16)

    spot = []

    def keep_resid():
        spot.append(len(kept))
        keep(hidden, resid_out)

    back_sem = [out_sem.at[10], out_sem.at[11]]
    unit_rows_per_chunk = units // pieces

    def back_store(r):
        cut = pl.ds(r * unit_rows_per_chunk, unit_rows_per_chunk)
        return pltpu.make_async_copy(back_stage.at[r % 2], back_out.at[:, cut], back_sem[r % 2])

    def back_chunk(r):
        weights_wait(8 + pieces + r, 9 + pieces + r)
        if r >= 2:
            back_store(r - 2).wait()

        @pl.loop(0, 4)
        def _(b):
            at = pl.ds(pl.multiple_of(b * own_rows, own_rows), own_rows)
            back_stage[r % 2, at, :] = lax.dot_general(
                cot_all[at, :],
                down_all[pl.ds(r * unit_rows_per_chunk, unit_rows_per_chunk), :],
                (((1,), (1,)), ((), ())),
                preferred_element_type=f32,
            ).astype(bf16)

        back_store(r).start()

    def second_norm():
        sums.finish(partial, True)
        kept.pop(spot[0]).wait()
        bias, gain, shift = vector_row(OUT_BIAS), vector_row(GAIN_TWO), vector_row(SHIFT_TWO)

        @pl.loop(0, own_rows // group_rows)
        def _(k):
            at = pl.ds(pl.multiple_of(k * group_rows, group_rows), group_rows)
            value = hidden[at, :] + sums.total(partial, True, at) + bias
            hidden[at, :] = value
            unit, _ = unit_rows(value)
            two[at, :] = (unit * gain + shift).astype(bf16)

        join_start(2)
        keep(hidden, hidden_out)

    def call(function, *arguments):
        return lambda: function(*arguments)

    plan = {}

    def at_step(step, *tasks):
        plan.setdefault(step, []).extend(tasks)

    at_step(0, begin)
    at_step(1, first_norm)
    at_step(5, call(rows_wait, 0), call(join_start, 0), call(rows_start, 1))
    at_step(10, call(rows_start, 2))
    at_step(10, call(rows_wait, 1), call(join_start, 1), call(join_pass, 0))
    at_step(18, call(join_pass, 1))
    at_step(11, call(weights_wait, 0, 6), call(project, 0))
    at_step(12, join(0, 0).wait, call(project, 1), lambda: keep(qkv_mat, qkv_mat_out))
    at_step(13, join(0, 1).wait_send, join(0, 2).wait, call(project, 2), lambda: keep(act, act_out))
    at_step(14, call(project, 3), head_rows, lambda: keep(qkv, qkv_out))
    at_step(15, call(attention_block, 0), call(attention_block, 1))
    at_step(16, call(attention_block, 2))
    at_step(17, call(attention_block, 3), lambda: keep(attended, attended_out))
    at_step(18, call(weights_wait, 6, 8), call(out_block, 3), call(out_block, 1))
    at_step(18, call(sums.start, 0, partial, True))
    at_step(19, call(out_block, 2), *(call(sums.middle, partial, True, part) for part in range(PARTS)))
    at_step(19, call(out_block, 0), lambda: keep(out_mat, out_mat_out))
    at_step(19, call(rows_wait, 2), keep_resid)
    at_step(21, call(join_end, 1), lambda: keep(cot_all, cot_out))
    at_step(23, call(back_chunk, 0))
    at_step(24, second_norm)
    at_step(24, call(back_chunk, 1))
    at_step(25, call(back_chunk, 2))
    at_step(26, call(back_chunk, 3))
    at_step(27, call(join_pass, 2), call(back_chunk, 4))
    lag = 2
    for i in range(count + 2 * lag):
        if i < count:
            y_copy(i).start()
            pl.when(even)(lambda i=i: x_copy(i, True).start())
            own_copy(i).start()
        j = i - lag
        if 0 <= j < count:
            y_copy(j).wait_recv()

            @pl.when(even)
            def _(j=j):
                x_copy(j, True).wait_recv()
                z_copy(j, True).start()

            pl.when(odd)(lambda j=j: x_copy(j, False).start())
        j = i - 2 * lag
        if 0 <= j < count:

            @pl.when(odd)
            def _(j=j):
                x_copy(j, False).wait_recv()
                z_copy(j, False).start()

        for task in plan.get(i, ()):
            task()

    for r in range(5, pieces):
        back_chunk(r)
    keep(down_all, down_out)
    join_end(2)
    keep(two, two_out)
    weights_wait(8, 8 + pieces)
    back_store(pieces - 2).wait()
    back_store(pieces - 1).wait()
    for i in range(count):
        y_copy(i).wait_send()
        x_copy(i, True).wait_send()
        z_copy(i, True).wait_send()
    for copy in kept:
        copy.wait()


def forward_all(
    head_size,
    length,
    vectors,
    head_vectors,
    query_weight,
    key_weight,
    value_weight,
    out_weight,
    up_weight,
    down_weight,
    arrived,
    cot,
):
    strip, features, units = query_weight.shape[0], query_weight.shape[1] // 2, up_weight.shape[1] // 2
    width = 4 * strip
    depth, block_rows = arrived.shape[:2]
    own_rows = depth * block_rows
    tokens = 4 * own_rows
    bf16, f32 = jnp.bfloat16, jnp.float32
    hbm = pl.BlockSpec(memory_space=pl.ANY)
    vmem = pl.BlockSpec(memory_space=pltpu.VMEM)
    count = 24
    dma = pltpu.SemaphoreType.DMA

    def made(shape, dtype=bf16):
        return jax.ShapeDtypeStruct(shape, dtype)

    def hold(shape, dtype=bf16):
        return pltpu.VMEM(shape, dtype)

    return pl.pallas_call(
        functools.partial(forward_kernel, head_size),
        out_shape=(
            made((width, 3 * features)),
            made((features, width)),
            made((width, units)),
            made((units, width)),
            made((tokens, width)),
            made((tokens, width)),
            made((tokens, 3 * features)),
            made((tokens, features)),
            made((own_rows, width), f32),
            made((own_rows, width), f32),
            made((tokens, width)),
            made((tokens, units)),
            made((8, width), f32),
            made((8, 128), f32),
        ),
        in_specs=[pl.BlockSpec(memory_space=pltpu.SMEM)] + [hbm] * 10,
        out_specs=(hbm,) * 12 + (vmem,) * 2,
        scratch_shapes=[
            hold((tokens, width)),
            hold((units, width)),
            hold((2, tokens, units // 8)),
            hold((width, 3 * features)),
            hold((features, width)),
            hold((depth, block_rows, width), f32),
            hold((depth, block_rows, width)),
            hold((tokens, width)),
            hold((own_rows, width), f32),
            hold((tokens, 3 * features)),
            hold((tokens, features)),
            hold((tokens, features)),
            hold((tokens, features)),
            hold((tokens, width)),
            hold((3, own_rows, width)),
            hold((own_rows, width)),
            hold((tokens, width)),
            hold((8, strip), f32),
            hold(head_vectors.shape, f32),
            hold((3,) + head_vectors.shape, f32),
            hold((8, 3 * features), f32),
            dma((count,)),
            dma((3, count)),
            dma((3, count)),
            dma((3, depth)),
            dma((3, depth)),
            dma((3, 3)),
            dma((3, 3)),
            dma((2, 3)),
            dma((2, 3)),
            dma((3,)),
            dma((2 + PARTS,)),
            dma((2 + PARTS,)),
            dma((12,)),
        ],
        compiler_params=pltpu.CompilerParams(
            collective_id=0, has_side_effects=True, vmem_limit_bytes=56 << 20
        ),
        cost_estimate=pl.CostEstimate(flops=0, bytes_accessed=64 << 20, transcendentals=0),
    )(
        length,
        vectors,
        head_vectors,
        query_weight,
        key_weight,
        value_weight,
        out_weight,
        up_weight,
        down_weight,
        arrived,
        cot,
    )


def backward_kernel(
    head_size,
    info,
    vector_ref,
    small_in,
    gelu_hbm,
    pre_hbm,
    act_two_hbm,
    up_hbm,
    down_hbm,
    hidden_hbm,
    cot_hbm,
    resid_hbm,
    out_hbm,
    qkv_mat_hbm,
    qkv_hbm,
    attended_hbm,
    act_hbm,
    down_sum,
    up_sum,
    out_sum,
    qkv_sums,
    rows_out,
    rows_grad,
    small,
    two_part,
    mlp_part,
    engine,
    base,
    hidden_grad,
    low,
    out_mat,
    attended_grad,
    qkv,
    qkv_grad,
    act,
    attended,
    qkv_mat,
    keys,
    values,
    key_sum,
    value_sum,
    strips,
    packed,
    arrived,
    sent,
    loaded,
    small_arrived,
    load_sem,
    sum_send,
    sum_recv,
    sum_load,
    join_send,
    join_recv,
    strip_sem,
    row_send,
    row_recv,
    share_send,
    share_recv,
    small_send,
    small_recv,
    core_free,
    y_free,
    low_core,
    low_y,
):
    f32, bf16 = jnp.float32, jnp.bfloat16
    own_rows, width = base.shape
    tokens, features = attended.shape
    heads = features // head_size
    depth = rows_out.shape[0] // 2
    block_rows = rows_out.shape[1]
    p = Place(depth)
    x, y, z, t = p.x, p.y, p.z, p.t
    entry_barrier(
        [p.over_x, p.over_y, p.over_core, p.mate, p.middle, p.hop] + p.row_targets()
    )
    length = info[0]
    scale = 1.0 / math.sqrt(head_size)
    column = 2 * t + y

    rows, cols = engine[0].shape[1:]
    down_rows = down_sum.shape[0] // 2
    up_cols = up_sum.shape[1] // 2
    strip = out_sum.shape[1]

    def over_tokens(left, right, target):
        target[...] = lax.dot_general(
            left, right, (((0,), (0,)), ((), ())), preferred_element_type=f32
        ).astype(target.dtype)

    per_down, per_up = down_rows // strip, up_cols // cols
    strip_count = per_down + per_up

    def strip_load(n):
        source = gelu_hbm if n < per_down else pre_hbm
        cut = pl.ds((n % per_down) * strip, strip)
        return pltpu.make_async_copy(source.at[:, cut], strips.at[n % 2], strip_sem.at[n % 2])

    def resident_load(k):
        source = (cot_hbm, act_two_hbm, act_hbm)[k]
        return pltpu.make_async_copy(source, act, load_sem.at[5])

    def strip_ready(n):
        strip_load(n).wait()
        if n + 1 < strip_count:
            strip_load(n + 1).start()

    def homes_of(far):
        return (p.homes[1], p.homes[3]) if far else (p.homes[0], p.homes[2])

    def down_item(r, far):
        def make(send, own):
            if far and r % 2 == 0:
                if r == 0:
                    resident_load(0).wait()
                strip_ready(r // 2)
            left = strips.at[(r // 2) % 2, :, pl.ds((r % 2) * rows, rows)]
            for home, target in zip(homes_of(far), (send, own)):
                over_tokens(left[...], act[:, aligned(home * strip, strip)], target)

        side = 1 - y if far else y
        return far, down_sum.at[aligned(side * down_rows + r * rows, rows), :], make

    def up_item(c, r, far):
        def make(send, own):
            if far and r == 0:
                if c == 0:
                    resident_load(1).start()
                    resident_load(1).wait()
                strip_ready(per_down + c)
            for home, target in zip(homes_of(far), (send, own)):
                over_tokens(
                    act[:, aligned(home * strip + r * rows, rows)], strips[c % 2], target
                )

        side = 1 - y if far else y
        place = up_sum.at[pl.ds(r * rows, rows), aligned(side * up_cols + c * cols, cols)]
        return far, place, make

    def out_item(r, far):
        def make(send, own):
            for home, target in zip(homes_of(far), (send, own)):
                over_tokens(
                    attended[:, pl.ds(r * rows, rows)], low[:, aligned(home * strip, strip)], target
                )

        side = 1 - y if far else y
        return far, out_sum.at[aligned(side * features + r * rows, rows), :], make

    def qkv_item(r, c, far):
        def make(send, own):
            if far and r == 0 and c == 0:
                resident_load(2).start()
                resident_load(2).wait()
            for home, target in zip(homes_of(far), (send, own)):
                over_tokens(
                    act[:, aligned(home * strip + r * rows, rows)],
                    qkv_grad[:, pl.ds(c * cols, cols)],
                    target,
                )

        side = 1 - y if far else y
        return far, qkv_sums[c].at[pl.ds(r * rows, rows), aligned(side * cols, cols)], make

    sides = (True, False)
    items = [down_item(r, far) for r in range(down_rows // rows) for far in sides]
    items += [up_item(c, r, far) for c in range(per_up) for r in range(strip // rows) for far in sides]
    items += [out_item(r, far) for r in range(features // rows) for far in sides]
    items += [qkv_item(r, c, far) for r in range(strip // rows) for c in range(3) for far in sides]
    run, steps = reduce_stages(p, items, engine)

    loads = [
        pltpu.make_async_copy(source, target, load_sem.at[k])
        for k, (source, target) in enumerate(
            (
                (hidden_hbm, base),
                (cot_hbm.at[pl.ds(0, own_rows), :], packed),
                (out_hbm, out_mat),
                (qkv_hbm, qkv),
                (attended_hbm, attended),
                (cot_hbm, act),
                (qkv_mat_hbm, qkv_mat),
                (resid_hbm, base),
            )
        )
    ]
    sums = RowSum(
        p, own_rows, arrived, sent, loaded, sum_send, sum_recv, sum_load, core_free, y_free, 3
    )
    group_rows = 16
    quarter = own_rows // 4 // group_rows

    def start():
        loads[5].start()
        strip_load(0).start()
        low_load(0).start()
        up_load(0).start()
        for k in (0, 1, 3, 4):
            loads[k].start()
        for n in range(3):
            down_load(n).start()
        small[...] = small_in[...]
        key_sum[...] = jnp.zeros_like(key_sum)
        value_sum[...] = jnp.zeros_like(value_sum)

    def low_load(k):
        return pltpu.make_async_copy((pre_hbm, gelu_hbm)[k], low, load_sem.at[8])

    def up_load(n):
        return pltpu.make_async_copy(up_hbm.at[pl.ds(n * strip, strip), :], out_mat, load_sem.at[9])

    def down_load(n):
        return pltpu.make_async_copy(
            down_hbm.at[:, pl.ds(n * strip, strip)],
            qkv_mat.at[:, pl.ds((n % 3) * strip, strip)],
            load_sem.at[10 + n % 3],
        )

    held = (keys, values)

    def part_store(k, n):
        target = (two_part, mlp_part)[k].at[:, pl.ds(n * strip, strip)]
        return pltpu.make_async_copy(held[n % 2], target, load_sem.at[13 + n % 2])

    def part_columns(k, n):
        if n == 0:
            low_load(k).wait()
        (down_load(n) if k else up_load(n)).wait()
        if n >= 2:
            part_store(k, n - 2).wait()

        @pl.loop(0, 4)
        def _(b):
            at = pl.ds(pl.multiple_of(b * own_rows, own_rows), own_rows)
            if k:
                right, side = qkv_mat[:, pl.ds((n % 3) * strip, strip)], 0
            else:
                right, side = out_mat[...], 1
            held[n % 2][at, :] = lax.dot_general(
                low[at, :], right, (((1,), (side,)), ((), ())), preferred_element_type=f32
            ).astype(bf16)

        part_store(k, n).start()
        if k == 0 and n < 3:
            up_load(n + 1).start()
        if k == 0 and n == 3:
            low_load(1).start()
            loads[2].start()
        if k == 1 and n == 0:
            down_load(3).start()
        if k == 1 and n == 3:
            loads[6].start()

    def part_end(k):
        part_store(k, 2).wait()
        part_store(k, 3).wait()
        if k == 0:
            sums.start(0, two_part, False)
        else:
            grant(low_core, p.over_core)
            grant(low_y, p.over_y)

    def two_middle(part):
        sums.middle(two_part, False, part)

    def two_finish():
        sums.finish(two_part, False)
        loads[0].wait()
        loads[1].wait()

    def accumulate(row, value):
        small[pl.ds(row, 1), :] += jnp.sum(value, 0, keepdims=True)

    def two_rows(part):
        gain = vector_ref[pl.ds(GAIN_TWO, 1), :]

        @pl.loop(part * quarter, (part + 1) * quarter)
        def _(k):
            at = pl.ds(pl.multiple_of(k * group_rows, group_rows), group_rows)
            upstream = sums.total(two_part, False, at)
            unit, inverse = unit_rows(base[at, :])
            grad = packed[at, :].astype(f32) + unit_back(upstream, unit, inverse, gain)
            hidden_grad[at, :] = grad
            low[at, :] = grad.astype(bf16)
            accumulate(GAIN_TWO, upstream * unit)
            accumulate(SHIFT_TWO, upstream)
            accumulate(OUT_BIAS, grad)

    def low_block(k):
        return low.at[pl.ds(k * own_rows, own_rows), :]

    def join(k):
        source, place = ((0, 1), (None, None), (2, 3))[k]
        return remote_copy(
            low_block(source), low_block(place), join_send.at[k], join_recv.at[k], p.over_core
        )

    def join_y(part):
        size = own_rows // PARTS
        return remote_copy(
            low.at[pl.ds(part * size, size), :],
            low.at[pl.ds(2 * own_rows + part * size, size), :],
            join_send.at[3 + part],
            join_recv.at[3 + part],
            p.over_y,
        )

    def join_start():
        pl.semaphore_wait(low_core, 1)
        pl.semaphore_wait(low_y, 1)
        join(0).start()
        join_y(0).start()
        sums.release(0)

    def join_pass():
        for part in range(PARTS):
            join_y(part).wait_recv()
        join(2).start()

    def attend_block(k):
        at = pl.ds(k * own_rows, own_rows)
        attended_grad[at, :] = lax.dot_general(
            low[at, :], out_mat[...], (((1,), (1,)), ((), ())), preferred_element_type=f32
        ).astype(bf16)

    def attend_own():
        loads[2].wait()
        attend_block(0)

    def attend_peer():
        join(0).wait()
        attend_block(1)

    def attend_far():
        attend_block(2)

    def attend_last():
        for part in range(PARTS):
            join_y(part).wait_send()
        join(2).wait()
        attend_block(3)

    def mlp_start():
        sums.start(1, mlp_part, False)

    def mlp_middle(part):
        sums.middle(mlp_part, False, part)

    def mlp_finish():
        sums.finish(mlp_part, False)
        bias = vector_ref[pl.ds(DOWN_BIAS, 1), :]

        @pl.loop(0, own_rows // group_rows)
        def _(k):
            at = pl.ds(pl.multiple_of(k * group_rows, group_rows), group_rows)
            packed[at, :] = (base[at, :] + sums.total(mlp_part, False, at) + bias).astype(bf16)

        sums.release(1)

    def row_source(k):
        return packed.at[pl.ds(k * block_rows, block_rows), :]

    row_ends = (rows_out, rows_grad)

    def row_copy(a, k):
        end = row_ends[a].at[x * depth + z]
        return remote_copy(row_source(k), end, row_send.at[a, k], row_recv.at[a, z], p.row_target(k))

    def row_arrival(a, k):
        end = row_ends[a].at[t * depth + k]
        return remote_copy(row_source(k), end, row_send.at[a, k], row_recv.at[a, k], p.row_target(k))

    def row_stay(a, k):
        return pltpu.make_async_copy(row_source(k), row_ends[a].at[x * depth + z], row_send.at[a, k])

    def rows_start(a):
        for k in range(depth):
            stays = (z == k) & (x == t)
            pl.when(stays)(lambda k=k: row_stay(a, k).start())
            pl.when(jnp.logical_not(stays))(lambda k=k: row_copy(a, k).start())

    def share(a):
        group = row_ends[a].at[pl.ds(t * depth, depth)]
        return remote_copy(group, group, share_send.at[a], share_recv.at[a], p.over_core)

    def rows_share(a):
        for k in range(depth):
            stays = (z == k) & (x == t)
            pl.when(stays)(lambda k=k: row_stay(a, k).wait())

            @pl.when(jnp.logical_not(stays))
            def _(k=k):
                row_copy(a, k).wait_send()
                row_arrival(a, k).wait_recv()

        share(a).start()

    def head_rows():
        loads[3].wait()
        loads[4].wait()
        for block in range(4):
            at = pl.ds(pl.multiple_of(p.block_place(block) * own_rows, own_rows), own_rows)
            keys[pl.ds(block * own_rows, own_rows), :] = qkv[at, pl.ds(features, features)]
            values[pl.ds(block * own_rows, own_rows), :] = qkv[at, pl.ds(2 * features, features)]

    def attention_block(block):
        at = pl.ds(pl.multiple_of(p.block_place(block) * own_rows, own_rows), own_rows)
        part = pl.ds(0, (block + 1) * own_rows)

        @pl.loop(0, heads)
        def _(head):
            lanes = aligned(head * head_size, head_size)
            queries, grads = qkv[at, lanes], attended_grad[at, lanes]
            probs, _ = attention_probs(queries, keys[part, lanes], block, length)
            prob_grad = lax.dot_general(
                grads, values[part, lanes], (((1,), (1,)), ((), ())), preferred_element_type=f32
            )
            inner = jnp.sum(probs * prob_grad, -1, keepdims=True)
            score_grad = (probs * (prob_grad - inner)).astype(bf16)
            query_grad = (
                jnp.dot(score_grad, keys[part, lanes], preferred_element_type=f32) * scale
            )
            spot = aligned(column * features + head * head_size, head_size)
            small[pl.ds(QUERY_BIAS, 1), spot] += jnp.sum(query_grad, 0, keepdims=True)
            qkv_grad[at, lanes] = query_grad.astype(bf16)
            key_sum[part, lanes] += lax.dot_general(
                score_grad, queries, (((0,), (0,)), ((), ())), preferred_element_type=f32
            )
            value_sum[part, lanes] += lax.dot_general(
                probs.astype(bf16), grads, (((0,), (0,)), ((), ())), preferred_element_type=f32
            )

    def attention_end(block):
        at = pl.ds(pl.multiple_of(p.block_place(block) * own_rows, own_rows), own_rows)
        part = pl.ds(block * own_rows, own_rows)
        qkv_grad[at, pl.ds(features, features)] = (key_sum[part, :] * scale).astype(bf16)
        value_grad = value_sum[part, :]
        qkv_grad[at, pl.ds(2 * features, features)] = value_grad.astype(bf16)
        spot = aligned(column * features, features)
        small[pl.ds(VALUE_BIAS, 1), spot] += jnp.sum(value_grad, 0, keepdims=True)

    def one_block(k):
        if k == 3:
            loads[6].wait()
        at = pl.ds(k * own_rows, own_rows)

        @pl.loop(0, 4)
        def _(n):
            cut = aligned(n * strip, strip)
            low[at, cut] = lax.dot_general(
                qkv_grad[at, :], qkv_mat[cut, :], (((1,), (1,)), ((), ())), preferred_element_type=f32
            ).astype(bf16)

    def one_start():
        sums.start(2, low, True)

    def one_middle(part):
        sums.middle(low, True, part)

    def one_finish():
        sums.finish(low, True)
        loads[7].wait()

    def one_rows(part):
        gain = vector_ref[pl.ds(GAIN_ONE, 1), :]

        @pl.loop(part * quarter, (part + 1) * quarter)
        def _(k):
            at = pl.ds(pl.multiple_of(k * group_rows, group_rows), group_rows)
            upstream = sums.total(low, True, at)
            unit, inverse = unit_rows(base[at, :])
            grad = hidden_grad[at, :] + unit_back(upstream, unit, inverse, gain)
            packed[at, :] = grad.astype(bf16)
            accumulate(GAIN_ONE, upstream * unit)
            accumulate(SHIFT_ONE, upstream)

    def small_copy(k):
        target = (p.over_core, p.over_x, p.over_y, p.mate, p.hop)[k]
        return remote_copy(small, small_arrived.at[k], small_send.at[k], small_recv.at[k], target)

    def small_add(k):
        small_copy(k).wait()
        mine, other = small[...], small_arrived[k]
        row = lax.broadcasted_iota(jnp.int32, mine.shape, 0)
        small[...] = jnp.where(row == PEAKS, jnp.maximum(mine, other), mine + other)

    def call(function, *arguments):
        return lambda: function(*arguments)

    plan = {}

    def at_step(step, *tasks):
        plan.setdefault(step, []).extend(tasks)

    for n in range(4):
        at_step(n, call(part_columns, 0, n))
        at_step(5 + 2 * n, call(part_columns, 1, n))
    at_step(4, call(part_end, 0))
    at_step(13, call(part_end, 1))
    for k in range(4):
        at_step(7 + k, call(two_middle, k))
    at_step(16, two_finish, call(two_rows, 0))
    for k in range(1, 4):
        at_step(16 + k // 2, call(two_rows, k))
    at_step(17, join_start)
    for k in range(1, 4):
        at_step(17 + k, join_y(k).start)
    at_step(18, attend_own)
    at_step(19, attend_peer)
    at_step(21, head_rows)
    at_step(24, join_pass)
    at_step(25, attend_far)
    at_step(26, attend_last)
    at_step(27, call(attention_block, 0), call(attention_block, 1))
    at_step(27 + 1, call(attention_block, 2))
    at_step(27 + 2, call(attention_block, 3))
    at_step(27 + 3, *(call(attention_end, k) for k in range(4)))
    at_step(21, mlp_start)
    for k in range(4):
        at_step(23 + 1 * k, call(mlp_middle, k))
    at_step(33, mlp_finish, loads[7].start, lambda: rows_start(0))
    at_step(42, lambda: rows_share(0))
    at_step(36, call(one_block, 3), call(one_block, 1), one_start)
    at_step(36 + 1, call(one_block, 2), call(one_block, 0))
    for k in range(4):
        at_step(38 + k, call(one_middle, k))
    at_step(47, one_finish, share(0).wait, call(one_rows, 0))
    for k in range(1, 4):
        at_step(47 + k // 2, call(one_rows, k))
    at_step(48, lambda: rows_start(1))
    at_step(49, small_copy(0).start)
    for k in range(4):
        at_step(49 + 2 + 2 * k, call(small_add, k), small_copy(k + 1).start)
    at_step(49 + 5 * 2, call(small_add, 4))
    at_step(57, lambda: rows_share(1))
    at_step(59, share(1).wait)
    start()
    for step in range(steps):
        run(step)
        for task in plan.get(step, ()):
            task()


def backward_all(
    head_size,
    length,
    vectors,
    small,
    gelu_low,
    pre_low,
    act_two,
    up_mat,
    down_mat,
    hidden,
    cot_low,
    resid,
    out_mat,
    qkv_mat,
    qkv,
    attended,
    act_one,
    slots,
):
    bf16, f32 = jnp.bfloat16, jnp.float32
    hbm = pl.BlockSpec(memory_space=pl.ANY)
    vmem = pl.BlockSpec(memory_space=pltpu.VMEM)
    down_rows, up_cols = gelu_low.shape[1], pre_low.shape[1]
    tokens, features = attended.shape
    own_rows, width = hidden.shape
    strip = width // 4
    depth = slots // 2
    engine = reduce_scratch(6, 4, 256, 512)
    n_engine = len(engine)

    def kernel(*refs):
        ins, rest = refs[:16], refs[16:]
        outs, scratch = rest[:11], rest[11:]
        backward_kernel(
            head_size,
            *ins,
            outs[0],
            outs[1],
            outs[2],
            outs[3:6],
            *outs[6:],
            scratch[:n_engine],
            *scratch[n_engine:],
        )

    dma, regular = pltpu.SemaphoreType.DMA, pltpu.SemaphoreType.REGULAR

    def hold(shape, dtype=bf16):
        return pltpu.VMEM(shape, dtype)

    return pl.pallas_call(
        kernel,
        out_shape=(
            jax.ShapeDtypeStruct((2 * down_rows, strip), bf16),
            jax.ShapeDtypeStruct((strip, 2 * up_cols), bf16),
            jax.ShapeDtypeStruct((2 * features, strip), bf16),
            jax.ShapeDtypeStruct((strip, 2 * features), bf16),
            jax.ShapeDtypeStruct((strip, 2 * features), bf16),
            jax.ShapeDtypeStruct((strip, 2 * features), bf16),
            jax.ShapeDtypeStruct((slots, own_rows // depth, width), bf16),
            jax.ShapeDtypeStruct((slots, own_rows // depth, width), bf16),
            jax.ShapeDtypeStruct(small.shape, f32),
            jax.ShapeDtypeStruct((tokens, width), bf16),
            jax.ShapeDtypeStruct((tokens, width), bf16),
        ),
        in_specs=[pl.BlockSpec(memory_space=pltpu.SMEM), vmem, vmem] + [hbm] * 13,
        out_specs=(hbm,) * 8 + (vmem,) + (hbm,) * 2,
        scratch_shapes=engine
        + [
            hold((own_rows, width), f32),
            hold((own_rows, width), f32),
            hold((tokens, width)),
            hold((features, width)),
            hold((tokens, features)),
            hold((tokens, 3 * features)),
            hold((tokens, 3 * features)),
            hold((tokens, width)),
            hold((tokens, features)),
            hold((width, 3 * features)),
            hold((tokens, features)),
            hold((tokens, features)),
            hold((tokens, features), f32),
            hold((tokens, features), f32),
            hold((2, tokens, strip)),
            hold((own_rows, width)),
            hold((3, own_rows, width)),
            hold((own_rows, width)),
            hold((own_rows, width)),
            hold((5,) + small.shape, f32),
            dma((15,)),
            dma((2 + PARTS,)),
            dma((2 + PARTS,)),
            dma(()),
            dma((3 + PARTS,)),
            dma((3 + PARTS,)),
            dma((2,)),
            dma((2, depth)),
            dma((2, depth)),
            dma((2,)),
            dma((2,)),
            dma((5,)),
            dma((5,)),
            regular,
            regular,
            regular,
            regular,
        ],
        compiler_params=pltpu.CompilerParams(
            collective_id=1, has_side_effects=True, vmem_limit_bytes=60 << 20
        ),
        cost_estimate=pl.CostEstimate(flops=0, bytes_accessed=64 << 20, transcendentals=0),
    )(
        length,
        vectors,
        small,
        gelu_low,
        pre_low,
        act_two,
        up_mat,
        down_mat,
        hidden,
        cot_low,
        resid,
        out_mat,
        qkv_mat,
        qkv,
        attended,
        act_one,
    )


def split_body(
    layer_input,
    cotangent,
    seq_lengths,
    dealing,
    attn_gain,
    attn_shift,
    query_weight,
    query_bias,
    key_weight,
    value_weight,
    value_bias,
    out_weight,
    out_bias,
    mlp_gain,
    mlp_shift,
    up_weight,
    up_bias,
    down_weight,
    down_bias,
    clip_level,
):
    f32, bf16 = jnp.float32, jnp.bfloat16
    f = lax.axis_index("fsdp")
    z = lax.axis_index("ctx")
    t = lax.axis_index("tp")
    y, x = f // 2, f % 2
    depth = lax.axis_size("ctx")
    slots, block_rows, width = layer_input.shape
    local_heads = query_bias.shape[0] // 2
    head_size = 4 * query_bias.shape[1]
    features = local_heads * head_size
    hidden_units = up_weight.shape[1] // 2
    strip = query_weight.shape[0]
    own_rows = depth * block_rows

    place = t[None]
    length = seq_lengths[dealing[x * depth + z]]
    arrived, cot_part, down_bias_part = prepare(
        dealing, seq_lengths, place, layer_input, cotangent, depth
    )
    vectors = jnp.concatenate(
        [attn_gain, attn_shift, out_bias, mlp_gain, mlp_shift, down_bias, up_bias.reshape(-1)]
    )
    vectors = vectors.reshape(8, strip).astype(f32)
    head_vectors = jnp.concatenate([query_bias, value_bias], 0).astype(f32)
    head_vectors = lax.dynamic_update_slice(
        jnp.zeros((head_vectors.shape[0], head_size), f32), head_vectors, (0, f * query_bias.shape[1])
    )
    (
        qkv_mat,
        out_mat,
        up_mat,
        down_mat,
        act_one,
        cot_low,
        qkv,
        attended,
        hidden,
        resid,
        act_two,
        back,
        vectors_whole,
        peaks,
    ) = forward_all(
        head_size,
        length[None],
        vectors,
        head_vectors,
        query_weight,
        key_weight,
        value_weight,
        out_weight,
        up_weight,
        down_weight,
        arrived,
        cot_part,
    )
    peaks = peaks[:local_heads, 0]
    up_vec = lax.dynamic_slice_in_dim(vectors_whole, 6 + y, 1, 0)

    pre = matmul(act_two, up_mat) + up_vec
    cdf = 0.5 * (1.0 + lax.erf(pre * INV_ROOT_TWO))
    gelu_low = (pre * cdf).astype(bf16)
    slope = cdf + pre * (jnp.exp(-0.5 * pre * pre) * INV_ROOT_TWO_PI)
    pre_grad = back.astype(f32) * slope
    pre_low = pre_grad.astype(bf16)
    up_bias_part = jnp.sum(pre_grad, 0)
    column = 2 * t + y
    small = jnp.zeros((16, width), f32).at[DOWN_BIAS].set(down_bias_part[0])
    small = lax.dynamic_update_slice(small, up_bias_part[None], (UP_BIAS + column, 0))
    small = small.at[PEAKS].set(NEG)
    small = lax.dynamic_update_slice(small, peaks[None], (PEAKS, local_heads * (2 * t + y)))
    (
        down_sum,
        up_sum,
        out_sum,
        query_sum,
        key_sum,
        value_sum,
        rows_out,
        rows_grad,
        totals,
        _,
        _,
    ) = backward_all(
        head_size,
        length[None],
        vectors_whole,
        small,
        gelu_low,
        pre_low,
        act_two,
        up_mat,
        down_mat,
        hidden,
        cot_low,
        resid,
        out_mat,
        qkv_mat,
        qkv,
        attended,
        act_one,
        slots,
    )
    rows_sum = lax.dynamic_slice(totals, (0, f * strip), (6, strip))
    head_sum = lax.dynamic_slice(totals, (QUERY_BIAS, 2 * t * features), (2, 2 * features))
    head_sum = head_sum.reshape(2, 2 * local_heads, head_size)
    head_sum = lax.dynamic_slice_in_dim(head_sum, f * query_bias.shape[1], query_bias.shape[1], 2)
    unit_sum = lax.dynamic_slice(
        totals, (UP_BIAS + up_bias.shape[0] * t, f * strip), (up_bias.shape[0], strip)
    )
    peak_all = lax.dynamic_slice(totals, (PEAKS, 2 * local_heads * t), (1, 2 * local_heads))[0]
    (
        final_output,
        final_grad,
        query_weight_grad,
        key_weight_grad,
        value_weight_grad,
        out_weight_grad,
        up_weight_grad,
        down_weight_grad,
        query_clipped,
        key_clipped,
    ) = finish_all(
        head_size,
        place,
        clip_level,
        totals,
        query_weight,
        key_weight,
        (rows_out, rows_grad, query_sum, key_sum, value_sum, out_sum, up_sum, down_sum),
    )
    return (
        final_output,
        final_grad,
        rows_sum[GAIN_ONE],
        rows_sum[SHIFT_ONE],
        query_weight_grad,
        head_sum[0],
        key_weight_grad,
        value_weight_grad,
        head_sum[1],
        out_weight_grad,
        rows_sum[OUT_BIAS],
        rows_sum[GAIN_TWO],
        rows_sum[SHIFT_TWO],
        up_weight_grad,
        unit_sum,
        down_weight_grad,
        rows_sum[DOWN_BIAS],
        peak_all,
        query_clipped,
        key_clipped,
    )


def solution(mesh):
    sizes = dict(mesh.shape)
    small_slice = sizes == {"fsdp": 4, "ctx": 4, "tp": 2}
    return jax.shard_map(
        split_body if small_slice else gathered_body,
        mesh=mesh,
        in_specs=(
            P(None, ("fsdp", "ctx"), None),
            P(None, ("fsdp", "ctx"), None),
            P(),
            P(),
            P("fsdp"),
            P("fsdp"),
            P("fsdp", "tp"),
            P("tp", "fsdp"),
            P("fsdp", "tp"),
            P("fsdp", "tp"),
            P("tp", "fsdp"),
            P("tp", "fsdp"),
            P("fsdp"),
            P("fsdp"),
            P("fsdp"),
            P("fsdp", "tp"),
            P("tp", "fsdp"),
            P("tp", "fsdp"),
            P("fsdp"),
            P(),
        ),
        out_specs=(
            P(None, ("fsdp", "ctx"), None),
            P(None, ("fsdp", "ctx"), None),
            P("fsdp"),
            P("fsdp"),
            P("fsdp", "tp"),
            P("tp", "fsdp"),
            P("fsdp", "tp"),
            P("fsdp", "tp"),
            P("tp", "fsdp"),
            P("tp", "fsdp"),
            P("fsdp"),
            P("fsdp"),
            P("fsdp"),
            P("fsdp", "tp"),
            P("tp", "fsdp"),
            P("tp", "fsdp"),
            P("fsdp"),
            P("tp"),
            P("fsdp", "tp"),
            P("fsdp", "tp"),
        ),
        check_vma=False,
    )
```

```python
import functools
import math

import jax
import jax.numpy as jnp
from jax import lax
from jax.experimental import pallas as pl
from jax.experimental.pallas import tpu as pltpu
from jax.sharding import PartitionSpec as P

EPS = 1e-05
NEG = -1e30
INV_ROOT_TWO = 0.7071067811865476
INV_ROOT_TWO_PI = 0.3989422804014327


def normalize(values, scale_vec, offset_vec):
    center = values - jnp.mean(values, -1, keepdims=True)
    inverse = lax.rsqrt(jnp.mean(center * center, -1, keepdims=True) + EPS)
    normed = center * inverse
    return (normed * scale_vec + offset_vec, normed, inverse)


def norm_back(upstream, normed, inverse, scale_vec):
    scaled = upstream * scale_vec
    inner = (
        scaled
        - jnp.mean(scaled, -1, keepdims=True)
        - normed * jnp.mean(scaled * normed, -1, keepdims=True)
    )
    return (inverse * inner, jnp.sum(upstream * normed, 0), jnp.sum(upstream, 0))


def pick_slots(rows, dealing, first, count):
    return jnp.concatenate(
        [lax.dynamic_slice_in_dim(rows, dealing[first + j], 1, 0) for j in range(count)], 0
    )


def matmul(left, right):
    return jnp.dot(left, right, preferred_element_type=jnp.float32)


def weight_product(left, right):
    return jnp.einsum("td,te->de", left, right, preferred_element_type=jnp.float32)


def back_product(left, right):
    return jnp.einsum("te,de->td", left, right, preferred_element_type=jnp.float32)


def gathered_body(
    layer_input,
    cotangent,
    seq_lengths,
    dealing,
    attn_gain,
    attn_shift,
    query_weight,
    query_bias,
    key_weight,
    value_weight,
    value_bias,
    out_weight,
    out_bias,
    mlp_gain,
    mlp_shift,
    up_weight,
    up_bias,
    down_weight,
    down_bias,
    clip_level,
):
    shard_count = lax.axis_size("fsdp")
    ctx_count = lax.axis_size("ctx")
    my_group = lax.axis_index("fsdp")
    ctx_place = lax.axis_index("ctx")
    slot_count, block_rows, width = layer_input.shape
    per_group = slot_count // shard_count
    local_rows = shard_count * block_rows
    tokens = per_group * local_rows
    dealt_input = pick_slots(layer_input, dealing, 0, slot_count).reshape(
        shard_count, per_group, block_rows, width
    )
    dealt_grad = cotangent.reshape(shard_count, per_group, block_rows, width)
    arrived_input, arrived_grad = (
        lax.all_to_all(dealt_input, "fsdp", split_axis=0, concat_axis=2, tiled=True),
        lax.all_to_all(dealt_grad, "fsdp", split_axis=0, concat_axis=2, tiled=True),
    )
    resid = arrived_input.reshape(tokens, width)
    upstream = arrived_grad.reshape(tokens, width)
    seq_lens = lax.dynamic_slice_in_dim(
        jnp.take(seq_lengths, dealing), my_group * per_group, per_group
    )
    gathered = (
        lax.all_gather(attn_gain, "fsdp", axis=0, tiled=True),
        lax.all_gather(attn_shift, "fsdp", axis=0, tiled=True),
        lax.all_gather(query_weight, "fsdp", axis=0, tiled=True),
        lax.all_gather(query_bias, "fsdp", axis=1, tiled=True),
        lax.all_gather(key_weight, "fsdp", axis=0, tiled=True),
        lax.all_gather(value_weight, "fsdp", axis=0, tiled=True),
        lax.all_gather(value_bias, "fsdp", axis=1, tiled=True),
        lax.all_gather(out_weight, "fsdp", axis=1, tiled=True),
        lax.all_gather(out_bias, "fsdp", axis=0, tiled=True),
        lax.all_gather(mlp_gain, "fsdp", axis=0, tiled=True),
        lax.all_gather(mlp_shift, "fsdp", axis=0, tiled=True),
        lax.all_gather(up_weight, "fsdp", axis=0, tiled=True),
        lax.all_gather(up_bias, "fsdp", axis=1, tiled=True),
        lax.all_gather(down_weight, "fsdp", axis=1, tiled=True),
        lax.all_gather(down_bias, "fsdp", axis=0, tiled=True),
    )
    (
        gain_one,
        shift_one,
        query_mat,
        query_vec,
        key_mat,
        value_mat,
        value_vec,
        out_mat,
        out_vec,
        gain_two,
        shift_two,
        up_mat,
        up_vec,
        down_mat,
        down_vec,
    ) = gathered
    head_count, head_size = query_vec.shape
    features = head_count * head_size
    scale_of_scores = 1.0 / math.sqrt(head_size)
    row_ids = jnp.arange(local_rows, dtype=jnp.int32)
    query_pos = (row_ids // block_rows * ctx_count + ctx_place) * block_rows + row_ids % block_rows
    key_ids = jnp.arange(ctx_count * local_rows, dtype=jnp.int32)
    key_rows = key_ids % local_rows
    key_pos = (
        key_rows // block_rows * ctx_count + key_ids // local_rows
    ) * block_rows + key_rows % block_rows
    allowed = (key_pos[None, None, :] <= query_pos[None, :, None]) & (
        key_pos[None, None, :] < seq_lens[:, None, None]
    )
    query_live = query_pos[None, :] < seq_lens[:, None]
    normed_a, unit_one, inverse_one = normalize(
        resid, gain_one.astype(jnp.float32), shift_one.astype(jnp.float32)
    )
    act_one = normed_a.astype(jnp.bfloat16)
    queries = (
        (matmul(act_one, query_mat) + query_vec.reshape(features).astype(jnp.float32))
        .astype(jnp.bfloat16)
        .reshape(per_group, local_rows, features)
    )
    keys_mine = (
        matmul(act_one, key_mat).astype(jnp.bfloat16).reshape(per_group, local_rows, features)
    )
    values_mine = (
        (matmul(act_one, value_mat) + value_vec.reshape(features).astype(jnp.float32))
        .astype(jnp.bfloat16)
        .reshape(per_group, local_rows, features)
    )
    keys_all, values_all = (
        lax.all_gather(keys_mine, "ctx", axis=1, tiled=True),
        lax.all_gather(values_mine, "ctx", axis=1, tiled=True),
    )

    def head_cut(array, head_index):
        return lax.dynamic_slice_in_dim(array, head_index * head_size, head_size, 2)

    def head_scores(head_queries, head_keys):
        return (
            jnp.einsum("sqd,skd->sqk", head_queries, head_keys, preferred_element_type=jnp.float32)
            * scale_of_scores
        )

    def forward_head(head_index):
        logit_scores = head_scores(head_cut(queries, head_index), head_cut(keys_all, head_index))
        masked = jnp.where(allowed, logit_scores, NEG)
        row_top = jnp.max(masked, -1, keepdims=True)
        exp_terms = jnp.where(allowed, jnp.exp(masked - row_top), 0.0)
        total = jnp.sum(exp_terms, -1, keepdims=True)
        attention_probabilities = exp_terms / total
        attended_rows = jnp.einsum(
            "sqk,skd->sqd",
            attention_probabilities.astype(jnp.bfloat16),
            head_cut(values_all, head_index),
            preferred_element_type=jnp.float32,
        )
        log_total = row_top[..., 0] + jnp.log(total[..., 0])
        peak = jnp.max(jnp.where(query_live, row_top[..., 0], NEG))
        return (attended_rows, log_total, peak)

    attended_rows, log_totals, peaks = lax.map(forward_head, jnp.arange(head_count))
    attn_low = attended_rows.transpose(1, 2, 0, 3).reshape(tokens, features).astype(jnp.bfloat16)
    attn_sum = lax.psum(matmul(attn_low, out_mat), "tp")
    hidden = resid + attn_sum + out_vec.astype(jnp.float32)
    normed_b, unit_two, inverse_two = normalize(
        hidden, gain_two.astype(jnp.float32), shift_two.astype(jnp.float32)
    )
    act_two = normed_b.astype(jnp.bfloat16)
    pre = matmul(act_two, up_mat) + up_vec.reshape(-1).astype(jnp.float32)
    gelu_low = jax.nn.gelu(pre, approximate=False).astype(jnp.bfloat16)
    mlp_sum = lax.psum(matmul(gelu_low, down_mat).astype(jnp.bfloat16), "tp").astype(jnp.float32)
    layer_output = hidden + mlp_sum + down_vec.astype(jnp.float32)
    peak_all = lax.pmax(peaks, ("fsdp", "ctx"))
    level = clip_level[0]
    factor = jnp.repeat(jnp.sqrt(level / jnp.maximum(peak_all, level)), head_size)
    query_clipped = (query_weight.astype(jnp.float32) * factor[None, :]).astype(jnp.bfloat16)
    key_clipped = (key_weight.astype(jnp.float32) * factor[None, :]).astype(jnp.bfloat16)
    grad_low = upstream.astype(jnp.bfloat16)
    down_weight_grad = weight_product(gelu_low, grad_low)
    down_bias_grad = jnp.sum(upstream, 0)
    cdf = 0.5 * (1.0 + lax.erf(pre * INV_ROOT_TWO))
    density = jnp.exp(-0.5 * pre * pre) * INV_ROOT_TWO_PI
    pre_grad = back_product(grad_low, down_mat) * (cdf + pre * density)
    pre_low = pre_grad.astype(jnp.bfloat16)
    up_weight_grad = weight_product(act_two, pre_low)
    up_bias_grad = jnp.sum(pre_grad, 0).reshape(up_vec.shape)
    normed_two_grad = lax.psum(back_product(pre_low, up_mat), "tp")
    hidden_in, mlp_gain_grad, mlp_shift_grad = norm_back(
        normed_two_grad, unit_two, inverse_two, gain_two.astype(jnp.float32)
    )
    hidden_grad = upstream + hidden_in
    hidden_low = hidden_grad.astype(jnp.bfloat16)
    out_weight_grad = weight_product(attn_low, hidden_low)
    out_bias_grad = jnp.sum(hidden_grad, 0)
    attended_grad = (
        back_product(hidden_low, out_mat)
        .astype(jnp.bfloat16)
        .reshape(per_group, local_rows, features)
    )

    def backward_head(head_index):
        head_queries = head_cut(queries, head_index)
        head_keys = head_cut(keys_all, head_index)
        head_values = head_cut(values_all, head_index)
        grad_head = head_cut(attended_grad, head_index)
        logit_scores = head_scores(head_queries, head_keys)
        masked = jnp.where(allowed, logit_scores, NEG)
        attention_probabilities = jnp.where(
            allowed, jnp.exp(masked - log_totals[head_index][..., None]), 0.0
        )
        prob_grad = jnp.einsum(
            "sqd,skd->sqk", grad_head, head_values, preferred_element_type=jnp.float32
        )
        inner = jnp.sum(attention_probabilities * prob_grad, -1, keepdims=True)
        score_grad = (attention_probabilities * (prob_grad - inner)).astype(jnp.bfloat16)
        query_grad = (
            jnp.einsum("sqk,skd->sqd", score_grad, head_keys, preferred_element_type=jnp.float32)
            * scale_of_scores
        )
        key_grad = (
            jnp.einsum("sqk,sqd->skd", score_grad, head_queries, preferred_element_type=jnp.float32)
            * scale_of_scores
        )
        value_grad = jnp.einsum(
            "sqk,sqd->skd",
            attention_probabilities.astype(jnp.bfloat16),
            grad_head,
            preferred_element_type=jnp.float32,
        )
        return (query_grad, key_grad, value_grad)

    query_parts, key_parts, value_parts = lax.map(backward_head, jnp.arange(head_count))
    query_grads = query_parts.transpose(1, 2, 0, 3).reshape(tokens, features)
    key_whole = key_parts.transpose(1, 2, 0, 3).reshape(per_group, ctx_count * local_rows, features)
    value_whole = value_parts.transpose(1, 2, 0, 3).reshape(
        per_group, ctx_count * local_rows, features
    )
    key_summed, value_summed = (
        lax.psum_scatter(key_whole, "ctx", scatter_dimension=1, tiled=True),
        lax.psum_scatter(value_whole, "ctx", scatter_dimension=1, tiled=True),
    )
    key_grads = key_summed.reshape(tokens, features)
    value_grads = value_summed.reshape(tokens, features)
    query_bias_grad = jnp.sum(query_grads, 0).reshape(head_count, head_size)
    value_bias_grad = jnp.sum(value_grads, 0).reshape(head_count, head_size)
    query_low = query_grads.astype(jnp.bfloat16)
    key_low = key_grads.astype(jnp.bfloat16)
    value_low = value_grads.astype(jnp.bfloat16)
    query_weight_grad = weight_product(act_one, query_low)
    key_weight_grad = weight_product(act_one, key_low)
    value_weight_grad = weight_product(act_one, value_low)
    normed_one_grad = lax.psum(
        (
            back_product(query_low, query_mat)
            + back_product(key_low, key_mat)
            + back_product(value_low, value_mat)
        ).astype(jnp.bfloat16),
        "tp",
    ).astype(jnp.float32)
    input_in, attn_gain_grad, attn_shift_grad = norm_back(
        normed_one_grad, unit_one, inverse_one, gain_one.astype(jnp.float32)
    )
    input_grad = hidden_grad + input_in
    partial_sums = (
        lax.psum_scatter(
            attn_gain_grad.astype(jnp.bfloat16), "fsdp", scatter_dimension=0, tiled=True
        ).astype(jnp.float32),
        lax.psum_scatter(
            attn_shift_grad.astype(jnp.bfloat16), "fsdp", scatter_dimension=0, tiled=True
        ).astype(jnp.float32),
        lax.psum_scatter(
            query_weight_grad.astype(jnp.bfloat16), "fsdp", scatter_dimension=0, tiled=True
        ).astype(jnp.float32),
        lax.psum_scatter(
            query_bias_grad.astype(jnp.bfloat16), "fsdp", scatter_dimension=1, tiled=True
        ).astype(jnp.float32),
        lax.psum_scatter(
            key_weight_grad.astype(jnp.bfloat16), "fsdp", scatter_dimension=0, tiled=True
        ).astype(jnp.float32),
        lax.psum_scatter(
            value_weight_grad.astype(jnp.bfloat16), "fsdp", scatter_dimension=0, tiled=True
        ).astype(jnp.float32),
        lax.psum_scatter(
            value_bias_grad.astype(jnp.bfloat16), "fsdp", scatter_dimension=1, tiled=True
        ).astype(jnp.float32),
        lax.psum_scatter(
            out_weight_grad.astype(jnp.bfloat16), "fsdp", scatter_dimension=1, tiled=True
        ).astype(jnp.float32),
        lax.psum_scatter(
            out_bias_grad.astype(jnp.bfloat16), "fsdp", scatter_dimension=0, tiled=True
        ).astype(jnp.float32),
        lax.psum_scatter(
            mlp_gain_grad.astype(jnp.bfloat16), "fsdp", scatter_dimension=0, tiled=True
        ).astype(jnp.float32),
        lax.psum_scatter(
            mlp_shift_grad.astype(jnp.bfloat16), "fsdp", scatter_dimension=0, tiled=True
        ).astype(jnp.float32),
        lax.psum_scatter(
            up_weight_grad.astype(jnp.bfloat16), "fsdp", scatter_dimension=0, tiled=True
        ).astype(jnp.float32),
        lax.psum_scatter(
            up_bias_grad.astype(jnp.bfloat16), "fsdp", scatter_dimension=1, tiled=True
        ).astype(jnp.float32),
        lax.psum_scatter(
            down_weight_grad.astype(jnp.bfloat16), "fsdp", scatter_dimension=1, tiled=True
        ).astype(jnp.float32),
        lax.psum_scatter(
            down_bias_grad.astype(jnp.bfloat16), "fsdp", scatter_dimension=0, tiled=True
        ).astype(jnp.float32),
    )
    shards = (
        lax.psum(partial_sums[0].astype(jnp.bfloat16), "ctx").astype(jnp.float32),
        lax.psum(partial_sums[1].astype(jnp.bfloat16), "ctx").astype(jnp.float32),
        lax.psum(partial_sums[2].astype(jnp.bfloat16), "ctx").astype(jnp.float32),
        lax.psum(partial_sums[3].astype(jnp.bfloat16), "ctx").astype(jnp.float32),
        lax.psum(partial_sums[4].astype(jnp.bfloat16), "ctx").astype(jnp.float32),
        lax.psum(partial_sums[5].astype(jnp.bfloat16), "ctx").astype(jnp.float32),
        lax.psum(partial_sums[6].astype(jnp.bfloat16), "ctx").astype(jnp.float32),
        lax.psum(partial_sums[7].astype(jnp.bfloat16), "ctx").astype(jnp.float32),
        lax.psum(partial_sums[8].astype(jnp.bfloat16), "ctx").astype(jnp.float32),
        lax.psum(partial_sums[9].astype(jnp.bfloat16), "ctx").astype(jnp.float32),
        lax.psum(partial_sums[10].astype(jnp.bfloat16), "ctx").astype(jnp.float32),
        lax.psum(partial_sums[11].astype(jnp.bfloat16), "ctx").astype(jnp.float32),
        lax.psum(partial_sums[12].astype(jnp.bfloat16), "ctx").astype(jnp.float32),
        lax.psum(partial_sums[13].astype(jnp.bfloat16), "ctx").astype(jnp.float32),
        lax.psum(partial_sums[14].astype(jnp.bfloat16), "ctx").astype(jnp.float32),
    )
    sent_output = layer_output.reshape(1, per_group, local_rows, width)
    sent_grad = input_grad.reshape(1, per_group, local_rows, width)
    back_output, back_grad = (
        lax.all_to_all(
            sent_output.astype(jnp.bfloat16), "fsdp", split_axis=2, concat_axis=0, tiled=True
        ).astype(sent_output.dtype),
        lax.all_to_all(
            sent_grad.astype(jnp.bfloat16), "fsdp", split_axis=2, concat_axis=0, tiled=True
        ).astype(sent_grad.dtype),
    )
    final_output = back_output.reshape(slot_count, block_rows, width)
    final_grad = back_grad.reshape(slot_count, block_rows, width)
    return (
        final_output,
        final_grad,
        shards[0],
        shards[1],
        shards[2],
        shards[3],
        shards[4],
        shards[5],
        shards[6],
        shards[7],
        shards[8],
        shards[9],
        shards[10],
        shards[11],
        shards[12],
        shards[13],
        shards[14],
        peak_all,
        query_clipped,
        key_clipped,
    )


def attention_probs(query_block, key_rows, block, length):
    rows, cols = query_block.shape[0], key_rows.shape[0]
    scores = lax.dot_general(
        query_block, key_rows, (((1,), (1,)), ((), ())), preferred_element_type=jnp.float32
    ) * (1.0 / math.sqrt(query_block.shape[1]))
    row_pos = block * rows + lax.broadcasted_iota(jnp.int32, (rows, cols), 0)
    col_pos = lax.broadcasted_iota(jnp.int32, (rows, cols), 1)
    scores = jnp.where((col_pos <= row_pos) & (col_pos < length), scores, NEG)
    top = jnp.max(scores, -1, keepdims=True)
    terms = jnp.exp(scores - top)
    return terms / jnp.sum(terms, -1, keepdims=True), top


def entry_barrier(targets):
    barrier = pltpu.get_barrier_semaphore()
    for target in targets:
        pl.semaphore_signal(barrier, inc=1, device_id=target, device_id_type=pl.DeviceIdType.MESH)
    pl.semaphore_wait(barrier, len(targets))


def remote_copy(src, dst, send, recv, target):
    return pltpu.make_async_remote_copy(
        src_ref=src,
        dst_ref=dst,
        send_sem=send,
        recv_sem=recv,
        device_id=target,
        device_id_type=pl.DeviceIdType.MESH,
    )


def grant(semaphore, target):
    pl.semaphore_signal(semaphore, inc=1, device_id=target, device_id_type=pl.DeviceIdType.MESH)


def aligned(start, size):
    return pl.ds(pl.multiple_of(start, 128), size)


class Place:
    def __init__(self, depth):
        self.depth = depth
        f = lax.axis_index("fsdp")
        z = lax.axis_index("ctx")
        t = lax.axis_index("tp")
        y, x = f // 2, f % 2
        self.f, self.z, self.t, self.y, self.x = f, z, t, y, x
        self.over_x = {"fsdp": 2 * y + 1 - x, "ctx": z, "tp": t}
        self.over_y = {"fsdp": 2 * (1 - y) + x, "ctx": z, "tp": t}
        self.over_core = {"fsdp": f, "ctx": z, "tp": 1 - t}
        self.mate = {"fsdp": f, "ctx": z + 1 - 2 * (z % 2), "tp": t}
        self.middle = {"fsdp": f, "ctx": 3 - z, "tp": t}
        self.hop = {"fsdp": f, "ctx": lax.rem(z + 2, 4), "tp": t}
        self.homes = (2 * y + 1 - x, 2 * (1 - y) + 1 - x, f, 2 * (1 - y) + x)

    def row_target(self, k):
        return {"fsdp": 2 * self.y + self.t, "ctx": k, "tp": self.x}

    def row_targets(self):
        others = [self.row_target(lax.rem(self.z + k, self.depth)) for k in range(1, self.depth)]
        return others + [{"fsdp": 2 * self.y + 1 - self.x, "ctx": self.z, "tp": 1 - self.t}]

    def block_place(self, block):
        return 2 * jnp.where(self.y == block // 2, 0, 1) + jnp.where(self.t == block % 2, 0, 1)


def reduce_stages(p, items, scratch):
    (
        x_slot,
        made_slot,
        own_slot,
        pair_slot,
        y_slot,
        z_slot,
        z_pair,
        inner_slot,
        total_slot,
        x_send,
        x_recv,
        y_send,
        y_recv,
        outer_send,
        outer_recv,
        inner_send,
        inner_recv,
        out_sem,
        x_free,
        y_free,
        outer_free,
        inner_free,
    ) = scratch
    y, z = p.y, p.z
    outer = (z == 0) | (z == 3)
    inner = (z == 1) | (z == 2)
    slots = x_slot.shape[0]
    count = len(items)
    far_count = count // 2
    far_slots = y_slot.shape[0]

    def x_copy(i):
        k = i % slots
        return remote_copy(made_slot.at[k], x_slot.at[k], x_send.at[k], x_recv.at[k], p.over_x)

    def y_copy(i):
        k, g = i % slots, (i // 2) % far_slots
        return remote_copy(pair_slot.at[k], y_slot.at[g], y_send.at[g], y_recv.at[g], p.over_y)

    def summed(i):
        return y_slot.at[(i // 2) % far_slots] if items[i][0] else pair_slot.at[i % slots]

    def outward(i):
        k = i % slots
        return remote_copy(summed(i), z_slot.at[k], outer_send.at[k], outer_recv.at[k], p.mate)

    def across(i):
        k = i % slots
        return remote_copy(z_pair.at[k], inner_slot.at[k], inner_send.at[k], inner_recv.at[k], p.middle)

    def backward(i):
        k = i % slots
        return remote_copy(total_slot.at[k], z_slot.at[k], outer_send.at[k], outer_recv.at[k], p.mate)

    def result_inner(i):
        k = i % slots
        return pltpu.make_async_copy(total_slot.at[k], items[i][1], out_sem.at[k])

    def result_outer(i):
        k = i % slots
        return pltpu.make_async_copy(z_slot.at[k], items[i][1], out_sem.at[k])

    def add(left, right, target):
        target[...] = (left[...].astype(jnp.float32) + right[...].astype(jnp.float32)).astype(
            target.dtype
        )

    def stage_send(i):
        k = i % slots
        items[i][2](made_slot.at[k], own_slot.at[k])
        if i >= slots:
            pl.semaphore_wait(x_free, 1)
        x_copy(i).start()

    def stage_pair(i):
        x_copy(i).wait()
        k = i % slots
        add(x_slot.at[k], own_slot.at[k], pair_slot.at[k])
        if i + slots < count:
            grant(x_free, p.over_x)
        if items[i][0]:
            if i // 2 >= far_slots:
                pl.semaphore_wait(y_free, 1)
            y_copy(i).start()

    def stage_outward(i):
        if items[i][0]:
            y_copy(i).wait()

        @pl.when(outer)
        def _():
            if i >= slots:
                pl.semaphore_wait(outer_free, 1)
            outward(i).start()

    def stage_across(i):
        k = i % slots

        @pl.when(outer)
        def _():
            outward(i).wait_send()

        @pl.when(inner)
        def _():
            outward(i).wait_recv()
            add(summed(i), z_slot.at[k], z_pair.at[k])
            if i + slots < count:
                grant(outer_free, p.mate)
            if i >= slots:
                pl.semaphore_wait(inner_free, 1)
            across(i).start()

        if items[i][0] and i // 2 + far_slots < far_count:
            grant(y_free, p.over_y)

    def stage_total(i):
        k = i % slots

        @pl.when(inner)
        def _():
            across(i).wait()
            add(z_pair.at[k], inner_slot.at[k], total_slot.at[k])
            if i + slots < count:
                grant(inner_free, p.middle)
            if i >= slots:
                pl.semaphore_wait(outer_free, 1)
            backward(i).start()
            result_inner(i).start()

    def stage_result(i):
        @pl.when(inner)
        def _():
            backward(i).wait_send()
            result_inner(i).wait()

        @pl.when(outer)
        def _():
            backward(i).wait_recv()
            result_outer(i).start()

    def stage_finish(i):
        @pl.when(outer)
        def _():
            result_outer(i).wait()
            if i + slots < count:
                grant(outer_free, p.mate)

    stages = (
        (11, stage_finish),
        (10, stage_result),
        (8, stage_total),
        (6, stage_across),
        (4, stage_outward),
        (2, stage_pair),
        (0, stage_send),
    )

    def run(step):
        for lag, stage in stages:
            if 0 <= step - lag < count:
                stage(step - lag)

    return run, count + 12


def reduce_scratch(slots, far_slots, rows, cols):
    dma, regular = pltpu.SemaphoreType.DMA, pltpu.SemaphoreType.REGULAR
    counts = (slots,) * 4 + (far_slots,) + (slots,) * 4
    return [pltpu.VMEM((n, rows, cols), jnp.bfloat16) for n in counts] + [
        dma((n,)) for n in (slots,) * 2 + (far_slots,) * 2 + (slots,) * 5
    ] + [regular] * 4


PARTS = 4


class RowSum:
    def __init__(self, p, rows, arrived, sent, loaded, send_sem, recv_sem, load_sem, core_free, y_free, uses):
        self.p, self.rows, self.uses = p, rows, uses
        self.arrived, self.sent, self.loaded = arrived, sent, loaded
        self.send_sem, self.recv_sem, self.load_sem = send_sem, recv_sem, load_sem
        self.core_free, self.y_free = core_free, y_free

    def block(self, ref, k):
        return ref.at[pl.ds(k * self.rows, self.rows), :]

    def hop(self, ref, k):
        return remote_copy(
            self.block(ref, 3 - 2 * k),
            self.arrived.at[k],
            self.send_sem.at[k],
            self.recv_sem.at[k],
            self.p.over_core,
        )

    def hop_y(self, part):
        size = self.rows // PARTS
        cut = pl.ds(part * size, size)
        return remote_copy(
            self.sent.at[cut, :],
            self.arrived.at[2, cut, :],
            self.send_sem.at[2 + part],
            self.recv_sem.at[2 + part],
            self.p.over_y,
        )

    def load(self, ref, k):
        return pltpu.make_async_copy(self.block(ref, k), self.loaded, self.load_sem)

    def start(self, use, ref, local):
        if use:
            pl.semaphore_wait(self.core_free, 1)
            pl.semaphore_wait(self.y_free, 1)
        self.hop(ref, 0).start()
        self.hop(ref, 1).start()
        if not local:
            self.load(ref, 2).start()

    def middle(self, ref, local, part):
        if part == 0:
            self.hop(ref, 0).wait()
            if not local:
                self.load(ref, 2).wait()
        base = self.block(ref, 2) if local else self.loaded
        size = self.rows // PARTS

        @pl.loop(part * size // 32, (part + 1) * size // 32)
        def _(k):
            at = pl.ds(pl.multiple_of(k * 32, 32), 32)
            self.sent[at, :] = (
                base[at, :].astype(jnp.float32) + self.arrived[0, at, :].astype(jnp.float32)
            ).astype(jnp.bfloat16)

        self.hop_y(part).start()
        if part == PARTS - 1 and not local:
            self.load(ref, 0).start()

    def finish(self, ref, local):
        self.hop(ref, 1).wait()
        for part in range(PARTS):
            self.hop_y(part).wait()
        if not local:
            self.load(ref, 0).wait()

    def total(self, ref, local, at):
        base = self.block(ref, 0) if local else self.loaded
        return (
            base[at, :].astype(jnp.float32)
            + self.arrived[1, at, :].astype(jnp.float32)
            + self.arrived[2, at, :].astype(jnp.float32)
        )

    def release(self, use):
        if use + 1 < self.uses:
            grant(self.core_free, self.p.over_core)
            grant(self.y_free, self.p.over_y)


def unit_rows(values):
    center = values - jnp.mean(values, -1, keepdims=True)
    inverse = lax.rsqrt(jnp.mean(center * center, -1, keepdims=True) + EPS)
    return center * inverse, inverse


def unit_back(upstream, unit, inverse, gain):
    scaled = upstream * gain
    return inverse * (
        scaled
        - jnp.mean(scaled, -1, keepdims=True)
        - unit * jnp.mean(scaled * unit, -1, keepdims=True)
    )


GAIN_ONE, SHIFT_ONE, OUT_BIAS, GAIN_TWO, SHIFT_TWO, DOWN_BIAS, QUERY_BIAS, VALUE_BIAS, UP_BIAS, PEAKS = (
    0,
    1,
    2,
    3,
    4,
    5,
    6,
    7,
    8,
    12,
)


def prepare_kernel(dealing, lengths, place, rows_ref, cot_ref, rows_out, cot_out, bias_ref, length_ref):
    step = pl.program_id(0)
    rows_out[...] = rows_ref[...]
    cot = cot_ref[...]
    cot_out[...] = cot.astype(cot_out.dtype)

    @pl.when(step == 0)
    def _():
        bias_ref[...] = jnp.zeros_like(bias_ref)
        length_ref[0] = lengths[dealing[place[1]]]

    bias_ref[pl.ds(0, 1), :] += jnp.sum(cot[0], 0, keepdims=True)


def prepare(dealing, seq_lengths, place, layer_input, cotangent, count):
    block = (1,) + layer_input.shape[1:]
    width = layer_input.shape[2]
    return pl.pallas_call(
        prepare_kernel,
        out_shape=(
            jax.ShapeDtypeStruct((count,) + block[1:], jnp.float32),
            jax.ShapeDtypeStruct((count,) + block[1:], jnp.bfloat16),
            jax.ShapeDtypeStruct((8, width), jnp.float32),
            jax.ShapeDtypeStruct((1,), jnp.int32),
        ),
        grid_spec=pltpu.PrefetchScalarGridSpec(
            num_scalar_prefetch=3,
            grid=(count,),
            in_specs=[
                pl.BlockSpec(block, lambda j, dealing, lengths, place: (dealing[place[0] * count + j], 0, 0)),
                pl.BlockSpec(block, lambda j, dealing, lengths, place: (place[0] * count + j, 0, 0)),
            ],
            out_specs=(
                pl.BlockSpec(block, lambda j, *_: (j, 0, 0)),
                pl.BlockSpec(block, lambda j, *_: (j, 0, 0)),
                pl.BlockSpec((8, width), lambda j, *_: (0, 0)),
                pl.BlockSpec(memory_space=pltpu.SMEM),
            ),
        ),
    )(dealing, seq_lengths, place, layer_input, cotangent)


def finish_kernel(head_size, place, level_ref, totals_ref, query_ref, key_ref, *refs):
    count = (len(refs) - 3) // 2
    for source, target in zip(refs[:count], refs[count : 2 * count]):
        target[...] = source[...].astype(target.dtype)
    query_out, key_out, factor = refs[2 * count :]
    level = level_ref[0]
    heads = factor.shape[1] // head_size

    @pl.when(pl.program_id(0) == 0)
    def _():
        peaks = totals_ref[pl.ds(PEAKS, 1), :]
        lane = lax.broadcasted_iota(jnp.int32, peaks.shape, 1)
        for h in range(heads):
            mine = jnp.where(lane == place[0] * heads + h, peaks, NEG)
            peak = jnp.max(mine, -1, keepdims=True)
            value = jnp.sqrt(level / jnp.maximum(peak, level))
            factor[:, pl.ds(h * head_size, head_size)] = jnp.broadcast_to(value, (8, head_size))

    scale = factor[pl.ds(0, 1), :]
    query_out[...] = (query_ref[...].astype(jnp.float32) * scale).astype(query_out.dtype)
    key_out[...] = (key_ref[...].astype(jnp.float32) * scale).astype(key_out.dtype)


def finish_all(head_size, place, level, totals, query_weight, key_weight, arrays):
    steps = 8

    def spec(v):
        block = (v.shape[0] // steps,) + v.shape[1:]
        return pl.BlockSpec(block, lambda i: (i,) + (0,) * (v.ndim - 1))

    smem = pl.BlockSpec(memory_space=pltpu.SMEM)
    weights = (query_weight, key_weight)
    return pl.pallas_call(
        functools.partial(finish_kernel, head_size),
        out_shape=tuple(jax.ShapeDtypeStruct(v.shape, jnp.float32) for v in arrays)
        + tuple(jax.ShapeDtypeStruct(v.shape, v.dtype) for v in weights),
        grid=(steps,),
        in_specs=[smem, smem, pl.BlockSpec(totals.shape, lambda i: (0, 0))]
        + [spec(v) for v in weights]
        + [spec(v) for v in arrays],
        out_specs=tuple(spec(v) for v in arrays) + tuple(spec(v) for v in weights),
        scratch_shapes=[pltpu.VMEM((8, query_weight.shape[1]), jnp.float32)],
        compiler_params=pltpu.CompilerParams(vmem_limit_bytes=60 << 20),
    )(place, level, totals, *weights, *arrays)


def forward_kernel(
    head_size,
    info,
    vec_hbm,
    head_hbm,
    q_ref,
    k_ref,
    v_ref,
    o_ref,
    u_ref,
    d_ref,
    arrived_hbm,
    cot_hbm,
    qkv_mat_out,
    out_mat_out,
    up_all,
    down_out,
    act_out,
    cot_out,
    qkv_out,
    attended_out,
    hidden_out,
    resid_out,
    two_out,
    back_out,
    vec_all,
    peaks,
    cot_all,
    down_all,
    back_stage,
    qkv_mat,
    out_mat,
    fresh,
    part,
    act,
    hidden,
    qkv,
    keys,
    values,
    attended,
    partial,
    arrived,
    sent,
    two,
    vec_own,
    head_own,
    head_got,
    qkv_bias,
    local_sem,
    send_sem,
    recv_sem,
    row_send,
    row_recv,
    join_send,
    join_recv,
    vec_send,
    vec_recv,
    load_sem,
    sum_send,
    sum_recv,
    out_sem,
):
    f32, bf16 = jnp.float32, jnp.bfloat16
    depth, block_rows, width = arrived_hbm.shape
    own_rows = depth * block_rows
    strip = q_ref.shape[0]
    features = q_ref.shape[1] // 2
    units = u_ref.shape[1] // 2
    heads = features // head_size
    p = Place(depth)
    f, x, y, z, t = p.f, p.x, p.y, p.z, p.t
    even = z % 2 == 0
    odd = jnp.logical_not(even)
    diagonal = {"fsdp": 3 - f, "ctx": z, "tp": t}
    entry_barrier([p.over_x, p.over_y, p.mate, p.over_core, diagonal] + p.row_targets())
    length = info[0]

    chunks = []
    rows = strip // 2
    for k, ref in enumerate((q_ref, k_ref, v_ref)):
        for r in range(2):
            chunks.append(
                (
                    lambda w, ref=ref, r=r: ref.at[pl.ds(r * rows, rows), aligned(w * features, features)],
                    lambda home, k=k, r=r: qkv_mat.at[
                        aligned(home * strip + r * rows, rows), pl.ds(k * features, features)
                    ],
                )
            )
    for r in range(2):
        chunks.append(
            (
                lambda w, r=r: o_ref.at[aligned(w * features + r * rows, rows), :],
                lambda home, r=r: out_mat.at[pl.ds(r * rows, rows), aligned(home * strip, strip)],
            )
        )
    pieces = 8
    for r in range(pieces):
        size = strip // pieces
        chunks.append(
            (
                lambda w, r=r, size=size: u_ref.at[pl.ds(r * size, size), aligned(w * units, units)],
                lambda home, r=r, size=size: up_all.at[
                    pl.ds(pl.multiple_of(home * strip + r * size, size), size), :
                ],
            )
        )
    for r in range(pieces):
        size = units // pieces
        chunks.append(
            (
                lambda w, r=r, size=size: d_ref.at[aligned(w * units + r * size, size), :],
                lambda home, r=r, size=size: down_all.at[pl.ds(r * size, size), aligned(home * strip, strip)],
            )
        )
    count = len(chunks)
    far_home = 2 * (1 - y) + x

    def own_copy(i):
        source, place = chunks[i]
        return pltpu.make_async_copy(source(y), place(f), local_sem.at[i])

    def y_copy(i):
        source, place = chunks[i]
        return remote_copy(source(1 - y), place(f), send_sem.at[0, i], recv_sem.at[0, i], p.over_y)

    def x_copy(i, is_even):
        source, place = chunks[i]
        start = source(y) if is_even else place(far_home)
        home = f if is_even else far_home
        return remote_copy(start, place(home), send_sem.at[1, i], recv_sem.at[1, i], p.over_x)

    def z_copy(i, is_even):
        place = chunks[i][1]
        home = 2 * y + 1 - x if is_even else 2 * (1 - y) + 1 - x
        return remote_copy(place(home), place(home), send_sem.at[2, i], recv_sem.at[2, i], p.mate)

    rows_of = ((part, act), (cot_hbm, cot_all), (arrived_hbm, hidden))

    def row_copy(a, k):
        source, place = rows_of[a]
        return remote_copy(
            source.at[k],
            place.at[pl.ds(pl.multiple_of(z * block_rows, block_rows), block_rows), :],
            row_send.at[a, k],
            row_recv.at[a, z],
            p.row_target(k),
        )

    def row_arrival(a, k):
        source, place = rows_of[a]
        return remote_copy(
            source.at[k],
            place.at[pl.ds(k * block_rows, block_rows), :],
            row_send.at[a, k],
            row_recv.at[a, k],
            p.row_target(k),
        )

    def row_stay(a, k):
        source, place = rows_of[a]
        return pltpu.make_async_copy(
            source.at[k], place.at[pl.ds(k * block_rows, block_rows), :], row_send.at[a, k]
        )

    def rows_start(a):
        for k in range(depth):
            stays = (z == k) & (x == t)
            pl.when(stays)(lambda k=k: row_stay(a, k).start())
            pl.when(jnp.logical_not(stays))(lambda k=k: row_copy(a, k).start())

    def rows_wait(a):
        for k in range(depth):
            stays = (z == k) & (x == t)
            pl.when(stays)(lambda k=k: row_stay(a, k).wait())

            @pl.when(jnp.logical_not(stays))
            def _(k=k):
                row_copy(a, k).wait_send()
                row_arrival(a, k).wait_recv()

    joined = (act, cot_all, two)

    def block(ref, k):
        return ref.at[pl.ds(k * own_rows, own_rows), :]

    def join(a, step):
        source, place, target = ((0, 1, p.over_core), (0, 2, p.over_y), (2, 3, p.over_core))[step]
        ref = joined[a]
        return remote_copy(
            block(ref, source), block(ref, place), join_send.at[a, step], join_recv.at[a, step], target
        )

    def join_start(a):
        join(a, 0).start()
        join(a, 1).start()

    def join_pass(a):
        join(a, 1).wait_recv()
        join(a, 2).start()

    def join_end(a):
        join(a, 0).wait()
        join(a, 1).wait_send()
        join(a, 2).wait()

    def vec_place(ref):
        return ref.at[:, aligned(f * strip, strip)]

    vec_targets = (p.over_x, p.over_y, diagonal)

    def vec_copy(k):
        return remote_copy(vec_own, vec_place(vec_all), vec_send.at[0, k], vec_recv.at[0, k], vec_targets[k])

    def head_copy(k):
        return remote_copy(head_own, head_got.at[k], vec_send.at[1, k], vec_recv.at[1, k], vec_targets[k])

    loads = [
        pltpu.make_async_copy(source, target, load_sem.at[k])
        for k, (source, target) in enumerate(
            ((vec_hbm, vec_own), (head_hbm, head_own), (arrived_hbm, fresh))
        )
    ]

    def begin():
        for load in loads:
            load.start()
        loads[0].wait()
        loads[1].wait()
        for k in range(3):
            vec_copy(k).start()
            head_copy(k).start()
        vec_place(vec_all)[...] = vec_own[...]
        peaks[...] = jnp.full_like(peaks, NEG)

    def vector_row(k):
        return vec_all[pl.ds(k, 1), :]

    group_rows = 16

    def first_norm():
        for k in range(3):
            vec_copy(k).wait()
            head_copy(k).wait()
        loads[2].wait()
        for k in range(3):
            head_own[...] += head_got[k]
        qkv_bias[...] = jnp.zeros_like(qkv_bias)
        for h in range(heads):
            lanes = pl.ds(h * head_size, head_size)
            qkv_bias[pl.ds(0, 1), lanes] = head_own[pl.ds(heads * y + h, 1), :]
            lanes = pl.ds(2 * features + h * head_size, head_size)
            qkv_bias[pl.ds(0, 1), lanes] = head_own[pl.ds(2 * heads + heads * y + h, 1), :]
        gain, shift = vector_row(GAIN_ONE), vector_row(SHIFT_ONE)
        for s in range(depth):

            @pl.loop(0, block_rows // group_rows)
            def _(k, s=s):
                at = pl.ds(pl.multiple_of(k * group_rows, group_rows), group_rows)
                unit, _ = unit_rows(fresh[s, at, :])
                part[s, at, :] = (unit * gain + shift).astype(bf16)

        rows_start(0)

    def weights_wait(start, stop):
        for i in range(start, stop):
            own_copy(i).wait()
            z_copy(i, True).wait_recv()

    kept, used = [], [0]

    def keep(source, target):
        copy = pltpu.make_async_copy(source, target, out_sem.at[used[0]])
        used[0] += 1
        copy.start()
        kept.append(copy)

    def project(k):
        at = pl.ds(k * own_rows, own_rows)

        @pl.loop(0, 3)
        def _(c):
            cut = aligned(c * features, features)
            qkv[at, cut] = (
                jnp.dot(act[at, :], qkv_mat[:, cut], preferred_element_type=f32)
                + qkv_bias[pl.ds(0, 1), cut]
            ).astype(bf16)

    def head_rows():
        for b in range(4):
            at = pl.ds(pl.multiple_of(p.block_place(b) * own_rows, own_rows), own_rows)
            keys[pl.ds(b * own_rows, own_rows), :] = qkv[at, pl.ds(features, features)]
            values[pl.ds(b * own_rows, own_rows), :] = qkv[at, pl.ds(2 * features, features)]

    def attention_block(b):
        at = pl.ds(pl.multiple_of(p.block_place(b) * own_rows, own_rows), own_rows)
        past = pl.ds(0, (b + 1) * own_rows)

        @pl.loop(0, heads)
        def _(head):
            lanes = aligned(head * head_size, head_size)
            probs, top = attention_probs(qkv[at, lanes], keys[past, lanes], b, length)
            attended[at, lanes] = jnp.dot(
                probs.astype(bf16), values[past, lanes], preferred_element_type=f32
            ).astype(bf16)
            live = b * own_rows + lax.broadcasted_iota(jnp.int32, top.shape, 0) < length
            peak = jnp.max(jnp.where(live, top, NEG), 0, keepdims=True)
            row = pl.ds(head, 1)
            peaks[row, :] = jnp.maximum(peaks[row, :], jnp.broadcast_to(peak, (1, peaks.shape[1])))

    sums = RowSum(p, own_rows, arrived, sent, None, sum_send, sum_recv, None, None, None, 1)

    def out_block(k):
        at = pl.ds(k * own_rows, own_rows)

        @pl.loop(0, 4)
        def _(n):
            cut = aligned(n * strip, strip)
            partial[at, cut] = jnp.dot(
                attended[at, :], out_mat[:, cut], preferred_element_type=f32
            ).astype(bf16)

    spot = []

    def keep_resid():
        spot.append(len(kept))
        keep(hidden, resid_out)

    back_sem = [out_sem.at[10], out_sem.at[11]]
    unit_rows_per_chunk = units // pieces

    def back_store(r):
        cut = pl.ds(r * unit_rows_per_chunk, unit_rows_per_chunk)
        return pltpu.make_async_copy(back_stage.at[r % 2], back_out.at[:, cut], back_sem[r % 2])

    def back_chunk(r):
        weights_wait(8 + pieces + r, 9 + pieces + r)
        if r >= 2:
            back_store(r - 2).wait()

        @pl.loop(0, 4)
        def _(b):
            at = pl.ds(pl.multiple_of(b * own_rows, own_rows), own_rows)
            back_stage[r % 2, at, :] = lax.dot_general(
                cot_all[at, :],
                down_all[pl.ds(r * unit_rows_per_chunk, unit_rows_per_chunk), :],
                (((1,), (1,)), ((), ())),
                preferred_element_type=f32,
            ).astype(bf16)

        back_store(r).start()

    def second_norm():
        sums.finish(partial, True)
        kept.pop(spot[0]).wait()
        bias, gain, shift = vector_row(OUT_BIAS), vector_row(GAIN_TWO), vector_row(SHIFT_TWO)

        @pl.loop(0, own_rows // group_rows)
        def _(k):
            at = pl.ds(pl.multiple_of(k * group_rows, group_rows), group_rows)
            value = hidden[at, :] + sums.total(partial, True, at) + bias
            hidden[at, :] = value
            unit, _ = unit_rows(value)
            two[at, :] = (unit * gain + shift).astype(bf16)

        join_start(2)
        keep(hidden, hidden_out)

    def call(function, *arguments):
        return lambda: function(*arguments)

    plan = {}

    def at_step(step, *tasks):
        plan.setdefault(step, []).extend(tasks)

    at_step(0, begin)
    at_step(1, first_norm)
    at_step(5, call(rows_wait, 0), call(join_start, 0), call(rows_start, 1))
    at_step(10, call(rows_start, 2))
    at_step(10, call(rows_wait, 1), call(join_start, 1), call(join_pass, 0))
    at_step(18, call(join_pass, 1))
    at_step(11, call(weights_wait, 0, 6), call(project, 0))
    at_step(12, join(0, 0).wait, call(project, 1), lambda: keep(qkv_mat, qkv_mat_out))
    at_step(13, join(0, 1).wait_send, join(0, 2).wait, call(project, 2), lambda: keep(act, act_out))
    at_step(14, call(project, 3), head_rows, lambda: keep(qkv, qkv_out))
    at_step(15, call(attention_block, 0), call(attention_block, 1))
    at_step(16, call(attention_block, 2))
    at_step(17, call(attention_block, 3), lambda: keep(attended, attended_out))
    at_step(18, call(weights_wait, 6, 8), call(out_block, 3), call(out_block, 1))
    at_step(18, call(sums.start, 0, partial, True))
    at_step(19, call(out_block, 2), *(call(sums.middle, partial, True, part) for part in range(PARTS)))
    at_step(19, call(out_block, 0), lambda: keep(out_mat, out_mat_out))
    at_step(19, call(rows_wait, 2), keep_resid)
    at_step(21, call(join_end, 1), lambda: keep(cot_all, cot_out))
    at_step(23, call(back_chunk, 0))
    at_step(24, second_norm)
    at_step(24, call(back_chunk, 1))
    at_step(25, call(back_chunk, 2))
    at_step(26, call(back_chunk, 3))
    at_step(27, call(join_pass, 2), call(back_chunk, 4))
    lag = 2
    for i in range(count + 2 * lag):
        if i < count:
            y_copy(i).start()
            pl.when(even)(lambda i=i: x_copy(i, True).start())
            own_copy(i).start()
        j = i - lag
        if 0 <= j < count:
            y_copy(j).wait_recv()

            @pl.when(even)
            def _(j=j):
                x_copy(j, True).wait_recv()
                z_copy(j, True).start()

            pl.when(odd)(lambda j=j: x_copy(j, False).start())
        j = i - 2 * lag
        if 0 <= j < count:

            @pl.when(odd)
            def _(j=j):
                x_copy(j, False).wait_recv()
                z_copy(j, False).start()

        for task in plan.get(i, ()):
            task()

    for r in range(5, pieces):
        back_chunk(r)
    keep(down_all, down_out)
    join_end(2)
    keep(two, two_out)
    weights_wait(8, 8 + pieces)
    back_store(pieces - 2).wait()
    back_store(pieces - 1).wait()
    for i in range(count):
        y_copy(i).wait_send()
        x_copy(i, True).wait_send()
        z_copy(i, True).wait_send()
    for copy in kept:
        copy.wait()


def forward_all(
    head_size,
    length,
    vectors,
    head_vectors,
    query_weight,
    key_weight,
    value_weight,
    out_weight,
    up_weight,
    down_weight,
    arrived,
    cot,
):
    strip, features, units = query_weight.shape[0], query_weight.shape[1] // 2, up_weight.shape[1] // 2
    width = 4 * strip
    depth, block_rows = arrived.shape[:2]
    own_rows = depth * block_rows
    tokens = 4 * own_rows
    bf16, f32 = jnp.bfloat16, jnp.float32
    hbm = pl.BlockSpec(memory_space=pl.ANY)
    vmem = pl.BlockSpec(memory_space=pltpu.VMEM)
    count = 24
    dma = pltpu.SemaphoreType.DMA

    def made(shape, dtype=bf16):
        return jax.ShapeDtypeStruct(shape, dtype)

    def hold(shape, dtype=bf16):
        return pltpu.VMEM(shape, dtype)

    return pl.pallas_call(
        functools.partial(forward_kernel, head_size),
        out_shape=(
            made((width, 3 * features)),
            made((features, width)),
            made((width, units)),
            made((units, width)),
            made((tokens, width)),
            made((tokens, width)),
            made((tokens, 3 * features)),
            made((tokens, features)),
            made((own_rows, width), f32),
            made((own_rows, width), f32),
            made((tokens, width)),
            made((tokens, units)),
            made((8, width), f32),
            made((8, 128), f32),
        ),
        in_specs=[pl.BlockSpec(memory_space=pltpu.SMEM)] + [hbm] * 10,
        out_specs=(hbm,) * 12 + (vmem,) * 2,
        scratch_shapes=[
            hold((tokens, width)),
            hold((units, width)),
            hold((2, tokens, units // 8)),
            hold((width, 3 * features)),
            hold((features, width)),
            hold((depth, block_rows, width), f32),
            hold((depth, block_rows, width)),
            hold((tokens, width)),
            hold((own_rows, width), f32),
            hold((tokens, 3 * features)),
            hold((tokens, features)),
            hold((tokens, features)),
            hold((tokens, features)),
            hold((tokens, width)),
            hold((3, own_rows, width)),
            hold((own_rows, width)),
            hold((tokens, width)),
            hold((8, strip), f32),
            hold(head_vectors.shape, f32),
            hold((3,) + head_vectors.shape, f32),
            hold((8, 3 * features), f32),
            dma((count,)),
            dma((3, count)),
            dma((3, count)),
            dma((3, depth)),
            dma((3, depth)),
            dma((3, 3)),
            dma((3, 3)),
            dma((2, 3)),
            dma((2, 3)),
            dma((3,)),
            dma((2 + PARTS,)),
            dma((2 + PARTS,)),
            dma((12,)),
        ],
        compiler_params=pltpu.CompilerParams(
            collective_id=0, has_side_effects=True, vmem_limit_bytes=56 << 20
        ),
        cost_estimate=pl.CostEstimate(flops=0, bytes_accessed=64 << 20, transcendentals=0),
    )(
        length,
        vectors,
        head_vectors,
        query_weight,
        key_weight,
        value_weight,
        out_weight,
        up_weight,
        down_weight,
        arrived,
        cot,
    )


def backward_kernel(
    head_size,
    info,
    vector_ref,
    small_in,
    gelu_hbm,
    pre_hbm,
    act_two_hbm,
    up_hbm,
    down_hbm,
    hidden_hbm,
    cot_hbm,
    resid_hbm,
    out_hbm,
    qkv_mat_hbm,
    qkv_hbm,
    attended_hbm,
    act_hbm,
    down_sum,
    up_sum,
    out_sum,
    qkv_sums,
    rows_out,
    rows_grad,
    small,
    two_part,
    mlp_part,
    engine,
    base,
    hidden_grad,
    low,
    out_mat,
    attended_grad,
    qkv,
    qkv_grad,
    act,
    attended,
    qkv_mat,
    keys,
    values,
    key_sum,
    value_sum,
    strips,
    packed,
    arrived,
    sent,
    loaded,
    small_arrived,
    load_sem,
    sum_send,
    sum_recv,
    sum_load,
    join_send,
    join_recv,
    strip_sem,
    row_send,
    row_recv,
    share_send,
    share_recv,
    small_send,
    small_recv,
    core_free,
    y_free,
    low_core,
    low_y,
):
    f32, bf16 = jnp.float32, jnp.bfloat16
    own_rows, width = base.shape
    tokens, features = attended.shape
    heads = features // head_size
    depth = rows_out.shape[0] // 2
    block_rows = rows_out.shape[1]
    p = Place(depth)
    x, y, z, t = p.x, p.y, p.z, p.t
    entry_barrier(
        [p.over_x, p.over_y, p.over_core, p.mate, p.middle, p.hop] + p.row_targets()
    )
    length = info[0]
    scale = 1.0 / math.sqrt(head_size)
    column = 2 * t + y

    rows, cols = engine[0].shape[1:]
    down_rows = down_sum.shape[0] // 2
    up_cols = up_sum.shape[1] // 2
    strip = out_sum.shape[1]

    def over_tokens(left, right, target):
        target[...] = lax.dot_general(
            left, right, (((0,), (0,)), ((), ())), preferred_element_type=f32
        ).astype(target.dtype)

    per_down, per_up = down_rows // strip, up_cols // cols
    strip_count = per_down + per_up

    def strip_load(n):
        source = gelu_hbm if n < per_down else pre_hbm
        cut = pl.ds((n % per_down) * strip, strip)
        return pltpu.make_async_copy(source.at[:, cut], strips.at[n % 2], strip_sem.at[n % 2])

    def resident_load(k):
        source = (cot_hbm, act_two_hbm, act_hbm)[k]
        return pltpu.make_async_copy(source, act, load_sem.at[5])

    def strip_ready(n):
        strip_load(n).wait()
        if n + 1 < strip_count:
            strip_load(n + 1).start()

    def homes_of(far):
        return (p.homes[1], p.homes[3]) if far else (p.homes[0], p.homes[2])

    def down_item(r, far):
        def make(send, own):
            if far and r % 2 == 0:
                if r == 0:
                    resident_load(0).wait()
                strip_ready(r // 2)
            left = strips.at[(r // 2) % 2, :, pl.ds((r % 2) * rows, rows)]
            for home, target in zip(homes_of(far), (send, own)):
                over_tokens(left[...], act[:, aligned(home * strip, strip)], target)

        side = 1 - y if far else y
        return far, down_sum.at[aligned(side * down_rows + r * rows, rows), :], make

    def up_item(c, r, far):
        def make(send, own):
            if far and r == 0:
                if c == 0:
                    resident_load(1).start()
                    resident_load(1).wait()
                strip_ready(per_down + c)
            for home, target in zip(homes_of(far), (send, own)):
                over_tokens(
                    act[:, aligned(home * strip + r * rows, rows)], strips[c % 2], target
                )

        side = 1 - y if far else y
        place = up_sum.at[pl.ds(r * rows, rows), aligned(side * up_cols + c * cols, cols)]
        return far, place, make

    def out_item(r, far):
        def make(send, own):
            for home, target in zip(homes_of(far), (send, own)):
                over_tokens(
                    attended[:, pl.ds(r * rows, rows)], low[:, aligned(home * strip, strip)], target
                )

        side = 1 - y if far else y
        return far, out_sum.at[aligned(side * features + r * rows, rows), :], make

    def qkv_item(r, c, far):
        def make(send, own):
            if far and r == 0 and c == 0:
                resident_load(2).start()
                resident_load(2).wait()
            for home, target in zip(homes_of(far), (send, own)):
                over_tokens(
                    act[:, aligned(home * strip + r * rows, rows)],
                    qkv_grad[:, pl.ds(c * cols, cols)],
                    target,
                )

        side = 1 - y if far else y
        return far, qkv_sums[c].at[pl.ds(r * rows, rows), aligned(side * cols, cols)], make

    sides = (True, False)
    items = [down_item(r, far) for r in range(down_rows // rows) for far in sides]
    items += [up_item(c, r, far) for c in range(per_up) for r in range(strip // rows) for far in sides]
    items += [out_item(r, far) for r in range(features // rows) for far in sides]
    items += [qkv_item(r, c, far) for r in range(strip // rows) for c in range(3) for far in sides]
    run, steps = reduce_stages(p, items, engine)

    loads = [
        pltpu.make_async_copy(source, target, load_sem.at[k])
        for k, (source, target) in enumerate(
            (
                (hidden_hbm, base),
                (cot_hbm.at[pl.ds(0, own_rows), :], packed),
                (out_hbm, out_mat),
                (qkv_hbm, qkv),
                (attended_hbm, attended),
                (cot_hbm, act),
                (qkv_mat_hbm, qkv_mat),
                (resid_hbm, base),
            )
        )
    ]
    sums = RowSum(
        p, own_rows, arrived, sent, loaded, sum_send, sum_recv, sum_load, core_free, y_free, 3
    )
    group_rows = 16
    quarter = own_rows // 4 // group_rows

    def start():
        loads[5].start()
        strip_load(0).start()
        low_load(0).start()
        up_load(0).start()
        for k in (0, 1, 3, 4):
            loads[k].start()
        for n in range(3):
            down_load(n).start()
        small[...] = small_in[...]
        key_sum[...] = jnp.zeros_like(key_sum)
        value_sum[...] = jnp.zeros_like(value_sum)

    def low_load(k):
        return pltpu.make_async_copy((pre_hbm, gelu_hbm)[k], low, load_sem.at[8])

    def up_load(n):
        return pltpu.make_async_copy(up_hbm.at[pl.ds(n * strip, strip), :], out_mat, load_sem.at[9])

    def down_load(n):
        return pltpu.make_async_copy(
            down_hbm.at[:, pl.ds(n * strip, strip)],
            qkv_mat.at[:, pl.ds((n % 3) * strip, strip)],
            load_sem.at[10 + n % 3],
        )

    held = (keys, values)

    def part_store(k, n):
        target = (two_part, mlp_part)[k].at[:, pl.ds(n * strip, strip)]
        return pltpu.make_async_copy(held[n % 2], target, load_sem.at[13 + n % 2])

    def part_columns(k, n):
        if n == 0:
            low_load(k).wait()
        (down_load(n) if k else up_load(n)).wait()
        if n >= 2:
            part_store(k, n - 2).wait()

        @pl.loop(0, 4)
        def _(b):
            at = pl.ds(pl.multiple_of(b * own_rows, own_rows), own_rows)
            if k:
                right, side = qkv_mat[:, pl.ds((n % 3) * strip, strip)], 0
            else:
                right, side = out_mat[...], 1
            held[n % 2][at, :] = lax.dot_general(
                low[at, :], right, (((1,), (side,)), ((), ())), preferred_element_type=f32
            ).astype(bf16)

        part_store(k, n).start()
        if k == 0 and n < 3:
            up_load(n + 1).start()
        if k == 0 and n == 3:
            low_load(1).start()
            loads[2].start()
        if k == 1 and n == 0:
            down_load(3).start()
        if k == 1 and n == 3:
            loads[6].start()

    def part_end(k):
        part_store(k, 2).wait()
        part_store(k, 3).wait()
        if k == 0:
            sums.start(0, two_part, False)
        else:
            grant(low_core, p.over_core)
            grant(low_y, p.over_y)

    def two_middle(part):
        sums.middle(two_part, False, part)

    def two_finish():
        sums.finish(two_part, False)
        loads[0].wait()
        loads[1].wait()

    def accumulate(row, value):
        small[pl.ds(row, 1), :] += jnp.sum(value, 0, keepdims=True)

    def two_rows(part):
        gain = vector_ref[pl.ds(GAIN_TWO, 1), :]

        @pl.loop(part * quarter, (part + 1) * quarter)
        def _(k):
            at = pl.ds(pl.multiple_of(k * group_rows, group_rows), group_rows)
            upstream = sums.total(two_part, False, at)
            unit, inverse = unit_rows(base[at, :])
            grad = packed[at, :].astype(f32) + unit_back(upstream, unit, inverse, gain)
            hidden_grad[at, :] = grad
            low[at, :] = grad.astype(bf16)
            accumulate(GAIN_TWO, upstream * unit)
            accumulate(SHIFT_TWO, upstream)
            accumulate(OUT_BIAS, grad)

    def low_block(k):
        return low.at[pl.ds(k * own_rows, own_rows), :]

    def join(k):
        source, place = ((0, 1), (None, None), (2, 3))[k]
        return remote_copy(
            low_block(source), low_block(place), join_send.at[k], join_recv.at[k], p.over_core
        )

    def join_y(part):
        size = own_rows // PARTS
        return remote_copy(
            low.at[pl.ds(part * size, size), :],
            low.at[pl.ds(2 * own_rows + part * size, size), :],
            join_send.at[3 + part],
            join_recv.at[3 + part],
            p.over_y,
        )

    def join_start():
        pl.semaphore_wait(low_core, 1)
        pl.semaphore_wait(low_y, 1)
        join(0).start()
        join_y(0).start()
        sums.release(0)

    def join_pass():
        for part in range(PARTS):
            join_y(part).wait_recv()
        join(2).start()

    def attend_block(k):
        at = pl.ds(k * own_rows, own_rows)
        attended_grad[at, :] = lax.dot_general(
            low[at, :], out_mat[...], (((1,), (1,)), ((), ())), preferred_element_type=f32
        ).astype(bf16)

    def attend_own():
        loads[2].wait()
        attend_block(0)

    def attend_peer():
        join(0).wait()
        attend_block(1)

    def attend_far():
        attend_block(2)

    def attend_last():
        for part in range(PARTS):
            join_y(part).wait_send()
        join(2).wait()
        attend_block(3)

    def mlp_start():
        sums.start(1, mlp_part, False)

    def mlp_middle(part):
        sums.middle(mlp_part, False, part)

    def mlp_finish():
        sums.finish(mlp_part, False)
        bias = vector_ref[pl.ds(DOWN_BIAS, 1), :]

        @pl.loop(0, own_rows // group_rows)
        def _(k):
            at = pl.ds(pl.multiple_of(k * group_rows, group_rows), group_rows)
            packed[at, :] = (base[at, :] + sums.total(mlp_part, False, at) + bias).astype(bf16)

        sums.release(1)

    def row_source(k):
        return packed.at[pl.ds(pl.multiple_of(k * block_rows, block_rows), block_rows), :]

    row_ends = (rows_out, rows_grad)

    def row_copy(a, k):
        end = row_ends[a].at[x * depth + z]
        return remote_copy(row_source(k), end, row_send.at[a, k], row_recv.at[a, z], p.row_target(k))

    def row_arrival(a, k):
        end = row_ends[a].at[t * depth + k]
        return remote_copy(row_source(k), end, row_send.at[a, k], row_recv.at[a, k], p.row_target(k))

    def row_stay(a, k):
        return pltpu.make_async_copy(row_source(k), row_ends[a].at[x * depth + z], row_send.at[a, k])

    def rows_start(a, turn):
        k = lax.rem(z + turn, depth)
        if turn:
            row_copy(a, k).start()
        else:
            pl.when(x == t)(lambda: row_stay(a, k).start())
            pl.when(x != t)(lambda: row_copy(a, k).start())

    def share(a):
        group = row_ends[a].at[pl.ds(t * depth, depth)]
        return remote_copy(group, group, share_send.at[a], share_recv.at[a], p.over_core)

    def rows_share(a):
        for k in range(depth):
            stays = (z == k) & (x == t)
            pl.when(stays)(lambda k=k: row_stay(a, k).wait())

            @pl.when(jnp.logical_not(stays))
            def _(k=k):
                row_copy(a, k).wait_send()
                row_arrival(a, k).wait_recv()

        share(a).start()

    def head_rows():
        loads[3].wait()
        loads[4].wait()
        for block in range(4):
            at = pl.ds(pl.multiple_of(p.block_place(block) * own_rows, own_rows), own_rows)
            keys[pl.ds(block * own_rows, own_rows), :] = qkv[at, pl.ds(features, features)]
            values[pl.ds(block * own_rows, own_rows), :] = qkv[at, pl.ds(2 * features, features)]

    def attention_block(block):
        at = pl.ds(pl.multiple_of(p.block_place(block) * own_rows, own_rows), own_rows)
        part = pl.ds(0, (block + 1) * own_rows)

        @pl.loop(0, heads)
        def _(head):
            lanes = aligned(head * head_size, head_size)
            queries, grads = qkv[at, lanes], attended_grad[at, lanes]
            probs, _ = attention_probs(queries, keys[part, lanes], block, length)
            prob_grad = lax.dot_general(
                grads, values[part, lanes], (((1,), (1,)), ((), ())), preferred_element_type=f32
            )
            inner = jnp.sum(probs * prob_grad, -1, keepdims=True)
            score_grad = (probs * (prob_grad - inner)).astype(bf16)
            query_grad = (
                jnp.dot(score_grad, keys[part, lanes], preferred_element_type=f32) * scale
            )
            spot = aligned(column * features + head * head_size, head_size)
            small[pl.ds(QUERY_BIAS, 1), spot] += jnp.sum(query_grad, 0, keepdims=True)
            qkv_grad[at, lanes] = query_grad.astype(bf16)
            key_sum[part, lanes] += lax.dot_general(
                score_grad, queries, (((0,), (0,)), ((), ())), preferred_element_type=f32
            )
            value_sum[part, lanes] += lax.dot_general(
                probs.astype(bf16), grads, (((0,), (0,)), ((), ())), preferred_element_type=f32
            )

    def attention_end(block):
        at = pl.ds(pl.multiple_of(p.block_place(block) * own_rows, own_rows), own_rows)
        part = pl.ds(block * own_rows, own_rows)
        qkv_grad[at, pl.ds(features, features)] = (key_sum[part, :] * scale).astype(bf16)
        value_grad = value_sum[part, :]
        qkv_grad[at, pl.ds(2 * features, features)] = value_grad.astype(bf16)
        spot = aligned(column * features, features)
        small[pl.ds(VALUE_BIAS, 1), spot] += jnp.sum(value_grad, 0, keepdims=True)

    def one_block(k):
        if k == 3:
            loads[6].wait()
        at = pl.ds(k * own_rows, own_rows)

        @pl.loop(0, 4)
        def _(n):
            cut = aligned(n * strip, strip)
            low[at, cut] = lax.dot_general(
                qkv_grad[at, :], qkv_mat[cut, :], (((1,), (1,)), ((), ())), preferred_element_type=f32
            ).astype(bf16)

    def one_start():
        sums.start(2, low, True)

    def one_middle(part):
        sums.middle(low, True, part)

    def one_finish():
        sums.finish(low, True)
        loads[7].wait()

    def one_rows(part):
        gain = vector_ref[pl.ds(GAIN_ONE, 1), :]

        @pl.loop(part * quarter, (part + 1) * quarter)
        def _(k):
            at = pl.ds(pl.multiple_of(k * group_rows, group_rows), group_rows)
            upstream = sums.total(low, True, at)
            unit, inverse = unit_rows(base[at, :])
            grad = hidden_grad[at, :] + unit_back(upstream, unit, inverse, gain)
            packed[at, :] = grad.astype(bf16)
            accumulate(GAIN_ONE, upstream * unit)
            accumulate(SHIFT_ONE, upstream)

    def small_copy(k):
        target = (p.over_core, p.over_x, p.over_y, p.mate, p.hop)[k]
        return remote_copy(small, small_arrived.at[k], small_send.at[k], small_recv.at[k], target)

    def small_add(k):
        small_copy(k).wait()
        mine, other = small[...], small_arrived[k]
        row = lax.broadcasted_iota(jnp.int32, mine.shape, 0)
        small[...] = jnp.where(row == PEAKS, jnp.maximum(mine, other), mine + other)

    def call(function, *arguments):
        return lambda: function(*arguments)

    plan = {}

    def at_step(step, *tasks):
        plan.setdefault(step, []).extend(tasks)

    for n in range(4):
        at_step(n, call(part_columns, 0, n))
        at_step(5 + 2 * n, call(part_columns, 1, n))
    at_step(4, call(part_end, 0))
    at_step(13, call(part_end, 1))
    for k in range(4):
        at_step(7 + k, call(two_middle, k))
    at_step(16, two_finish, call(two_rows, 0))
    for k in range(1, 4):
        at_step(16 + k // 2, call(two_rows, k))
    at_step(17, join_start)
    for k in range(1, 4):
        at_step(17 + k, join_y(k).start)
    at_step(18, attend_own)
    at_step(19, attend_peer)
    at_step(21, head_rows)
    at_step(24, join_pass)
    at_step(25, attend_far)
    at_step(26, attend_last)
    at_step(27, call(attention_block, 0), call(attention_block, 1))
    at_step(27 + 1, call(attention_block, 2))
    at_step(27 + 2, call(attention_block, 3))
    at_step(27 + 3, *(call(attention_end, k) for k in range(4)))
    at_step(21, mlp_start)
    for k in range(4):
        at_step(23 + 1 * k, call(mlp_middle, k))
    at_step(33, mlp_finish, loads[7].start, call(rows_start, 0, 0))
    for k in range(1, 4):
        at_step(33 + k, call(rows_start, 0, k))
    at_step(42, lambda: rows_share(0))
    at_step(36, call(one_block, 3), call(one_block, 1), one_start)
    at_step(36 + 1, call(one_block, 2), call(one_block, 0))
    for k in range(4):
        at_step(38 + k, call(one_middle, k))
    at_step(47, one_finish, share(0).wait, call(one_rows, 0))
    for k in range(1, 4):
        at_step(47 + k // 2, call(one_rows, k))
    for k in range(4):
        at_step(48 + k, call(rows_start, 1, k))
    at_step(49, small_copy(0).start)
    for k in range(4):
        at_step(49 + 2 + 2 * k, call(small_add, k), small_copy(k + 1).start)
    at_step(49 + 5 * 2, call(small_add, 4))
    at_step(57, lambda: rows_share(1))
    at_step(59, share(1).wait)
    start()
    for step in range(steps):
        run(step)
        for task in plan.get(step, ()):
            task()


def backward_all(
    head_size,
    length,
    vectors,
    small,
    gelu_low,
    pre_low,
    act_two,
    up_mat,
    down_mat,
    hidden,
    cot_low,
    resid,
    out_mat,
    qkv_mat,
    qkv,
    attended,
    act_one,
    slots,
):
    bf16, f32 = jnp.bfloat16, jnp.float32
    hbm = pl.BlockSpec(memory_space=pl.ANY)
    vmem = pl.BlockSpec(memory_space=pltpu.VMEM)
    down_rows, up_cols = gelu_low.shape[1], pre_low.shape[1]
    tokens, features = attended.shape
    own_rows, width = hidden.shape
    strip = width // 4
    depth = slots // 2
    engine = reduce_scratch(6, 4, 256, 512)
    n_engine = len(engine)

    def kernel(*refs):
        ins, rest = refs[:16], refs[16:]
        outs, scratch = rest[:11], rest[11:]
        backward_kernel(
            head_size,
            *ins,
            outs[0],
            outs[1],
            outs[2],
            outs[3:6],
            *outs[6:],
            scratch[:n_engine],
            *scratch[n_engine:],
        )

    dma, regular = pltpu.SemaphoreType.DMA, pltpu.SemaphoreType.REGULAR

    def hold(shape, dtype=bf16):
        return pltpu.VMEM(shape, dtype)

    return pl.pallas_call(
        kernel,
        out_shape=(
            jax.ShapeDtypeStruct((2 * down_rows, strip), bf16),
            jax.ShapeDtypeStruct((strip, 2 * up_cols), bf16),
            jax.ShapeDtypeStruct((2 * features, strip), bf16),
            jax.ShapeDtypeStruct((strip, 2 * features), bf16),
            jax.ShapeDtypeStruct((strip, 2 * features), bf16),
            jax.ShapeDtypeStruct((strip, 2 * features), bf16),
            jax.ShapeDtypeStruct((slots, own_rows // depth, width), bf16),
            jax.ShapeDtypeStruct((slots, own_rows // depth, width), bf16),
            jax.ShapeDtypeStruct(small.shape, f32),
            jax.ShapeDtypeStruct((tokens, width), bf16),
            jax.ShapeDtypeStruct((tokens, width), bf16),
        ),
        in_specs=[pl.BlockSpec(memory_space=pltpu.SMEM), vmem, vmem] + [hbm] * 13,
        out_specs=(hbm,) * 8 + (vmem,) + (hbm,) * 2,
        scratch_shapes=engine
        + [
            hold((own_rows, width), f32),
            hold((own_rows, width), f32),
            hold((tokens, width)),
            hold((features, width)),
            hold((tokens, features)),
            hold((tokens, 3 * features)),
            hold((tokens, 3 * features)),
            hold((tokens, width)),
            hold((tokens, features)),
            hold((width, 3 * features)),
            hold((tokens, features)),
            hold((tokens, features)),
            hold((tokens, features), f32),
            hold((tokens, features), f32),
            hold((2, tokens, strip)),
            hold((own_rows, width)),
            hold((3, own_rows, width)),
            hold((own_rows, width)),
            hold((own_rows, width)),
            hold((5,) + small.shape, f32),
            dma((15,)),
            dma((2 + PARTS,)),
            dma((2 + PARTS,)),
            dma(()),
            dma((3 + PARTS,)),
            dma((3 + PARTS,)),
            dma((2,)),
            dma((2, depth)),
            dma((2, depth)),
            dma((2,)),
            dma((2,)),
            dma((5,)),
            dma((5,)),
            regular,
            regular,
            regular,
            regular,
        ],
        compiler_params=pltpu.CompilerParams(
            collective_id=1, has_side_effects=True, vmem_limit_bytes=60 << 20
        ),
        cost_estimate=pl.CostEstimate(flops=0, bytes_accessed=64 << 20, transcendentals=0),
    )(
        length,
        vectors,
        small,
        gelu_low,
        pre_low,
        act_two,
        up_mat,
        down_mat,
        hidden,
        cot_low,
        resid,
        out_mat,
        qkv_mat,
        qkv,
        attended,
        act_one,
    )


def split_body(
    layer_input,
    cotangent,
    seq_lengths,
    dealing,
    attn_gain,
    attn_shift,
    query_weight,
    query_bias,
    key_weight,
    value_weight,
    value_bias,
    out_weight,
    out_bias,
    mlp_gain,
    mlp_shift,
    up_weight,
    up_bias,
    down_weight,
    down_bias,
    clip_level,
):
    f32, bf16 = jnp.float32, jnp.bfloat16
    f = lax.axis_index("fsdp")
    z = lax.axis_index("ctx")
    t = lax.axis_index("tp")
    y, x = f // 2, f % 2
    depth = lax.axis_size("ctx")
    slots, block_rows, width = layer_input.shape
    local_heads = query_bias.shape[0] // 2
    head_size = 4 * query_bias.shape[1]
    features = local_heads * head_size
    hidden_units = up_weight.shape[1] // 2
    strip = query_weight.shape[0]
    own_rows = depth * block_rows

    place = jnp.stack([t, x * depth + z])
    arrived, cot_part, down_bias_part, length = prepare(
        dealing, seq_lengths, place, layer_input, cotangent, depth
    )
    vectors = jnp.concatenate(
        [attn_gain, attn_shift, out_bias, mlp_gain, mlp_shift, down_bias, up_bias.reshape(-1)]
    )
    vectors = vectors.reshape(8, strip).astype(f32)
    head_vectors = jnp.concatenate([query_bias, value_bias], 0).astype(f32)
    head_vectors = lax.dynamic_update_slice(
        jnp.zeros((head_vectors.shape[0], head_size), f32), head_vectors, (0, f * query_bias.shape[1])
    )
    (
        qkv_mat,
        out_mat,
        up_mat,
        down_mat,
        act_one,
        cot_low,
        qkv,
        attended,
        hidden,
        resid,
        act_two,
        back,
        vectors_whole,
        peaks,
    ) = forward_all(
        head_size,
        length,
        vectors,
        head_vectors,
        query_weight,
        key_weight,
        value_weight,
        out_weight,
        up_weight,
        down_weight,
        arrived,
        cot_part,
    )
    peaks = peaks[:local_heads, 0]
    up_vec = lax.dynamic_slice_in_dim(vectors_whole, 6 + y, 1, 0)

    pre = matmul(act_two, up_mat) + up_vec
    cdf = 0.5 * (1.0 + lax.erf(pre * INV_ROOT_TWO))
    gelu_low = (pre * cdf).astype(bf16)
    slope = cdf + pre * (jnp.exp(-0.5 * pre * pre) * INV_ROOT_TWO_PI)
    pre_grad = back.astype(f32) * slope
    pre_low = pre_grad.astype(bf16)
    up_bias_part = jnp.sum(pre_grad, 0)
    column = 2 * t + y
    small = jnp.zeros((16, width), f32).at[DOWN_BIAS].set(down_bias_part[0])
    small = lax.dynamic_update_slice(small, up_bias_part[None], (UP_BIAS + column, 0))
    small = small.at[PEAKS].set(NEG)
    small = lax.dynamic_update_slice(small, peaks[None], (PEAKS, local_heads * (2 * t + y)))
    (
        down_sum,
        up_sum,
        out_sum,
        query_sum,
        key_sum,
        value_sum,
        rows_out,
        rows_grad,
        totals,
        _,
        _,
    ) = backward_all(
        head_size,
        length,
        vectors_whole,
        small,
        gelu_low,
        pre_low,
        act_two,
        up_mat,
        down_mat,
        hidden,
        cot_low,
        resid,
        out_mat,
        qkv_mat,
        qkv,
        attended,
        act_one,
        slots,
    )
    rows_sum = lax.dynamic_slice(totals, (0, f * strip), (6, strip))
    head_sum = lax.dynamic_slice(totals, (QUERY_BIAS, 2 * t * features), (2, 2 * features))
    head_sum = head_sum.reshape(2, 2 * local_heads, head_size)
    head_sum = lax.dynamic_slice_in_dim(head_sum, f * query_bias.shape[1], query_bias.shape[1], 2)
    unit_sum = lax.dynamic_slice(
        totals, (UP_BIAS + up_bias.shape[0] * t, f * strip), (up_bias.shape[0], strip)
    )
    peak_all = lax.dynamic_slice(totals, (PEAKS, 2 * local_heads * t), (1, 2 * local_heads))[0]
    (
        final_output,
        final_grad,
        query_weight_grad,
        key_weight_grad,
        value_weight_grad,
        out_weight_grad,
        up_weight_grad,
        down_weight_grad,
        query_clipped,
        key_clipped,
    ) = finish_all(
        head_size,
        place,
        clip_level,
        totals,
        query_weight,
        key_weight,
        (rows_out, rows_grad, query_sum, key_sum, value_sum, out_sum, up_sum, down_sum),
    )
    return (
        final_output,
        final_grad,
        rows_sum[GAIN_ONE],
        rows_sum[SHIFT_ONE],
        query_weight_grad,
        head_sum[0],
        key_weight_grad,
        value_weight_grad,
        head_sum[1],
        out_weight_grad,
        rows_sum[OUT_BIAS],
        rows_sum[GAIN_TWO],
        rows_sum[SHIFT_TWO],
        up_weight_grad,
        unit_sum,
        down_weight_grad,
        rows_sum[DOWN_BIAS],
        peak_all,
        query_clipped,
        key_clipped,
    )


def solution(mesh):
    sizes = dict(mesh.shape)
    small_slice = sizes == {"fsdp": 4, "ctx": 4, "tp": 2}
    return jax.shard_map(
        split_body if small_slice else gathered_body,
        mesh=mesh,
        in_specs=(
            P(None, ("fsdp", "ctx"), None),
            P(None, ("fsdp", "ctx"), None),
            P(),
            P(),
            P("fsdp"),
            P("fsdp"),
            P("fsdp", "tp"),
            P("tp", "fsdp"),
            P("fsdp", "tp"),
            P("fsdp", "tp"),
            P("tp", "fsdp"),
            P("tp", "fsdp"),
            P("fsdp"),
            P("fsdp"),
            P("fsdp"),
            P("fsdp", "tp"),
            P("tp", "fsdp"),
            P("tp", "fsdp"),
            P("fsdp"),
            P(),
        ),
        out_specs=(
            P(None, ("fsdp", "ctx"), None),
            P(None, ("fsdp", "ctx"), None),
            P("fsdp"),
            P("fsdp"),
            P("fsdp", "tp"),
            P("tp", "fsdp"),
            P("fsdp", "tp"),
            P("fsdp", "tp"),
            P("tp", "fsdp"),
            P("tp", "fsdp"),
            P("fsdp"),
            P("fsdp"),
            P("fsdp"),
            P("fsdp", "tp"),
            P("tp", "fsdp"),
            P("tp", "fsdp"),
            P("fsdp"),
            P("tp"),
            P("fsdp", "tp"),
            P("fsdp", "tp"),
        ),
        check_vma=False,
    )
```

```python
import functools
import math

import jax
import jax.numpy as jnp
from jax import lax
from jax.experimental import pallas as pl
from jax.experimental.pallas import tpu as pltpu
from jax.sharding import PartitionSpec as P

EPS = 1e-05
NEG = -1e30
INV_ROOT_TWO = 0.7071067811865476
INV_ROOT_TWO_PI = 0.3989422804014327


def normalize(values, scale_vec, offset_vec):
    center = values - jnp.mean(values, -1, keepdims=True)
    inverse = lax.rsqrt(jnp.mean(center * center, -1, keepdims=True) + EPS)
    normed = center * inverse
    return (normed * scale_vec + offset_vec, normed, inverse)


def norm_back(upstream, normed, inverse, scale_vec):
    scaled = upstream * scale_vec
    inner = (
        scaled
        - jnp.mean(scaled, -1, keepdims=True)
        - normed * jnp.mean(scaled * normed, -1, keepdims=True)
    )
    return (inverse * inner, jnp.sum(upstream * normed, 0), jnp.sum(upstream, 0))


def pick_slots(rows, dealing, first, count):
    return jnp.concatenate(
        [lax.dynamic_slice_in_dim(rows, dealing[first + j], 1, 0) for j in range(count)], 0
    )


def matmul(left, right):
    return jnp.dot(left, right, preferred_element_type=jnp.float32)


def weight_product(left, right):
    return jnp.einsum("td,te->de", left, right, preferred_element_type=jnp.float32)


def back_product(left, right):
    return jnp.einsum("te,de->td", left, right, preferred_element_type=jnp.float32)


def gathered_body(
    layer_input,
    cotangent,
    seq_lengths,
    dealing,
    attn_gain,
    attn_shift,
    query_weight,
    query_bias,
    key_weight,
    value_weight,
    value_bias,
    out_weight,
    out_bias,
    mlp_gain,
    mlp_shift,
    up_weight,
    up_bias,
    down_weight,
    down_bias,
    clip_level,
):
    shard_count = lax.axis_size("fsdp")
    ctx_count = lax.axis_size("ctx")
    my_group = lax.axis_index("fsdp")
    ctx_place = lax.axis_index("ctx")
    slot_count, block_rows, width = layer_input.shape
    per_group = slot_count // shard_count
    local_rows = shard_count * block_rows
    tokens = per_group * local_rows
    dealt_input = pick_slots(layer_input, dealing, 0, slot_count).reshape(
        shard_count, per_group, block_rows, width
    )
    dealt_grad = cotangent.reshape(shard_count, per_group, block_rows, width)
    arrived_input, arrived_grad = (
        lax.all_to_all(dealt_input, "fsdp", split_axis=0, concat_axis=2, tiled=True),
        lax.all_to_all(dealt_grad, "fsdp", split_axis=0, concat_axis=2, tiled=True),
    )
    resid = arrived_input.reshape(tokens, width)
    upstream = arrived_grad.reshape(tokens, width)
    seq_lens = lax.dynamic_slice_in_dim(
        jnp.take(seq_lengths, dealing), my_group * per_group, per_group
    )
    gathered = (
        lax.all_gather(attn_gain, "fsdp", axis=0, tiled=True),
        lax.all_gather(attn_shift, "fsdp", axis=0, tiled=True),
        lax.all_gather(query_weight, "fsdp", axis=0, tiled=True),
        lax.all_gather(query_bias, "fsdp", axis=1, tiled=True),
        lax.all_gather(key_weight, "fsdp", axis=0, tiled=True),
        lax.all_gather(value_weight, "fsdp", axis=0, tiled=True),
        lax.all_gather(value_bias, "fsdp", axis=1, tiled=True),
        lax.all_gather(out_weight, "fsdp", axis=1, tiled=True),
        lax.all_gather(out_bias, "fsdp", axis=0, tiled=True),
        lax.all_gather(mlp_gain, "fsdp", axis=0, tiled=True),
        lax.all_gather(mlp_shift, "fsdp", axis=0, tiled=True),
        lax.all_gather(up_weight, "fsdp", axis=0, tiled=True),
        lax.all_gather(up_bias, "fsdp", axis=1, tiled=True),
        lax.all_gather(down_weight, "fsdp", axis=1, tiled=True),
        lax.all_gather(down_bias, "fsdp", axis=0, tiled=True),
    )
    (
        gain_one,
        shift_one,
        query_mat,
        query_vec,
        key_mat,
        value_mat,
        value_vec,
        out_mat,
        out_vec,
        gain_two,
        shift_two,
        up_mat,
        up_vec,
        down_mat,
        down_vec,
    ) = gathered
    head_count, head_size = query_vec.shape
    features = head_count * head_size
    scale_of_scores = 1.0 / math.sqrt(head_size)
    row_ids = jnp.arange(local_rows, dtype=jnp.int32)
    query_pos = (row_ids // block_rows * ctx_count + ctx_place) * block_rows + row_ids % block_rows
    key_ids = jnp.arange(ctx_count * local_rows, dtype=jnp.int32)
    key_rows = key_ids % local_rows
    key_pos = (
        key_rows // block_rows * ctx_count + key_ids // local_rows
    ) * block_rows + key_rows % block_rows
    allowed = (key_pos[None, None, :] <= query_pos[None, :, None]) & (
        key_pos[None, None, :] < seq_lens[:, None, None]
    )
    query_live = query_pos[None, :] < seq_lens[:, None]
    normed_a, unit_one, inverse_one = normalize(
        resid, gain_one.astype(jnp.float32), shift_one.astype(jnp.float32)
    )
    act_one = normed_a.astype(jnp.bfloat16)
    queries = (
        (matmul(act_one, query_mat) + query_vec.reshape(features).astype(jnp.float32))
        .astype(jnp.bfloat16)
        .reshape(per_group, local_rows, features)
    )
    keys_mine = (
        matmul(act_one, key_mat).astype(jnp.bfloat16).reshape(per_group, local_rows, features)
    )
    values_mine = (
        (matmul(act_one, value_mat) + value_vec.reshape(features).astype(jnp.float32))
        .astype(jnp.bfloat16)
        .reshape(per_group, local_rows, features)
    )
    keys_all, values_all = (
        lax.all_gather(keys_mine, "ctx", axis=1, tiled=True),
        lax.all_gather(values_mine, "ctx", axis=1, tiled=True),
    )

    def head_cut(array, head_index):
        return lax.dynamic_slice_in_dim(array, head_index * head_size, head_size, 2)

    def head_scores(head_queries, head_keys):
        return (
            jnp.einsum("sqd,skd->sqk", head_queries, head_keys, preferred_element_type=jnp.float32)
            * scale_of_scores
        )

    def forward_head(head_index):
        logit_scores = head_scores(head_cut(queries, head_index), head_cut(keys_all, head_index))
        masked = jnp.where(allowed, logit_scores, NEG)
        row_top = jnp.max(masked, -1, keepdims=True)
        exp_terms = jnp.where(allowed, jnp.exp(masked - row_top), 0.0)
        total = jnp.sum(exp_terms, -1, keepdims=True)
        attention_probabilities = exp_terms / total
        attended_rows = jnp.einsum(
            "sqk,skd->sqd",
            attention_probabilities.astype(jnp.bfloat16),
            head_cut(values_all, head_index),
            preferred_element_type=jnp.float32,
        )
        log_total = row_top[..., 0] + jnp.log(total[..., 0])
        peak = jnp.max(jnp.where(query_live, row_top[..., 0], NEG))
        return (attended_rows, log_total, peak)

    attended_rows, log_totals, peaks = lax.map(forward_head, jnp.arange(head_count))
    attn_low = attended_rows.transpose(1, 2, 0, 3).reshape(tokens, features).astype(jnp.bfloat16)
    attn_sum = lax.psum(matmul(attn_low, out_mat), "tp")
    hidden = resid + attn_sum + out_vec.astype(jnp.float32)
    normed_b, unit_two, inverse_two = normalize(
        hidden, gain_two.astype(jnp.float32), shift_two.astype(jnp.float32)
    )
    act_two = normed_b.astype(jnp.bfloat16)
    pre = matmul(act_two, up_mat) + up_vec.reshape(-1).astype(jnp.float32)
    gelu_low = jax.nn.gelu(pre, approximate=False).astype(jnp.bfloat16)
    mlp_sum = lax.psum(matmul(gelu_low, down_mat).astype(jnp.bfloat16), "tp").astype(jnp.float32)
    layer_output = hidden + mlp_sum + down_vec.astype(jnp.float32)
    peak_all = lax.pmax(peaks, ("fsdp", "ctx"))
    level = clip_level[0]
    factor = jnp.repeat(jnp.sqrt(level / jnp.maximum(peak_all, level)), head_size)
    query_clipped = (query_weight.astype(jnp.float32) * factor[None, :]).astype(jnp.bfloat16)
    key_clipped = (key_weight.astype(jnp.float32) * factor[None, :]).astype(jnp.bfloat16)
    grad_low = upstream.astype(jnp.bfloat16)
    down_weight_grad = weight_product(gelu_low, grad_low)
    down_bias_grad = jnp.sum(upstream, 0)
    cdf = 0.5 * (1.0 + lax.erf(pre * INV_ROOT_TWO))
    density = jnp.exp(-0.5 * pre * pre) * INV_ROOT_TWO_PI
    pre_grad = back_product(grad_low, down_mat) * (cdf + pre * density)
    pre_low = pre_grad.astype(jnp.bfloat16)
    up_weight_grad = weight_product(act_two, pre_low)
    up_bias_grad = jnp.sum(pre_grad, 0).reshape(up_vec.shape)
    normed_two_grad = lax.psum(back_product(pre_low, up_mat), "tp")
    hidden_in, mlp_gain_grad, mlp_shift_grad = norm_back(
        normed_two_grad, unit_two, inverse_two, gain_two.astype(jnp.float32)
    )
    hidden_grad = upstream + hidden_in
    hidden_low = hidden_grad.astype(jnp.bfloat16)
    out_weight_grad = weight_product(attn_low, hidden_low)
    out_bias_grad = jnp.sum(hidden_grad, 0)
    attended_grad = (
        back_product(hidden_low, out_mat)
        .astype(jnp.bfloat16)
        .reshape(per_group, local_rows, features)
    )

    def backward_head(head_index):
        head_queries = head_cut(queries, head_index)
        head_keys = head_cut(keys_all, head_index)
        head_values = head_cut(values_all, head_index)
        grad_head = head_cut(attended_grad, head_index)
        logit_scores = head_scores(head_queries, head_keys)
        masked = jnp.where(allowed, logit_scores, NEG)
        attention_probabilities = jnp.where(
            allowed, jnp.exp(masked - log_totals[head_index][..., None]), 0.0
        )
        prob_grad = jnp.einsum(
            "sqd,skd->sqk", grad_head, head_values, preferred_element_type=jnp.float32
        )
        inner = jnp.sum(attention_probabilities * prob_grad, -1, keepdims=True)
        score_grad = (attention_probabilities * (prob_grad - inner)).astype(jnp.bfloat16)
        query_grad = (
            jnp.einsum("sqk,skd->sqd", score_grad, head_keys, preferred_element_type=jnp.float32)
            * scale_of_scores
        )
        key_grad = (
            jnp.einsum("sqk,sqd->skd", score_grad, head_queries, preferred_element_type=jnp.float32)
            * scale_of_scores
        )
        value_grad = jnp.einsum(
            "sqk,sqd->skd",
            attention_probabilities.astype(jnp.bfloat16),
            grad_head,
            preferred_element_type=jnp.float32,
        )
        return (query_grad, key_grad, value_grad)

    query_parts, key_parts, value_parts = lax.map(backward_head, jnp.arange(head_count))
    query_grads = query_parts.transpose(1, 2, 0, 3).reshape(tokens, features)
    key_whole = key_parts.transpose(1, 2, 0, 3).reshape(per_group, ctx_count * local_rows, features)
    value_whole = value_parts.transpose(1, 2, 0, 3).reshape(
        per_group, ctx_count * local_rows, features
    )
    key_summed, value_summed = (
        lax.psum_scatter(key_whole, "ctx", scatter_dimension=1, tiled=True),
        lax.psum_scatter(value_whole, "ctx", scatter_dimension=1, tiled=True),
    )
    key_grads = key_summed.reshape(tokens, features)
    value_grads = value_summed.reshape(tokens, features)
    query_bias_grad = jnp.sum(query_grads, 0).reshape(head_count, head_size)
    value_bias_grad = jnp.sum(value_grads, 0).reshape(head_count, head_size)
    query_low = query_grads.astype(jnp.bfloat16)
    key_low = key_grads.astype(jnp.bfloat16)
    value_low = value_grads.astype(jnp.bfloat16)
    query_weight_grad = weight_product(act_one, query_low)
    key_weight_grad = weight_product(act_one, key_low)
    value_weight_grad = weight_product(act_one, value_low)
    normed_one_grad = lax.psum(
        (
            back_product(query_low, query_mat)
            + back_product(key_low, key_mat)
            + back_product(value_low, value_mat)
        ).astype(jnp.bfloat16),
        "tp",
    ).astype(jnp.float32)
    input_in, attn_gain_grad, attn_shift_grad = norm_back(
        normed_one_grad, unit_one, inverse_one, gain_one.astype(jnp.float32)
    )
    input_grad = hidden_grad + input_in
    partial_sums = (
        lax.psum_scatter(
            attn_gain_grad.astype(jnp.bfloat16), "fsdp", scatter_dimension=0, tiled=True
        ).astype(jnp.float32),
        lax.psum_scatter(
            attn_shift_grad.astype(jnp.bfloat16), "fsdp", scatter_dimension=0, tiled=True
        ).astype(jnp.float32),
        lax.psum_scatter(
            query_weight_grad.astype(jnp.bfloat16), "fsdp", scatter_dimension=0, tiled=True
        ).astype(jnp.float32),
        lax.psum_scatter(
            query_bias_grad.astype(jnp.bfloat16), "fsdp", scatter_dimension=1, tiled=True
        ).astype(jnp.float32),
        lax.psum_scatter(
            key_weight_grad.astype(jnp.bfloat16), "fsdp", scatter_dimension=0, tiled=True
        ).astype(jnp.float32),
        lax.psum_scatter(
            value_weight_grad.astype(jnp.bfloat16), "fsdp", scatter_dimension=0, tiled=True
        ).astype(jnp.float32),
        lax.psum_scatter(
            value_bias_grad.astype(jnp.bfloat16), "fsdp", scatter_dimension=1, tiled=True
        ).astype(jnp.float32),
        lax.psum_scatter(
            out_weight_grad.astype(jnp.bfloat16), "fsdp", scatter_dimension=1, tiled=True
        ).astype(jnp.float32),
        lax.psum_scatter(
            out_bias_grad.astype(jnp.bfloat16), "fsdp", scatter_dimension=0, tiled=True
        ).astype(jnp.float32),
        lax.psum_scatter(
            mlp_gain_grad.astype(jnp.bfloat16), "fsdp", scatter_dimension=0, tiled=True
        ).astype(jnp.float32),
        lax.psum_scatter(
            mlp_shift_grad.astype(jnp.bfloat16), "fsdp", scatter_dimension=0, tiled=True
        ).astype(jnp.float32),
        lax.psum_scatter(
            up_weight_grad.astype(jnp.bfloat16), "fsdp", scatter_dimension=0, tiled=True
        ).astype(jnp.float32),
        lax.psum_scatter(
            up_bias_grad.astype(jnp.bfloat16), "fsdp", scatter_dimension=1, tiled=True
        ).astype(jnp.float32),
        lax.psum_scatter(
            down_weight_grad.astype(jnp.bfloat16), "fsdp", scatter_dimension=1, tiled=True
        ).astype(jnp.float32),
        lax.psum_scatter(
            down_bias_grad.astype(jnp.bfloat16), "fsdp", scatter_dimension=0, tiled=True
        ).astype(jnp.float32),
    )
    shards = (
        lax.psum(partial_sums[0].astype(jnp.bfloat16), "ctx").astype(jnp.float32),
        lax.psum(partial_sums[1].astype(jnp.bfloat16), "ctx").astype(jnp.float32),
        lax.psum(partial_sums[2].astype(jnp.bfloat16), "ctx").astype(jnp.float32),
        lax.psum(partial_sums[3].astype(jnp.bfloat16), "ctx").astype(jnp.float32),
        lax.psum(partial_sums[4].astype(jnp.bfloat16), "ctx").astype(jnp.float32),
        lax.psum(partial_sums[5].astype(jnp.bfloat16), "ctx").astype(jnp.float32),
        lax.psum(partial_sums[6].astype(jnp.bfloat16), "ctx").astype(jnp.float32),
        lax.psum(partial_sums[7].astype(jnp.bfloat16), "ctx").astype(jnp.float32),
        lax.psum(partial_sums[8].astype(jnp.bfloat16), "ctx").astype(jnp.float32),
        lax.psum(partial_sums[9].astype(jnp.bfloat16), "ctx").astype(jnp.float32),
        lax.psum(partial_sums[10].astype(jnp.bfloat16), "ctx").astype(jnp.float32),
        lax.psum(partial_sums[11].astype(jnp.bfloat16), "ctx").astype(jnp.float32),
        lax.psum(partial_sums[12].astype(jnp.bfloat16), "ctx").astype(jnp.float32),
        lax.psum(partial_sums[13].astype(jnp.bfloat16), "ctx").astype(jnp.float32),
        lax.psum(partial_sums[14].astype(jnp.bfloat16), "ctx").astype(jnp.float32),
    )
    sent_output = layer_output.reshape(1, per_group, local_rows, width)
    sent_grad = input_grad.reshape(1, per_group, local_rows, width)
    back_output, back_grad = (
        lax.all_to_all(
            sent_output.astype(jnp.bfloat16), "fsdp", split_axis=2, concat_axis=0, tiled=True
        ).astype(sent_output.dtype),
        lax.all_to_all(
            sent_grad.astype(jnp.bfloat16), "fsdp", split_axis=2, concat_axis=0, tiled=True
        ).astype(sent_grad.dtype),
    )
    final_output = back_output.reshape(slot_count, block_rows, width)
    final_grad = back_grad.reshape(slot_count, block_rows, width)
    return (
        final_output,
        final_grad,
        shards[0],
        shards[1],
        shards[2],
        shards[3],
        shards[4],
        shards[5],
        shards[6],
        shards[7],
        shards[8],
        shards[9],
        shards[10],
        shards[11],
        shards[12],
        shards[13],
        shards[14],
        peak_all,
        query_clipped,
        key_clipped,
    )


def attention_probs(query_block, key_rows, block, length):
    rows, cols = query_block.shape[0], key_rows.shape[0]
    scores = lax.dot_general(
        query_block, key_rows, (((1,), (1,)), ((), ())), preferred_element_type=jnp.float32
    ) * (1.0 / math.sqrt(query_block.shape[1]))
    row_pos = block * rows + lax.broadcasted_iota(jnp.int32, (rows, cols), 0)
    col_pos = lax.broadcasted_iota(jnp.int32, (rows, cols), 1)
    scores = jnp.where((col_pos <= row_pos) & (col_pos < length), scores, NEG)
    top = jnp.max(scores, -1, keepdims=True)
    terms = jnp.exp(scores - top)
    return terms / jnp.sum(terms, -1, keepdims=True), top


def entry_barrier(targets):
    barrier = pltpu.get_barrier_semaphore()
    for target in targets:
        pl.semaphore_signal(barrier, inc=1, device_id=target, device_id_type=pl.DeviceIdType.MESH)
    pl.semaphore_wait(barrier, len(targets))


def remote_copy(src, dst, send, recv, target):
    return pltpu.make_async_remote_copy(
        src_ref=src,
        dst_ref=dst,
        send_sem=send,
        recv_sem=recv,
        device_id=target,
        device_id_type=pl.DeviceIdType.MESH,
    )


def grant(semaphore, target):
    pl.semaphore_signal(semaphore, inc=1, device_id=target, device_id_type=pl.DeviceIdType.MESH)


def aligned(start, size):
    return pl.ds(pl.multiple_of(start, 128), size)


class Place:
    def __init__(self, depth):
        self.depth = depth
        f = lax.axis_index("fsdp")
        z = lax.axis_index("ctx")
        t = lax.axis_index("tp")
        y, x = f // 2, f % 2
        self.f, self.z, self.t, self.y, self.x = f, z, t, y, x
        self.over_x = {"fsdp": 2 * y + 1 - x, "ctx": z, "tp": t}
        self.over_y = {"fsdp": 2 * (1 - y) + x, "ctx": z, "tp": t}
        self.over_core = {"fsdp": f, "ctx": z, "tp": 1 - t}
        self.mate = {"fsdp": f, "ctx": z + 1 - 2 * (z % 2), "tp": t}
        self.middle = {"fsdp": f, "ctx": 3 - z, "tp": t}
        self.hop = {"fsdp": f, "ctx": lax.rem(z + 2, 4), "tp": t}
        self.homes = (2 * y + 1 - x, 2 * (1 - y) + 1 - x, f, 2 * (1 - y) + x)

    def row_target(self, k):
        return {"fsdp": 2 * self.y + self.t, "ctx": k, "tp": self.x}

    def row_targets(self):
        others = [self.row_target(lax.rem(self.z + k, self.depth)) for k in range(1, self.depth)]
        return others + [{"fsdp": 2 * self.y + 1 - self.x, "ctx": self.z, "tp": 1 - self.t}]

    def block_place(self, block):
        return 2 * jnp.where(self.y == block // 2, 0, 1) + jnp.where(self.t == block % 2, 0, 1)


def reduce_stages(p, items, scratch):
    (
        x_slot,
        made_slot,
        own_slot,
        pair_slot,
        y_slot,
        z_slot,
        z_pair,
        inner_slot,
        total_slot,
        x_send,
        x_recv,
        y_send,
        y_recv,
        outer_send,
        outer_recv,
        inner_send,
        inner_recv,
        out_sem,
        x_free,
        y_free,
        outer_free,
        inner_free,
    ) = scratch
    y, z = p.y, p.z
    outer = (z == 0) | (z == 3)
    inner = (z == 1) | (z == 2)
    slots = x_slot.shape[0]
    count = len(items)
    far_count = count // 2
    far_slots = y_slot.shape[0]

    def x_copy(i):
        k = i % slots
        return remote_copy(made_slot.at[k], x_slot.at[k], x_send.at[k], x_recv.at[k], p.over_x)

    def y_copy(i):
        k, g = i % slots, (i // 2) % far_slots
        return remote_copy(pair_slot.at[k], y_slot.at[g], y_send.at[g], y_recv.at[g], p.over_y)

    def summed(i):
        return y_slot.at[(i // 2) % far_slots] if items[i][0] else pair_slot.at[i % slots]

    def outward(i):
        k = i % slots
        return remote_copy(summed(i), z_slot.at[k], outer_send.at[k], outer_recv.at[k], p.mate)

    def across(i):
        k = i % slots
        return remote_copy(z_pair.at[k], inner_slot.at[k], inner_send.at[k], inner_recv.at[k], p.middle)

    def backward(i):
        k = i % slots
        return remote_copy(total_slot.at[k], z_slot.at[k], outer_send.at[k], outer_recv.at[k], p.mate)

    def result_inner(i):
        k = i % slots
        return pltpu.make_async_copy(total_slot.at[k], items[i][1], out_sem.at[k])

    def result_outer(i):
        k = i % slots
        return pltpu.make_async_copy(z_slot.at[k], items[i][1], out_sem.at[k])

    def add(left, right, target):
        target[...] = (left[...].astype(jnp.float32) + right[...].astype(jnp.float32)).astype(
            target.dtype
        )

    def stage_send(i):
        k = i % slots
        items[i][2](made_slot.at[k], own_slot.at[k])
        if i >= slots:
            pl.semaphore_wait(x_free, 1)
        x_copy(i).start()

    def stage_pair(i):
        x_copy(i).wait()
        k = i % slots
        add(x_slot.at[k], own_slot.at[k], pair_slot.at[k])
        if i + slots < count:
            grant(x_free, p.over_x)
        if items[i][0]:
            if i // 2 >= far_slots:
                pl.semaphore_wait(y_free, 1)
            y_copy(i).start()

    def stage_outward(i):
        if items[i][0]:
            y_copy(i).wait()

        @pl.when(outer)
        def _():
            if i >= slots:
                pl.semaphore_wait(outer_free, 1)
            outward(i).start()

    def stage_across(i):
        k = i % slots

        @pl.when(outer)
        def _():
            outward(i).wait_send()

        @pl.when(inner)
        def _():
            outward(i).wait_recv()
            add(summed(i), z_slot.at[k], z_pair.at[k])
            if i + slots < count:
                grant(outer_free, p.mate)
            if i >= slots:
                pl.semaphore_wait(inner_free, 1)
            across(i).start()

        if items[i][0] and i // 2 + far_slots < far_count:
            grant(y_free, p.over_y)

    def stage_total(i):
        k = i % slots

        @pl.when(inner)
        def _():
            across(i).wait()
            add(z_pair.at[k], inner_slot.at[k], total_slot.at[k])
            if i + slots < count:
                grant(inner_free, p.middle)
            if i >= slots:
                pl.semaphore_wait(outer_free, 1)
            backward(i).start()
            result_inner(i).start()

    def stage_result(i):
        @pl.when(inner)
        def _():
            backward(i).wait_send()
            result_inner(i).wait()

        @pl.when(outer)
        def _():
            backward(i).wait_recv()
            result_outer(i).start()

    def stage_finish(i):
        @pl.when(outer)
        def _():
            result_outer(i).wait()
            if i + slots < count:
                grant(outer_free, p.mate)

    stages = (
        (11, stage_finish),
        (10, stage_result),
        (8, stage_total),
        (6, stage_across),
        (4, stage_outward),
        (2, stage_pair),
        (0, stage_send),
    )

    def run(step):
        for lag, stage in stages:
            if 0 <= step - lag < count:
                stage(step - lag)

    return run, count + 12


def reduce_scratch(slots, far_slots, rows, cols):
    dma, regular = pltpu.SemaphoreType.DMA, pltpu.SemaphoreType.REGULAR
    counts = (slots,) * 4 + (far_slots,) + (slots,) * 4
    return [pltpu.VMEM((n, rows, cols), jnp.bfloat16) for n in counts] + [
        dma((n,)) for n in (slots,) * 2 + (far_slots,) * 2 + (slots,) * 5
    ] + [regular] * 4


PARTS = 4


class RowSum:
    def __init__(self, p, rows, arrived, sent, loaded, send_sem, recv_sem, load_sem, core_free, y_free, uses):
        self.p, self.rows, self.uses = p, rows, uses
        self.arrived, self.sent, self.loaded = arrived, sent, loaded
        self.send_sem, self.recv_sem, self.load_sem = send_sem, recv_sem, load_sem
        self.core_free, self.y_free = core_free, y_free

    def block(self, ref, k):
        return ref.at[pl.ds(k * self.rows, self.rows), :]

    def hop(self, ref, k):
        return remote_copy(
            self.block(ref, 3 - 2 * k),
            self.arrived.at[k],
            self.send_sem.at[k],
            self.recv_sem.at[k],
            self.p.over_core,
        )

    def hop_y(self, part):
        size = self.rows // PARTS
        cut = pl.ds(part * size, size)
        return remote_copy(
            self.sent.at[cut, :],
            self.arrived.at[2, cut, :],
            self.send_sem.at[2 + part],
            self.recv_sem.at[2 + part],
            self.p.over_y,
        )

    def load(self, ref, k):
        return pltpu.make_async_copy(self.block(ref, k), self.loaded, self.load_sem)

    def start(self, use, ref, local):
        if use:
            pl.semaphore_wait(self.core_free, 1)
            pl.semaphore_wait(self.y_free, 1)
        self.hop(ref, 0).start()
        self.hop(ref, 1).start()
        if not local:
            self.load(ref, 2).start()

    def middle(self, ref, local, part):
        if part == 0:
            self.hop(ref, 0).wait()
            if not local:
                self.load(ref, 2).wait()
        base = self.block(ref, 2) if local else self.loaded
        size = self.rows // PARTS

        @pl.loop(part * size // 32, (part + 1) * size // 32)
        def _(k):
            at = pl.ds(pl.multiple_of(k * 32, 32), 32)
            self.sent[at, :] = (
                base[at, :].astype(jnp.float32) + self.arrived[0, at, :].astype(jnp.float32)
            ).astype(jnp.bfloat16)

        self.hop_y(part).start()
        if part == PARTS - 1 and not local:
            self.load(ref, 0).start()

    def finish(self, ref, local):
        self.hop(ref, 1).wait()
        for part in range(PARTS):
            self.hop_y(part).wait()
        if not local:
            self.load(ref, 0).wait()

    def total(self, ref, local, at):
        base = self.block(ref, 0) if local else self.loaded
        return (
            base[at, :].astype(jnp.float32)
            + self.arrived[1, at, :].astype(jnp.float32)
            + self.arrived[2, at, :].astype(jnp.float32)
        )

    def release(self, use):
        if use + 1 < self.uses:
            grant(self.core_free, self.p.over_core)
            grant(self.y_free, self.p.over_y)


def unit_rows(values):
    center = values - jnp.mean(values, -1, keepdims=True)
    inverse = lax.rsqrt(jnp.mean(center * center, -1, keepdims=True) + EPS)
    return center * inverse, inverse


def unit_back(upstream, unit, inverse, gain):
    scaled = upstream * gain
    return inverse * (
        scaled
        - jnp.mean(scaled, -1, keepdims=True)
        - unit * jnp.mean(scaled * unit, -1, keepdims=True)
    )


GAIN_ONE, SHIFT_ONE, OUT_BIAS, GAIN_TWO, SHIFT_TWO, DOWN_BIAS, QUERY_BIAS, VALUE_BIAS, UP_BIAS, PEAKS = (
    0,
    1,
    2,
    3,
    4,
    5,
    6,
    7,
    8,
    12,
)


def prepare_kernel(dealing, lengths, place, rows_ref, cot_ref, rows_out, cot_out, bias_ref, length_ref):
    step = pl.program_id(0)
    rows_out[...] = rows_ref[...]
    cot = cot_ref[...]
    cot_out[...] = cot.astype(cot_out.dtype)

    @pl.when(step == 0)
    def _():
        bias_ref[...] = jnp.zeros_like(bias_ref)
        length_ref[0] = lengths[dealing[place[1]]]

    bias_ref[pl.ds(0, 1), :] += jnp.sum(cot[0], 0, keepdims=True)


def prepare(dealing, seq_lengths, place, layer_input, cotangent, count):
    block = (1,) + layer_input.shape[1:]
    width = layer_input.shape[2]
    return pl.pallas_call(
        prepare_kernel,
        out_shape=(
            jax.ShapeDtypeStruct((count,) + block[1:], jnp.float32),
            jax.ShapeDtypeStruct((count,) + block[1:], jnp.bfloat16),
            jax.ShapeDtypeStruct((8, width), jnp.float32),
            jax.ShapeDtypeStruct((1,), jnp.int32),
        ),
        grid_spec=pltpu.PrefetchScalarGridSpec(
            num_scalar_prefetch=3,
            grid=(count,),
            in_specs=[
                pl.BlockSpec(block, lambda j, dealing, lengths, place: (dealing[place[0] * count + j], 0, 0)),
                pl.BlockSpec(block, lambda j, dealing, lengths, place: (place[0] * count + j, 0, 0)),
            ],
            out_specs=(
                pl.BlockSpec(block, lambda j, *_: (j, 0, 0)),
                pl.BlockSpec(block, lambda j, *_: (j, 0, 0)),
                pl.BlockSpec((8, width), lambda j, *_: (0, 0)),
                pl.BlockSpec(memory_space=pltpu.SMEM),
            ),
        ),
    )(dealing, seq_lengths, place, layer_input, cotangent)


def finish_kernel(head_size, place, level_ref, totals_ref, query_ref, key_ref, *refs):
    count = (len(refs) - 3) // 2
    for source, target in zip(refs[:count], refs[count : 2 * count]):
        target[...] = source[...].astype(target.dtype)
    query_out, key_out, factor = refs[2 * count :]
    level = level_ref[0]
    heads = factor.shape[1] // head_size

    @pl.when(pl.program_id(0) == 0)
    def _():
        peaks = totals_ref[pl.ds(PEAKS, 1), :]
        lane = lax.broadcasted_iota(jnp.int32, peaks.shape, 1)
        for h in range(heads):
            mine = jnp.where(lane == place[0] * heads + h, peaks, NEG)
            peak = jnp.max(mine, -1, keepdims=True)
            value = jnp.sqrt(level / jnp.maximum(peak, level))
            factor[:, pl.ds(h * head_size, head_size)] = jnp.broadcast_to(value, (8, head_size))

    scale = factor[pl.ds(0, 1), :]
    query_out[...] = (query_ref[...].astype(jnp.float32) * scale).astype(query_out.dtype)
    key_out[...] = (key_ref[...].astype(jnp.float32) * scale).astype(key_out.dtype)


def finish_all(head_size, place, level, totals, query_weight, key_weight, arrays):
    steps = 8

    def spec(v):
        block = (v.shape[0] // steps,) + v.shape[1:]
        return pl.BlockSpec(block, lambda i: (i,) + (0,) * (v.ndim - 1))

    smem = pl.BlockSpec(memory_space=pltpu.SMEM)
    weights = (query_weight, key_weight)
    return pl.pallas_call(
        functools.partial(finish_kernel, head_size),
        out_shape=tuple(jax.ShapeDtypeStruct(v.shape, jnp.float32) for v in arrays)
        + tuple(jax.ShapeDtypeStruct(v.shape, v.dtype) for v in weights),
        grid=(steps,),
        in_specs=[smem, smem, pl.BlockSpec(totals.shape, lambda i: (0, 0))]
        + [spec(v) for v in weights]
        + [spec(v) for v in arrays],
        out_specs=tuple(spec(v) for v in arrays) + tuple(spec(v) for v in weights),
        scratch_shapes=[pltpu.VMEM((8, query_weight.shape[1]), jnp.float32)],
        compiler_params=pltpu.CompilerParams(vmem_limit_bytes=60 << 20),
    )(place, level, totals, *weights, *arrays)


def forward_kernel(
    head_size,
    info,
    vec_hbm,
    head_hbm,
    q_ref,
    k_ref,
    v_ref,
    o_ref,
    u_ref,
    d_ref,
    arrived_hbm,
    cot_hbm,
    qkv_mat_out,
    out_mat_out,
    up_all,
    down_out,
    act_out,
    cot_out,
    qkv_out,
    attended_out,
    hidden_out,
    resid_out,
    two_out,
    back_out,
    vec_all,
    peaks,
    cot_all,
    down_all,
    back_stage,
    qkv_mat,
    out_mat,
    fresh,
    part,
    act,
    hidden,
    qkv,
    keys,
    values,
    attended,
    partial,
    arrived,
    sent,
    two,
    vec_own,
    head_own,
    head_got,
    qkv_bias,
    local_sem,
    send_sem,
    recv_sem,
    row_send,
    row_recv,
    join_send,
    join_recv,
    vec_send,
    vec_recv,
    load_sem,
    sum_send,
    sum_recv,
    out_sem,
):
    f32, bf16 = jnp.float32, jnp.bfloat16
    depth, block_rows, width = arrived_hbm.shape
    own_rows = depth * block_rows
    strip = q_ref.shape[0]
    features = q_ref.shape[1] // 2
    units = u_ref.shape[1] // 2
    heads = features // head_size
    p = Place(depth)
    f, x, y, z, t = p.f, p.x, p.y, p.z, p.t
    even = z % 2 == 0
    odd = jnp.logical_not(even)
    diagonal = {"fsdp": 3 - f, "ctx": z, "tp": t}
    entry_barrier([p.over_x, p.over_y, p.mate, p.over_core, diagonal] + p.row_targets())
    length = info[0]

    chunks = []
    rows = strip // 2
    for k, ref in enumerate((q_ref, k_ref, v_ref)):
        for r in range(2):
            chunks.append(
                (
                    lambda w, ref=ref, r=r: ref.at[pl.ds(r * rows, rows), aligned(w * features, features)],
                    lambda home, k=k, r=r: qkv_mat.at[
                        aligned(home * strip + r * rows, rows), pl.ds(k * features, features)
                    ],
                )
            )
    for r in range(2):
        chunks.append(
            (
                lambda w, r=r: o_ref.at[aligned(w * features + r * rows, rows), :],
                lambda home, r=r: out_mat.at[pl.ds(r * rows, rows), aligned(home * strip, strip)],
            )
        )
    pieces = 8
    for r in range(pieces):
        size = strip // pieces
        chunks.append(
            (
                lambda w, r=r, size=size: u_ref.at[pl.ds(r * size, size), aligned(w * units, units)],
                lambda home, r=r, size=size: up_all.at[
                    pl.ds(pl.multiple_of(home * strip + r * size, size), size), :
                ],
            )
        )
    for r in range(pieces):
        size = units // pieces
        chunks.append(
            (
                lambda w, r=r, size=size: d_ref.at[aligned(w * units + r * size, size), :],
                lambda home, r=r, size=size: down_all.at[pl.ds(r * size, size), aligned(home * strip, strip)],
            )
        )
    count = len(chunks)
    far_home = 2 * (1 - y) + x

    def own_copy(i):
        source, place = chunks[i]
        return pltpu.make_async_copy(source(y), place(f), local_sem.at[i])

    def y_copy(i):
        source, place = chunks[i]
        return remote_copy(source(1 - y), place(f), send_sem.at[0, i], recv_sem.at[0, i], p.over_y)

    def x_copy(i, is_even):
        source, place = chunks[i]
        start = source(y) if is_even else place(far_home)
        home = f if is_even else far_home
        return remote_copy(start, place(home), send_sem.at[1, i], recv_sem.at[1, i], p.over_x)

    def z_copy(i, is_even):
        place = chunks[i][1]
        home = 2 * y + 1 - x if is_even else 2 * (1 - y) + 1 - x
        return remote_copy(place(home), place(home), send_sem.at[2, i], recv_sem.at[2, i], p.mate)

    rows_of = ((part, act), (cot_hbm, cot_all), (arrived_hbm, hidden))

    def row_copy(a, k):
        source, place = rows_of[a]
        return remote_copy(
            source.at[k],
            place.at[pl.ds(pl.multiple_of(z * block_rows, block_rows), block_rows), :],
            row_send.at[a, k],
            row_recv.at[a, z],
            p.row_target(k),
        )

    def row_arrival(a, k):
        source, place = rows_of[a]
        return remote_copy(
            source.at[k],
            place.at[pl.ds(k * block_rows, block_rows), :],
            row_send.at[a, k],
            row_recv.at[a, k],
            p.row_target(k),
        )

    def row_stay(a, k):
        source, place = rows_of[a]
        return pltpu.make_async_copy(
            source.at[k], place.at[pl.ds(k * block_rows, block_rows), :], row_send.at[a, k]
        )

    def rows_start(a):
        for k in range(depth):
            stays = (z == k) & (x == t)
            pl.when(stays)(lambda k=k: row_stay(a, k).start())
            pl.when(jnp.logical_not(stays))(lambda k=k: row_copy(a, k).start())

    def rows_wait(a):
        for k in range(depth):
            stays = (z == k) & (x == t)
            pl.when(stays)(lambda k=k: row_stay(a, k).wait())

            @pl.when(jnp.logical_not(stays))
            def _(k=k):
                row_copy(a, k).wait_send()
                row_arrival(a, k).wait_recv()

    joined = (act, cot_all, two)

    def block(ref, k):
        return ref.at[pl.ds(k * own_rows, own_rows), :]

    def join(a, step):
        source, place, target = ((0, 1, p.over_core), (0, 2, p.over_y), (2, 3, p.over_core))[step]
        ref = joined[a]
        return remote_copy(
            block(ref, source), block(ref, place), join_send.at[a, step], join_recv.at[a, step], target
        )

    def join_start(a):
        join(a, 0).start()
        join(a, 1).start()

    def join_pass(a):
        join(a, 1).wait_recv()
        join(a, 2).start()

    def join_end(a):
        join(a, 0).wait()
        join(a, 1).wait_send()
        join(a, 2).wait()

    def vec_place(ref):
        return ref.at[:, aligned(f * strip, strip)]

    vec_targets = (p.over_x, p.over_y, diagonal)

    def vec_copy(k):
        return remote_copy(vec_own, vec_place(vec_all), vec_send.at[0, k], vec_recv.at[0, k], vec_targets[k])

    def head_copy(k):
        return remote_copy(head_own, head_got.at[k], vec_send.at[1, k], vec_recv.at[1, k], vec_targets[k])

    loads = [
        pltpu.make_async_copy(source, target, load_sem.at[k])
        for k, (source, target) in enumerate(
            ((vec_hbm, vec_own), (head_hbm, head_own), (arrived_hbm, fresh))
        )
    ]

    def begin():
        for load in loads:
            load.start()
        loads[0].wait()
        loads[1].wait()
        for k in range(3):
            vec_copy(k).start()
            head_copy(k).start()
        vec_place(vec_all)[...] = vec_own[...]
        peaks[...] = jnp.full_like(peaks, NEG)

    def vector_row(k):
        return vec_all[pl.ds(k, 1), :]

    group_rows = 16

    def first_norm():
        for k in range(3):
            vec_copy(k).wait()
            head_copy(k).wait()
        loads[2].wait()
        for k in range(3):
            head_own[...] += head_got[k]
        qkv_bias[...] = jnp.zeros_like(qkv_bias)
        for h in range(heads):
            lanes = pl.ds(h * head_size, head_size)
            qkv_bias[pl.ds(0, 1), lanes] = head_own[pl.ds(heads * y + h, 1), :]
            lanes = pl.ds(2 * features + h * head_size, head_size)
            qkv_bias[pl.ds(0, 1), lanes] = head_own[pl.ds(2 * heads + heads * y + h, 1), :]
        gain, shift = vector_row(GAIN_ONE), vector_row(SHIFT_ONE)
        for s in range(depth):

            @pl.loop(0, block_rows // group_rows)
            def _(k, s=s):
                at = pl.ds(pl.multiple_of(k * group_rows, group_rows), group_rows)
                unit, _ = unit_rows(fresh[s, at, :])
                part[s, at, :] = (unit * gain + shift).astype(bf16)

        rows_start(0)

    def weights_wait(start, stop):
        for i in range(start, stop):
            own_copy(i).wait()
            z_copy(i, True).wait_recv()

    kept, used = [], [0]

    def keep(source, target):
        copy = pltpu.make_async_copy(source, target, out_sem.at[used[0]])
        used[0] += 1
        copy.start()
        kept.append(copy)

    def project(k):
        at = pl.ds(k * own_rows, own_rows)

        @pl.loop(0, 3)
        def _(c):
            cut = aligned(c * features, features)
            qkv[at, cut] = (
                jnp.dot(act[at, :], qkv_mat[:, cut], preferred_element_type=f32)
                + qkv_bias[pl.ds(0, 1), cut]
            ).astype(bf16)

    def head_rows():
        for b in range(4):
            at = pl.ds(pl.multiple_of(p.block_place(b) * own_rows, own_rows), own_rows)
            keys[pl.ds(b * own_rows, own_rows), :] = qkv[at, pl.ds(features, features)]
            values[pl.ds(b * own_rows, own_rows), :] = qkv[at, pl.ds(2 * features, features)]

    def attention_block(b):
        at = pl.ds(pl.multiple_of(p.block_place(b) * own_rows, own_rows), own_rows)
        past = pl.ds(0, (b + 1) * own_rows)

        @pl.loop(0, heads)
        def _(head):
            lanes = aligned(head * head_size, head_size)
            probs, top = attention_probs(qkv[at, lanes], keys[past, lanes], b, length)
            attended[at, lanes] = jnp.dot(
                probs.astype(bf16), values[past, lanes], preferred_element_type=f32
            ).astype(bf16)
            live = b * own_rows + lax.broadcasted_iota(jnp.int32, top.shape, 0) < length
            peak = jnp.max(jnp.where(live, top, NEG), 0, keepdims=True)
            row = pl.ds(head, 1)
            peaks[row, :] = jnp.maximum(peaks[row, :], jnp.broadcast_to(peak, (1, peaks.shape[1])))

    sums = RowSum(p, own_rows, arrived, sent, None, sum_send, sum_recv, None, None, None, 1)

    def out_block(k):
        at = pl.ds(k * own_rows, own_rows)

        @pl.loop(0, 4)
        def _(n):
            cut = aligned(n * strip, strip)
            partial[at, cut] = jnp.dot(
                attended[at, :], out_mat[:, cut], preferred_element_type=f32
            ).astype(bf16)

    spot = []

    def keep_resid():
        spot.append(len(kept))
        keep(hidden, resid_out)

    back_sem = [out_sem.at[10], out_sem.at[11]]
    unit_rows_per_chunk = units // pieces

    def back_store(r):
        cut = pl.ds(r * unit_rows_per_chunk, unit_rows_per_chunk)
        return pltpu.make_async_copy(back_stage.at[r % 2], back_out.at[:, cut], back_sem[r % 2])

    def back_chunk(r):
        weights_wait(8 + pieces + r, 9 + pieces + r)
        if r >= 2:
            back_store(r - 2).wait()

        @pl.loop(0, 4)
        def _(b):
            at = pl.ds(pl.multiple_of(b * own_rows, own_rows), own_rows)
            back_stage[r % 2, at, :] = lax.dot_general(
                cot_all[at, :],
                down_all[pl.ds(r * unit_rows_per_chunk, unit_rows_per_chunk), :],
                (((1,), (1,)), ((), ())),
                preferred_element_type=f32,
            ).astype(bf16)

        back_store(r).start()

    def second_norm():
        sums.finish(partial, True)
        kept.pop(spot[0]).wait()
        bias, gain, shift = vector_row(OUT_BIAS), vector_row(GAIN_TWO), vector_row(SHIFT_TWO)

        @pl.loop(0, own_rows // group_rows)
        def _(k):
            at = pl.ds(pl.multiple_of(k * group_rows, group_rows), group_rows)
            value = hidden[at, :] + sums.total(partial, True, at) + bias
            hidden[at, :] = value
            unit, _ = unit_rows(value)
            two[at, :] = (unit * gain + shift).astype(bf16)

        join_start(2)
        keep(hidden, hidden_out)

    def call(function, *arguments):
        return lambda: function(*arguments)

    plan = {}

    def at_step(step, *tasks):
        plan.setdefault(step, []).extend(tasks)

    at_step(0, begin)
    at_step(1, first_norm)
    at_step(5, call(rows_wait, 0), call(join_start, 0), call(rows_start, 1))
    at_step(10, call(rows_start, 2))
    at_step(10, call(rows_wait, 1), call(join_start, 1), call(join_pass, 0))
    at_step(18, call(join_pass, 1))
    at_step(11, call(weights_wait, 0, 6), call(project, 0))
    at_step(12, join(0, 0).wait, call(project, 1), lambda: keep(qkv_mat, qkv_mat_out))
    at_step(13, join(0, 1).wait_send, join(0, 2).wait, call(project, 2), lambda: keep(act, act_out))
    at_step(14, call(project, 3), head_rows, lambda: keep(qkv, qkv_out))
    at_step(15, call(attention_block, 0), call(attention_block, 1))
    at_step(16, call(attention_block, 2))
    at_step(17, call(attention_block, 3), lambda: keep(attended, attended_out))
    at_step(18, call(weights_wait, 6, 8), call(out_block, 3), call(out_block, 1))
    at_step(18, call(sums.start, 0, partial, True))
    at_step(19, call(out_block, 2), *(call(sums.middle, partial, True, part) for part in range(PARTS)))
    at_step(19, call(out_block, 0), lambda: keep(out_mat, out_mat_out))
    at_step(19, call(rows_wait, 2), keep_resid)
    at_step(21, call(join_end, 1), lambda: keep(cot_all, cot_out))
    at_step(23, call(back_chunk, 0))
    at_step(24, second_norm)
    at_step(24, call(back_chunk, 1))
    at_step(25, call(back_chunk, 2))
    at_step(26, call(back_chunk, 3))
    at_step(27, call(join_pass, 2), call(back_chunk, 4))
    lag = 2
    for i in range(count + 2 * lag):
        for k in (0, 1) if i == 0 else (i + 1,):
            if k < count:
                y_copy(k).start()
        if i < count:
            pl.when(even)(lambda i=i: x_copy(i, True).start())
            own_copy(i).start()
        j = i - lag
        if 0 <= j < count:
            y_copy(j).wait_recv()

            @pl.when(even)
            def _(j=j):
                x_copy(j, True).wait_recv()
                z_copy(j, True).start()

            pl.when(odd)(lambda j=j: x_copy(j, False).start())
        j = i - 2 * lag
        if 0 <= j < count:

            @pl.when(odd)
            def _(j=j):
                x_copy(j, False).wait_recv()
                z_copy(j, False).start()

        for task in plan.get(i, ()):
            task()

    for r in range(5, pieces):
        back_chunk(r)
    keep(down_all, down_out)
    join_end(2)
    keep(two, two_out)
    weights_wait(8, 8 + pieces)
    back_store(pieces - 2).wait()
    back_store(pieces - 1).wait()
    for i in range(count):
        y_copy(i).wait_send()
        x_copy(i, True).wait_send()
        z_copy(i, True).wait_send()
    for copy in kept:
        copy.wait()


def forward_all(
    head_size,
    length,
    vectors,
    head_vectors,
    query_weight,
    key_weight,
    value_weight,
    out_weight,
    up_weight,
    down_weight,
    arrived,
    cot,
):
    strip, features, units = query_weight.shape[0], query_weight.shape[1] // 2, up_weight.shape[1] // 2
    width = 4 * strip
    depth, block_rows = arrived.shape[:2]
    own_rows = depth * block_rows
    tokens = 4 * own_rows
    bf16, f32 = jnp.bfloat16, jnp.float32
    hbm = pl.BlockSpec(memory_space=pl.ANY)
    vmem = pl.BlockSpec(memory_space=pltpu.VMEM)
    count = 24
    dma = pltpu.SemaphoreType.DMA

    def made(shape, dtype=bf16):
        return jax.ShapeDtypeStruct(shape, dtype)

    def hold(shape, dtype=bf16):
        return pltpu.VMEM(shape, dtype)

    return pl.pallas_call(
        functools.partial(forward_kernel, head_size),
        out_shape=(
            made((width, 3 * features)),
            made((features, width)),
            made((width, units)),
            made((units, width)),
            made((tokens, width)),
            made((tokens, width)),
            made((tokens, 3 * features)),
            made((tokens, features)),
            made((own_rows, width), f32),
            made((own_rows, width), f32),
            made((tokens, width)),
            made((tokens, units)),
            made((8, width), f32),
            made((8, 128), f32),
        ),
        in_specs=[pl.BlockSpec(memory_space=pltpu.SMEM)] + [hbm] * 10,
        out_specs=(hbm,) * 12 + (vmem,) * 2,
        scratch_shapes=[
            hold((tokens, width)),
            hold((units, width)),
            hold((2, tokens, units // 8)),
            hold((width, 3 * features)),
            hold((features, width)),
            hold((depth, block_rows, width), f32),
            hold((depth, block_rows, width)),
            hold((tokens, width)),
            hold((own_rows, width), f32),
            hold((tokens, 3 * features)),
            hold((tokens, features)),
            hold((tokens, features)),
            hold((tokens, features)),
            hold((tokens, width)),
            hold((3, own_rows, width)),
            hold((own_rows, width)),
            hold((tokens, width)),
            hold((8, strip), f32),
            hold(head_vectors.shape, f32),
            hold((3,) + head_vectors.shape, f32),
            hold((8, 3 * features), f32),
            dma((count,)),
            dma((3, count)),
            dma((3, count)),
            dma((3, depth)),
            dma((3, depth)),
            dma((3, 3)),
            dma((3, 3)),
            dma((2, 3)),
            dma((2, 3)),
            dma((3,)),
            dma((2 + PARTS,)),
            dma((2 + PARTS,)),
            dma((12,)),
        ],
        compiler_params=pltpu.CompilerParams(
            collective_id=0, has_side_effects=True, vmem_limit_bytes=56 << 20
        ),
        cost_estimate=pl.CostEstimate(flops=0, bytes_accessed=64 << 20, transcendentals=0),
    )(
        length,
        vectors,
        head_vectors,
        query_weight,
        key_weight,
        value_weight,
        out_weight,
        up_weight,
        down_weight,
        arrived,
        cot,
    )


def backward_kernel(
    head_size,
    info,
    vector_ref,
    small_in,
    gelu_hbm,
    pre_hbm,
    act_two_hbm,
    up_hbm,
    down_hbm,
    hidden_hbm,
    cot_hbm,
    resid_hbm,
    out_hbm,
    qkv_mat_hbm,
    qkv_hbm,
    attended_hbm,
    act_hbm,
    down_sum,
    up_sum,
    out_sum,
    qkv_sums,
    rows_out,
    rows_grad,
    small,
    two_part,
    mlp_part,
    engine,
    base,
    hidden_grad,
    low,
    out_mat,
    attended_grad,
    qkv,
    qkv_grad,
    act,
    attended,
    qkv_mat,
    keys,
    values,
    key_sum,
    value_sum,
    strips,
    packed,
    arrived,
    sent,
    loaded,
    small_arrived,
    load_sem,
    sum_send,
    sum_recv,
    sum_load,
    join_send,
    join_recv,
    strip_sem,
    row_send,
    row_recv,
    share_send,
    share_recv,
    small_send,
    small_recv,
    core_free,
    y_free,
    low_core,
    low_y,
):
    f32, bf16 = jnp.float32, jnp.bfloat16
    own_rows, width = base.shape
    tokens, features = attended.shape
    heads = features // head_size
    depth = rows_out.shape[0] // 2
    block_rows = rows_out.shape[1]
    p = Place(depth)
    x, y, z, t = p.x, p.y, p.z, p.t
    entry_barrier(
        [p.over_x, p.over_y, p.over_core, p.mate, p.middle, p.hop] + p.row_targets()
    )
    length = info[0]
    scale = 1.0 / math.sqrt(head_size)
    column = 2 * t + y

    rows, cols = engine[0].shape[1:]
    down_rows = down_sum.shape[0] // 2
    up_cols = up_sum.shape[1] // 2
    strip = out_sum.shape[1]

    def over_tokens(left, right, target):
        target[...] = lax.dot_general(
            left, right, (((0,), (0,)), ((), ())), preferred_element_type=f32
        ).astype(target.dtype)

    per_down, per_up = down_rows // strip, up_cols // cols
    strip_count = per_down + per_up

    def strip_load(n):
        source = gelu_hbm if n < per_down else pre_hbm
        cut = pl.ds((n % per_down) * strip, strip)
        return pltpu.make_async_copy(source.at[:, cut], strips.at[n % 2], strip_sem.at[n % 2])

    def resident_load(k):
        source = (cot_hbm, act_two_hbm, act_hbm)[k]
        return pltpu.make_async_copy(source, act, load_sem.at[5])

    def strip_ready(n):
        strip_load(n).wait()
        if n + 1 < strip_count:
            strip_load(n + 1).start()

    def homes_of(far):
        return (p.homes[1], p.homes[3]) if far else (p.homes[0], p.homes[2])

    def down_item(r, far):
        def make(send, own):
            if far and r % 2 == 0:
                if r == 0:
                    resident_load(0).wait()
                strip_ready(r // 2)
            left = strips.at[(r // 2) % 2, :, pl.ds((r % 2) * rows, rows)]
            for home, target in zip(homes_of(far), (send, own)):
                over_tokens(left[...], act[:, aligned(home * strip, strip)], target)

        side = 1 - y if far else y
        return far, down_sum.at[aligned(side * down_rows + r * rows, rows), :], make

    def up_item(c, r, far):
        def make(send, own):
            if far and r == 0:
                if c == 0:
                    resident_load(1).start()
                    resident_load(1).wait()
                strip_ready(per_down + c)
            for home, target in zip(homes_of(far), (send, own)):
                over_tokens(
                    act[:, aligned(home * strip + r * rows, rows)], strips[c % 2], target
                )

        side = 1 - y if far else y
        place = up_sum.at[pl.ds(r * rows, rows), aligned(side * up_cols + c * cols, cols)]
        return far, place, make

    def out_item(r, far):
        def make(send, own):
            for home, target in zip(homes_of(far), (send, own)):
                over_tokens(
                    attended[:, pl.ds(r * rows, rows)], low[:, aligned(home * strip, strip)], target
                )

        side = 1 - y if far else y
        return far, out_sum.at[aligned(side * features + r * rows, rows), :], make

    def qkv_item(r, c, far):
        def make(send, own):
            if far and r == 0 and c == 0:
                resident_load(2).start()
                resident_load(2).wait()
            for home, target in zip(homes_of(far), (send, own)):
                over_tokens(
                    act[:, aligned(home * strip + r * rows, rows)],
                    qkv_grad[:, pl.ds(c * cols, cols)],
                    target,
                )

        side = 1 - y if far else y
        return far, qkv_sums[c].at[pl.ds(r * rows, rows), aligned(side * cols, cols)], make

    sides = (True, False)
    items = [down_item(r, far) for r in range(down_rows // rows) for far in sides]
    items += [up_item(c, r, far) for c in range(per_up) for r in range(strip // rows) for far in sides]
    items += [out_item(r, far) for r in range(features // rows) for far in sides]
    items += [qkv_item(r, c, far) for r in range(strip // rows) for c in range(3) for far in sides]
    run, steps = reduce_stages(p, items, engine)

    loads = [
        pltpu.make_async_copy(source, target, load_sem.at[k])
        for k, (source, target) in enumerate(
            (
                (hidden_hbm, base),
                (cot_hbm.at[pl.ds(0, own_rows), :], packed),
                (out_hbm, out_mat),
                (qkv_hbm, qkv),
                (attended_hbm, attended),
                (cot_hbm, act),
                (qkv_mat_hbm, qkv_mat),
                (resid_hbm, base),
            )
        )
    ]
    sums = RowSum(
        p, own_rows, arrived, sent, loaded, sum_send, sum_recv, sum_load, core_free, y_free, 3
    )
    group_rows = 16
    quarter = own_rows // 4 // group_rows

    def start():
        loads[5].start()
        strip_load(0).start()
        low_load(0).start()
        up_load(0).start()
        for k in (0, 1, 3, 4):
            loads[k].start()
        for n in range(3):
            down_load(n).start()
        small[...] = small_in[...]
        key_sum[...] = jnp.zeros_like(key_sum)
        value_sum[...] = jnp.zeros_like(value_sum)

    def low_load(k):
        return pltpu.make_async_copy((pre_hbm, gelu_hbm)[k], low, load_sem.at[8])

    def up_load(n):
        return pltpu.make_async_copy(up_hbm.at[pl.ds(n * strip, strip), :], out_mat, load_sem.at[9])

    def down_load(n):
        return pltpu.make_async_copy(
            down_hbm.at[:, pl.ds(n * strip, strip)],
            qkv_mat.at[:, pl.ds((n % 3) * strip, strip)],
            load_sem.at[10 + n % 3],
        )

    held = (keys, values)

    def part_store(k, n):
        target = (two_part, mlp_part)[k].at[:, pl.ds(n * strip, strip)]
        return pltpu.make_async_copy(held[n % 2], target, load_sem.at[13 + n % 2])

    def part_columns(k, n):
        if n == 0:
            low_load(k).wait()
        (down_load(n) if k else up_load(n)).wait()
        if n >= 2:
            part_store(k, n - 2).wait()

        @pl.loop(0, 4)
        def _(b):
            at = pl.ds(pl.multiple_of(b * own_rows, own_rows), own_rows)
            if k:
                right, side = qkv_mat[:, pl.ds((n % 3) * strip, strip)], 0
            else:
                right, side = out_mat[...], 1
            held[n % 2][at, :] = lax.dot_general(
                low[at, :], right, (((1,), (side,)), ((), ())), preferred_element_type=f32
            ).astype(bf16)

        part_store(k, n).start()
        if k == 0 and n < 3:
            up_load(n + 1).start()
        if k == 0 and n == 3:
            low_load(1).start()
            loads[2].start()
        if k == 1 and n == 0:
            down_load(3).start()
        if k == 1 and n == 3:
            loads[6].start()

    def part_end(k):
        part_store(k, 2).wait()
        part_store(k, 3).wait()
        if k == 0:
            sums.start(0, two_part, False)
        else:
            grant(low_core, p.over_core)
            grant(low_y, p.over_y)

    def two_middle(part):
        sums.middle(two_part, False, part)

    def two_finish():
        sums.finish(two_part, False)
        loads[0].wait()
        loads[1].wait()

    def accumulate(row, value):
        small[pl.ds(row, 1), :] += jnp.sum(value, 0, keepdims=True)

    def two_rows(part):
        gain = vector_ref[pl.ds(GAIN_TWO, 1), :]

        @pl.loop(part * quarter, (part + 1) * quarter)
        def _(k):
            at = pl.ds(pl.multiple_of(k * group_rows, group_rows), group_rows)
            upstream = sums.total(two_part, False, at)
            unit, inverse = unit_rows(base[at, :])
            grad = packed[at, :].astype(f32) + unit_back(upstream, unit, inverse, gain)
            hidden_grad[at, :] = grad
            low[at, :] = grad.astype(bf16)
            accumulate(GAIN_TWO, upstream * unit)
            accumulate(SHIFT_TWO, upstream)
            accumulate(OUT_BIAS, grad)

    def low_block(k):
        return low.at[pl.ds(k * own_rows, own_rows), :]

    def join(k):
        source, place = ((0, 1), (None, None), (2, 3))[k]
        return remote_copy(
            low_block(source), low_block(place), join_send.at[k], join_recv.at[k], p.over_core
        )

    def join_y(part):
        size = own_rows // PARTS
        return remote_copy(
            low.at[pl.ds(part * size, size), :],
            low.at[pl.ds(2 * own_rows + part * size, size), :],
            join_send.at[3 + part],
            join_recv.at[3 + part],
            p.over_y,
        )

    def join_start():
        pl.semaphore_wait(low_core, 1)
        pl.semaphore_wait(low_y, 1)
        join(0).start()
        join_y(0).start()
        sums.release(0)

    def join_pass():
        for part in range(PARTS):
            join_y(part).wait_recv()
        join(2).start()

    def attend_block(k):
        at = pl.ds(k * own_rows, own_rows)
        attended_grad[at, :] = lax.dot_general(
            low[at, :], out_mat[...], (((1,), (1,)), ((), ())), preferred_element_type=f32
        ).astype(bf16)

    def attend_own():
        loads[2].wait()
        attend_block(0)

    def attend_peer():
        join(0).wait()
        attend_block(1)

    def attend_far():
        attend_block(2)

    def attend_last():
        for part in range(PARTS):
            join_y(part).wait_send()
        join(2).wait()
        attend_block(3)

    def mlp_start():
        sums.start(1, mlp_part, False)

    def mlp_middle(part):
        sums.middle(mlp_part, False, part)

    def mlp_finish():
        sums.finish(mlp_part, False)
        bias = vector_ref[pl.ds(DOWN_BIAS, 1), :]

        @pl.loop(0, own_rows // group_rows)
        def _(k):
            at = pl.ds(pl.multiple_of(k * group_rows, group_rows), group_rows)
            packed[at, :] = (base[at, :] + sums.total(mlp_part, False, at) + bias).astype(bf16)

        sums.release(1)

    def row_source(k):
        return packed.at[pl.ds(pl.multiple_of(k * block_rows, block_rows), block_rows), :]

    row_ends = (rows_out, rows_grad)

    def row_copy(a, k):
        end = row_ends[a].at[x * depth + z]
        return remote_copy(row_source(k), end, row_send.at[a, k], row_recv.at[a, z], p.row_target(k))

    def row_arrival(a, k):
        end = row_ends[a].at[t * depth + k]
        return remote_copy(row_source(k), end, row_send.at[a, k], row_recv.at[a, k], p.row_target(k))

    def row_stay(a, k):
        return pltpu.make_async_copy(row_source(k), row_ends[a].at[x * depth + z], row_send.at[a, k])

    def rows_start(a, turn):
        k = lax.rem(z + turn, depth)
        if turn:
            row_copy(a, k).start()
        else:
            pl.when(x == t)(lambda: row_stay(a, k).start())
            pl.when(x != t)(lambda: row_copy(a, k).start())

    def share(a):
        group = row_ends[a].at[pl.ds(t * depth, depth)]
        return remote_copy(group, group, share_send.at[a], share_recv.at[a], p.over_core)

    def rows_share(a):
        for k in range(depth):
            stays = (z == k) & (x == t)
            pl.when(stays)(lambda k=k: row_stay(a, k).wait())

            @pl.when(jnp.logical_not(stays))
            def _(k=k):
                row_copy(a, k).wait_send()
                row_arrival(a, k).wait_recv()

        share(a).start()

    def head_rows():
        loads[3].wait()
        loads[4].wait()
        for block in range(4):
            at = pl.ds(pl.multiple_of(p.block_place(block) * own_rows, own_rows), own_rows)
            keys[pl.ds(block * own_rows, own_rows), :] = qkv[at, pl.ds(features, features)]
            values[pl.ds(block * own_rows, own_rows), :] = qkv[at, pl.ds(2 * features, features)]

    def attention_block(block):
        at = pl.ds(pl.multiple_of(p.block_place(block) * own_rows, own_rows), own_rows)
        part = pl.ds(0, (block + 1) * own_rows)

        @pl.loop(0, heads)
        def _(head):
            lanes = aligned(head * head_size, head_size)
            queries, grads = qkv[at, lanes], attended_grad[at, lanes]
            probs, _ = attention_probs(queries, keys[part, lanes], block, length)
            prob_grad = lax.dot_general(
                grads, values[part, lanes], (((1,), (1,)), ((), ())), preferred_element_type=f32
            )
            inner = jnp.sum(probs * prob_grad, -1, keepdims=True)
            score_grad = (probs * (prob_grad - inner)).astype(bf16)
            query_grad = (
                jnp.dot(score_grad, keys[part, lanes], preferred_element_type=f32) * scale
            )
            spot = aligned(column * features + head * head_size, head_size)
            small[pl.ds(QUERY_BIAS, 1), spot] += jnp.sum(query_grad, 0, keepdims=True)
            qkv_grad[at, lanes] = query_grad.astype(bf16)
            key_sum[part, lanes] += lax.dot_general(
                score_grad, queries, (((0,), (0,)), ((), ())), preferred_element_type=f32
            )
            value_sum[part, lanes] += lax.dot_general(
                probs.astype(bf16), grads, (((0,), (0,)), ((), ())), preferred_element_type=f32
            )

    def attention_end(block):
        at = pl.ds(pl.multiple_of(p.block_place(block) * own_rows, own_rows), own_rows)
        part = pl.ds(block * own_rows, own_rows)
        qkv_grad[at, pl.ds(features, features)] = (key_sum[part, :] * scale).astype(bf16)
        value_grad = value_sum[part, :]
        qkv_grad[at, pl.ds(2 * features, features)] = value_grad.astype(bf16)
        spot = aligned(column * features, features)
        small[pl.ds(VALUE_BIAS, 1), spot] += jnp.sum(value_grad, 0, keepdims=True)

    def one_block(k):
        if k == 3:
            loads[6].wait()
        at = pl.ds(k * own_rows, own_rows)

        @pl.loop(0, 4)
        def _(n):
            cut = aligned(n * strip, strip)
            low[at, cut] = lax.dot_general(
                qkv_grad[at, :], qkv_mat[cut, :], (((1,), (1,)), ((), ())), preferred_element_type=f32
            ).astype(bf16)

    def one_start():
        sums.start(2, low, True)

    def one_middle(part):
        sums.middle(low, True, part)

    def one_finish():
        sums.finish(low, True)
        loads[7].wait()

    def one_rows(part):
        gain = vector_ref[pl.ds(GAIN_ONE, 1), :]

        @pl.loop(part * quarter, (part + 1) * quarter)
        def _(k):
            at = pl.ds(pl.multiple_of(k * group_rows, group_rows), group_rows)
            upstream = sums.total(low, True, at)
            unit, inverse = unit_rows(base[at, :])
            grad = hidden_grad[at, :] + unit_back(upstream, unit, inverse, gain)
            packed[at, :] = grad.astype(bf16)
            accumulate(GAIN_ONE, upstream * unit)
            accumulate(SHIFT_ONE, upstream)

    def small_copy(k):
        target = (p.over_core, p.over_x, p.over_y, p.mate, p.hop)[k]
        return remote_copy(small, small_arrived.at[k], small_send.at[k], small_recv.at[k], target)

    def small_add(k):
        small_copy(k).wait()
        mine, other = small[...], small_arrived[k]
        row = lax.broadcasted_iota(jnp.int32, mine.shape, 0)
        small[...] = jnp.where(row == PEAKS, jnp.maximum(mine, other), mine + other)

    def call(function, *arguments):
        return lambda: function(*arguments)

    plan = {}

    def at_step(step, *tasks):
        plan.setdefault(step, []).extend(tasks)

    for n in range(4):
        at_step(n, call(part_columns, 0, n))
        at_step(5 + 2 * n, call(part_columns, 1, n))
    at_step(4, call(part_end, 0))
    at_step(13, call(part_end, 1))
    for k in range(4):
        at_step(7 + k, call(two_middle, k))
    at_step(16, two_finish, call(two_rows, 0))
    for k in range(1, 4):
        at_step(16 + k // 2, call(two_rows, k))
    at_step(17, join_start)
    for k in range(1, 4):
        at_step(17 + k, join_y(k).start)
    at_step(18, attend_own)
    at_step(19, attend_peer)
    at_step(21, head_rows)
    at_step(24, join_pass)
    at_step(25, attend_far)
    at_step(26, attend_last)
    at_step(27, call(attention_block, 0), call(attention_block, 1))
    at_step(27 + 1, call(attention_block, 2))
    at_step(27 + 2, call(attention_block, 3))
    at_step(27 + 3, *(call(attention_end, k) for k in range(4)))
    at_step(21, mlp_start)
    for k in range(4):
        at_step(23 + 1 * k, call(mlp_middle, k))
    at_step(33, mlp_finish, loads[7].start, call(rows_start, 0, 0))
    for k in range(1, 4):
        at_step(33 + k, call(rows_start, 0, k))
    at_step(42, lambda: rows_share(0))
    at_step(36, call(one_block, 3), call(one_block, 1), one_start)
    at_step(36 + 1, call(one_block, 2), call(one_block, 0))
    for k in range(4):
        at_step(38 + k, call(one_middle, k))
    at_step(47, one_finish, share(0).wait, call(one_rows, 0))
    for k in range(1, 4):
        at_step(47 + k // 2, call(one_rows, k))
    for k in range(4):
        at_step(48 + k, call(rows_start, 1, k))
    at_step(49, small_copy(0).start)
    for k in range(4):
        at_step(49 + 2 + 2 * k, call(small_add, k), small_copy(k + 1).start)
    at_step(49 + 5 * 2, call(small_add, 4))
    at_step(57, lambda: rows_share(1))
    at_step(59, share(1).wait)
    start()
    for step in range(steps):
        run(step)
        for task in plan.get(step, ()):
            task()


def backward_all(
    head_size,
    length,
    vectors,
    small,
    gelu_low,
    pre_low,
    act_two,
    up_mat,
    down_mat,
    hidden,
    cot_low,
    resid,
    out_mat,
    qkv_mat,
    qkv,
    attended,
    act_one,
    slots,
):
    bf16, f32 = jnp.bfloat16, jnp.float32
    hbm = pl.BlockSpec(memory_space=pl.ANY)
    vmem = pl.BlockSpec(memory_space=pltpu.VMEM)
    down_rows, up_cols = gelu_low.shape[1], pre_low.shape[1]
    tokens, features = attended.shape
    own_rows, width = hidden.shape
    strip = width // 4
    depth = slots // 2
    engine = reduce_scratch(6, 4, 256, 512)
    n_engine = len(engine)

    def kernel(*refs):
        ins, rest = refs[:16], refs[16:]
        outs, scratch = rest[:11], rest[11:]
        backward_kernel(
            head_size,
            *ins,
            outs[0],
            outs[1],
            outs[2],
            outs[3:6],
            *outs[6:],
            scratch[:n_engine],
            *scratch[n_engine:],
        )

    dma, regular = pltpu.SemaphoreType.DMA, pltpu.SemaphoreType.REGULAR

    def hold(shape, dtype=bf16):
        return pltpu.VMEM(shape, dtype)

    return pl.pallas_call(
        kernel,
        out_shape=(
            jax.ShapeDtypeStruct((2 * down_rows, strip), bf16),
            jax.ShapeDtypeStruct((strip, 2 * up_cols), bf16),
            jax.ShapeDtypeStruct((2 * features, strip), bf16),
            jax.ShapeDtypeStruct((strip, 2 * features), bf16),
            jax.ShapeDtypeStruct((strip, 2 * features), bf16),
            jax.ShapeDtypeStruct((strip, 2 * features), bf16),
            jax.ShapeDtypeStruct((slots, own_rows // depth, width), bf16),
            jax.ShapeDtypeStruct((slots, own_rows // depth, width), bf16),
            jax.ShapeDtypeStruct(small.shape, f32),
            jax.ShapeDtypeStruct((tokens, width), bf16),
            jax.ShapeDtypeStruct((tokens, width), bf16),
        ),
        in_specs=[pl.BlockSpec(memory_space=pltpu.SMEM), vmem, vmem] + [hbm] * 13,
        out_specs=(hbm,) * 8 + (vmem,) + (hbm,) * 2,
        scratch_shapes=engine
        + [
            hold((own_rows, width), f32),
            hold((own_rows, width), f32),
            hold((tokens, width)),
            hold((features, width)),
            hold((tokens, features)),
            hold((tokens, 3 * features)),
            hold((tokens, 3 * features)),
            hold((tokens, width)),
            hold((tokens, features)),
            hold((width, 3 * features)),
            hold((tokens, features)),
            hold((tokens, features)),
            hold((tokens, features), f32),
            hold((tokens, features), f32),
            hold((2, tokens, strip)),
            hold((own_rows, width)),
            hold((3, own_rows, width)),
            hold((own_rows, width)),
            hold((own_rows, width)),
            hold((5,) + small.shape, f32),
            dma((15,)),
            dma((2 + PARTS,)),
            dma((2 + PARTS,)),
            dma(()),
            dma((3 + PARTS,)),
            dma((3 + PARTS,)),
            dma((2,)),
            dma((2, depth)),
            dma((2, depth)),
            dma((2,)),
            dma((2,)),
            dma((5,)),
            dma((5,)),
            regular,
            regular,
            regular,
            regular,
        ],
        compiler_params=pltpu.CompilerParams(
            collective_id=1, has_side_effects=True, vmem_limit_bytes=60 << 20
        ),
        cost_estimate=pl.CostEstimate(flops=0, bytes_accessed=64 << 20, transcendentals=0),
    )(
        length,
        vectors,
        small,
        gelu_low,
        pre_low,
        act_two,
        up_mat,
        down_mat,
        hidden,
        cot_low,
        resid,
        out_mat,
        qkv_mat,
        qkv,
        attended,
        act_one,
    )


def split_body(
    layer_input,
    cotangent,
    seq_lengths,
    dealing,
    attn_gain,
    attn_shift,
    query_weight,
    query_bias,
    key_weight,
    value_weight,
    value_bias,
    out_weight,
    out_bias,
    mlp_gain,
    mlp_shift,
    up_weight,
    up_bias,
    down_weight,
    down_bias,
    clip_level,
):
    f32, bf16 = jnp.float32, jnp.bfloat16
    f = lax.axis_index("fsdp")
    z = lax.axis_index("ctx")
    t = lax.axis_index("tp")
    y, x = f // 2, f % 2
    depth = lax.axis_size("ctx")
    slots, block_rows, width = layer_input.shape
    local_heads = query_bias.shape[0] // 2
    head_size = 4 * query_bias.shape[1]
    features = local_heads * head_size
    hidden_units = up_weight.shape[1] // 2
    strip = query_weight.shape[0]
    own_rows = depth * block_rows

    place = jnp.stack([t, x * depth + z])
    arrived, cot_part, down_bias_part, length = prepare(
        dealing, seq_lengths, place, layer_input, cotangent, depth
    )
    vectors = jnp.concatenate(
        [attn_gain, attn_shift, out_bias, mlp_gain, mlp_shift, down_bias, up_bias.reshape(-1)]
    )
    vectors = vectors.reshape(8, strip).astype(f32)
    head_vectors = jnp.concatenate([query_bias, value_bias], 0).astype(f32)
    head_vectors = lax.dynamic_update_slice(
        jnp.zeros((head_vectors.shape[0], head_size), f32), head_vectors, (0, f * query_bias.shape[1])
    )
    (
        qkv_mat,
        out_mat,
        up_mat,
        down_mat,
        act_one,
        cot_low,
        qkv,
        attended,
        hidden,
        resid,
        act_two,
        back,
        vectors_whole,
        peaks,
    ) = forward_all(
        head_size,
        length,
        vectors,
        head_vectors,
        query_weight,
        key_weight,
        value_weight,
        out_weight,
        up_weight,
        down_weight,
        arrived,
        cot_part,
    )
    peaks = peaks[:local_heads, 0]
    up_vec = lax.dynamic_slice_in_dim(vectors_whole, 6 + y, 1, 0)

    pre = matmul(act_two, up_mat) + up_vec
    cdf = 0.5 * (1.0 + lax.erf(pre * INV_ROOT_TWO))
    gelu_low = (pre * cdf).astype(bf16)
    slope = cdf + pre * (jnp.exp(-0.5 * pre * pre) * INV_ROOT_TWO_PI)
    pre_grad = back.astype(f32) * slope
    pre_low = pre_grad.astype(bf16)
    up_bias_part = jnp.sum(pre_grad, 0)
    column = 2 * t + y
    small = jnp.zeros((16, width), f32).at[DOWN_BIAS].set(down_bias_part[0])
    small = lax.dynamic_update_slice(small, up_bias_part[None], (UP_BIAS + column, 0))
    small = small.at[PEAKS].set(NEG)
    small = lax.dynamic_update_slice(small, peaks[None], (PEAKS, local_heads * (2 * t + y)))
    (
        down_sum,
        up_sum,
        out_sum,
        query_sum,
        key_sum,
        value_sum,
        rows_out,
        rows_grad,
        totals,
        _,
        _,
    ) = backward_all(
        head_size,
        length,
        vectors_whole,
        small,
        gelu_low,
        pre_low,
        act_two,
        up_mat,
        down_mat,
        hidden,
        cot_low,
        resid,
        out_mat,
        qkv_mat,
        qkv,
        attended,
        act_one,
        slots,
    )
    rows_sum = lax.dynamic_slice(totals, (0, f * strip), (6, strip))
    head_sum = lax.dynamic_slice(totals, (QUERY_BIAS, 2 * t * features), (2, 2 * features))
    head_sum = head_sum.reshape(2, 2 * local_heads, head_size)
    head_sum = lax.dynamic_slice_in_dim(head_sum, f * query_bias.shape[1], query_bias.shape[1], 2)
    unit_sum = lax.dynamic_slice(
        totals, (UP_BIAS + up_bias.shape[0] * t, f * strip), (up_bias.shape[0], strip)
    )
    peak_all = lax.dynamic_slice(totals, (PEAKS, 2 * local_heads * t), (1, 2 * local_heads))[0]
    (
        final_output,
        final_grad,
        query_weight_grad,
        key_weight_grad,
        value_weight_grad,
        out_weight_grad,
        up_weight_grad,
        down_weight_grad,
        query_clipped,
        key_clipped,
    ) = finish_all(
        head_size,
        place,
        clip_level,
        totals,
        query_weight,
        key_weight,
        (rows_out, rows_grad, query_sum, key_sum, value_sum, out_sum, up_sum, down_sum),
    )
    return (
        final_output,
        final_grad,
        rows_sum[GAIN_ONE],
        rows_sum[SHIFT_ONE],
        query_weight_grad,
        head_sum[0],
        key_weight_grad,
        value_weight_grad,
        head_sum[1],
        out_weight_grad,
        rows_sum[OUT_BIAS],
        rows_sum[GAIN_TWO],
        rows_sum[SHIFT_TWO],
        up_weight_grad,
        unit_sum,
        down_weight_grad,
        rows_sum[DOWN_BIAS],
        peak_all,
        query_clipped,
        key_clipped,
    )


def solution(mesh):
    sizes = dict(mesh.shape)
    small_slice = sizes == {"fsdp": 4, "ctx": 4, "tp": 2}
    return jax.shard_map(
        split_body if small_slice else gathered_body,
        mesh=mesh,
        in_specs=(
            P(None, ("fsdp", "ctx"), None),
            P(None, ("fsdp", "ctx"), None),
            P(),
            P(),
            P("fsdp"),
            P("fsdp"),
            P("fsdp", "tp"),
            P("tp", "fsdp"),
            P("fsdp", "tp"),
            P("fsdp", "tp"),
            P("tp", "fsdp"),
            P("tp", "fsdp"),
            P("fsdp"),
            P("fsdp"),
            P("fsdp"),
            P("fsdp", "tp"),
            P("tp", "fsdp"),
            P("tp", "fsdp"),
            P("fsdp"),
            P(),
        ),
        out_specs=(
            P(None, ("fsdp", "ctx"), None),
            P(None, ("fsdp", "ctx"), None),
            P("fsdp"),
            P("fsdp"),
            P("fsdp", "tp"),
            P("tp", "fsdp"),
            P("fsdp", "tp"),
            P("fsdp", "tp"),
            P("tp", "fsdp"),
            P("tp", "fsdp"),
            P("fsdp"),
            P("fsdp"),
            P("fsdp"),
            P("fsdp", "tp"),
            P("tp", "fsdp"),
            P("tp", "fsdp"),
            P("fsdp"),
            P("tp"),
            P("fsdp", "tp"),
            P("fsdp", "tp"),
        ),
        check_vma=False,
    )
```
